32 devices in a mesh: sys: 2 (over y), row: 4 (over z), col: 4 (over x, core).
Axes of the slice: x: 2, y: 2, z: 4, core: 2. Of those that a mesh axis runs over, the one named last changes fastest.
Arguments:
- a_blocks: bfloat16 [8, 64, 4096], P(('sys', 'row'), 'col'), parts along dimension 0, may hold values from -0.75 to 0.75
- a_index: int32 [2, 8, 64], P(None, ('sys', 'row'), 'col'), parts along dimension 1, may hold values from -1 to 15, as said below
- b_blocks: bfloat16 [128, 16, 4096], P(('sys', 'row'), 'col'), parts along dimension 0, may hold values from -4 to 4
- b_cols: int32 [128, 16], P(('sys', 'row'), 'col'), parts along dimension 0, may hold values from -1 to 15, as said below
- c_cols: int32 [128, 16], P(('sys', 'row'), 'col'), parts along dimension 0, may hold values from 0 to 15, as said below
Outputs:
- c_blocks: float32 [128, 16, 4096], P(('sys', 'row'), 'col'), parts along dimension 0
The draws below stay inside these ranges and needn't reach their ends.
There are 2 independent parts, one for each index of `sys`. The reference program is written for one: setup_inputs(seed, part) draws one part's arguments, and reference() takes and returns one part's arrays. A program takes and returns all parts, laid end to end along the dimension named above; each array names one. Nothing has to cross between parts.
Inputs may be any that keep to these rules, and one draw needn't show every extreme that they name: a_index[0] is -1 for an empty slot; the live slots of one entry (p, g) name distinct blocks; some entry has all 16 slots live and some entry only one. `b_cols`: -1 marks an empty slot; the live entries of one block row within one column group are distinct; some block row has all 4 slots of a column group live and some only one. `c_cols`: the 4 entries of one block row within one column group are distinct.
All inputs are finite; a program needn't handle non-finite values.
Results may differ from the reference program's by a relative error of at most 0.0003.
Values may be sent and summed in bfloat16 or wider, within the bound.
No kernel may reach another device: no remote copies, remote signals or barrier semaphores. Data moves between devices by JAX's collectives and lax.ppermute only.
A program may use at most 64 MiB of HBM per device.

```python
from functools import partial
import jax
import jax.numpy as jnp
from jax import lax

BS = 64
RB = 16
SA = 16
NZB = 4
NZC = 4
GROUPS = 4
NB = 64
CB = 16
N_COL = 4


def live_counts(key, total, most):
    counts = jax.random.randint(key, (total,), 1, most + 1)
    first = jax.random.randint(jax.random.fold_in(key, 1), (), 0, total)
    second = (first + 1 + jax.random.randint(jax.random.fold_in(key, 2), (), 0, total - 1)) % total
    counts = counts.at[first].set(most)
    return counts.at[second].set(1)


def chosen_columns(key, total, span, taken):
    keys = jax.random.split(key, total)
    return jax.vmap(lambda single: jax.random.permutation(single, span)[:taken])(keys)


def draw_a_index(key, part):
    key = jax.random.fold_in(key, 3)
    places = chosen_columns(jax.random.fold_in(key, 4), GROUPS * GROUPS, RB * RB, SA)
    counts = live_counts(jax.random.fold_in(key, 5), GROUPS * GROUPS, SA)
    living = jnp.arange(SA)[None, :] < counts[:, None]
    block_rows = jnp.where(living, places // RB, -1)
    inner_cols = places % RB
    return jnp.stack([block_rows, inner_cols]).reshape(2, GROUPS, GROUPS * SA).astype(jnp.int32)


def draw_b_cols(key, part):
    key = jax.random.fold_in(key, 7)
    places = chosen_columns(jax.random.fold_in(key, 8), NB * N_COL, CB, NZB)
    counts = live_counts(jax.random.fold_in(key, 9), NB * N_COL, NZB)
    living = jnp.arange(NZB)[None, :] < counts[:, None]
    return jnp.where(living, places, -1).reshape(NB, N_COL * NZB).astype(jnp.int32)


def draw_c_cols(key, part):
    key = jax.random.fold_in(key, 13)
    places = chosen_columns(jax.random.fold_in(key, 14), NB * N_COL, CB, NZC)
    return places.reshape(NB, N_COL * NZC).astype(jnp.int32)


def block_levels(key, dims, cuts, smallest, largest):
    def one(axis_at, shards_of):
        draws = jax.random.uniform(jax.random.fold_in(jax.random.fold_in(key, 6), axis_at), (shards_of,), jnp.float32, smallest / len(cuts), largest / len(cuts))
        return jnp.repeat(jnp.exp(draws), dims[axis_at] // shards_of).reshape((-1,) + (1,) * (len(dims) - axis_at - 1))

    level = one(*cuts[0])
    for cut in cuts[1:]:
        level = level * one(*cut)
    return level


def scatter_about(stream_key, extent, deviation, reach, cuts=(), held_as=jnp.bfloat16):
    result = jax.random.normal(stream_key, extent, jnp.float32) * deviation
    if len(cuts) > 0:
        result = block_levels(stream_key, extent, cuts, -0.22, 0.18) * result
    return jnp.clip(result, min=-reach, max=reach).astype(held_as)


def setup_inputs(seed: int = 0, part: int = 0) -> dict:
    key_of = jax.random.split(jax.random.key(seed), 6)
    own_keys = jax.random.split(jax.random.fold_in(key_of[5], part), 6)
    return {
        "a_blocks": scatter_about(own_keys[0], (GROUPS, GROUPS * SA, BS * BS), BS ** -0.5, 0.75, ((0, 4), (1, 4))),
        "a_index": draw_a_index(jax.random.fold_in(jax.random.fold_in(key_of[5], part), 71), part),
        "b_blocks": scatter_about(own_keys[2], (NB, N_COL * NZB, BS * BS), 0.6, 4.0, ((0, 4), (1, 4))),
        "b_cols": draw_b_cols(jax.random.fold_in(jax.random.fold_in(key_of[5], part), 71), part),
        "c_cols": draw_c_cols(jax.random.fold_in(jax.random.fold_in(key_of[5], part), 71), part),
    }


def block_terms(a_values, a_rows, a_inner, b_values, b_columns, c_columns):
    safe_rows = jnp.maximum(a_rows, 0)
    wanted = c_columns[safe_rows]
    offered = b_columns[a_inner]
    matches = wanted[:, :, None] == offered[:, None, :]
    located = jnp.any(matches, axis=2) & (a_rows >= 0)[:, None]
    position = jnp.sum(jnp.where(matches, jnp.arange(NZB, dtype=jnp.int32), 0), axis=2).astype(jnp.int32)
    flat_index = (a_inner[:, None] * NZB + position).astype(jnp.int32)
    picked = b_values.reshape(RB * NZB, BS * BS)[flat_index].astype(jnp.float32)
    picked = jnp.where(located[:, :, None], picked, jnp.zeros((), picked.dtype))
    left_blocks = a_values.reshape(SA, BS, BS).astype(jnp.float32)
    products = jnp.einsum("sxj,smjk->smxk", left_blocks, picked.reshape(SA, NZC, BS, BS))
    target = jnp.where(a_rows >= 0, a_rows, RB).astype(jnp.int32)
    return jax.ops.segment_sum(products, target, num_segments=RB + 1)[:RB]


def reference(a_blocks, a_index, b_blocks, b_cols, c_cols):
    a_values = a_blocks.reshape(GROUPS, GROUPS, SA, BS * BS)
    a_rows = a_index[0].reshape(GROUPS, GROUPS, SA)
    a_inner = a_index[1].reshape(GROUPS, GROUPS, SA)
    b_values = b_blocks.reshape(GROUPS, RB, N_COL, NZB, BS * BS)
    b_columns = b_cols.reshape(GROUPS, RB, N_COL, NZB)
    c_columns = c_cols.reshape(GROUPS, RB, N_COL, NZC)

    def one_row(grid_row):
        def one_group(running, k_group):
            single = partial(block_terms, a_values[grid_row, k_group], a_rows[grid_row, k_group], a_inner[grid_row, k_group])
            block_sums = jax.vmap(single, in_axes=(1, 1, 1))(b_values[k_group], b_columns[k_group], c_columns[grid_row])
            return running + block_sums, None

        initial = jnp.zeros((N_COL, RB, NZC, BS, BS), jnp.float32)
        running, unused = lax.scan(one_group, initial, jnp.arange(GROUPS, dtype=jnp.int32))
        return running

    rows_out = lax.map(one_row, jnp.arange(GROUPS, dtype=jnp.int32))
    return jnp.transpose(rows_out, (0, 2, 1, 3, 4, 5)).reshape(NB, N_COL * NZC, BS * BS)
```

```python
import functools

import jax
import jax.numpy as jnp
from jax import lax
from jax.experimental import pallas as pl
from jax.experimental.pallas import tpu as pltpu
from jax.sharding import PartitionSpec as P

BS = 64
LANES = 128
ROWS = BS * BS // LANES
CAPACITY = 16
UNROLL = 4
IDLE = 63
VMEM = pltpu.VMEM
SMEM = pltpu.SMEM
BF16 = jnp.bfloat16
F32 = jnp.float32
I32 = jnp.int32


def shifted(block, axis, distance):
    size = lax.axis_size(axis)
    route = [(i, (i + distance) % size) for i in range(size)]
    return lax.ppermute(block, axis, route)


def prepare_kernel(a_ref, b_ref, a_out, b_out, a_wide, b_wide):
    source = lax.broadcasted_iota(I32, (LANES, LANES), 0)
    target = lax.broadcasted_iota(I32, (LANES, LANES), 1)
    wanted = (target // BS) * BS + 2 * (target % ROWS) + (target // ROWS) % 2
    order = (source == wanted).astype(BF16)
    for t in range(ROWS):
        piece = a_ref[0, :, pl.ds(t * LANES, LANES)]
        a_wide[:, t, :] = jnp.dot(piece, order, preferred_element_type=F32)
    a_out[...] = a_wide[...].astype(BF16)
    row_count, slots = b_ref.shape[0], b_ref.shape[1]

    def one_row(k, carry):
        for t in range(ROWS):
            b_wide[pl.ds(t * slots, slots), :] = b_ref[k, :, pl.ds(t * LANES, LANES)].astype(F32)
        for n in range(slots):
            b_out[k * slots + n] = b_wide[pl.ds(n, ROWS, stride=slots), :].astype(BF16)
        return carry

    lax.fori_loop(0, row_count, one_row, 0)


def prepare(a_blocks, b_blocks):
    slots = a_blocks.shape[1]
    blocks = b_blocks.shape[0] * b_blocks.shape[1]
    return pl.pallas_call(
        prepare_kernel,
        out_shape=(
            jax.ShapeDtypeStruct((slots, ROWS, LANES), BF16),
            jax.ShapeDtypeStruct((blocks, ROWS, LANES), BF16),
        ),
        in_specs=[pl.BlockSpec(memory_space=VMEM)] * 2,
        out_specs=(pl.BlockSpec(memory_space=VMEM),) * 2,
        scratch_shapes=[
            VMEM((slots, ROWS, LANES), F32),
            VMEM((b_blocks.shape[1] * ROWS, LANES), F32),
        ],
        compiler_params=pltpu.CompilerParams(vmem_limit_bytes=24 << 20),
        cost_estimate=pl.CostEstimate(flops=1 << 24, bytes_accessed=2 << 20, transcendentals=0),
        name="prepare",
    )(a_blocks, b_blocks)


def offered_hits(i, wanted, offered):
    kept = [wanted(m, i) for m in range(len(offered[1]))]
    return [functools.reduce(jnp.logical_or, [o == w for w in kept]) for o in offered[0]], kept


def fetch(copies, sems):
    started = [
        pltpu.make_async_copy(source, target, sems.at[at])
        for at, (source, target) in enumerate(copies)
    ]
    for copy in started:
        copy.start()
    for copy in started:
        copy.wait()


def pack_kernel(first, peers, per_col, *refs):
    refs = list(refs)
    base_ref = None if first else refs.pop(0)
    c_refs = [refs.pop(0) for _ in range(peers)]
    a_refs = [refs.pop(0) for _ in range(peers)]
    b_cols, blocks = refs.pop(0), refs.pop(0)
    outs = [refs.pop(0) for _ in range(peers - 1)]
    most = refs.pop(0)
    c_s, a_s, b_s, chosen, seen, sems = refs
    row_count, slots = b_cols.shape[1], b_cols.shape[0]
    kept, a_slots = c_refs[0].shape[0], a_refs[0].shape[2]
    copies = [(c_refs[d], c_s.at[d]) for d in range(1, peers)]
    copies += [(a_refs[d], a_s.at[d]) for d in range(peers)]
    copies += [(b_cols, b_s)]
    fetch(copies, sems)
    base = 0 if first else base_ref[0]
    col_count = peers // per_col
    grid_row = lax.axis_index("row")
    grid_col = lax.axis_index("col")
    turn = grid_row % per_col * col_count + grid_col
    top = 0
    for d in range(1, peers):
        place = (turn - grid_row + d + peers) % peers
        for k in range(row_count):
            seen[k] = 0

        def one_slot(s, count, d=d, place=place):
            i = a_s[place, 0, 0, s]
            k = jnp.maximum(a_s[place, 1, 0, s], 0)
            safe = jnp.maximum(i, 0)
            kept_cols = [c_s[d, m, safe] for m in range(kept)]
            before = seen[k]
            after = before
            for n in range(slots):
                column = b_s[n, k]
                hit = functools.reduce(jnp.logical_or, [column == c for c in kept_cols])
                hit = hit & (i >= 0)
                fresh = hit & ((before >> n) & 1 == 0)
                chosen[count] = k * slots + n
                count = count + fresh.astype(I32)
                after = after | (hit.astype(I32) << n)
            seen[k] = after
            return count

        count = lax.fori_loop(0, a_slots, one_slot, jnp.int32(0))
        for x in range(outs[d - 1].shape[0]):
            index = jnp.where(base + x < count, chosen[base + x], 0)
            outs[d - 1][x] = blocks[index]
        top = jnp.maximum(top, count)
    most[0] = top


def pack(base, c_parts, a_parts, b_cols, blocks, per_col):
    peers = len(c_parts)
    slots, row_count = b_cols.shape
    first = base is None
    any_spec = pl.BlockSpec(memory_space=pl.ANY)
    smem_spec = pl.BlockSpec(memory_space=SMEM)
    vmem_spec = pl.BlockSpec(memory_space=VMEM)
    given = [] if first else [base]
    results = pl.pallas_call(
        functools.partial(pack_kernel, first, peers, per_col),
        out_shape=[jax.ShapeDtypeStruct((CAPACITY, ROWS, LANES), BF16)] * (peers - 1)
        + [jax.ShapeDtypeStruct((1,), I32)],
        in_specs=[smem_spec] * len(given) + [any_spec] * (2 * peers + 1) + [vmem_spec],
        out_specs=[vmem_spec] * (peers - 1) + [smem_spec],
        scratch_shapes=[
            SMEM((peers,) + c_parts[0].shape, I32),
            SMEM((peers,) + a_parts[0].shape, I32),
            SMEM(b_cols.shape, I32),
            SMEM((row_count * slots + CAPACITY + 1,), I32),
            SMEM((row_count,), I32),
            pltpu.SemaphoreType.DMA((2 * peers + 1,)),
        ],
        compiler_params=pltpu.CompilerParams(vmem_limit_bytes=24 << 20),
        cost_estimate=pl.CostEstimate(flops=1 << 20, bytes_accessed=1 << 20, transcendentals=0),
        name="pack",
    )(*given, *c_parts, *a_parts, b_cols, blocks)
    return results[:-1], results[-1]


def encode(a_slot, out, peer, place):
    return ((a_slot * 64 + out) * 64 + place) * 64 + peer


def list_kernel(peers, cols, per_col, most_items, *refs):
    refs = list(refs)
    a_refs = [refs.pop(0) for _ in range(cols)]
    b_refs = [refs.pop(0) for _ in range(peers)]
    c_ref = refs.pop(0)
    items, total = refs.pop(0), refs.pop(0)
    a_s, b_s, c_s, seen, places, sems = refs
    kept, row_count = c_ref.shape
    slots = b_refs[0].shape[0]
    a_slots = a_refs[0].shape[2] // per_col
    copies = [(a_refs[h], a_s.at[h]) for h in range(cols)]
    copies += [(b_refs[d], b_s.at[d]) for d in range(peers)]
    copies += [(c_ref, c_s)]
    fetch(copies, sems)
    grid_row = lax.axis_index("row")
    grid_col = lax.axis_index("col")

    def one_peer(d, length):
        group = (grid_row + d) % peers
        holder = (group // per_col - grid_col + cols) % cols
        part = group % per_col
        for k in range(row_count):
            seen[k] = 0

        def one_slot(s, state):
            length, count = state
            i = a_s[holder, 0, 0, part * a_slots + s]
            k = jnp.maximum(a_s[holder, 1, 0, part * a_slots + s], 0)
            safe = jnp.maximum(i, 0)
            kept_cols = [c_s[m, safe] for m in range(kept)]
            before = seen[k]
            after = before
            a_slot = (holder * per_col + part) * a_slots + s
            for n in range(slots):
                column = b_s[d, n, k]
                equal = [column == c for c in kept_cols]
                hit = functools.reduce(jnp.logical_or, equal) & (i >= 0)
                which = sum(m * e.astype(I32) for m, e in enumerate(equal))
                fresh = hit & ((before >> n) & 1 == 0)
                spot = k * slots + n
                place = jnp.where(fresh, count, places[spot])
                places[spot] = place
                stored = jnp.where(d == 0, spot, place)
                items[length] = encode(a_slot, safe * kept + which, d, stored)
                length = length + hit.astype(I32)
                count = count + fresh.astype(I32)
                after = after | (hit.astype(I32) << n)
            seen[k] = after
            return length, count

        length, _ = lax.fori_loop(0, a_slots, one_slot, (length, jnp.int32(0)))
        return length

    for spot in range(row_count * slots):
        places[spot] = 0
    length = lax.fori_loop(0, peers, one_peer, jnp.int32(0))
    for u in range(UNROLL):
        items[length + u] = IDLE
    total[0] = length


def work_list(a_parts, b_parts, c_cols, per_col):
    cols, peers = len(a_parts), len(b_parts)
    slots, row_count = b_parts[0].shape
    a_slots = a_parts[0].shape[2] // per_col
    most_items = peers * a_slots * slots + UNROLL + slots
    any_spec = pl.BlockSpec(memory_space=pl.ANY)
    smem_spec = pl.BlockSpec(memory_space=SMEM)
    return pl.pallas_call(
        functools.partial(list_kernel, peers, cols, per_col, most_items),
        out_shape=[
            jax.ShapeDtypeStruct((most_items,), I32),
            jax.ShapeDtypeStruct((1,), I32),
        ],
        in_specs=[any_spec] * (cols + peers + 1),
        out_specs=[smem_spec] * 2,
        scratch_shapes=[
            SMEM((cols,) + a_parts[0].shape, I32),
            SMEM((peers,) + b_parts[0].shape, I32),
            SMEM(c_cols.shape, I32),
            SMEM((row_count,), I32),
            SMEM((row_count * slots,), I32),
            pltpu.SemaphoreType.DMA((cols + peers + 1,)),
        ],
        cost_estimate=pl.CostEstimate(flops=1 << 20, bytes_accessed=1 << 16, transcendentals=0),
        name="work_list",
    )(*a_parts, *b_parts, c_cols)


def multiply_kernel(first, peers, cols, *refs):
    refs = list(refs)
    base_ref = previous = None
    if not first:
        base_ref, previous = refs.pop(0), refs.pop(0)
    items, total = refs.pop(0), refs.pop(0)
    a_refs = [refs.pop(0) for _ in range(cols)]
    own = refs.pop(0)
    b_refs = [refs.pop(0) for _ in range(peers - 1)]
    out = refs.pop(0)
    a_v, b_v, sums, sems = refs
    held, own_count = a_refs[0].shape[0], own.shape[0]
    row_count, kept = out.shape[0], out.shape[1]
    copies = [(a_refs[h], a_v.at[pl.ds(h * held, held)]) for h in range(cols)]
    copies += [(own, b_v.at[pl.ds(0, own_count)])]
    copies += [
        (b_refs[d], b_v.at[pl.ds(own_count + d * CAPACITY, CAPACITY)]) for d in range(peers - 1)
    ]
    started = [
        pltpu.make_async_copy(source, target, sems.at[at])
        for at, (source, target) in enumerate(copies)
    ]
    for copy in started:
        copy.start()
    sums[...] = jnp.zeros_like(sums)
    for copy in started:
        copy.wait()
    base = 0 if first else base_ref[0]
    low = lax.broadcasted_iota(I32, (ROWS, LANES), 1) < BS
    nothing = jnp.zeros((ROWS, LANES), BF16)

    def some_items(step, carry):
        for u in range(UNROLL):
            word = items[step * UNROLL + u]
            peer = word & 63
            place = (word >> 6) & 63
            target = (word >> 12) & 63
            a_slot = word >> 18
            inside = (place >= base) & (place < base + CAPACITY)
            own_item = peer == 0
            used = (inside & (peer > 0) & (peer < IDLE)) | (own_item if first else False)
            spot = jnp.where(own_item, place, own_count + (peer - 1) * CAPACITY + place - base)
            spot = jnp.where(used, spot, 0)
            left = a_v[a_slot]
            block = b_v[spot]
            turned = jnp.concatenate([block[:, BS:], block[:, :BS]], axis=1)
            right = jnp.concatenate(
                [
                    jnp.where(low, block, nothing),
                    jnp.where(low, turned, nothing),
                    jnp.where(low, nothing, turned),
                    jnp.where(low, nothing, block),
                ],
                axis=0,
            )
            term = jnp.dot(left, right, preferred_element_type=F32)
            i = jnp.where(used, target // kept, row_count)
            m = target % kept
            sums[i, pl.ds(m, ROWS, stride=kept), :] += term
        return carry

    lax.fori_loop(0, (total[0] + UNROLL - 1) // UNROLL, some_items, 0)

    def one_row(i, carry):
        for t in range(ROWS):
            piece = sums[i, pl.ds(t * kept, kept), :]
            if previous is not None:
                piece = piece + previous[i, :, pl.ds(t * LANES, LANES)]
            out[i, :, pl.ds(t * LANES, LANES)] = piece
        return carry

    lax.fori_loop(0, row_count, one_row, 0)


def multiply(base, previous, items, total, a_parts, own, b_parts, shape):
    first = base is None
    cols, peers = len(a_parts), len(b_parts) + 1
    any_spec = pl.BlockSpec(memory_space=pl.ANY)
    smem_spec = pl.BlockSpec(memory_space=SMEM)
    vmem_spec = pl.BlockSpec(memory_space=VMEM)
    given = [] if first else [base, previous]
    specs = [] if first else [smem_spec, vmem_spec]
    held = a_parts[0].shape[0]
    stored = own.shape[0] + (peers - 1) * CAPACITY
    return pl.pallas_call(
        functools.partial(multiply_kernel, first, peers, cols),
        out_shape=jax.ShapeDtypeStruct(shape, F32),
        in_specs=specs + [smem_spec] * 2 + [any_spec] * (cols + peers),
        out_specs=vmem_spec,
        scratch_shapes=[
            VMEM((cols * held, ROWS, LANES), BF16),
            VMEM((stored, ROWS, LANES), BF16),
            VMEM((shape[0] + 1, ROWS * shape[1], LANES), F32),
            pltpu.SemaphoreType.DMA((cols + peers,)),
        ],
        compiler_params=pltpu.CompilerParams(vmem_limit_bytes=32 << 20),
        cost_estimate=pl.CostEstimate(flops=1 << 26, bytes_accessed=4 << 20, transcendentals=0),
        name="multiply",
    )(*given, items, total, *a_parts, own, *b_parts)


def send_rows(parts):
    return [shifted(part, "row", -(d + 1)) for d, part in enumerate(parts)]


def index_parts(a_index, rows, cols, per_col):
    count = a_index.shape[2] // per_col
    grid_row = lax.axis_index("row")
    parts = []
    for d in range(rows):
        route = []
        for r in range(rows):
            for c in range(cols):
                turn = (r + d) % rows
                target = (c * per_col + turn // cols) * cols + turn % cols
                route.append((r * cols + c, target))
        mine = a_index
        if per_col > 1:
            turn = (grid_row + d) % rows
            mine = lax.dynamic_slice_in_dim(a_index, turn // cols * count, count, axis=2)
        parts.append(lax.ppermute(mine, ("row", "col"), route))
    return parts


def shards(a_blocks, a_index, b_blocks, b_cols, c_cols):
    rows = lax.axis_size("row")
    cols = lax.axis_size("col")
    per_col = rows // cols
    b_turned = b_cols.T
    c_turned = c_cols.T
    c_parts = [c_turned] + [shifted(c_turned, "row", d) for d in range(1, rows)]
    a_near = index_parts(a_index, rows, cols, per_col)
    a_ready, own = prepare(a_blocks, b_blocks)
    a_far = [a_index] + [shifted(a_index, "col", -h) for h in range(1, cols)]
    b_parts = [b_turned] + [shifted(b_turned, "row", -d) for d in range(1, rows)]
    a_parts = [a_ready] + [shifted(a_ready, "col", -h) for h in range(1, cols)]

    packed, most = pack(None, c_parts, a_near, b_turned, own, per_col)
    arrived = send_rows(packed)
    rounds = (lax.pmax(most[0], ("sys", "row", "col")) + CAPACITY - 1) // CAPACITY
    items, total = work_list(a_far, b_parts, c_turned, per_col)
    shape = (b_blocks.shape[0], c_cols.shape[1], BS * BS)
    sums = multiply(None, None, items, total, a_parts, own, arrived, shape)

    def more(state):
        return state[0] < rounds

    def one_round(state):
        at, sums = state
        base = jnp.reshape(at * CAPACITY, (1,))
        packed, _ = pack(base, c_parts, a_near, b_turned, own, per_col)
        arrived = send_rows(packed)
        sums = multiply(base, sums, items, total, a_parts, own, arrived, shape)
        return at + 1, sums

    return lax.while_loop(more, one_round, (jnp.int32(1), sums))[1]


def solution(mesh):
    return jax.shard_map(
        shards,
        mesh=mesh,
        in_specs=(
            P(("sys", "row"), "col", None),
            P(None, ("sys", "row"), "col"),
            P(("sys", "row"), "col", None),
            P(("sys", "row"), "col"),
            P(("sys", "row"), "col"),
        ),
        out_specs=P(("sys", "row"), "col", None),
        check_vma=False,
    )
```

```python
import functools

import jax
import jax.numpy as jnp
from jax import lax
from jax.experimental import pallas as pl
from jax.experimental.pallas import tpu as pltpu
from jax.sharding import PartitionSpec as P

BS = 64
LANES = 128
ROWS = BS * BS // LANES
CAPACITY = 16
UNROLL = 4
SLOTS = 4
WORD = 16
TAIL = 16
FLAG = 16
CHOSEN = LANES - 1
IDLE = 63
VMEM = pltpu.VMEM
SMEM = pltpu.SMEM
BF16 = jnp.bfloat16
F32 = jnp.float32
I32 = jnp.int32


def shifted(block, axis, distance):
    size = lax.axis_size(axis)
    route = [(i, (i + distance) % size) for i in range(size)]
    return lax.ppermute(block, axis, route)


def words_of(rows, cols, row_count):
    return -(-rows * row_count // cols // WORD)


def describe_kernel(words, a_ref, b_ref, c_ref, out):
    count, slots = a_ref.shape[2], b_ref.shape[0]
    row_count = b_ref.shape[1]
    out[...] = jnp.zeros_like(out)
    out[0:2, 0:count] = a_ref[:, 0, :]
    columns = c_ref[...]
    bits = jnp.left_shift(1, columns % WORD)
    for w in range(words):
        here = jnp.where(columns // WORD == w, bits, 0)
        out[2 + w : 3 + w, 0:row_count] = jnp.sum(here, axis=0, keepdims=True)
    offered = b_ref[...]
    at = 2 + words
    out[at : at + slots, 0:row_count] = jnp.where(offered < 0, 31, offered % WORD)
    if words > 1:
        at = at + slots
        out[at : at + slots, 0:row_count] = jnp.where(offered < 0, 0, offered // WORD)


def describe(a_index, b_cols, c_cols, words):
    used = 2 + words + b_cols.shape[0] * (1 if words == 1 else 2)
    return pl.pallas_call(
        functools.partial(describe_kernel, words),
        out_shape=jax.ShapeDtypeStruct((-(-used // 8) * 8, LANES), I32),
        in_specs=[pl.BlockSpec(memory_space=VMEM)] * 3,
        out_specs=pl.BlockSpec(memory_space=VMEM),
        name="describe",
    )(a_index, b_cols, c_cols)


def is_kept(words, kept, row, offer, slot, k):
    bit = offer[2 + words + slot, k]
    if words == 1:
        word = kept[2, row]
    else:
        word = kept[2 + offer[2 + words + SLOTS + slot, k], row]
    return (word >> bit) & 1


def prepare_kernel(a_any, told, b_any, a_out, b_out, a_ref, b_ref, a_wide, b_wide, sems):
    copies = [
        pltpu.make_async_copy(a_any, a_ref, sems.at[0]),
        pltpu.make_async_copy(b_any, b_ref, sems.at[1]),
    ]
    for copy in copies:
        copy.start()
    source = lax.broadcasted_iota(I32, (LANES, LANES), 0)
    target = lax.broadcasted_iota(I32, (LANES, LANES), 1)
    wanted = (target // BS) * BS + 2 * (target % ROWS) + (target // ROWS) % 2
    order = (source == wanted).astype(BF16)
    copies[0].wait()
    slots = a_ref.shape[1]
    for t in range(ROWS):
        piece = a_ref[0, :, pl.ds(t * LANES, LANES)]
        a_wide[:, t, :] = jnp.dot(piece, order, preferred_element_type=F32)
    for s in range(slots):
        a_out[pl.ds(s * ROWS, ROWS), :] = a_wide[s].astype(BF16)
    indices = told[...].astype(F32)
    tail = jnp.concatenate([indices[:8], jnp.zeros((TAIL - 8, LANES), F32)], axis=0)
    a_out[pl.ds(slots * ROWS, TAIL), :] = tail.astype(BF16)
    copies[1].wait()
    row_count, slots = b_ref.shape[0], b_ref.shape[1]

    def one_row(k, carry):
        for t in range(ROWS):
            b_wide[pl.ds(t * slots, slots), :] = b_ref[k, :, pl.ds(t * LANES, LANES)].astype(F32)
        for n in range(slots):
            at = pl.multiple_of((k * slots + n) * ROWS, ROWS)
            b_out[pl.ds(at, ROWS), :] = b_wide[pl.ds(n, ROWS, stride=slots), :].astype(BF16)
        return carry

    lax.fori_loop(0, row_count, one_row, 0)


def prepare(a_blocks, told, b_blocks):
    slots = a_blocks.shape[1]
    blocks = b_blocks.shape[0] * b_blocks.shape[1]
    return pl.pallas_call(
        prepare_kernel,
        out_shape=(
            jax.ShapeDtypeStruct((slots * ROWS + TAIL, LANES), BF16),
            jax.ShapeDtypeStruct((blocks * ROWS, LANES), BF16),
        ),
        in_specs=[
            pl.BlockSpec(memory_space=pltpu.HBM),
            pl.BlockSpec(memory_space=VMEM),
            pl.BlockSpec(memory_space=pltpu.HBM),
        ],
        out_specs=(pl.BlockSpec(memory_space=VMEM),) * 2,
        scratch_shapes=[
            VMEM(a_blocks.shape, BF16),
            VMEM(b_blocks.shape, BF16),
            VMEM((slots, ROWS, LANES), F32),
            VMEM((b_blocks.shape[1] * ROWS, LANES), F32),
            pltpu.SemaphoreType.DMA((2,)),
        ],
        compiler_params=pltpu.CompilerParams(vmem_limit_bytes=24 << 20),
        cost_estimate=pl.CostEstimate(flops=1 << 24, bytes_accessed=16 << 20, transcendentals=0),
        name="prepare",
    )(a_blocks, told, b_blocks)


def fetch(copies, sems):
    started = [
        pltpu.make_async_copy(source, target, sems.at[at])
        for at, (source, target) in enumerate(copies)
    ]
    for copy in started:
        copy.start()
    for copy in started:
        copy.wait()


def pack_kernel(first, words, per_col, a_slots, *refs):
    refs = list(refs)
    base_ref = None if first else refs.pop(0)
    c_refs, a_refs, blocks, outs, most, c_s, a_s, chosen, seen, sems = refs
    peers = len(c_refs)
    row_count = blocks.shape[0] // ROWS // SLOTS
    fetch(
        [(ref, c_s.at[d]) for d, ref in enumerate(c_refs)]
        + [(ref, a_s.at[d]) for d, ref in enumerate(a_refs)],
        sems,
    )
    base = 0 if first else base_ref[0]
    grid_row = lax.axis_index("row")
    turn = grid_row % per_col * (peers // per_col) + lax.axis_index("col")

    def one_peer(d, top):
        place = (turn - grid_row + d + peers) % peers
        for k in range(row_count):
            seen[k] = 0
        count = jnp.int32(0)
        part = grid_row % per_col * a_slots if per_col > 1 else 0
        for s in range(a_slots):
            i = a_s[place, 0, part + s]
            k = jnp.maximum(a_s[place, 1, part + s], 0)
            live = (i >= 0).astype(I32)
            row = jnp.maximum(i, 0)
            before = seen[k]
            after = before
            for n in range(SLOTS):
                hit = is_kept(words, c_s.at[d], row, c_s.at[0], n, k) & live
                chosen[d, count] = k * SLOTS + n
                count = count + (hit & ~(before >> n))
                after = after | (hit << n)
            seen[k] = after
        chosen[d, CHOSEN] = count
        return jnp.maximum(top, count)

    top = lax.fori_loop(1, peers, one_peer, jnp.int32(0))
    most[0] = top
    sign = jnp.full((FLAG, LANES), top, I32).astype(F32).astype(BF16)
    for d in range(1, peers):
        out = outs[d - 1]
        count = chosen[d, CHOSEN]
        for x in range(CAPACITY):
            index = jnp.where(base + x < count, chosen[d, base + x], 0)
            block = blocks[pl.ds(pl.multiple_of(index * ROWS, ROWS), ROWS), :]
            out[pl.ds(x * ROWS, ROWS), :] = block
        out[pl.ds(CAPACITY * ROWS, FLAG), :] = sign


def pack(base, c_parts, a_parts, blocks, words, per_col, a_slots):
    peers = len(c_parts)
    first = base is None
    any_spec = pl.BlockSpec(memory_space=pl.ANY)
    smem_spec = pl.BlockSpec(memory_space=SMEM)
    vmem_spec = pl.BlockSpec(memory_space=VMEM)
    given = [] if first else [base]

    def kernel(*refs):
        refs = list(refs)
        base_refs = [] if first else [refs.pop(0)]
        grouped = [refs[:peers], refs[peers : 2 * peers], refs[2 * peers]]
        refs = refs[2 * peers + 1 :]
        grouped += [refs[: peers - 1]] + refs[peers - 1 :]
        pack_kernel(first, words, per_col, a_slots, *base_refs, *grouped)

    results = pl.pallas_call(
        kernel,
        out_shape=[jax.ShapeDtypeStruct((CAPACITY * ROWS + FLAG, LANES), BF16)] * (peers - 1)
        + [jax.ShapeDtypeStruct((1,), I32)],
        in_specs=[smem_spec] * len(given) + [any_spec] * (2 * peers) + [vmem_spec],
        out_specs=[vmem_spec] * (peers - 1) + [smem_spec],
        scratch_shapes=[
            SMEM((peers,) + c_parts[0].shape, I32),
            SMEM((peers,) + a_parts[0].shape, I32),
            SMEM((peers, LANES), I32),
            SMEM((blocks.shape[0] // ROWS // SLOTS,), I32),
            pltpu.SemaphoreType.DMA((2 * peers,)),
        ],
        compiler_params=pltpu.CompilerParams(vmem_limit_bytes=24 << 20),
        cost_estimate=pl.CostEstimate(flops=1 << 20, bytes_accessed=4 << 20, transcendentals=0),
        name="pack",
    )(*given, *c_parts, *a_parts, blocks)
    return results[:-1], results[-1]


def encode(a_slot, out, peer, place):
    return ((a_slot * 64 + out) * 64 + place) * 64 + peer


def list_kernel(words, span, per_col, a_slots, peers, *refs):
    a_all, b_refs = refs[0], refs[1 : 1 + peers]
    c_ref, items, total, a_s, a_v, a_i, b_s, c_s, spots, seen, places, sems = refs[1 + peers :]
    kept, row_count = c_ref.shape
    cols, a_rows = a_all.shape[0], a_all.shape[1]
    tails = [(a_all.at[h, pl.ds(a_rows - TAIL, TAIL)], a_v.at[h]) for h in range(cols)]
    fetch(
        tails + [(ref, b_s.at[d]) for d, ref in enumerate(b_refs)] + [(c_ref, c_s)],
        sems,
    )
    a_i[...] = a_v[:, 0:8, :].astype(F32).astype(I32)
    fetch([(a_i, a_s)], sems)
    grid_row = lax.axis_index("row")
    for i in range(row_count):
        for m in range(kept):
            spots[i * span + c_s[m, i]] = m

    def one_peer(d, length):
        group = (grid_row + d) % peers
        holder = group // per_col
        part = group % per_col * a_slots if per_col > 1 else 0
        own = d == 0
        for k in range(row_count):
            seen[k] = 0
        count = jnp.int32(0)
        for s in range(a_slots):
            i = a_s[holder, 0, part + s]
            k = jnp.maximum(a_s[holder, 1, part + s], 0)
            live = (i >= 0).astype(I32)
            row = jnp.maximum(i, 0)
            before = seen[k]
            after = before
            a_slot = holder * (per_col * a_slots) + part + s
            for n in range(SLOTS):
                hit = is_kept(words, b_s.at[0], row, b_s.at[d], n, k) & live
                column = b_s[d, 2 + words + n, k]
                if words > 1:
                    column = column + WORD * b_s[d, 2 + words + SLOTS + n, k]
                which = spots[row * span + jnp.where(hit == 1, column, 0)]
                fresh = hit & ~(before >> n)
                spot = k * SLOTS + n
                place = jnp.where(fresh == 1, count, places[spot])
                places[spot] = place
                stored = jnp.where(own, spot, place)
                items[length] = encode(a_slot, row * kept + which, d, stored)
                length = length + hit
                count = count + fresh
                after = after | (hit << n)
            seen[k] = after
        return length

    for spot in range(row_count * SLOTS):
        places[spot] = 0
    length = lax.fori_loop(0, peers, one_peer, jnp.int32(0))
    for u in range(UNROLL):
        items[length + u] = IDLE
    total[0] = length


def work_list(a_all, b_parts, c_cols, words, span, per_col, a_slots):
    cols, peers = a_all.shape[0], len(b_parts)
    row_count = c_cols.shape[1]
    most_items = peers * a_slots * SLOTS + UNROLL + SLOTS
    any_spec = pl.BlockSpec(memory_space=pl.ANY)
    smem_spec = pl.BlockSpec(memory_space=SMEM)
    return pl.pallas_call(
        functools.partial(list_kernel, words, span, per_col, a_slots, peers),
        out_shape=[
            jax.ShapeDtypeStruct((most_items,), I32),
            jax.ShapeDtypeStruct((1,), I32),
        ],
        in_specs=[any_spec] * (peers + 2),
        out_specs=[smem_spec] * 2,
        scratch_shapes=[
            SMEM((cols, 8, LANES), I32),
            VMEM((cols, TAIL, LANES), BF16),
            VMEM((cols, 8, LANES), I32),
            SMEM((peers,) + b_parts[0].shape, I32),
            SMEM(c_cols.shape, I32),
            SMEM((row_count * span,), I32),
            SMEM((row_count,), I32),
            SMEM((row_count * SLOTS,), I32),
            pltpu.SemaphoreType.DMA((cols + peers + 1,)),
        ],
        cost_estimate=pl.CostEstimate(flops=1 << 20, bytes_accessed=1 << 16, transcendentals=0),
        name="work_list",
    )(a_all, *b_parts, c_cols)


def multiply_kernel(first, peers, *refs):
    refs = list(refs)
    base_ref = previous = None
    if not first:
        base_ref, previous = refs.pop(0), refs.pop(0)
    items, total, most = refs.pop(0), refs.pop(0), refs.pop(0)
    a_all = refs.pop(0)
    own = refs.pop(0)
    b_refs = [refs.pop(0) for _ in range(peers - 1)]
    out, rounds, a_v, b_v, flags, sums, sems = refs
    own_rows = own.shape[0]
    held = (a_all.shape[1] - TAIL) // ROWS
    row_count, kept = out.shape[0], out.shape[1]
    copies = [(a_all, a_v)]
    copies += [(own, b_v.at[pl.ds(0, own_rows)])]
    width = CAPACITY * ROWS
    for d in range(peers - 1):
        copies += [
            (b_refs[d].at[pl.ds(0, width)], b_v.at[pl.ds(own_rows + d * width, width)]),
            (b_refs[d].at[pl.ds(width, FLAG)], flags.at[pl.ds(d * FLAG, FLAG)]),
        ]
    started = [
        pltpu.make_async_copy(source, target, sems.at[at])
        for at, (source, target) in enumerate(copies)
    ]
    for copy in started:
        copy.start()
    sums[...] = jnp.zeros_like(sums)
    for copy in started:
        copy.wait()
    base = 0 if first else base_ref[0]
    needed = jnp.maximum(most[0], jnp.max(flags[...].astype(F32)).astype(I32))
    rounds[0] = (needed + CAPACITY - 1) // CAPACITY
    low = lax.broadcasted_iota(I32, (ROWS, LANES), 1) < BS
    nothing = jnp.zeros((ROWS, LANES), BF16)

    def some_items(step, carry):
        for u in range(UNROLL):
            word = items[step * UNROLL + u]
            peer = word & 63
            place = (word >> 6) & 63
            target = (word >> 12) & 63
            a_slot = word >> 18
            inside = (place >= base) & (place < base + CAPACITY)
            own_item = peer == 0
            used = (inside & (peer > 0) & (peer < IDLE)) | (own_item if first else False)
            spot = jnp.where(
                own_item, place, own_rows // ROWS + (peer - 1) * CAPACITY + place - base
            )
            spot = jnp.where(used, spot, 0)
            inner = pl.multiple_of(a_slot % held * ROWS, ROWS)
            left = a_v[a_slot // held, pl.ds(inner, ROWS), :]
            block = b_v[pl.ds(pl.multiple_of(spot * ROWS, ROWS), ROWS), :]
            turned = jnp.concatenate([block[:, BS:], block[:, :BS]], axis=1)
            right = jnp.concatenate(
                [
                    jnp.where(low, block, nothing),
                    jnp.where(low, turned, nothing),
                    jnp.where(low, nothing, turned),
                    jnp.where(low, nothing, block),
                ],
                axis=0,
            )
            term = jnp.dot(left, right, preferred_element_type=F32)
            i = jnp.where(used, target // kept, row_count)
            m = target % kept
            sums[i, pl.ds(m, ROWS, stride=kept), :] += term
        return carry

    lax.fori_loop(0, (total[0] + UNROLL - 1) // UNROLL, some_items, 0)

    def one_row(i, carry):
        for t in range(ROWS):
            piece = sums[i, pl.ds(t * kept, kept), :]
            if previous is not None:
                piece = piece + previous[i, :, pl.ds(t * LANES, LANES)]
            out[i, :, pl.ds(t * LANES, LANES)] = piece
        return carry

    lax.fori_loop(0, row_count, one_row, 0)


def multiply(base, previous, items, total, most, a_all, own, b_parts, shape):
    first = base is None
    peers = len(b_parts) + 1
    any_spec = pl.BlockSpec(memory_space=pl.ANY)
    smem_spec = pl.BlockSpec(memory_space=SMEM)
    vmem_spec = pl.BlockSpec(memory_space=VMEM)
    given = [] if first else [base, previous]
    specs = [] if first else [smem_spec, vmem_spec]
    stored = own.shape[0] + (peers - 1) * CAPACITY * ROWS
    return pl.pallas_call(
        functools.partial(multiply_kernel, first, peers),
        out_shape=[jax.ShapeDtypeStruct(shape, F32), jax.ShapeDtypeStruct((1,), I32)],
        in_specs=specs + [smem_spec] * 3 + [any_spec] * (1 + peers),
        out_specs=[vmem_spec, smem_spec],
        scratch_shapes=[
            VMEM(a_all.shape, BF16),
            VMEM((stored, LANES), BF16),
            VMEM(((peers - 1) * FLAG, LANES), BF16),
            VMEM((shape[0] + 1, ROWS * shape[1], LANES), F32),
            pltpu.SemaphoreType.DMA((2 * peers,)),
        ],
        compiler_params=pltpu.CompilerParams(vmem_limit_bytes=32 << 20),
        cost_estimate=pl.CostEstimate(flops=1 << 26, bytes_accessed=4 << 20, transcendentals=0),
        name="multiply",
    )(*given, items, total, most, a_all, own, *b_parts)


def send_rows(parts):
    return [shifted(part, "row", -(d + 1)) for d, part in enumerate(parts)]


def index_parts(told, rows, cols, per_col):
    parts = []
    for d in range(rows):
        route = []
        for r in range(rows):
            for c in range(cols):
                turn = (r + d) % rows
                target = (c * per_col + turn // cols) * cols + turn % cols
                route.append((r * cols + c, target))
        parts.append(lax.ppermute(told, ("row", "col"), route))
    return parts


def shards(a_blocks, a_index, b_blocks, b_cols, c_cols):
    rows = lax.axis_size("row")
    cols = lax.axis_size("col")
    per_col = rows // cols
    a_slots = a_blocks.shape[1] // per_col
    row_count = b_blocks.shape[0]
    words = words_of(rows, cols, row_count)
    span = words * WORD
    c_turned = c_cols.T
    told = describe(a_index, b_cols.T, c_turned, words)
    a_near = index_parts(told, rows, cols, per_col)
    told_rows = [told] + [shifted(told, "row", d) for d in range(1, rows)]
    a_ready, own = prepare(a_blocks, told, b_blocks)
    a_all = lax.all_gather(a_ready, "col")

    packed, most = pack(None, told_rows, a_near, own, words, per_col, a_slots)
    arrived = send_rows(packed)
    ahead = [told_rows[(rows - d) % rows] for d in range(rows)]
    items, total = work_list(a_all, ahead, c_turned, words, span, per_col, a_slots)
    shape = (row_count, c_cols.shape[1], BS * BS)
    sums, rounds = multiply(None, None, items, total, most, a_all, own, arrived, shape)

    def more(state):
        return state[0] < rounds[0]

    def one_round(state):
        at, sums = state
        base = jnp.reshape(at * CAPACITY, (1,))
        packed, _ = pack(base, told_rows, a_near, own, words, per_col, a_slots)
        arrived = send_rows(packed)
        sums, _ = multiply(base, sums, items, total, most, a_all, own, arrived, shape)
        return at + 1, sums

    return lax.while_loop(more, one_round, (jnp.int32(1), sums))[1]


def solution(mesh):
    return jax.shard_map(
        shards,
        mesh=mesh,
        in_specs=(
            P(("sys", "row"), "col", None),
            P(None, ("sys", "row"), "col"),
            P(("sys", "row"), "col", None),
            P(("sys", "row"), "col"),
            P(("sys", "row"), "col"),
        ),
        out_specs=P(("sys", "row"), "col", None),
        check_vma=False,
    )
```

```python
import functools

import jax
import jax.numpy as jnp
from jax import lax
from jax.experimental import pallas as pl
from jax.experimental.pallas import tpu as pltpu
from jax.sharding import PartitionSpec as P

BS = 64
LANES = 128
ROWS = BS * BS // LANES
CAPACITY = 16
UNROLL = 4
SLOTS = 4
WORD = 16
FLAG = 16
IDLE = 63
VMEM = pltpu.VMEM
SMEM = pltpu.SMEM
BF16 = jnp.bfloat16
F32 = jnp.float32
I32 = jnp.int32


def shifted(block, axis, distance):
    size = lax.axis_size(axis)
    route = [(i, (i + distance) % size) for i in range(size)]
    return lax.ppermute(block, axis, route)


A_ROW, A_COLUMN, RETAINED = 0, 1, 2
OFFERED = RETAINED + SLOTS
TOLD = 8


def describe_kernel(a_ref, b_ref, c_ref, out):
    count, row_count = a_ref.shape[2], b_ref.shape[1]
    out[...] = jnp.full(out.shape, -1, I32)
    out[0:2, 0:count] = a_ref[:, 0, :]
    out[RETAINED : RETAINED + c_ref.shape[0], 0:row_count] = c_ref[...]
    for n in range(b_ref.shape[0]):
        at = n * row_count
        out[OFFERED : OFFERED + 1, at : at + row_count] = b_ref[n : n + 1, :]


def describe(a_index, b_cols, c_cols):
    return pl.pallas_call(
        describe_kernel,
        out_shape=jax.ShapeDtypeStruct((TOLD, LANES), I32),
        in_specs=[pl.BlockSpec(memory_space=VMEM)] * 3,
        out_specs=pl.BlockSpec(memory_space=VMEM),
        name="describe",
    )(a_index, b_cols, c_cols)


def iota(shape, axis):
    return lax.broadcasted_iota(I32, shape, axis)


def along_lanes(left, right):
    return lax.dot_general(
        left.astype(BF16), right.astype(BF16), (((1,), (1,)), ((), ())), preferred_element_type=F32
    )


def demand(retained, offered, a_rows, a_columns, row_count, first_slot, a_slots):
    shape = (row_count, LANES)
    turned = along_lanes((iota(shape, 0) == iota(shape, 1)).astype(F32), retained.astype(F32))
    wanted = offered.astype(F32)
    kept = turned[:, 0:1] == wanted
    for m in range(1, SLOTS):
        kept = kept | (turned[:, m : m + 1] == wanted)
    lane = iota(shape, 1)
    mine = (lane >= first_slot) & (lane < first_slot + a_slots)
    by_row = ((iota(shape, 0) == a_rows) & mine).astype(F32)
    by_column = (iota((LANES, LANES), 0) % row_count == a_columns).astype(F32)
    uses = along_lanes(by_row, by_column)
    return jnp.max(jnp.where(kept & (uses > 0.5), 1.0, 0.0), axis=0, keepdims=True)


def layout_kernel(a_ref, b_ref, a_out, b_out, a_wide, b_wide):
    source = iota((LANES, LANES), 0)
    target = iota((LANES, LANES), 1)
    wanted = (target // BS) * BS + 2 * (target % ROWS) + (target // ROWS) % 2
    order = (source == wanted).astype(BF16)
    slots = a_ref.shape[1]
    for t in range(ROWS):
        piece = a_ref[0, :, pl.ds(t * LANES, LANES)]
        a_wide[:, t, :] = jnp.dot(piece, order, preferred_element_type=F32)
    for s in range(slots):
        a_out[pl.ds(s * ROWS, ROWS), :] = a_wide[s].astype(BF16)
    row_count, slots = b_ref.shape[0], b_ref.shape[1]

    def one_row(k, carry):
        for t in range(ROWS):
            b_wide[pl.ds(t * slots, slots), :] = b_ref[k, :, pl.ds(t * LANES, LANES)].astype(F32)
        for n in range(slots):
            at = pl.multiple_of((n * row_count + k) * ROWS, ROWS)
            b_out[pl.ds(at, ROWS), :] = b_wide[pl.ds(n, ROWS, stride=slots), :].astype(BF16)
        return carry

    lax.fori_loop(0, row_count, one_row, 0)


def layout(a_blocks, b_blocks):
    slots = a_blocks.shape[1]
    blocks = b_blocks.shape[0] * b_blocks.shape[1]
    return pl.pallas_call(
        layout_kernel,
        out_shape=(
            jax.ShapeDtypeStruct((slots * ROWS, LANES), BF16),
            jax.ShapeDtypeStruct((blocks * ROWS, LANES), BF16),
        ),
        in_specs=[pl.BlockSpec(memory_space=VMEM)] * 2,
        out_specs=(pl.BlockSpec(memory_space=VMEM),) * 2,
        scratch_shapes=[
            VMEM((slots, ROWS, LANES), F32),
            VMEM((b_blocks.shape[1] * ROWS, LANES), F32),
        ],
        compiler_params=pltpu.CompilerParams(vmem_limit_bytes=24 << 20),
        cost_estimate=pl.CostEstimate(flops=1 << 24, bytes_accessed=4 << 20, transcendentals=0),
        name="layout",
    )(a_blocks, b_blocks)


def fetch(copies, sems):
    started = [
        pltpu.make_async_copy(source, target, sems.at[at])
        for at, (source, target) in enumerate(copies)
    ]
    for copy in started:
        copy.start()
    for copy in started:
        copy.wait()


def pack_kernel(first, peers, per_col, a_slots, *refs):
    refs = list(refs)
    base = 0 if first else refs.pop(0)[0]
    told, b_ref = refs.pop(0), refs.pop(0)
    outs = refs[: peers - 1]
    most, picks, wide, packed = refs[peers - 1 :]
    row_count, slots = b_ref.shape[0], b_ref.shape[1]
    blocks = row_count * slots
    cols = told.shape[0] // peers
    grid_row = lax.axis_index("row")
    grid_col = lax.axis_index("col")
    offered = told[grid_row * cols + grid_col, pl.ds(OFFERED, 1), :]
    before = (iota((LANES, LANES), 0) < iota((LANES, LANES), 1)).astype(BF16)

    def one_peer(d, top):
        row = (grid_row + peers - d) % peers
        retained = told[row * cols + grid_col, pl.ds(RETAINED, SLOTS), :]
        a_from = row * cols + grid_row // per_col
        a_rows, a_columns = told[a_from, pl.ds(A_ROW, 1), :], told[a_from, pl.ds(A_COLUMN, 1), :]
        needed = demand(
            retained, offered, a_rows, a_columns, row_count, grid_row % per_col * a_slots, a_slots
        )
        many = jnp.broadcast_to(needed, (8, LANES)).astype(BF16)
        place = jnp.dot(many, before, preferred_element_type=F32)[0:1]
        place = jnp.where(needed > 0.5, place, -1.0).astype(I32)
        pick = (place == iota((CAPACITY, LANES), 0) + base).astype(BF16)
        picks[pl.ds(pl.multiple_of((d - 1) * CAPACITY, CAPACITY), CAPACITY), :] = pick
        return jnp.maximum(top, jnp.sum(needed, axis=1, keepdims=True))

    if peers <= 8:
        top = jnp.zeros((1, 1), F32)
        for d in range(1, peers):
            top = one_peer(d, top)
    else:
        top = lax.fori_loop(1, peers, one_peer, jnp.zeros((1, 1), F32))
    most[...] = jnp.broadcast_to(top, most.shape)
    wide[...] = b_ref[...].astype(F32)
    pick = picks[...][:, :blocks]
    for t in range(ROWS):
        lanes = pl.ds(t * LANES, LANES)
        flat = jnp.concatenate([wide[:, n, lanes] for n in range(slots)], axis=0).astype(BF16)
        packed[:, t, :] = jnp.dot(pick, flat, preferred_element_type=F32)
    for d in range(1, peers):
        out = outs[d - 1]
        for x in range(CAPACITY):
            out[pl.ds(x * ROWS, ROWS), :] = packed[(d - 1) * CAPACITY + x].astype(BF16)
        out[pl.ds(CAPACITY * ROWS, FLAG), :] = jnp.broadcast_to(top, (FLAG, LANES)).astype(BF16)


def pack(base, told_all, b_blocks, peers, per_col, a_slots):
    first = base is None
    smem_spec = pl.BlockSpec(memory_space=SMEM)
    vmem_spec = pl.BlockSpec(memory_space=VMEM)
    given = [] if first else [base]
    results = pl.pallas_call(
        functools.partial(pack_kernel, first, peers, per_col, a_slots),
        out_shape=[jax.ShapeDtypeStruct((CAPACITY * ROWS + FLAG, LANES), BF16)] * (peers - 1)
        + [jax.ShapeDtypeStruct((8, LANES), F32)],
        in_specs=[smem_spec] * len(given) + [vmem_spec] * 2,
        out_specs=[vmem_spec] * peers,
        scratch_shapes=[
            VMEM(((peers - 1) * CAPACITY, LANES), BF16),
            VMEM(b_blocks.shape, F32),
            VMEM(((peers - 1) * CAPACITY, ROWS, LANES), F32),
        ],
        compiler_params=pltpu.CompilerParams(vmem_limit_bytes=32 << 20),
        cost_estimate=pl.CostEstimate(flops=1 << 20, bytes_accessed=4 << 20, transcendentals=0),
        name="pack",
    )(*given, told_all, b_blocks)
    return results[:-1], results[-1]


def encode(a_slot, out, peer, place):
    return ((a_slot * 64 + out) * 64 + place) * 64 + peer


def list_kernel(span, per_col, a_slots, peers, told, items, total, *scratch):
    a_s, b_s, c_s, spots, bits, seen, places, sems = scratch
    cols = told.shape[0] // peers
    row_count = seen.shape[0]
    grid_row = lax.axis_index("row")
    grid_col = lax.axis_index("col")
    own = grid_row * cols + grid_col
    copies = [(told.at[own], c_s)]
    copies += [(told.at[grid_row * cols + h], a_s.at[h]) for h in range(cols)]
    copies += [(told.at[g * cols + grid_col], b_s.at[g]) for g in range(peers)]
    fetch(copies, sems)
    words = span // WORD
    for i in range(row_count):
        columns = [c_s[RETAINED + m, i] for m in range(SLOTS)]
        for w in range(words):
            held = [jnp.left_shift(1, c % WORD) for c in columns]
            if words > 1:
                held = [jnp.where(c // WORD == w, h, 0) for c, h in zip(columns, held)]
            bits[i * words + w] = functools.reduce(jnp.bitwise_or, held)
        for m, c in enumerate(columns):
            spots[i * span + c] = m

    def one_peer(d, length):
        group = (grid_row + d) % peers
        holder = group // per_col
        part = group % per_col * a_slots if per_col > 1 else 0
        for spot in range(row_count * SLOTS):
            seen_row = spot % row_count
            if spot < row_count:
                seen[seen_row] = 0
        for s in range(a_slots):
            i = a_s[holder, A_ROW, part + s]
            k = jnp.maximum(a_s[holder, A_COLUMN, part + s], 0)
            live = (i >= 0).astype(I32)
            row = jnp.maximum(i, 0)
            after = seen[k]
            for n in range(SLOTS):
                column = b_s[group, OFFERED, n * row_count + k]
                safe = jnp.maximum(column, 0)
                word = bits[row * words + (safe // WORD if words > 1 else 0)]
                hit = (word >> (safe % WORD)) & live & (column >= 0).astype(I32)
                after = after | (hit << n)
                which = spots[row * span + jnp.where(hit == 1, safe, c_s[RETAINED, row])]
                items[length] = encode(
                    holder * per_col * a_slots + part + s,
                    row * SLOTS + which,
                    d,
                    n * row_count + k,
                )
                length = length + hit
            seen[k] = after
        count = jnp.int32(0)
        for n in range(SLOTS):
            for k in range(row_count):
                spot = n * row_count + k
                places[d, spot] = jnp.where(d == 0, spot, count)
                count = count + ((seen[k] >> n) & 1)
        return length

    length = lax.fori_loop(0, peers, one_peer, jnp.int32(0))
    for u in range(UNROLL):
        items[length + u] = IDLE
    total[0] = length

    def settle(y, carry):
        word = items[y]
        peer, spot = word & 63, (word >> 6) & 63
        items[y] = word + ((places[peer, spot] - spot) << 6)
        return carry

    lax.fori_loop(0, length, settle, 0)


def work_list(told_all, peers, row_count, span, per_col, a_slots):
    cols = told_all.shape[0] // peers
    most_items = peers * a_slots * SLOTS + UNROLL + SLOTS
    return pl.pallas_call(
        functools.partial(list_kernel, span, per_col, a_slots, peers),
        out_shape=[
            jax.ShapeDtypeStruct((most_items,), I32),
            jax.ShapeDtypeStruct((1,), I32),
        ],
        in_specs=[pl.BlockSpec(memory_space=pl.ANY)],
        out_specs=[pl.BlockSpec(memory_space=SMEM)] * 2,
        scratch_shapes=[
            SMEM((cols, TOLD, LANES), I32),
            SMEM((peers, TOLD, LANES), I32),
            SMEM((TOLD, LANES), I32),
            SMEM((row_count * span,), I32),
            SMEM((row_count * (span // WORD),), I32),
            SMEM((row_count,), I32),
            SMEM((peers, LANES), I32),
            pltpu.SemaphoreType.DMA((cols + peers + 1,)),
        ],
        cost_estimate=pl.CostEstimate(flops=1 << 20, bytes_accessed=1 << 16, transcendentals=0),
        name="work_list",
    )(told_all)


def multiply_kernel(first, peers, cols, *refs):
    refs = list(refs)
    base_ref = previous = None
    if not first:
        base_ref, previous = refs.pop(0), refs.pop(0)
    items, total, most = refs.pop(0), refs.pop(0), refs.pop(0)
    a_refs = [refs.pop(0) for _ in range(cols)]
    own = refs.pop(0)
    b_refs = [refs.pop(0) for _ in range(peers - 1)]
    out, rounds, a_v, b_v, flags, sums, sems = refs
    own_rows = own.shape[0]
    held = a_refs[0].shape[0] // ROWS
    grid_col = lax.axis_index("col")
    row_count, kept = out.shape[0], out.shape[1]
    copies = [(ref, a_v.at[(grid_col + h) % cols]) for h, ref in enumerate(a_refs)]
    copies += [(own, b_v.at[pl.ds(0, own_rows)])]
    width = CAPACITY * ROWS
    for d in range(peers - 1):
        copies += [
            (b_refs[d].at[pl.ds(0, width)], b_v.at[pl.ds(own_rows + d * width, width)]),
            (b_refs[d].at[pl.ds(width, FLAG)], flags.at[pl.ds(d * FLAG, FLAG)]),
        ]
    started = [
        pltpu.make_async_copy(source, target, sems.at[at])
        for at, (source, target) in enumerate(copies)
    ]
    for copy in started:
        copy.start()
    sums[...] = jnp.zeros_like(sums)
    for copy in started:
        copy.wait()
    base = 0 if first else base_ref[0]
    needed = jnp.maximum(jnp.max(most[...]), jnp.max(flags[...].astype(F32))).astype(I32)
    rounds[0] = (needed + CAPACITY - 1) // CAPACITY
    low = lax.broadcasted_iota(I32, (ROWS, LANES), 1) < BS
    nothing = jnp.zeros((ROWS, LANES), BF16)

    def some_items(step, carry):
        for u in range(UNROLL):
            word = items[step * UNROLL + u]
            peer = word & 63
            place = (word >> 6) & 63
            target = (word >> 12) & 63
            a_slot = word >> 18
            inside = (place >= base) & (place < base + CAPACITY)
            own_item = peer == 0
            used = (inside & (peer > 0) & (peer < IDLE)) | (own_item if first else False)
            spot = jnp.where(
                own_item, place, own_rows // ROWS + (peer - 1) * CAPACITY + place - base
            )
            spot = jnp.where(used, spot, 0)
            inner = pl.multiple_of(a_slot % held * ROWS, ROWS)
            left = a_v[a_slot // held, pl.ds(inner, ROWS), :]
            block = b_v[pl.ds(pl.multiple_of(spot * ROWS, ROWS), ROWS), :]
            turned = jnp.concatenate([block[:, BS:], block[:, :BS]], axis=1)
            right = jnp.concatenate(
                [
                    jnp.where(low, block, nothing),
                    jnp.where(low, turned, nothing),
                    jnp.where(low, nothing, turned),
                    jnp.where(low, nothing, block),
                ],
                axis=0,
            )
            term = jnp.dot(left, right, preferred_element_type=F32)
            i = jnp.where(used, target // kept, row_count)
            m = target % kept
            sums[i, pl.ds(m, ROWS, stride=kept), :] += term
        return carry

    lax.fori_loop(0, (total[0] + UNROLL - 1) // UNROLL, some_items, 0)

    def one_row(i, carry):
        for t in range(ROWS):
            piece = sums[i, pl.ds(t * kept, kept), :]
            if previous is not None:
                piece = piece + previous[i, :, pl.ds(t * LANES, LANES)]
            out[i, :, pl.ds(t * LANES, LANES)] = piece
        return carry

    lax.fori_loop(0, row_count, one_row, 0)


def multiply(base, previous, items, total, most, a_parts, own, b_parts, shape):
    first = base is None
    cols, peers = len(a_parts), len(b_parts) + 1
    any_spec = pl.BlockSpec(memory_space=pl.ANY)
    smem_spec = pl.BlockSpec(memory_space=SMEM)
    vmem_spec = pl.BlockSpec(memory_space=VMEM)
    given = [] if first else [base, previous]
    specs = [] if first else [smem_spec, vmem_spec]
    stored = own.shape[0] + (peers - 1) * CAPACITY * ROWS
    return pl.pallas_call(
        functools.partial(multiply_kernel, first, peers, cols),
        out_shape=[jax.ShapeDtypeStruct(shape, F32), jax.ShapeDtypeStruct((1,), I32)],
        in_specs=specs + [smem_spec] * 2 + [vmem_spec] + [any_spec] * (cols + peers),
        out_specs=[vmem_spec, smem_spec],
        scratch_shapes=[
            VMEM((cols,) + a_parts[0].shape, BF16),
            VMEM((stored, LANES), BF16),
            VMEM(((peers - 1) * FLAG, LANES), BF16),
            VMEM((shape[0] + 1, ROWS * shape[1], LANES), F32),
            pltpu.SemaphoreType.DMA((cols + 2 * peers - 1,)),
        ],
        compiler_params=pltpu.CompilerParams(vmem_limit_bytes=32 << 20),
        cost_estimate=pl.CostEstimate(flops=1 << 26, bytes_accessed=4 << 20, transcendentals=0),
        name="multiply",
    )(*given, items, total, most, *a_parts, own, *b_parts)


def send_rows(parts):
    return [shifted(part, "row", -(d + 1)) for d, part in enumerate(parts)]


def shards(a_blocks, a_index, b_blocks, b_cols, c_cols):
    rows = lax.axis_size("row")
    cols = lax.axis_size("col")
    per_col = rows // cols
    a_slots = a_blocks.shape[1] // per_col
    row_count = b_blocks.shape[0]
    span = -(-rows * row_count // cols // WORD) * WORD
    told = describe(a_index, b_cols.T, c_cols.T)
    told_all = lax.all_gather(told, ("row", "col"))
    packed, most = pack(None, told_all, b_blocks, rows, per_col, a_slots)
    arrived = send_rows(packed)
    a_late, b_late, _ = lax.optimization_barrier((a_blocks, b_blocks, most))
    a_ready, own = layout(a_late, b_late)
    a_parts = [a_ready] + [shifted(a_ready, "col", -h) for h in range(1, cols)]
    items, total = work_list(told_all, rows, row_count, span, per_col, a_slots)
    shape = (row_count, c_cols.shape[1], BS * BS)
    sums, rounds = multiply(None, None, items, total, most, a_parts, own, arrived, shape)

    def more(state):
        return state[0] < rounds[0]

    def one_round(state):
        at, sums = state
        base = jnp.reshape(at * CAPACITY, (1,))
        packed, _ = pack(base, told_all, b_blocks, rows, per_col, a_slots)
        arrived = send_rows(packed)
        sums, _ = multiply(base, sums, items, total, most, a_parts, own, arrived, shape)
        return at + 1, sums

    return lax.while_loop(more, one_round, (jnp.int32(1), sums))[1]


def solution(mesh):
    return jax.shard_map(
        shards,
        mesh=mesh,
        in_specs=(
            P(("sys", "row"), "col", None),
            P(None, ("sys", "row"), "col"),
            P(("sys", "row"), "col", None),
            P(("sys", "row"), "col"),
            P(("sys", "row"), "col"),
        ),
        out_specs=P(("sys", "row"), "col", None),
        check_vma=False,
    )
```

```python
import functools

import jax
import jax.numpy as jnp
from jax import lax
from jax.experimental import pallas as pl
from jax.experimental.pallas import tpu as pltpu
from jax.sharding import PartitionSpec as P

BS = 64
LANES = 128
ROWS = BS * BS // LANES
CAPACITY = 16
UNROLL = 4
SLOTS = 4
FLAG = 16
IDLE = 63
VMEM = pltpu.VMEM
SMEM = pltpu.SMEM
BF16 = jnp.bfloat16
F32 = jnp.float32
I32 = jnp.int32


def shifted(block, axis, distance):
    size = lax.axis_size(axis)
    route = [(i, (i + distance) % size) for i in range(size)]
    return lax.ppermute(block, axis, route)


A_ROW, A_COLUMN, RETAINED = 0, 1, 2
OFFERED = RETAINED + SLOTS
TOLD = 8


def describe_kernel(a_any, b_any, c_any, blocks_any, out, flat, a_ref, b_ref, c_ref, blocks, wide, sems):
    sources = [(blocks_any, blocks), (a_any, a_ref), (b_any, b_ref), (c_any, c_ref)]
    copies = [
        pltpu.make_async_copy(source, target, sems.at[at])
        for at, (source, target) in enumerate(sources)
    ]
    for copy in copies:
        copy.start()
    out[...] = jnp.full(out.shape, -1, I32)
    count, row_count = a_ref.shape[2], b_ref.shape[1]
    for copy in copies[1:]:
        copy.wait()
    out[0:2, 0:count] = a_ref[:, 0, :]
    out[RETAINED : RETAINED + c_ref.shape[0], 0:row_count] = c_ref[...]
    for n in range(b_ref.shape[0]):
        at = n * row_count
        out[OFFERED : OFFERED + 1, at : at + row_count] = b_ref[n : n + 1, :]
    copies[0].wait()
    wide[...] = blocks[...].astype(F32)
    for n in range(b_ref.shape[0]):
        flat[pl.ds(n * row_count, row_count), :] = wide[:, n, :].astype(BF16)


def describe(a_index, b_cols, c_cols, b_blocks):
    slots, row_count = b_cols.shape
    return pl.pallas_call(
        describe_kernel,
        out_shape=(
            jax.ShapeDtypeStruct((TOLD, LANES), I32),
            jax.ShapeDtypeStruct((slots * row_count, BS * BS), BF16),
        ),
        in_specs=[pl.BlockSpec(memory_space=pl.ANY)] * 4,
        out_specs=(pl.BlockSpec(memory_space=VMEM),) * 2,
        scratch_shapes=[
            VMEM(a_index.shape, I32),
            VMEM(b_cols.shape, I32),
            VMEM(c_cols.shape, I32),
            VMEM(b_blocks.shape, BF16),
            VMEM(b_blocks.shape, F32),
            pltpu.SemaphoreType.DMA((4,)),
        ],
        compiler_params=pltpu.CompilerParams(vmem_limit_bytes=32 << 20),
        name="describe",
    )(a_index, b_cols, c_cols, b_blocks)


def iota(shape, axis):
    return lax.broadcasted_iota(I32, shape, axis)


def turn_to_columns(rows, first, count):
    pick = (iota((count, LANES), 0) + first == iota((count, LANES), 1)).astype(BF16)
    return lax.dot_general(
        pick,
        rows.astype(F32).astype(BF16),
        (((1,), (1,)), ((), ())),
        preferred_element_type=F32,
    )


def matches(retained, offered, a_told, row_count, first_slot, a_slots):
    kept_columns = turn_to_columns(retained, 0, row_count)
    slot_columns = turn_to_columns(a_told, first_slot, a_slots)
    wanted = offered.astype(F32)
    kept = jnp.zeros((row_count, LANES), F32)
    which = jnp.zeros((row_count, LANES), F32)
    for m in range(SLOTS):
        column = kept_columns[:, RETAINED + m : RETAINED + m + 1]
        equal = (column == wanted) & (wanted >= 0)
        kept = jnp.where(equal, 1.0, kept)
        which = jnp.where(equal, float(m), which)
    a_rows = slot_columns[:, A_ROW : A_ROW + 1]
    a_columns = slot_columns[:, A_COLUMN : A_COLUMN + 1]
    shape = (a_slots, row_count)
    by_row = (a_rows == iota(shape, 1).astype(F32)).astype(BF16)
    by_column = a_columns == (iota((a_slots, LANES), 1) % row_count).astype(F32)
    both = jnp.concatenate([kept, which], axis=1).astype(BF16)
    both = jnp.dot(by_row, both, preferred_element_type=F32)
    pairs = jnp.where(by_column & (both[:, :LANES] > 0.5), 1.0, 0.0)
    return pairs, both[:, LANES:], a_rows


def places(needed):
    before = (iota((LANES, LANES), 0) < iota((LANES, LANES), 1)).astype(BF16)
    many = jnp.broadcast_to(needed, (8, LANES)).astype(BF16)
    return jnp.dot(many, before, preferred_element_type=F32)[0:1]


def each(count, body, start):
    if count > 8:
        return lax.fori_loop(0, count, body, start)
    for at in range(count):
        start = body(at, start)
    return start


def pack_kernel(first, peers, per_col, a_slots, row_count, *refs):
    refs = list(refs)
    base = 0 if first else refs.pop(0)[0]
    told = refs[:peers]
    flat = refs[peers]
    outs = refs[peers + 1 : 2 * peers]
    most, picks, packed = refs[2 * peers :]
    grid_row = lax.axis_index("row")
    grid_col = lax.axis_index("col")
    offered = told[0][grid_col, pl.ds(OFFERED, 1), :]
    top = jnp.zeros((1, 1), F32)
    first_slot = grid_row % per_col * a_slots if per_col > 1 else 0
    for d in range(1, peers):
        pairs, _, _ = matches(
            told[d][grid_col], offered, told[d][grid_row // per_col], row_count, first_slot, a_slots
        )
        needed = jnp.max(pairs, axis=0, keepdims=True)
        place = jnp.where(needed > 0.5, places(needed), -1.0).astype(I32)
        pick = (place == iota((CAPACITY, LANES), 0) + base).astype(BF16)
        picks[pl.ds((d - 1) * CAPACITY, CAPACITY), :] = pick
        top = jnp.maximum(top, jnp.sum(needed, axis=1, keepdims=True))
    most[...] = jnp.broadcast_to(top, most.shape)
    pick = picks[...][:, : flat.shape[0]]
    for t in range(0, ROWS, 2):
        both = flat[:, pl.ds(t * LANES, 2 * LANES)]
        both = jnp.dot(pick, both, preferred_element_type=F32)
        packed[:, t, :] = both[:, :LANES]
        packed[:, t + 1, :] = both[:, LANES:]
    for d in range(1, peers):
        out = outs[d - 1]
        for x in range(CAPACITY):
            out[pl.ds(x * ROWS, ROWS), :] = packed[(d - 1) * CAPACITY + x].astype(BF16)
        out[pl.ds(CAPACITY * ROWS, FLAG), :] = jnp.broadcast_to(top, (FLAG, LANES)).astype(BF16)


def pack(base, told, flat, row_count, per_col, a_slots):
    first = base is None
    peers = len(told)
    smem_spec = pl.BlockSpec(memory_space=SMEM)
    vmem_spec = pl.BlockSpec(memory_space=VMEM)
    given = [] if first else [base]
    results = pl.pallas_call(
        functools.partial(pack_kernel, first, peers, per_col, a_slots, row_count),
        out_shape=[jax.ShapeDtypeStruct((CAPACITY * ROWS + FLAG, LANES), BF16)] * (peers - 1)
        + [jax.ShapeDtypeStruct((8, LANES), F32)],
        in_specs=[smem_spec] * len(given) + [vmem_spec] * (peers + 1),
        out_specs=[vmem_spec] * peers,
        scratch_shapes=[
            VMEM(((peers - 1) * CAPACITY, LANES), BF16),
            VMEM(((peers - 1) * CAPACITY, ROWS, LANES), F32),
        ],
        compiler_params=pltpu.CompilerParams(vmem_limit_bytes=32 << 20),
        cost_estimate=pl.CostEstimate(flops=1 << 20, bytes_accessed=4 << 20, transcendentals=0),
        name="pack",
    )(*given, *told, flat)
    return results[:-1], results[-1]


def list_kernel(per_col, a_slots, row_count, peers, *refs):
    told = refs[:peers]
    items, starts, words, words_s, sem = refs[peers:]
    grid_row = lax.axis_index("row")
    grid_col = lax.axis_index("col")
    lane = iota((a_slots, LANES), 1)
    slot = iota((a_slots, LANES), 0)
    words[...] = jnp.full(words.shape, IDLE, I32)
    for d in range(peers):
        group = (grid_row + d) % peers
        holder = group // per_col
        first_slot = group % per_col * a_slots if per_col > 1 else 0
        offered = told[(peers - d) % peers][grid_col, pl.ds(OFFERED, 1), :]
        pairs, which, a_rows = matches(
            told[0][grid_col], offered, told[0][holder], row_count, first_slot, a_slots
        )
        if d == 0:
            place = iota((1, LANES), 1).astype(F32)
        else:
            place = places(jnp.max(pairs, axis=0, keepdims=True))
        stacked = jnp.concatenate([pairs, pairs * place, pairs * which], axis=0).astype(BF16)
        to_slot = iota((LANES, LANES), 1) == iota((LANES, LANES), 0) // row_count + d * SLOTS
        by_slot = jnp.dot(stacked, to_slot.astype(BF16), preferred_element_type=F32)
        hit = by_slot[:a_slots] > 0.5
        at = by_slot[a_slots : 2 * a_slots].astype(I32)
        out = (a_rows * SLOTS + by_slot[2 * a_slots :]).astype(I32)
        a_slot = holder * per_col * a_slots + first_slot + slot
        word = ((a_slot * 64 + out) * 64 + at) * 64 + d
        words[...] = jnp.where(hit & (lane // SLOTS == d), word, words[...])
    fetch([(words, words_s)], sem)

    def one_peer(d, length):
        starts[d] = length
        for n in range(SLOTS):
            for s in range(a_slots):
                word = words_s[s, d * SLOTS + n]
                items[length] = word
                length = length + (word & IDLE != IDLE).astype(I32)
        for u in range(UNROLL):
            items[length + u] = IDLE
        return (length + UNROLL - 1) // UNROLL * UNROLL

    starts[peers] = lax.fori_loop(0, peers, one_peer, jnp.int32(0))


def work_list(told, row_count, per_col, a_slots):
    peers = len(told)
    most_items = peers * (a_slots * SLOTS + UNROLL) + UNROLL
    return pl.pallas_call(
        functools.partial(list_kernel, per_col, a_slots, row_count, peers),
        out_shape=[
            jax.ShapeDtypeStruct((most_items,), I32),
            jax.ShapeDtypeStruct((peers + 1,), I32),
        ],
        in_specs=[pl.BlockSpec(memory_space=VMEM)] * peers,
        out_specs=[pl.BlockSpec(memory_space=SMEM)] * 2,
        scratch_shapes=[
            VMEM((a_slots, LANES), I32),
            SMEM((a_slots, LANES), I32),
            pltpu.SemaphoreType.DMA((1,)),
        ],
        cost_estimate=pl.CostEstimate(flops=1 << 20, bytes_accessed=1 << 16, transcendentals=0),
        name="work_list",
    )(*told)


def fetch(copies, sems):
    started = [
        pltpu.make_async_copy(source, target, sems.at[at])
        for at, (source, target) in enumerate(copies)
    ]
    for copy in started:
        copy.start()
    for copy in started:
        copy.wait()


def add_products(items, start, stop, a_ref, b_ref, sums, window=None):
    low = iota((ROWS, LANES), 1) < BS
    nothing = jnp.zeros((ROWS, LANES), BF16)
    idle_row = sums.shape[0] - 1

    def some_items(step, carry):
        for u in range(UNROLL):
            word = items[step * UNROLL + u]
            place = (word >> 6) & 63
            target = (word >> 12) & 63
            used = (word & IDLE) != IDLE
            if window is not None:
                place = place - window
                used = used & (place >= 0) & (place < CAPACITY)
                place = jnp.where(used, place, 0)
            a_at = pl.multiple_of((word >> 18) * ROWS, ROWS)
            b_at = pl.multiple_of(place * ROWS, ROWS)
            block = b_ref[pl.ds(b_at, ROWS), :]
            turned = jnp.concatenate([block[:, BS:], block[:, :BS]], axis=1)
            right = jnp.concatenate(
                [
                    jnp.where(low, block, nothing),
                    jnp.where(low, turned, nothing),
                    jnp.where(low, nothing, turned),
                    jnp.where(low, nothing, block),
                ],
                axis=0,
            )
            term = jnp.dot(a_ref[pl.ds(a_at, ROWS), :], right, preferred_element_type=F32)
            i = jnp.where(used, target // SLOTS, idle_row)
            sums[i, pl.ds(target % SLOTS, ROWS, stride=SLOTS), :] += term
        return carry

    lax.fori_loop(start // UNROLL, stop // UNROLL, some_items, 0)


def stage_kernel(cols, *refs):
    a_refs, b_ref, items, starts = refs[:cols], refs[cols], refs[cols + 1], refs[cols + 2]
    a_out, sums, a_wide, b_wide, b_own = refs[cols + 3 :]
    source = iota((LANES, LANES), 0)
    target = iota((LANES, LANES), 1)
    wanted = (target // BS) * BS + 2 * (target % ROWS) + (target // ROWS) % 2
    order = (source == wanted).astype(BF16)
    slots = a_refs[0].shape[1]
    grid_col = lax.axis_index("col")
    for t in range(ROWS):
        pieces = [ref[0, :, pl.ds(t * LANES, LANES)] for ref in a_refs]
        done = jnp.dot(jnp.concatenate(pieces, axis=0), order, preferred_element_type=F32)
        a_wide[:, t, :] = done
    for h in range(cols):
        first = (grid_col + h) % cols * slots
        for s in range(slots):
            at = pl.multiple_of((first + s) * ROWS, ROWS)
            a_out[pl.ds(at, ROWS), :] = a_wide[h * slots + s].astype(BF16)
    row_count, slots = b_ref.shape[0], b_ref.shape[1]

    def one_row(k, carry):
        for t in range(ROWS):
            b_wide[pl.ds(t * slots, slots), :] = b_ref[k, :, pl.ds(t * LANES, LANES)].astype(F32)
        for n in range(slots):
            at = pl.multiple_of((n * row_count + k) * ROWS, ROWS)
            b_own[pl.ds(at, ROWS), :] = b_wide[pl.ds(n, ROWS, stride=slots), :].astype(BF16)
        return carry

    lax.fori_loop(0, row_count, one_row, 0)
    sums[...] = jnp.zeros_like(sums)
    add_products(items, 0, starts[1], a_out, b_own, sums)


def stage(a_parts, b_blocks, items, starts):
    cols, slots = len(a_parts), a_parts[0].shape[1]
    row_count, b_slots = b_blocks.shape[0], b_blocks.shape[1]
    vmem_spec = pl.BlockSpec(memory_space=VMEM)
    smem_spec = pl.BlockSpec(memory_space=SMEM)
    return pl.pallas_call(
        functools.partial(stage_kernel, cols),
        out_shape=(
            jax.ShapeDtypeStruct((cols * slots * ROWS, LANES), BF16),
            jax.ShapeDtypeStruct((row_count + 1, ROWS * b_slots, LANES), F32),
        ),
        in_specs=[vmem_spec] * (cols + 1) + [smem_spec] * 2,
        out_specs=(vmem_spec,) * 2,
        scratch_shapes=[
            VMEM((cols * slots, ROWS, LANES), F32),
            VMEM((b_slots * ROWS, LANES), F32),
            VMEM((row_count * b_slots * ROWS, LANES), BF16),
        ],
        compiler_params=pltpu.CompilerParams(vmem_limit_bytes=40 << 20),
        cost_estimate=pl.CostEstimate(flops=1 << 24, bytes_accessed=4 << 20, transcendentals=0),
        name="stage",
    )(*a_parts, b_blocks, items, starts)


def multiply_kernel(first, peers, *refs):
    refs = list(refs)
    base = 0 if first else refs.pop(0)[0]
    items, starts, most, a_ref, sums_in = refs[:5]
    b_refs = refs[5 : 4 + peers]
    out, rounds, sums = refs[4 + peers :]
    width = CAPACITY * ROWS
    needed = jnp.max(most[...])
    for ref in b_refs:
        needed = jnp.maximum(needed, jnp.max(ref[pl.ds(width, FLAG), :].astype(F32)))
    rounds[0] = (needed.astype(I32) + CAPACITY - 1) // CAPACITY
    for d in range(1, peers):
        add_products(items, starts[d], starts[d + 1], a_ref, b_refs[d - 1], sums, window=base)
    row_count, kept = out.shape[0], out.shape[1]

    def one_row(i, carry):
        for t in range(ROWS):
            out[i, :, pl.ds(t * LANES, LANES)] = sums[i, pl.ds(t * kept, kept), :]
        return carry

    lax.fori_loop(0, row_count, one_row, 0)


def multiply(base, items, starts, most, a_ready, sums, b_parts, shape):
    first = base is None
    peers = len(b_parts) + 1
    smem_spec = pl.BlockSpec(memory_space=SMEM)
    vmem_spec = pl.BlockSpec(memory_space=VMEM)
    given = [] if first else [base]
    return pl.pallas_call(
        functools.partial(multiply_kernel, first, peers),
        out_shape=[
            jax.ShapeDtypeStruct(shape, F32),
            jax.ShapeDtypeStruct((1,), I32),
            jax.ShapeDtypeStruct(sums.shape, F32),
        ],
        in_specs=[smem_spec] * (len(given) + 2) + [vmem_spec] * (2 + peers),
        out_specs=[vmem_spec, smem_spec, vmem_spec],
        input_output_aliases={len(given) + 4: 2},
        compiler_params=pltpu.CompilerParams(vmem_limit_bytes=32 << 20),
        cost_estimate=pl.CostEstimate(flops=1 << 26, bytes_accessed=4 << 20, transcendentals=0),
        name="multiply",
    )(*given, items, starts, most, a_ready, sums, *b_parts)


def send_rows(parts):
    return [shifted(part, "row", -(d + 1)) for d, part in enumerate(parts)]


def shards(a_blocks, a_index, b_blocks, b_cols, c_cols):
    rows = lax.axis_size("row")
    cols = lax.axis_size("col")
    per_col = rows // cols
    a_slots = a_blocks.shape[1] // per_col
    row_count = b_blocks.shape[0]
    told, flat = describe(a_index, b_cols.T, c_cols.T, b_blocks)
    told = lax.all_gather(told, "col")
    told = [told] + [shifted(told, "row", d) for d in range(1, rows)]
    packed, most = pack(None, told, flat, row_count, per_col, a_slots)
    arrived = send_rows(packed)
    items, starts = work_list(told, row_count, per_col, a_slots)
    a_late, _ = lax.optimization_barrier((a_blocks, most))
    a_parts = [a_blocks] + [shifted(a_late, "col", -h) for h in range(1, cols)]
    a_ready, sums = stage(a_parts, b_blocks, items, starts)
    shape = (row_count, c_cols.shape[1], BS * BS)
    out, rounds, sums = multiply(None, items, starts, most, a_ready, sums, arrived, shape)

    def more(state):
        return state[0] < rounds[0]

    def one_round(state):
        at, sums, _ = state
        base = jnp.reshape(at * CAPACITY, (1,))
        packed, most = pack(base, told, flat, row_count, per_col, a_slots)
        arrived = send_rows(packed)
        out, _, sums = multiply(base, items, starts, most, a_ready, sums, arrived, shape)
        return at + 1, sums, out

    return lax.while_loop(more, one_round, (jnp.int32(1), sums, out))[2]


def solution(mesh):
    return jax.shard_map(
        shards,
        mesh=mesh,
        in_specs=(
            P(("sys", "row"), "col", None),
            P(None, ("sys", "row"), "col"),
            P(("sys", "row"), "col", None),
            P(("sys", "row"), "col"),
            P(("sys", "row"), "col"),
        ),
        out_specs=P(("sys", "row"), "col", None),
        check_vma=False,
    )
```

```python
import functools

import jax
import jax.numpy as jnp
from jax import lax
from jax.experimental import pallas as pl
from jax.experimental.pallas import tpu as pltpu
from jax.sharding import PartitionSpec as P

BS = 64
LANES = 128
ROWS = BS * BS // LANES
CAPACITY = 16
UNROLL = 4
SLOTS = 4
FLAG = 16
IDLE = 63
VMEM = pltpu.VMEM
SMEM = pltpu.SMEM
BF16 = jnp.bfloat16
F32 = jnp.float32
I32 = jnp.int32


def exchanged(block, axis, distance):
    size = lax.axis_size(axis)
    return lax.ppermute(block, axis, [(i, i ^ distance) for i in range(size)])


def describe(a_parts, b_cols, c_cols):
    parts = [part[:, 0, :] for part in a_parts] + [c_cols, b_cols]
    rows = sum(part.shape[0] for part in parts)
    wide = [jnp.pad(p, ((0, 0), (0, LANES - p.shape[1])), constant_values=-1) for p in parts]
    return jnp.concatenate(wide + [jnp.full((-rows % 8, LANES), -1, I32)], axis=0)


def offers(told, cols, row_count):
    start = 2 * cols + SLOTS
    rows = told[pl.ds(start, SLOTS), :]
    lane = iota((1, LANES), 1)
    result = rows[0:1]
    for n in range(1, SLOTS):
        moved = pltpu.roll(rows, n * row_count, 1)[n : n + 1]
        result = jnp.where(lane // row_count == n, moved, result)
    return result


def flatten_kernel(b_ref, flat, wide):
    wide[...] = b_ref[...].astype(F32)
    row_count = b_ref.shape[0]
    for n in range(SLOTS):
        flat[pl.ds(n * row_count, row_count), :] = wide[:, n, :].astype(BF16)


def flatten(b_blocks):
    vmem_spec = pl.BlockSpec(memory_space=VMEM)
    count = b_blocks.shape[0] * b_blocks.shape[1]
    return pl.pallas_call(
        flatten_kernel,
        out_shape=jax.ShapeDtypeStruct((count, BS * BS), BF16),
        in_specs=[vmem_spec],
        out_specs=vmem_spec,
        scratch_shapes=[VMEM(b_blocks.shape, F32)],
        compiler_params=pltpu.CompilerParams(vmem_limit_bytes=24 << 20),
        cost_estimate=pl.CostEstimate(flops=1 << 20, bytes_accessed=8 << 20, transcendentals=0),
        name="flatten",
    )(b_blocks)


def iota(shape, axis):
    return lax.broadcasted_iota(I32, shape, axis)


def turn_to_columns(rows, first, count):
    pick = (iota((count, LANES), 0) + first == iota((count, LANES), 1)).astype(BF16)
    return lax.dot_general(
        pick,
        rows.astype(F32).astype(BF16),
        (((1,), (1,)), ((), ())),
        preferred_element_type=F32,
    )


def matches(receiver, offered, holder, cols, row_count, first_slot, a_slots):
    turned = 2 * (holder ^ lax.axis_index("col"))
    rows = [receiver[pl.ds(turned, 1), :], receiver[pl.ds(turned + 1, 1), :]]
    rows += [receiver[pl.ds(2 * cols, SLOTS), :]]
    rows = jnp.concatenate(rows + [jnp.zeros((8 - 2 - SLOTS, LANES), I32)], axis=0)
    kept_columns = turn_to_columns(rows, 0, row_count)
    if isinstance(first_slot, int) and first_slot == 0 and a_slots == row_count:
        slot_columns = kept_columns
    else:
        slot_columns = turn_to_columns(rows, first_slot, a_slots)
    wanted = offered.astype(F32)
    kept = jnp.zeros((row_count, LANES), F32)
    which = jnp.zeros((row_count, LANES), F32)
    for m in range(SLOTS):
        column = kept_columns[:, 2 + m : 3 + m]
        equal = (column == wanted) & (wanted >= 0)
        kept = jnp.where(equal, 1.0, kept)
        which = jnp.where(equal, float(m), which)
    a_rows = slot_columns[:, 0:1]
    a_columns = slot_columns[:, 1:2]
    shape = (a_slots, row_count)
    by_row = (a_rows == iota(shape, 1).astype(F32)).astype(BF16)
    by_column = a_columns == (iota((a_slots, LANES), 1) % row_count).astype(F32)
    both = jnp.concatenate([kept, which], axis=1).astype(BF16)
    both = jnp.dot(by_row, both, preferred_element_type=F32)
    pairs = jnp.where(by_column & (both[:, :LANES] > 0.5), 1.0, 0.0)
    return pairs, both[:, LANES:], a_rows


def places(needed):
    before = (iota((LANES, LANES), 0) < iota((LANES, LANES), 1)).astype(BF16)
    many = jnp.broadcast_to(needed, (8, LANES)).astype(BF16)
    return jnp.dot(many, before, preferred_element_type=F32)[0:1]


def each(count, body, start):
    if count > 8:
        return lax.fori_loop(0, count, body, start)
    for at in range(count):
        start = body(at, start)
    return start


def pack_kernel(first, peers, cols, a_slots, row_count, *refs):
    refs = list(refs)
    base = 0 if first else refs.pop(0)[0]
    told = refs[:peers]
    flat = refs[peers]
    outs = refs[peers + 1 : 2 * peers]
    most, picks, packed = refs[2 * peers :]
    grid_row = lax.axis_index("row")
    per_col = peers // cols
    offered = offers(told[0], cols, row_count)
    top = jnp.zeros((1, 1), F32)
    first_slot = grid_row % per_col * a_slots if per_col > 1 else 0
    for d in range(1, peers):
        pairs, _, _ = matches(
            told[d], offered, grid_row // per_col, cols, row_count, first_slot, a_slots
        )
        needed = jnp.max(pairs, axis=0, keepdims=True)
        place = jnp.where(needed > 0.5, places(needed), -1.0).astype(I32)
        pick = (place == iota((CAPACITY, LANES), 0) + base).astype(BF16)
        picks[pl.ds((d - 1) * CAPACITY, CAPACITY), :] = pick
        top = jnp.maximum(top, jnp.sum(needed, axis=1, keepdims=True))
    most[...] = jnp.broadcast_to(top, most.shape)
    pick = picks[...][:, : flat.shape[0]]
    for t in range(0, ROWS, 2):
        both = flat[:, pl.ds(t * LANES, 2 * LANES)]
        both = jnp.dot(pick, both, preferred_element_type=F32)
        packed[:, t, :] = both[:, :LANES]
        packed[:, t + 1, :] = both[:, LANES:]
    for d in range(1, peers):
        out = outs[d - 1]
        for x in range(CAPACITY):
            out[pl.ds(x * ROWS, ROWS), :] = packed[(d - 1) * CAPACITY + x].astype(BF16)
        out[pl.ds(CAPACITY * ROWS, FLAG), :] = jnp.broadcast_to(top, (FLAG, LANES)).astype(BF16)


def pack(base, told, flat, cols, row_count, a_slots):
    first = base is None
    peers = len(told)
    smem_spec = pl.BlockSpec(memory_space=SMEM)
    vmem_spec = pl.BlockSpec(memory_space=VMEM)
    given = [] if first else [base]
    results = pl.pallas_call(
        functools.partial(pack_kernel, first, peers, cols, a_slots, row_count),
        out_shape=[jax.ShapeDtypeStruct((CAPACITY * ROWS + FLAG, LANES), BF16)] * (peers - 1)
        + [jax.ShapeDtypeStruct((8, LANES), F32)],
        in_specs=[smem_spec] * len(given) + [vmem_spec] * (peers + 1),
        out_specs=[vmem_spec] * peers,
        scratch_shapes=[
            VMEM(((peers - 1) * CAPACITY, LANES), BF16),
            VMEM(((peers - 1) * CAPACITY, ROWS, LANES), F32),
        ],
        compiler_params=pltpu.CompilerParams(vmem_limit_bytes=32 << 20),
        cost_estimate=pl.CostEstimate(flops=1 << 20, bytes_accessed=4 << 20, transcendentals=0),
        name="pack",
    )(*given, *told, flat)
    return results[:-1], results[-1]


def list_kernel(cols, a_slots, row_count, peers, *refs):
    told = refs[:peers]
    items, starts, words, words_s, sem = refs[peers:]
    grid_row = lax.axis_index("row")
    per_col = peers // cols
    lane = iota((a_slots, LANES), 1)
    slot = iota((a_slots, LANES), 0)
    words[...] = jnp.full(words.shape, IDLE, I32)
    for d in range(peers):
        group = grid_row ^ d
        holder = group // per_col
        first_slot = group % per_col * a_slots if per_col > 1 else 0
        offered = offers(told[d], cols, row_count)
        pairs, which, a_rows = matches(
            told[0], offered, holder, cols, row_count, first_slot, a_slots
        )
        if d == 0:
            place = iota((1, LANES), 1).astype(F32)
        else:
            place = places(jnp.max(pairs, axis=0, keepdims=True))
        stacked = jnp.concatenate([pairs, pairs * place, pairs * which], axis=0).astype(BF16)
        to_slot = iota((LANES, LANES), 1) == iota((LANES, LANES), 0) // row_count + d * SLOTS
        by_slot = jnp.dot(stacked, to_slot.astype(BF16), preferred_element_type=F32)
        hit = by_slot[:a_slots] > 0.5
        at = by_slot[a_slots : 2 * a_slots].astype(I32)
        out = (a_rows * SLOTS + by_slot[2 * a_slots :]).astype(I32)
        a_slot = holder * per_col * a_slots + first_slot + slot
        word = ((a_slot * 64 + out) * 64 + at) * 64 + d
        words[...] = jnp.where(hit & (lane // SLOTS == d), word, words[...])
    fetch([(words, words_s)], sem)

    def one_peer(d, length):
        starts[d] = length
        for n in range(SLOTS):
            for s in range(a_slots):
                word = words_s[s, d * SLOTS + n]
                items[length] = word
                length = length + (word & IDLE != IDLE).astype(I32)
        for u in range(UNROLL):
            items[length + u] = IDLE
        return (length + UNROLL - 1) // UNROLL * UNROLL

    starts[peers] = lax.fori_loop(0, peers, one_peer, jnp.int32(0))


def work_list(told, cols, row_count, a_slots):
    peers = len(told)
    most_items = peers * (a_slots * SLOTS + UNROLL) + UNROLL
    return pl.pallas_call(
        functools.partial(list_kernel, cols, a_slots, row_count, peers),
        out_shape=[
            jax.ShapeDtypeStruct((most_items,), I32),
            jax.ShapeDtypeStruct((peers + 1,), I32),
        ],
        in_specs=[pl.BlockSpec(memory_space=VMEM)] * peers,
        out_specs=[pl.BlockSpec(memory_space=SMEM)] * 2,
        scratch_shapes=[
            VMEM((a_slots, LANES), I32),
            SMEM((a_slots, LANES), I32),
            pltpu.SemaphoreType.DMA((1,)),
        ],
        cost_estimate=pl.CostEstimate(flops=1 << 20, bytes_accessed=1 << 16, transcendentals=0),
        name="work_list",
    )(*told)


def fetch(copies, sems):
    started = [
        pltpu.make_async_copy(source, target, sems.at[at])
        for at, (source, target) in enumerate(copies)
    ]
    for copy in started:
        copy.start()
    for copy in started:
        copy.wait()


def add_products(items, start, stop, a_ref, b_ref, sums, window=None):
    low = iota((ROWS, LANES), 1) < BS
    nothing = jnp.zeros((ROWS, LANES), BF16)
    idle_row = sums.shape[0] - 1

    def some_items(step, carry):
        for u in range(UNROLL):
            word = items[step * UNROLL + u]
            place = (word >> 6) & 63
            target = (word >> 12) & 63
            used = (word & IDLE) != IDLE
            if window is not None:
                place = place - window
                used = used & (place >= 0) & (place < CAPACITY)
                place = jnp.where(used, place, 0)
            a_at = pl.multiple_of((word >> 18) * ROWS, ROWS)
            b_at = pl.multiple_of(place * ROWS, ROWS)
            block = b_ref[pl.ds(b_at, ROWS), :]
            turned = jnp.concatenate([block[:, BS:], block[:, :BS]], axis=1)
            right = jnp.concatenate(
                [
                    jnp.where(low, block, nothing),
                    jnp.where(low, turned, nothing),
                    jnp.where(low, nothing, turned),
                    jnp.where(low, nothing, block),
                ],
                axis=0,
            )
            term = jnp.dot(a_ref[pl.ds(a_at, ROWS), :], right, preferred_element_type=F32)
            i = jnp.where(used, target // SLOTS, idle_row)
            sums[i, pl.ds(target % SLOTS, ROWS, stride=SLOTS), :] += term
        return carry

    lax.fori_loop(start // UNROLL, stop // UNROLL, some_items, 0)


def stage_kernel(cols, *refs):
    a_refs, b_ref, items, starts = refs[:cols], refs[cols], refs[cols + 1], refs[cols + 2]
    a_out, sums, a_wide, b_wide, b_own = refs[cols + 3 :]
    source = iota((LANES, LANES), 0)
    target = iota((LANES, LANES), 1)
    wanted = (target // BS) * BS + 2 * (target % ROWS) + (target // ROWS) % 2
    order = (source == wanted).astype(BF16)
    slots = a_refs[0].shape[1]
    grid_col = lax.axis_index("col")
    for t in range(ROWS):
        pieces = [ref[0, :, pl.ds(t * LANES, LANES)] for ref in a_refs]
        done = jnp.dot(jnp.concatenate(pieces, axis=0), order, preferred_element_type=F32)
        a_wide[:, t, :] = done
    for h in range(cols):
        first = (grid_col ^ h) * slots
        for s in range(slots):
            at = pl.multiple_of((first + s) * ROWS, ROWS)
            a_out[pl.ds(at, ROWS), :] = a_wide[h * slots + s].astype(BF16)
    row_count, slots = b_ref.shape[0], b_ref.shape[1]

    def one_row(k, carry):
        for t in range(ROWS):
            b_wide[pl.ds(t * slots, slots), :] = b_ref[k, :, pl.ds(t * LANES, LANES)].astype(F32)
        for n in range(slots):
            at = pl.multiple_of((n * row_count + k) * ROWS, ROWS)
            b_own[pl.ds(at, ROWS), :] = b_wide[pl.ds(n, ROWS, stride=slots), :].astype(BF16)
        return carry

    lax.fori_loop(0, row_count, one_row, 0)
    sums[...] = jnp.zeros_like(sums)
    add_products(items, 0, starts[1], a_out, b_own, sums)


def stage(a_parts, b_blocks, items, starts):
    cols, slots = len(a_parts), a_parts[0].shape[1]
    row_count, b_slots = b_blocks.shape[0], b_blocks.shape[1]
    vmem_spec = pl.BlockSpec(memory_space=VMEM)
    smem_spec = pl.BlockSpec(memory_space=SMEM)
    return pl.pallas_call(
        functools.partial(stage_kernel, cols),
        out_shape=(
            jax.ShapeDtypeStruct((cols * slots * ROWS, LANES), BF16),
            jax.ShapeDtypeStruct((row_count + 1, ROWS * b_slots, LANES), F32),
        ),
        in_specs=[vmem_spec] * (cols + 1) + [smem_spec] * 2,
        out_specs=(vmem_spec,) * 2,
        scratch_shapes=[
            VMEM((cols * slots, ROWS, LANES), F32),
            VMEM((b_slots * ROWS, LANES), F32),
            VMEM((row_count * b_slots * ROWS, LANES), BF16),
        ],
        compiler_params=pltpu.CompilerParams(vmem_limit_bytes=40 << 20),
        cost_estimate=pl.CostEstimate(flops=1 << 24, bytes_accessed=4 << 20, transcendentals=0),
        name="stage",
    )(*a_parts, b_blocks, items, starts)


def multiply_kernel(first, peers, *refs):
    refs = list(refs)
    base = 0 if first else refs.pop(0)[0]
    items, starts, most, a_ref, sums_in = refs[:5]
    b_refs = refs[5 : 4 + peers]
    out, rounds, sums, rows, sems = refs[4 + peers :]
    width = CAPACITY * ROWS
    needed = jnp.max(most[...])
    for ref in b_refs:
        needed = jnp.maximum(needed, jnp.max(ref[pl.ds(width, FLAG), :].astype(F32)))
    rounds[0] = (needed.astype(I32) + CAPACITY - 1) // CAPACITY
    for d in range(1, peers):
        add_products(items, starts[d], starts[d + 1], a_ref, b_refs[d - 1], sums, window=base)
    row_count, kept = out.shape[0], out.shape[1]
    copies = []
    for i in range(row_count):
        for t in range(ROWS):
            rows[i, :, pl.ds(t * LANES, LANES)] = sums[i, pl.ds(t * kept, kept), :]
        copies.append(pltpu.make_async_copy(rows.at[i], out.at[i], sems.at[i]))
        copies[-1].start()
    for copy in copies:
        copy.wait()


def multiply(base, items, starts, most, a_ready, sums, b_parts, shape):
    first = base is None
    peers = len(b_parts) + 1
    smem_spec = pl.BlockSpec(memory_space=SMEM)
    vmem_spec = pl.BlockSpec(memory_space=VMEM)
    given = [] if first else [base]
    return pl.pallas_call(
        functools.partial(multiply_kernel, first, peers),
        out_shape=[
            jax.ShapeDtypeStruct(shape, F32),
            jax.ShapeDtypeStruct((1,), I32),
            jax.ShapeDtypeStruct(sums.shape, F32),
        ],
        in_specs=[smem_spec] * (len(given) + 2) + [vmem_spec] * (2 + peers),
        out_specs=[pl.BlockSpec(memory_space=pl.ANY), smem_spec, vmem_spec],
        input_output_aliases={len(given) + 4: 2},
        scratch_shapes=[VMEM(shape, F32), pltpu.SemaphoreType.DMA((shape[0],))],
        compiler_params=pltpu.CompilerParams(vmem_limit_bytes=32 << 20),
        cost_estimate=pl.CostEstimate(flops=1 << 26, bytes_accessed=4 << 20, transcendentals=0),
        name="multiply",
    )(*given, items, starts, most, a_ready, sums, *b_parts)


def shards(a_blocks, a_index, b_blocks, b_cols, c_cols):
    rows = lax.axis_size("row")
    cols = lax.axis_size("col")
    a_slots = a_blocks.shape[1] * cols // rows
    row_count = b_blocks.shape[0]

    def send_rows(parts):
        return [exchanged(part, "row", d + 1) for d, part in enumerate(parts)]

    index_parts = [a_index] + [exchanged(a_index, "col", h) for h in range(1, cols)]
    told = describe(index_parts, b_cols.T, c_cols.T)
    told = [told] + send_rows([told] * (rows - 1))
    flat = flatten(b_blocks)
    packed, most = pack(None, told, flat, cols, row_count, a_slots)
    arrived = send_rows(packed)
    items, starts = work_list(told, cols, row_count, a_slots)
    a_late, _ = lax.optimization_barrier((a_blocks, most))
    a_parts = [a_blocks] + [exchanged(a_late, "col", h) for h in range(1, cols)]
    a_ready, sums = stage(a_parts, b_blocks, items, starts)
    shape = (row_count, c_cols.shape[1], BS * BS)
    out, rounds, sums = multiply(None, items, starts, most, a_ready, sums, arrived, shape)

    def more(state):
        return state[0] < rounds[0]

    def one_round(state):
        at, sums, _ = state
        base = jnp.reshape(at * CAPACITY, (1,))
        packed, most = pack(base, told, flat, cols, row_count, a_slots)
        arrived = send_rows(packed)
        out, _, sums = multiply(base, items, starts, most, a_ready, sums, arrived, shape)
        return at + 1, sums, out

    return lax.while_loop(more, one_round, (jnp.int32(1), sums, out))[2]


def solution(mesh):
    return jax.shard_map(
        shards,
        mesh=mesh,
        in_specs=(
            P(("sys", "row"), "col", None),
            P(None, ("sys", "row"), "col"),
            P(("sys", "row"), "col", None),
            P(("sys", "row"), "col"),
            P(("sys", "row"), "col"),
        ),
        out_specs=P(("sys", "row"), "col", None),
        check_vma=False,
    )
```

```python
import functools

import jax
import jax.numpy as jnp
from jax import lax
from jax.experimental import pallas as pl
from jax.experimental.pallas import tpu as pltpu
from jax.sharding import PartitionSpec as P

BS = 64
LANES = 128
ROWS = BS * BS // LANES
CAPACITY = 16
UNROLL = 4
SLOTS = 4
FLAG = 16
IDLE = 63
VMEM = pltpu.VMEM
SMEM = pltpu.SMEM
BF16 = jnp.bfloat16
F32 = jnp.float32
I32 = jnp.int32


def exchanged(block, axis, distance):
    size = lax.axis_size(axis)
    return lax.ppermute(block, axis, [(i, i ^ distance) for i in range(size)])


def describe(a_parts, b_cols, c_cols):
    cols = len(a_parts)
    total = -(-(2 * cols + 2 * SLOTS) // 8) * 8

    def placed(part, at):
        after = (total - at - part.shape[0], LANES - part.shape[1])
        return jnp.pad(part, ((at, after[0]), (0, after[1])), constant_values=-1)

    own = jnp.maximum(placed(c_cols, 2 * cols), placed(b_cols, 2 * cols + SLOTS))
    told = lax.optimization_barrier(jnp.maximum(own, placed(a_parts[0][:, 0, :], 0)))
    for h in range(1, cols):
        told = jnp.maximum(told, placed(a_parts[h][:, 0, :], 2 * h))
    return told


def offers(told, cols, row_count):
    start = 2 * cols + SLOTS
    rows = told[pl.ds(start, SLOTS), :]
    lane = iota((1, LANES), 1)
    result = rows[0:1]
    for n in range(1, SLOTS):
        moved = pltpu.roll(rows, n * row_count, 1)[n : n + 1]
        result = jnp.where(lane // row_count == n, moved, result)
    return result


def flatten_kernel(b_ref, flat, wide):
    row_count = b_ref.shape[0]
    for k in range(row_count):
        for t in range(ROWS):
            wide[k, pl.ds(t * SLOTS, SLOTS), :] = b_ref[k, :, pl.ds(t * LANES, LANES)].astype(F32)
    for t in range(ROWS):
        for n in range(SLOTS):
            piece = wide[:, t * SLOTS + n, :].astype(BF16)
            flat[pl.ds(n * row_count, row_count), pl.ds(t * LANES, LANES)] = piece


def flatten(b_blocks):
    vmem_spec = pl.BlockSpec(memory_space=VMEM)
    count = b_blocks.shape[0] * b_blocks.shape[1]
    return pl.pallas_call(
        flatten_kernel,
        out_shape=jax.ShapeDtypeStruct((count, BS * BS), BF16),
        in_specs=[vmem_spec],
        out_specs=vmem_spec,
        scratch_shapes=[VMEM((b_blocks.shape[0], b_blocks.shape[1] * ROWS, LANES), F32)],
        compiler_params=pltpu.CompilerParams(vmem_limit_bytes=24 << 20),
        cost_estimate=pl.CostEstimate(flops=1 << 20, bytes_accessed=8 << 20, transcendentals=0),
        name="flatten",
    )(b_blocks)


def iota(shape, axis):
    return lax.broadcasted_iota(I32, shape, axis)


def turn_to_columns(rows, first, count):
    pick = (iota((count, LANES), 0) + first == iota((count, LANES), 1)).astype(BF16)
    return lax.dot_general(
        pick,
        rows.astype(F32).astype(BF16),
        (((1,), (1,)), ((), ())),
        preferred_element_type=F32,
    )


def matches(receiver, offered, holder, cols, row_count, first_slot, a_slots):
    turned = 2 * (holder ^ lax.axis_index("col"))
    rows = [receiver[pl.ds(turned, 1), :], receiver[pl.ds(turned + 1, 1), :]]
    rows += [receiver[pl.ds(2 * cols, SLOTS), :]]
    rows = jnp.concatenate(rows + [jnp.zeros((8 - 2 - SLOTS, LANES), I32)], axis=0)
    kept_columns = turn_to_columns(rows, 0, row_count)
    if isinstance(first_slot, int) and first_slot == 0 and a_slots == row_count:
        slot_columns = kept_columns
    else:
        slot_columns = turn_to_columns(rows, first_slot, a_slots)
    wanted = offered.astype(F32)
    kept = jnp.zeros((row_count, LANES), F32)
    which = jnp.zeros((row_count, LANES), F32)
    for m in range(SLOTS):
        column = kept_columns[:, 2 + m : 3 + m]
        equal = (column == wanted) & (wanted >= 0)
        kept = jnp.where(equal, 1.0, kept)
        which = jnp.where(equal, float(m), which)
    a_rows = slot_columns[:, 0:1]
    a_columns = slot_columns[:, 1:2]
    shape = (a_slots, row_count)
    by_row = (a_rows == iota(shape, 1).astype(F32)).astype(BF16)
    by_column = a_columns == (iota((a_slots, LANES), 1) % row_count).astype(F32)
    both = jnp.concatenate([kept, which], axis=1).astype(BF16)
    both = jnp.dot(by_row, both, preferred_element_type=F32)
    pairs = jnp.where(by_column & (both[:, :LANES] > 0.5), 1.0, 0.0)
    return pairs, both[:, LANES:], a_rows


def places(needed):
    before = (iota((LANES, LANES), 0) < iota((LANES, LANES), 1)).astype(BF16)
    many = jnp.broadcast_to(needed, (8, LANES)).astype(BF16)
    return jnp.dot(many, before, preferred_element_type=F32)[0:1]


def each(count, body, start):
    if count > 8:
        return lax.fori_loop(0, count, body, start)
    for at in range(count):
        start = body(at, start)
    return start


def pack_kernel(first, peers, cols, a_slots, row_count, *refs):
    refs = list(refs)
    base = 0 if first else refs.pop(0)[0]
    told = refs[:peers]
    flat = refs[peers]
    outs = refs[peers + 1 : 2 * peers]
    most, picks, packed = refs[2 * peers :]
    grid_row = lax.axis_index("row")
    per_col = peers // cols
    offered = offers(told[0], cols, row_count)
    top = jnp.zeros((1, 1), F32)
    first_slot = grid_row % per_col * a_slots if per_col > 1 else 0
    for d in range(1, peers):
        pairs, _, _ = matches(
            told[d], offered, grid_row // per_col, cols, row_count, first_slot, a_slots
        )
        needed = jnp.max(pairs, axis=0, keepdims=True)
        place = jnp.where(needed > 0.5, places(needed), -1.0).astype(I32)
        pick = (place == iota((CAPACITY, LANES), 0) + base).astype(BF16)
        picks[pl.ds((d - 1) * CAPACITY, CAPACITY), :] = pick
        top = jnp.maximum(top, jnp.sum(needed, axis=1, keepdims=True))
    most[...] = jnp.broadcast_to(top, most.shape)
    pick = picks[...][:, : flat.shape[0]]
    for t in range(0, ROWS, 2):
        both = flat[:, pl.ds(t * LANES, 2 * LANES)]
        both = jnp.dot(pick, both, preferred_element_type=F32)
        packed[:, t, :] = both[:, :LANES]
        packed[:, t + 1, :] = both[:, LANES:]
    for d in range(1, peers):
        out = outs[d - 1]
        for x in range(CAPACITY):
            out[pl.ds(x * ROWS, ROWS), :] = packed[(d - 1) * CAPACITY + x].astype(BF16)
        out[pl.ds(CAPACITY * ROWS, FLAG), :] = jnp.broadcast_to(top, (FLAG, LANES)).astype(BF16)


def pack(base, told, flat, cols, row_count, a_slots):
    first = base is None
    peers = len(told)
    smem_spec = pl.BlockSpec(memory_space=SMEM)
    vmem_spec = pl.BlockSpec(memory_space=VMEM)
    given = [] if first else [base]
    results = pl.pallas_call(
        functools.partial(pack_kernel, first, peers, cols, a_slots, row_count),
        out_shape=[jax.ShapeDtypeStruct((CAPACITY * ROWS + FLAG, LANES), BF16)] * (peers - 1)
        + [jax.ShapeDtypeStruct((8, LANES), F32)],
        in_specs=[smem_spec] * len(given) + [vmem_spec] * (peers + 1),
        out_specs=[vmem_spec] * peers,
        scratch_shapes=[
            VMEM(((peers - 1) * CAPACITY, LANES), BF16),
            VMEM(((peers - 1) * CAPACITY, ROWS, LANES), F32),
        ],
        compiler_params=pltpu.CompilerParams(vmem_limit_bytes=32 << 20),
        cost_estimate=pl.CostEstimate(flops=1 << 20, bytes_accessed=4 << 20, transcendentals=0),
        name="pack",
    )(*given, *told, flat)
    return results[:-1], results[-1]


def list_kernel(cols, a_slots, row_count, peers, *refs):
    told = refs[:peers]
    items, starts, words, words_s, sem = refs[peers:]
    grid_row = lax.axis_index("row")
    per_col = peers // cols
    lane = iota((a_slots, LANES), 1)
    slot = iota((a_slots, LANES), 0)
    words[...] = jnp.full(words.shape, IDLE, I32)
    for d in range(peers):
        group = grid_row ^ d
        holder = group // per_col
        first_slot = group % per_col * a_slots if per_col > 1 else 0
        offered = offers(told[d], cols, row_count)
        pairs, which, a_rows = matches(
            told[0], offered, holder, cols, row_count, first_slot, a_slots
        )
        if d == 0:
            place = iota((1, LANES), 1).astype(F32)
        else:
            place = places(jnp.max(pairs, axis=0, keepdims=True))
        stacked = jnp.concatenate([pairs, pairs * place, pairs * which], axis=0).astype(BF16)
        to_slot = iota((LANES, LANES), 1) == iota((LANES, LANES), 0) // row_count + d * SLOTS
        by_slot = jnp.dot(stacked, to_slot.astype(BF16), preferred_element_type=F32)
        hit = by_slot[:a_slots] > 0.5
        at = by_slot[a_slots : 2 * a_slots].astype(I32)
        out = (a_rows * SLOTS + by_slot[2 * a_slots :]).astype(I32)
        a_slot = holder * per_col * a_slots + first_slot + slot
        word = ((a_slot * 64 + out) * 64 + at) * 64 + d
        words[...] = jnp.where(hit & (lane // SLOTS == d), word, words[...])
    fetch([(words, words_s)], sem)

    def one_peer(d, length):
        starts[d] = length
        for n in range(SLOTS):
            for s in range(a_slots):
                word = words_s[s, d * SLOTS + n]
                items[length] = word
                length = length + (word & IDLE != IDLE).astype(I32)
        return length

    length = lax.fori_loop(0, peers, one_peer, jnp.int32(0))
    starts[peers] = length
    items[length] = IDLE


def work_list(told, cols, row_count, a_slots):
    peers = len(told)
    most_items = peers * a_slots * SLOTS + 1
    return pl.pallas_call(
        functools.partial(list_kernel, cols, a_slots, row_count, peers),
        out_shape=[
            jax.ShapeDtypeStruct((most_items,), I32),
            jax.ShapeDtypeStruct((peers + 1,), I32),
        ],
        in_specs=[pl.BlockSpec(memory_space=VMEM)] * peers,
        out_specs=[pl.BlockSpec(memory_space=SMEM)] * 2,
        scratch_shapes=[
            VMEM((a_slots, LANES), I32),
            SMEM((a_slots, LANES), I32),
            pltpu.SemaphoreType.DMA((1,)),
        ],
        cost_estimate=pl.CostEstimate(flops=1 << 20, bytes_accessed=1 << 16, transcendentals=0),
        name="work_list",
    )(*told)


def fetch(copies, sems):
    started = [
        pltpu.make_async_copy(source, target, sems.at[at])
        for at, (source, target) in enumerate(copies)
    ]
    for copy in started:
        copy.start()
    for copy in started:
        copy.wait()


def add_products(items, starts, a_ref, peer_refs, sums, window=None):
    low = iota((ROWS, LANES), 1) < BS
    nothing = jnp.zeros((ROWS, LANES), BF16)
    idle_row = sums.shape[0] - 1

    def add_one(word, used, b_ref):
        place = (word >> 6) & 63
        target = (word >> 12) & 63
        used = used & ((word & IDLE) != IDLE)
        if window is not None:
            place = place - window
            used = used & (place >= 0) & (place < CAPACITY)
        place = jnp.where(used, place, 0)
        a_at = pl.multiple_of((word >> 18) * ROWS, ROWS)
        b_at = pl.multiple_of(place * ROWS, ROWS)
        block = b_ref[pl.ds(b_at, ROWS), :]
        turned = jnp.concatenate([block[:, BS:], block[:, :BS]], axis=1)
        right = jnp.concatenate(
            [
                jnp.where(low, block, nothing),
                jnp.where(low, turned, nothing),
                jnp.where(low, nothing, turned),
                jnp.where(low, nothing, block),
            ],
            axis=0,
        )
        term = jnp.dot(a_ref[pl.ds(a_at, ROWS), :], right, preferred_element_type=F32)
        i = jnp.where(used, target // SLOTS, idle_row)
        sums[i, pl.ds(target % SLOTS, ROWS, stride=SLOTS), :] += term

    for at in range(0, len(peer_refs), 3):
        chosen = peer_refs[at : at + 3]
        bounds = [(starts[d], starts[d + 1]) for d, _ in chosen]
        longest = functools.reduce(jnp.maximum, [stop - start for start, stop in bounds])
        width = UNROLL if len(chosen) < 3 else UNROLL - 1

        def some_items(step, carry, chosen=chosen, bounds=bounds, width=width):
            for u in range(width):
                for (_, b_ref), (start, stop) in zip(chosen, bounds):
                    y = start + step * width + u
                    used = y < stop
                    add_one(items[jnp.where(used, y, start)], used, b_ref)
            return carry

        lax.fori_loop(0, (longest + width - 1) // width, some_items, 0)


def stage_kernel(cols, *refs):
    a_refs, b_ref, items, starts = refs[:cols], refs[cols], refs[cols + 1], refs[cols + 2]
    a_out, sums, a_wide, b_wide, b_own = refs[cols + 3 :]
    source = iota((LANES, LANES), 0)
    target = iota((LANES, LANES), 1)
    wanted = (target // BS) * BS + 2 * (target % ROWS) + (target // ROWS) % 2
    order = (source == wanted).astype(BF16)
    slots = a_refs[0].shape[1]
    grid_col = lax.axis_index("col")
    for t in range(ROWS):
        pieces = [ref[0, :, pl.ds(t * LANES, LANES)] for ref in a_refs]
        done = jnp.dot(jnp.concatenate(pieces, axis=0), order, preferred_element_type=F32)
        a_wide[:, t, :] = done
    for h in range(cols):
        first = (grid_col ^ h) * slots
        for s in range(slots):
            at = pl.multiple_of((first + s) * ROWS, ROWS)
            a_out[pl.ds(at, ROWS), :] = a_wide[h * slots + s].astype(BF16)
    row_count, slots = b_ref.shape[0], b_ref.shape[1]

    def one_row(k, carry):
        for t in range(ROWS):
            b_wide[pl.ds(t * slots, slots), :] = b_ref[k, :, pl.ds(t * LANES, LANES)].astype(F32)
        for n in range(slots):
            at = pl.multiple_of((n * row_count + k) * ROWS, ROWS)
            b_own[pl.ds(at, ROWS), :] = b_wide[pl.ds(n, ROWS, stride=slots), :].astype(BF16)
        return carry

    lax.fori_loop(0, row_count, one_row, 0)
    sums[...] = jnp.zeros_like(sums)
    add_products(items, starts, a_out, [(0, b_own)], sums)


def stage(a_parts, b_blocks, items, starts):
    cols, slots = len(a_parts), a_parts[0].shape[1]
    row_count, b_slots = b_blocks.shape[0], b_blocks.shape[1]
    vmem_spec = pl.BlockSpec(memory_space=VMEM)
    smem_spec = pl.BlockSpec(memory_space=SMEM)
    return pl.pallas_call(
        functools.partial(stage_kernel, cols),
        out_shape=(
            jax.ShapeDtypeStruct((cols * slots * ROWS, LANES), BF16),
            jax.ShapeDtypeStruct((row_count + 1, ROWS * b_slots, LANES), F32),
        ),
        in_specs=[vmem_spec] * (cols + 1) + [smem_spec] * 2,
        out_specs=(vmem_spec,) * 2,
        scratch_shapes=[
            VMEM((cols * slots, ROWS, LANES), F32),
            VMEM((b_slots * ROWS, LANES), F32),
            VMEM((row_count * b_slots * ROWS, LANES), BF16),
        ],
        compiler_params=pltpu.CompilerParams(vmem_limit_bytes=40 << 20),
        cost_estimate=pl.CostEstimate(flops=1 << 24, bytes_accessed=4 << 20, transcendentals=0),
        name="stage",
    )(*a_parts, b_blocks, items, starts)


def multiply_kernel(first, peers, *refs):
    refs = list(refs)
    base = 0 if first else refs.pop(0)[0]
    items, starts, most, a_ref = refs[:4]
    b_refs = refs[5 : 4 + peers][::-1]
    out, rounds, sums, rows, sems = refs[4 + peers :]
    add_products(items, starts, a_ref, list(enumerate(b_refs, 1)), sums, window=base)
    row_count, kept = out.shape[0], out.shape[1]
    copies = []
    for i in range(row_count):
        for t in range(ROWS):
            rows[i, :, pl.ds(t * LANES, LANES)] = sums[i, pl.ds(t * kept, kept), :]
        copies.append(pltpu.make_async_copy(rows.at[i], out.at[i], sems.at[i]))
        copies[-1].start()
    flags = most[...]
    for ref in b_refs:
        flag = ref[pl.ds(CAPACITY * ROWS, FLAG), :].astype(F32)
        flags = jnp.maximum(flags, jnp.max(flag, axis=0, keepdims=True))
    rounds[0] = (jnp.max(flags).astype(I32) + CAPACITY - 1) // CAPACITY
    for copy in copies:
        copy.wait()


def multiply(base, items, starts, most, a_ready, sums, b_parts, shape):
    first = base is None
    peers = len(b_parts) + 1
    smem_spec = pl.BlockSpec(memory_space=SMEM)
    vmem_spec = pl.BlockSpec(memory_space=VMEM)
    given = [] if first else [base]
    return pl.pallas_call(
        functools.partial(multiply_kernel, first, peers),
        out_shape=[
            jax.ShapeDtypeStruct(shape, F32),
            jax.ShapeDtypeStruct((1,), I32),
            jax.ShapeDtypeStruct(sums.shape, F32),
        ],
        in_specs=[smem_spec] * (len(given) + 2) + [vmem_spec] * (2 + peers),
        out_specs=[pl.BlockSpec(memory_space=pl.ANY), smem_spec, vmem_spec],
        input_output_aliases={len(given) + 4: 2},
        scratch_shapes=[VMEM(shape, F32), pltpu.SemaphoreType.DMA((shape[0],))],
        compiler_params=pltpu.CompilerParams(vmem_limit_bytes=32 << 20),
        cost_estimate=pl.CostEstimate(flops=1 << 26, bytes_accessed=4 << 20, transcendentals=0),
        name="multiply",
    )(*given, items, starts, most, a_ready, sums, *b_parts[::-1])


def shards(a_blocks, a_index, b_blocks, b_cols, c_cols):
    rows = lax.axis_size("row")
    cols = lax.axis_size("col")
    a_slots = a_blocks.shape[1] * cols // rows
    row_count = b_blocks.shape[0]

    def send_rows(parts):
        far_first = range(len(parts), 0, -1)
        return [exchanged(parts[d - 1], "row", d) for d in far_first][::-1]

    def finish(base, most, sums, arrived):
        return multiply(base, items, starts, most, a_ready, sums, arrived, shape)

    shape = (row_count, c_cols.shape[1], BS * BS)
    index_parts = [a_index] + [exchanged(a_index, "col", h) for h in range(1, cols)]
    told = describe(index_parts, b_cols.T, c_cols.T)
    a_soon, _ = lax.optimization_barrier((a_blocks, told))
    told = [told] + send_rows([told] * (rows - 1))
    flat = flatten(b_blocks)
    packed, most = pack(None, told, flat, cols, row_count, a_slots)
    arrived = send_rows(packed)
    items, starts = work_list(told, cols, row_count, a_slots)
    a_late, _ = lax.optimization_barrier((a_blocks, most))
    a_parts = [a_blocks, exchanged(a_soon, "col", 1)]
    a_parts += [exchanged(a_late, "col", h) for h in range(2, cols)]
    a_ready, sums = stage(a_parts, b_blocks, items, starts)
    out, rounds, sums = finish(None, most, sums, arrived)

    def more(state):
        return state[0] < rounds[0]

    def one_round(state):
        at, sums, _ = state
        base = jnp.reshape(at * CAPACITY, (1,))
        packed, most = pack(base, told, flat, cols, row_count, a_slots)
        out, _, sums = finish(base, most, sums, send_rows(packed))
        return at + 1, sums, out

    return lax.while_loop(more, one_round, (jnp.int32(1), sums, out))[2]


def solution(mesh):
    return jax.shard_map(
        shards,
        mesh=mesh,
        in_specs=(
            P(("sys", "row"), "col", None),
            P(None, ("sys", "row"), "col"),
            P(("sys", "row"), "col", None),
            P(("sys", "row"), "col"),
            P(("sys", "row"), "col"),
        ),
        out_specs=P(("sys", "row"), "col", None),
        check_vma=False,
    )
```

```python
import functools

import jax
import jax.numpy as jnp
from jax import lax
from jax.experimental import pallas as pl
from jax.experimental.pallas import tpu as pltpu
from jax.sharding import PartitionSpec as P

BS = 64
LANES = 128
ROWS = BS * BS // LANES
CAPACITY = 16
UNROLL = 4
SLOTS = 4
FLAG = 16
IDLE = 63
VMEM = pltpu.VMEM
SMEM = pltpu.SMEM
BF16 = jnp.bfloat16
F32 = jnp.float32
I32 = jnp.int32


def exchanged(block, axis, distance):
    size = lax.axis_size(axis)
    return lax.ppermute(block, axis, [(i, i ^ distance) for i in range(size)])


def describe(a_index, b_cols, c_cols, cols):
    total = -(-(2 * cols + 2 * SLOTS) // 8) * 8

    def placed(part, at):
        after = (total - at - part.shape[0], LANES - part.shape[1])
        return jnp.pad(part, ((at, after[0]), (0, after[1])), constant_values=-1)

    own = jnp.maximum(placed(c_cols, 2 * cols), placed(b_cols, 2 * cols + SLOTS))
    told = lax.optimization_barrier(jnp.maximum(own, placed(a_index[:, 0, :], 0)))
    h = 1
    while h < cols:
        if h == 1:
            came = exchanged(a_index, "col", 1)[:, 0, :]
        else:
            came = exchanged(told, "col", h)[: 2 * h]
        told = jnp.maximum(told, placed(came, 2 * h))
        h = 2 * h
    return told


def tell_rows(told):
    parts = [told]
    d = 1
    while d < lax.axis_size("row"):
        known = parts[0] if d == 1 else jnp.concatenate(parts, axis=0)
        parts.append(exchanged(known, "row", d))
        d = 2 * d
    return parts


def told_views(refs):
    height = refs[0].shape[0]
    return [
        ref.at[pl.ds(at, height), :] for ref in refs for at in range(0, ref.shape[0], height)
    ]


def offers(told, cols, row_count):
    start = 2 * cols + SLOTS
    rows = told[pl.ds(start, SLOTS), :]
    lane = iota((1, LANES), 1)
    result = rows[0:1]
    for n in range(1, SLOTS):
        moved = pltpu.roll(rows, n * row_count, 1)[n : n + 1]
        result = jnp.where(lane // row_count == n, moved, result)
    return result


def iota(shape, axis):
    return lax.broadcasted_iota(I32, shape, axis)


def turn_to_columns(rows, first, count):
    pick = (iota((count, LANES), 0) + first == iota((count, LANES), 1)).astype(BF16)
    return lax.dot_general(
        pick,
        rows.astype(F32).astype(BF16),
        (((1,), (1,)), ((), ())),
        preferred_element_type=F32,
    )


def matches(receiver, offered, holder, cols, row_count, first_slot, a_slots):
    turned = 2 * (holder ^ lax.axis_index("col"))
    rows = [receiver[pl.ds(turned, 1), :], receiver[pl.ds(turned + 1, 1), :]]
    rows += [receiver[pl.ds(2 * cols, SLOTS), :]]
    rows = jnp.concatenate(rows + [jnp.zeros((8 - 2 - SLOTS, LANES), I32)], axis=0)
    kept_columns = turn_to_columns(rows, 0, row_count)
    if isinstance(first_slot, int) and first_slot == 0 and a_slots == row_count:
        slot_columns = kept_columns
    else:
        slot_columns = turn_to_columns(rows, first_slot, a_slots)
    wanted = offered.astype(F32)
    kept = jnp.zeros((row_count, LANES), F32)
    which = jnp.zeros((row_count, LANES), F32)
    for m in range(SLOTS):
        column = kept_columns[:, 2 + m : 3 + m]
        equal = (column == wanted) & (wanted >= 0)
        kept = jnp.where(equal, 1.0, kept)
        which = jnp.where(equal, float(m), which)
    a_rows = slot_columns[:, 0:1]
    a_columns = slot_columns[:, 1:2]
    shape = (a_slots, row_count)
    by_row = (a_rows == iota(shape, 1).astype(F32)).astype(BF16)
    by_column = a_columns == (iota((a_slots, LANES), 1) % row_count).astype(F32)
    both = jnp.concatenate([kept, which], axis=1).astype(BF16)
    both = jnp.dot(by_row, both, preferred_element_type=F32)
    pairs = jnp.where(by_column & (both[:, :LANES] > 0.5), 1.0, 0.0)
    return pairs, both[:, LANES:], a_rows


def places(needed):
    before = (iota((LANES, LANES), 0) < iota((LANES, LANES), 1)).astype(BF16)
    many = jnp.broadcast_to(needed, (8, LANES)).astype(BF16)
    return jnp.dot(many, before, preferred_element_type=F32)[0:1]


def each(count, body, start):
    if count > 8:
        return lax.fori_loop(0, count, body, start)
    for at in range(count):
        start = body(at, start)
    return start


def pack_kernel(first, peers, cols, a_slots, tellers, *refs):
    refs = list(refs)
    base = 0 if first else refs.pop(0)[0]
    told = told_views(refs[:tellers])
    b_any = refs[tellers]
    outs = refs[tellers + 1 : tellers + peers]
    most, b_ref, picks, wide, packed, sem = refs[tellers + peers :]
    loading = pltpu.make_async_copy(b_any, b_ref, sem.at[0])
    loading.start()
    row_count = b_ref.shape[0]
    grid_row = lax.axis_index("row")
    per_col = peers // cols
    offered = offers(told[0], cols, row_count)
    top = jnp.zeros((1, 1), F32)
    first_slot = grid_row % per_col * a_slots if per_col > 1 else 0
    for d in range(1, peers):
        pairs, _, _ = matches(
            told[d], offered, grid_row // per_col, cols, row_count, first_slot, a_slots
        )
        needed = jnp.max(pairs, axis=0, keepdims=True)
        place = jnp.where(needed > 0.5, places(needed), -1.0).astype(I32)
        pick = (place == iota((CAPACITY, LANES), 0) + base).astype(BF16)
        picks[pl.ds((d - 1) * CAPACITY, CAPACITY), :] = pick
        top = jnp.maximum(top, jnp.sum(needed, axis=1, keepdims=True))
    most[...] = jnp.broadcast_to(top, most.shape)
    loading.wait()
    for k in range(row_count):
        for t in range(ROWS):
            wide[k, pl.ds(t * SLOTS, SLOTS), :] = b_ref[k, :, pl.ds(t * LANES, LANES)].astype(F32)
    pick = picks[...][:, : row_count * SLOTS]
    for t in range(0, ROWS, 2):
        pair = [
            jnp.concatenate([wide[:, at * SLOTS + n, :] for n in range(SLOTS)], axis=0)
            for at in (t, t + 1)
        ]
        both = jnp.concatenate(pair, axis=1).astype(BF16)
        both = jnp.dot(pick, both, preferred_element_type=F32)
        packed[:, t, :] = both[:, :LANES]
        packed[:, t + 1, :] = both[:, LANES:]
    for d in range(1, peers):
        out = outs[d - 1]
        for x in range(CAPACITY):
            out[pl.ds(x * ROWS, ROWS), :] = packed[(d - 1) * CAPACITY + x].astype(BF16)
        out[pl.ds(CAPACITY * ROWS, FLAG), :] = jnp.broadcast_to(top, (FLAG, LANES)).astype(BF16)


def pack(base, told, b_blocks, peers, cols, a_slots):
    first = base is None
    smem_spec = pl.BlockSpec(memory_space=SMEM)
    vmem_spec = pl.BlockSpec(memory_space=VMEM)
    given = [] if first else [base]
    results = pl.pallas_call(
        functools.partial(pack_kernel, first, peers, cols, a_slots, len(told)),
        out_shape=[jax.ShapeDtypeStruct((CAPACITY * ROWS + FLAG, LANES), BF16)] * (peers - 1)
        + [jax.ShapeDtypeStruct((8, LANES), F32)],
        in_specs=[smem_spec] * len(given)
        + [vmem_spec] * len(told)
        + [pl.BlockSpec(memory_space=pl.ANY)],
        out_specs=[vmem_spec] * peers,
        scratch_shapes=[
            VMEM(b_blocks.shape, BF16),
            VMEM(((peers - 1) * CAPACITY, LANES), BF16),
            VMEM((b_blocks.shape[0], SLOTS * ROWS, LANES), F32),
            VMEM(((peers - 1) * CAPACITY, ROWS, LANES), F32),
            pltpu.SemaphoreType.DMA((1,)),
        ],
        compiler_params=pltpu.CompilerParams(vmem_limit_bytes=32 << 20),
        cost_estimate=pl.CostEstimate(flops=1 << 20, bytes_accessed=4 << 20, transcendentals=0),
        name="pack",
    )(*given, *told, b_blocks)
    return results[:-1], results[-1]


def list_kernel(cols, a_slots, row_count, peers, tellers, *refs):
    told = told_views(refs[:tellers])
    items, starts, words, words_s, sem = refs[tellers:]
    grid_row = lax.axis_index("row")
    per_col = peers // cols
    lane = iota((a_slots, LANES), 1)
    slot = iota((a_slots, LANES), 0)
    words[...] = jnp.full(words.shape, IDLE, I32)
    for d in range(peers):
        group = grid_row ^ d
        holder = group // per_col
        first_slot = group % per_col * a_slots if per_col > 1 else 0
        offered = offers(told[d], cols, row_count)
        pairs, which, a_rows = matches(
            told[0], offered, holder, cols, row_count, first_slot, a_slots
        )
        if d == 0:
            place = iota((1, LANES), 1).astype(F32)
        else:
            place = places(jnp.max(pairs, axis=0, keepdims=True))
        stacked = jnp.concatenate([pairs, pairs * place, pairs * which], axis=0).astype(BF16)
        to_slot = iota((LANES, LANES), 1) == iota((LANES, LANES), 0) // row_count + d * SLOTS
        by_slot = jnp.dot(stacked, to_slot.astype(BF16), preferred_element_type=F32)
        hit = by_slot[:a_slots] > 0.5
        at = by_slot[a_slots : 2 * a_slots].astype(I32)
        out = (a_rows * SLOTS + by_slot[2 * a_slots :]).astype(I32)
        a_slot = holder * per_col * a_slots + first_slot + slot
        word = ((a_slot * 64 + out) * 64 + at) * 64 + d
        words[...] = jnp.where(hit & (lane // SLOTS == d), word, words[...])
    fetch([(words, words_s)], sem)

    def one_peer(d, length):
        starts[d] = length
        for n in range(SLOTS):
            for s in range(a_slots):
                word = words_s[s, d * SLOTS + n]
                items[length] = word
                length = length + (word & IDLE != IDLE).astype(I32)
        return length

    length = lax.fori_loop(0, peers, one_peer, jnp.int32(0))
    starts[peers] = length
    items[length] = IDLE


def work_list(told, peers, cols, row_count, a_slots):
    most_items = peers * a_slots * SLOTS + 1
    return pl.pallas_call(
        functools.partial(list_kernel, cols, a_slots, row_count, peers, len(told)),
        out_shape=[
            jax.ShapeDtypeStruct((most_items,), I32),
            jax.ShapeDtypeStruct((peers + 1,), I32),
        ],
        in_specs=[pl.BlockSpec(memory_space=VMEM)] * len(told),
        out_specs=[pl.BlockSpec(memory_space=SMEM)] * 2,
        scratch_shapes=[
            VMEM((a_slots, LANES), I32),
            SMEM((a_slots, LANES), I32),
            pltpu.SemaphoreType.DMA((1,)),
        ],
        cost_estimate=pl.CostEstimate(flops=1 << 20, bytes_accessed=1 << 16, transcendentals=0),
        name="work_list",
    )(*told)


def fetch(copies, sems):
    started = [
        pltpu.make_async_copy(source, target, sems.at[at])
        for at, (source, target) in enumerate(copies)
    ]
    for copy in started:
        copy.start()
    for copy in started:
        copy.wait()


def add_products(items, starts, a_ref, peer_refs, sums, window=None):
    low = iota((ROWS, LANES), 1) < BS
    nothing = jnp.zeros((ROWS, LANES), BF16)
    idle_row = sums.shape[0] - 1

    def add_one(word, used, b_ref):
        place = (word >> 6) & 63
        target = (word >> 12) & 63
        used = used & ((word & IDLE) != IDLE)
        if window is not None:
            place = place - window
            used = used & (place >= 0) & (place < CAPACITY)
        place = jnp.where(used, place, 0)
        a_at = pl.multiple_of((word >> 18) * ROWS, ROWS)
        b_at = pl.multiple_of(place * ROWS, ROWS)
        block = b_ref[pl.ds(b_at, ROWS), :]
        turned = jnp.concatenate([block[:, BS:], block[:, :BS]], axis=1)
        right = jnp.concatenate(
            [
                jnp.where(low, block, nothing),
                jnp.where(low, turned, nothing),
                jnp.where(low, nothing, turned),
                jnp.where(low, nothing, block),
            ],
            axis=0,
        )
        term = jnp.dot(a_ref[pl.ds(a_at, ROWS), :], right, preferred_element_type=F32)
        i = jnp.where(used, target // SLOTS, idle_row)
        sums[i, pl.ds(target % SLOTS, ROWS, stride=SLOTS), :] += term

    for at in range(0, len(peer_refs), 3):
        chosen = peer_refs[at : at + 3]
        bounds = [(starts[d], starts[d + 1]) for d, _ in chosen]
        longest = functools.reduce(jnp.maximum, [stop - start for start, stop in bounds])
        width = UNROLL if len(chosen) < 3 else UNROLL - 1

        def some_items(step, carry, chosen=chosen, bounds=bounds, width=width):
            for u in range(width):
                for (_, b_ref), (start, stop) in zip(chosen, bounds):
                    y = start + step * width + u
                    used = y < stop
                    add_one(items[jnp.where(used, y, start)], used, b_ref)
            return carry

        lax.fori_loop(0, (longest + width - 1) // width, some_items, 0)


def stage_kernel(cols, *refs):
    a_refs, b_any, items, starts = list(refs[:cols]), refs[cols], refs[cols + 1], refs[cols + 2]
    a_out, sums, a_ref, b_ref, a_wide, b_wide, b_own, sems = refs[cols + 3 :]
    loading = [
        pltpu.make_async_copy(a_refs[0], a_ref, sems.at[0]),
        pltpu.make_async_copy(b_any, b_ref, sems.at[1]),
    ]
    for copy in loading:
        copy.start()
    a_refs[0] = a_ref
    sums[...] = jnp.zeros_like(sums)
    source = iota((LANES, LANES), 0)
    target = iota((LANES, LANES), 1)
    wanted = (target // BS) * BS + 2 * (target % ROWS) + (target // ROWS) % 2
    order = (source == wanted).astype(BF16)
    slots = a_refs[0].shape[1]
    grid_col = lax.axis_index("col")
    loading[0].wait()
    for t in range(ROWS):
        pieces = [ref[0, :, pl.ds(t * LANES, LANES)] for ref in a_refs]
        done = jnp.dot(jnp.concatenate(pieces, axis=0), order, preferred_element_type=F32)
        a_wide[:, t, :] = done
    for h in range(cols):
        first = (grid_col ^ h) * slots
        for s in range(slots):
            at = pl.multiple_of((first + s) * ROWS, ROWS)
            a_out[pl.ds(at, ROWS), :] = a_wide[h * slots + s].astype(BF16)
    row_count, slots = b_ref.shape[0], b_ref.shape[1]

    def one_row(k, carry):
        for t in range(ROWS):
            b_wide[pl.ds(t * slots, slots), :] = b_ref[k, :, pl.ds(t * LANES, LANES)].astype(F32)
        for n in range(slots):
            at = pl.multiple_of((n * row_count + k) * ROWS, ROWS)
            b_own[pl.ds(at, ROWS), :] = b_wide[pl.ds(n, ROWS, stride=slots), :].astype(BF16)
        return carry

    loading[1].wait()
    lax.fori_loop(0, row_count, one_row, 0)
    add_products(items, starts, a_out, [(0, b_own)], sums)


def stage(a_parts, b_blocks, items, starts):
    cols, slots = len(a_parts), a_parts[0].shape[1]
    row_count, b_slots = b_blocks.shape[0], b_blocks.shape[1]
    any_spec = pl.BlockSpec(memory_space=pl.ANY)
    vmem_spec = pl.BlockSpec(memory_space=VMEM)
    smem_spec = pl.BlockSpec(memory_space=SMEM)
    return pl.pallas_call(
        functools.partial(stage_kernel, cols),
        out_shape=(
            jax.ShapeDtypeStruct((cols * slots * ROWS, LANES), BF16),
            jax.ShapeDtypeStruct((row_count + 1, ROWS * b_slots, LANES), F32),
        ),
        in_specs=[any_spec] + [vmem_spec] * (cols - 1) + [any_spec] + [smem_spec] * 2,
        out_specs=(vmem_spec,) * 2,
        scratch_shapes=[
            VMEM(a_parts[0].shape, BF16),
            VMEM(b_blocks.shape, BF16),
            VMEM((cols * slots, ROWS, LANES), F32),
            VMEM((b_slots * ROWS, LANES), F32),
            VMEM((row_count * b_slots * ROWS, LANES), BF16),
            pltpu.SemaphoreType.DMA((2,)),
        ],
        compiler_params=pltpu.CompilerParams(vmem_limit_bytes=40 << 20),
        cost_estimate=pl.CostEstimate(flops=1 << 24, bytes_accessed=4 << 20, transcendentals=0),
        name="stage",
    )(*a_parts, b_blocks, items, starts)


def multiply_kernel(first, peers, *refs):
    refs = list(refs)
    base = 0 if first else refs.pop(0)[0]
    items, starts, most, a_ref = refs[:4]
    b_refs = refs[5 : 4 + peers][::-1]
    out, rounds, sums, rows, sems = refs[4 + peers :]
    add_products(items, starts, a_ref, list(enumerate(b_refs, 1)), sums, window=base)
    row_count, kept = out.shape[0], out.shape[1]
    copies = []
    for i in range(row_count):
        for t in range(ROWS):
            rows[i, :, pl.ds(t * LANES, LANES)] = sums[i, pl.ds(t * kept, kept), :]
        copies.append(pltpu.make_async_copy(rows.at[i], out.at[i], sems.at[i]))
        copies[-1].start()
    flags = most[...]
    for ref in b_refs:
        flag = ref[pl.ds(CAPACITY * ROWS, FLAG), :].astype(F32)
        flags = jnp.maximum(flags, jnp.max(flag, axis=0, keepdims=True))
    rounds[0] = (jnp.max(flags).astype(I32) + CAPACITY - 1) // CAPACITY
    for copy in copies:
        copy.wait()


def multiply(base, items, starts, most, a_ready, sums, b_parts, shape):
    first = base is None
    peers = len(b_parts) + 1
    smem_spec = pl.BlockSpec(memory_space=SMEM)
    vmem_spec = pl.BlockSpec(memory_space=VMEM)
    given = [] if first else [base]
    return pl.pallas_call(
        functools.partial(multiply_kernel, first, peers),
        out_shape=[
            jax.ShapeDtypeStruct(shape, F32),
            jax.ShapeDtypeStruct((1,), I32),
            jax.ShapeDtypeStruct(sums.shape, F32),
        ],
        in_specs=[smem_spec] * (len(given) + 2) + [vmem_spec] * (2 + peers),
        out_specs=[pl.BlockSpec(memory_space=pl.ANY), smem_spec, vmem_spec],
        input_output_aliases={len(given) + 4: 2},
        scratch_shapes=[VMEM(shape, F32), pltpu.SemaphoreType.DMA((shape[0],))],
        compiler_params=pltpu.CompilerParams(vmem_limit_bytes=32 << 20),
        cost_estimate=pl.CostEstimate(flops=1 << 26, bytes_accessed=4 << 20, transcendentals=0),
        name="multiply",
    )(*given, items, starts, most, a_ready, sums, *b_parts[::-1])


def shards(a_blocks, a_index, b_blocks, b_cols, c_cols):
    rows = lax.axis_size("row")
    cols = lax.axis_size("col")
    a_slots = a_blocks.shape[1] * cols // rows
    row_count = b_blocks.shape[0]

    def send_rows(parts):
        far_first = range(len(parts), 0, -1)
        return [exchanged(parts[d - 1], "row", d) for d in far_first][::-1]

    def finish(base, most, sums, arrived):
        return multiply(base, items, starts, most, a_ready, sums, arrived, shape)

    shape = (row_count, c_cols.shape[1], BS * BS)
    told = tell_rows(describe(a_index, b_cols.T, c_cols.T, cols))
    packed, most = pack(None, told, b_blocks, rows, cols, a_slots)
    arrived = send_rows(packed)
    items, starts = work_list(told, rows, cols, row_count, a_slots)
    a_late, _ = lax.optimization_barrier((a_blocks, most))
    a_parts = [a_blocks, exchanged(a_late, "col", 1)]
    a_soon, _ = lax.optimization_barrier((a_blocks, told[1]))
    for h in range(2, cols, 2):
        far = exchanged(a_soon, "col", h)
        a_parts += [far, exchanged(far, "col", 1)]
    a_ready, sums = stage(a_parts, b_blocks, items, starts)
    out, rounds, sums = finish(None, most, sums, arrived)

    def more(state):
        return state[0] < rounds[0]

    def one_round(state):
        at, sums, _ = state
        base = jnp.reshape(at * CAPACITY, (1,))
        packed, most = pack(base, told, b_blocks, rows, cols, a_slots)
        out, _, sums = finish(base, most, sums, send_rows(packed))
        return at + 1, sums, out

    return lax.while_loop(more, one_round, (jnp.int32(1), sums, out))[2]


def solution(mesh):
    return jax.shard_map(
        shards,
        mesh=mesh,
        in_specs=(
            P(("sys", "row"), "col", None),
            P(None, ("sys", "row"), "col"),
            P(("sys", "row"), "col", None),
            P(("sys", "row"), "col"),
            P(("sys", "row"), "col"),
        ),
        out_specs=P(("sys", "row"), "col", None),
        check_vma=False,
    )
```

```python
import functools

import jax
import jax.numpy as jnp
from jax import lax
from jax.experimental import pallas as pl
from jax.experimental.pallas import tpu as pltpu
from jax.sharding import PartitionSpec as P

BS = 64
LANES = 128
ROWS = BS * BS // LANES
CAPACITY = 16
UNROLL = 4
SLOTS = 4
FLAG = 16
IDLE = 63
VMEM = pltpu.VMEM
SMEM = pltpu.SMEM
BF16 = jnp.bfloat16
F32 = jnp.float32
I32 = jnp.int32


def exchanged(block, axis, distance):
    size = lax.axis_size(axis)
    return lax.ppermute(block, axis, [(i, i ^ distance) for i in range(size)])


def describe(a_parts, b_cols, c_cols):
    cols = len(a_parts)
    total = -(-(2 * cols + 2 * SLOTS) // 8) * 8

    def placed(part, at):
        after = (total - at - part.shape[0], LANES - part.shape[1])
        return jnp.pad(part, ((at, after[0]), (0, after[1])), constant_values=-1)

    own = jnp.maximum(placed(c_cols, 2 * cols), placed(b_cols, 2 * cols + SLOTS))
    told = lax.optimization_barrier(jnp.maximum(own, placed(a_parts[0][:, 0, :], 0)))
    for h in range(1, cols):
        told = jnp.maximum(told, placed(a_parts[h][:, 0, :], 2 * h))
    return told


def offers(told, cols, row_count):
    start = 2 * cols + SLOTS
    rows = told[pl.ds(start, SLOTS), :]
    lane = iota((1, LANES), 1)
    result = rows[0:1]
    for n in range(1, SLOTS):
        moved = pltpu.roll(rows, n * row_count, 1)[n : n + 1]
        result = jnp.where(lane // row_count == n, moved, result)
    return result


def flatten_kernel(b_ref, flat, wide):
    row_count = b_ref.shape[0]
    for k in range(row_count):
        for t in range(ROWS):
            wide[k, pl.ds(t * SLOTS, SLOTS), :] = b_ref[k, :, pl.ds(t * LANES, LANES)].astype(F32)
    for t in range(ROWS):
        for n in range(SLOTS):
            piece = wide[:, t * SLOTS + n, :].astype(BF16)
            flat[pl.ds(n * row_count, row_count), pl.ds(t * LANES, LANES)] = piece


def flatten(b_blocks):
    vmem_spec = pl.BlockSpec(memory_space=VMEM)
    count = b_blocks.shape[0] * b_blocks.shape[1]
    return pl.pallas_call(
        flatten_kernel,
        out_shape=jax.ShapeDtypeStruct((count, BS * BS), BF16),
        in_specs=[vmem_spec],
        out_specs=vmem_spec,
        scratch_shapes=[VMEM((b_blocks.shape[0], b_blocks.shape[1] * ROWS, LANES), F32)],
        compiler_params=pltpu.CompilerParams(vmem_limit_bytes=24 << 20),
        cost_estimate=pl.CostEstimate(flops=1 << 20, bytes_accessed=8 << 20, transcendentals=0),
        name="flatten",
    )(b_blocks)


def iota(shape, axis):
    return lax.broadcasted_iota(I32, shape, axis)


def turn_to_columns(rows, first, count):
    pick = (iota((count, LANES), 0) + first == iota((count, LANES), 1)).astype(BF16)
    return lax.dot_general(
        pick,
        rows.astype(F32).astype(BF16),
        (((1,), (1,)), ((), ())),
        preferred_element_type=F32,
    )


def matches(receiver, offered, holder, cols, row_count, first_slot, a_slots):
    turned = 2 * (holder ^ lax.axis_index("col"))
    rows = [receiver[pl.ds(turned, 1), :], receiver[pl.ds(turned + 1, 1), :]]
    rows += [receiver[pl.ds(2 * cols, SLOTS), :]]
    rows = jnp.concatenate(rows + [jnp.zeros((8 - 2 - SLOTS, LANES), I32)], axis=0)
    kept_columns = turn_to_columns(rows, 0, row_count)
    if isinstance(first_slot, int) and first_slot == 0 and a_slots == row_count:
        slot_columns = kept_columns
    else:
        slot_columns = turn_to_columns(rows, first_slot, a_slots)
    wanted = offered.astype(F32)
    kept = jnp.zeros((row_count, LANES), F32)
    which = jnp.zeros((row_count, LANES), F32)
    for m in range(SLOTS):
        column = kept_columns[:, 2 + m : 3 + m]
        equal = (column == wanted) & (wanted >= 0)
        kept = jnp.where(equal, 1.0, kept)
        which = jnp.where(equal, float(m), which)
    a_rows = slot_columns[:, 0:1]
    a_columns = slot_columns[:, 1:2]
    shape = (a_slots, row_count)
    by_row = (a_rows == iota(shape, 1).astype(F32)).astype(BF16)
    by_column = a_columns == (iota((a_slots, LANES), 1) % row_count).astype(F32)
    both = jnp.concatenate([kept, which], axis=1).astype(BF16)
    both = jnp.dot(by_row, both, preferred_element_type=F32)
    pairs = jnp.where(by_column & (both[:, :LANES] > 0.5), 1.0, 0.0)
    return pairs, both[:, LANES:], a_rows


def places(needed):
    before = (iota((LANES, LANES), 0) < iota((LANES, LANES), 1)).astype(BF16)
    many = jnp.broadcast_to(needed, (8, LANES)).astype(BF16)
    return jnp.dot(many, before, preferred_element_type=F32)[0:1]


def each(count, body, start):
    if count > 8:
        return lax.fori_loop(0, count, body, start)
    for at in range(count):
        start = body(at, start)
    return start


def pack_kernel(first, peers, cols, a_slots, row_count, *refs):
    refs = list(refs)
    base = 0 if first else refs.pop(0)[0]
    told = refs[:peers]
    flat = refs[peers]
    outs = refs[peers + 1 : 2 * peers]
    most, picks, packed = refs[2 * peers :]
    grid_row = lax.axis_index("row")
    per_col = peers // cols
    offered = offers(told[0], cols, row_count)
    top = jnp.zeros((1, 1), F32)
    first_slot = grid_row % per_col * a_slots if per_col > 1 else 0
    for d in range(1, peers):
        pairs, _, _ = matches(
            told[d], offered, grid_row // per_col, cols, row_count, first_slot, a_slots
        )
        needed = jnp.max(pairs, axis=0, keepdims=True)
        place = jnp.where(needed > 0.5, places(needed), -1.0).astype(I32)
        pick = (place == iota((CAPACITY, LANES), 0) + base).astype(BF16)
        picks[pl.ds((d - 1) * CAPACITY, CAPACITY), :] = pick
        top = jnp.maximum(top, jnp.sum(needed, axis=1, keepdims=True))
    most[...] = jnp.broadcast_to(top, most.shape)
    pick = picks[...][:, : flat.shape[0]]
    for t in range(0, ROWS, 2):
        both = flat[:, pl.ds(t * LANES, 2 * LANES)]
        both = jnp.dot(pick, both, preferred_element_type=F32)
        packed[:, t, :] = both[:, :LANES]
        packed[:, t + 1, :] = both[:, LANES:]
    for d in range(1, peers):
        out = outs[d - 1]
        for x in range(CAPACITY):
            out[pl.ds(x * ROWS, ROWS), :] = packed[(d - 1) * CAPACITY + x].astype(BF16)
        out[pl.ds(CAPACITY * ROWS, FLAG), :] = jnp.broadcast_to(top, (FLAG, LANES)).astype(BF16)


def pack(base, told, flat, cols, row_count, a_slots):
    first = base is None
    peers = len(told)
    smem_spec = pl.BlockSpec(memory_space=SMEM)
    vmem_spec = pl.BlockSpec(memory_space=VMEM)
    given = [] if first else [base]
    results = pl.pallas_call(
        functools.partial(pack_kernel, first, peers, cols, a_slots, row_count),
        out_shape=[jax.ShapeDtypeStruct((CAPACITY * ROWS + FLAG, LANES), BF16)] * (peers - 1)
        + [jax.ShapeDtypeStruct((8, LANES), F32)],
        in_specs=[smem_spec] * len(given) + [vmem_spec] * (peers + 1),
        out_specs=[vmem_spec] * peers,
        scratch_shapes=[
            VMEM(((peers - 1) * CAPACITY, LANES), BF16),
            VMEM(((peers - 1) * CAPACITY, ROWS, LANES), F32),
        ],
        compiler_params=pltpu.CompilerParams(vmem_limit_bytes=32 << 20),
        cost_estimate=pl.CostEstimate(flops=1 << 20, bytes_accessed=4 << 20, transcendentals=0),
        name="pack",
    )(*given, *told, flat)
    return results[:-1], results[-1]


def list_kernel(cols, a_slots, row_count, peers, *refs):
    told = refs[:peers]
    items, starts, words, words_s, sem = refs[peers:]
    grid_row = lax.axis_index("row")
    per_col = peers // cols
    lane = iota((a_slots, LANES), 1)
    slot = iota((a_slots, LANES), 0)
    words[...] = jnp.full(words.shape, IDLE, I32)
    for d in range(peers):
        group = grid_row ^ d
        holder = group // per_col
        first_slot = group % per_col * a_slots if per_col > 1 else 0
        offered = offers(told[d], cols, row_count)
        pairs, which, a_rows = matches(
            told[0], offered, holder, cols, row_count, first_slot, a_slots
        )
        if d == 0:
            place = iota((1, LANES), 1).astype(F32)
        else:
            place = places(jnp.max(pairs, axis=0, keepdims=True))
        stacked = jnp.concatenate([pairs, pairs * place, pairs * which], axis=0).astype(BF16)
        to_slot = iota((LANES, LANES), 1) == iota((LANES, LANES), 0) // row_count + d * SLOTS
        by_slot = jnp.dot(stacked, to_slot.astype(BF16), preferred_element_type=F32)
        hit = by_slot[:a_slots] > 0.5
        at = by_slot[a_slots : 2 * a_slots].astype(I32)
        out = (a_rows * SLOTS + by_slot[2 * a_slots :]).astype(I32)
        a_slot = holder * per_col * a_slots + first_slot + slot
        word = ((a_slot * 64 + out) * 64 + at) * 64 + d
        words[...] = jnp.where(hit & (lane // SLOTS == d), word, words[...])
    fetch([(words, words_s)], sem)

    def one_peer(d, length):
        starts[d] = length
        for n in range(SLOTS):
            for s in range(a_slots):
                word = words_s[s, d * SLOTS + n]
                items[length] = word
                length = length + (word & IDLE != IDLE).astype(I32)
        return length

    length = lax.fori_loop(0, peers, one_peer, jnp.int32(0))
    starts[peers] = length
    items[length] = IDLE


def work_list(told, cols, row_count, a_slots):
    peers = len(told)
    most_items = peers * a_slots * SLOTS + 1
    return pl.pallas_call(
        functools.partial(list_kernel, cols, a_slots, row_count, peers),
        out_shape=[
            jax.ShapeDtypeStruct((most_items,), I32),
            jax.ShapeDtypeStruct((peers + 1,), I32),
        ],
        in_specs=[pl.BlockSpec(memory_space=VMEM)] * peers,
        out_specs=[pl.BlockSpec(memory_space=SMEM)] * 2,
        scratch_shapes=[
            VMEM((a_slots, LANES), I32),
            SMEM((a_slots, LANES), I32),
            pltpu.SemaphoreType.DMA((1,)),
        ],
        cost_estimate=pl.CostEstimate(flops=1 << 33, bytes_accessed=1 << 16, transcendentals=0),
        name="work_list",
    )(*told)


def fetch(copies, sems):
    started = [
        pltpu.make_async_copy(source, target, sems.at[at])
        for at, (source, target) in enumerate(copies)
    ]
    for copy in started:
        copy.start()
    for copy in started:
        copy.wait()


def add_products(items, starts, a_ref, peer_refs, sums, window=None):
    low = iota((ROWS, LANES), 1) < BS
    nothing = jnp.zeros((ROWS, LANES), BF16)
    idle_row = sums.shape[0] - 1

    def add_one(word, used, b_ref):
        place = (word >> 6) & 63
        target = (word >> 12) & 63
        used = used & ((word & IDLE) != IDLE)
        if window is not None:
            place = place - window
            used = used & (place >= 0) & (place < CAPACITY)
        place = jnp.where(used, place, 0)
        a_at = pl.multiple_of((word >> 18) * ROWS, ROWS)
        b_at = pl.multiple_of(place * ROWS, ROWS)
        block = b_ref[pl.ds(b_at, ROWS), :]
        turned = jnp.concatenate([block[:, BS:], block[:, :BS]], axis=1)
        right = jnp.concatenate(
            [
                jnp.where(low, block, nothing),
                jnp.where(low, turned, nothing),
                jnp.where(low, nothing, turned),
                jnp.where(low, nothing, block),
            ],
            axis=0,
        )
        term = jnp.dot(a_ref[pl.ds(a_at, ROWS), :], right, preferred_element_type=F32)
        i = jnp.where(used, target // SLOTS, idle_row)
        sums[i, pl.ds(target % SLOTS, ROWS, stride=SLOTS), :] += term

    for at in range(0, len(peer_refs), 3):
        chosen = peer_refs[at : at + 3]
        bounds = [(starts[d], starts[d + 1]) for d, _ in chosen]
        longest = functools.reduce(jnp.maximum, [stop - start for start, stop in bounds])
        width = UNROLL if len(chosen) < 3 else UNROLL - 1

        def some_items(step, carry, chosen=chosen, bounds=bounds, width=width):
            for u in range(width):
                for (_, b_ref), (start, stop) in zip(chosen, bounds):
                    y = start + step * width + u
                    used = y < stop
                    add_one(items[jnp.where(used, y, start)], used, b_ref)
            return carry

        lax.fori_loop(0, (longest + width - 1) // width, some_items, 0)


def stage_kernel(cols, *refs):
    a_refs, b_ref, items, starts = refs[:cols], refs[cols], refs[cols + 1], refs[cols + 2]
    a_out, sums, a_wide, b_wide, b_own = refs[cols + 3 :]
    source = iota((LANES, LANES), 0)
    target = iota((LANES, LANES), 1)
    wanted = (target // BS) * BS + 2 * (target % ROWS) + (target // ROWS) % 2
    order = (source == wanted).astype(BF16)
    slots = a_refs[0].shape[1]
    grid_col = lax.axis_index("col")
    for t in range(ROWS):
        pieces = [ref[0, :, pl.ds(t * LANES, LANES)] for ref in a_refs]
        done = jnp.dot(jnp.concatenate(pieces, axis=0), order, preferred_element_type=F32)
        a_wide[:, t, :] = done
    for h in range(cols):
        first = (grid_col ^ h) * slots
        for s in range(slots):
            at = pl.multiple_of((first + s) * ROWS, ROWS)
            a_out[pl.ds(at, ROWS), :] = a_wide[h * slots + s].astype(BF16)
    row_count, slots = b_ref.shape[0], b_ref.shape[1]

    def one_row(k, carry):
        for t in range(ROWS):
            b_wide[pl.ds(t * slots, slots), :] = b_ref[k, :, pl.ds(t * LANES, LANES)].astype(F32)
        for n in range(slots):
            at = pl.multiple_of((n * row_count + k) * ROWS, ROWS)
            b_own[pl.ds(at, ROWS), :] = b_wide[pl.ds(n, ROWS, stride=slots), :].astype(BF16)
        return carry

    lax.fori_loop(0, row_count, one_row, 0)
    sums[...] = jnp.zeros_like(sums)
    add_products(items, starts, a_out, [(0, b_own)], sums)


def stage(a_parts, b_blocks, items, starts):
    cols, slots = len(a_parts), a_parts[0].shape[1]
    row_count, b_slots = b_blocks.shape[0], b_blocks.shape[1]
    vmem_spec = pl.BlockSpec(memory_space=VMEM)
    smem_spec = pl.BlockSpec(memory_space=SMEM)
    return pl.pallas_call(
        functools.partial(stage_kernel, cols),
        out_shape=(
            jax.ShapeDtypeStruct((cols * slots * ROWS, LANES), BF16),
            jax.ShapeDtypeStruct((row_count + 1, ROWS * b_slots, LANES), F32),
        ),
        in_specs=[vmem_spec] * (cols + 1) + [smem_spec] * 2,
        out_specs=(vmem_spec,) * 2,
        scratch_shapes=[
            VMEM((cols * slots, ROWS, LANES), F32),
            VMEM((b_slots * ROWS, LANES), F32),
            VMEM((row_count * b_slots * ROWS, LANES), BF16),
        ],
        compiler_params=pltpu.CompilerParams(vmem_limit_bytes=40 << 20),
        cost_estimate=pl.CostEstimate(flops=1 << 24, bytes_accessed=4 << 20, transcendentals=0),
        name="stage",
    )(*a_parts, b_blocks, items, starts)


def multiply_kernel(first, peers, *refs):
    refs = list(refs)
    base = 0 if first else refs.pop(0)[0]
    items, starts, most, a_ref = refs[:4]
    b_refs = refs[5 : 4 + peers][::-1]
    out, rounds, sums, rows, sems = refs[4 + peers :]
    add_products(items, starts, a_ref, list(enumerate(b_refs, 1)), sums, window=base)
    row_count, kept = out.shape[0], out.shape[1]
    copies = []
    for i in range(row_count):
        for t in range(ROWS):
            rows[i, :, pl.ds(t * LANES, LANES)] = sums[i, pl.ds(t * kept, kept), :]
        copies.append(pltpu.make_async_copy(rows.at[i], out.at[i], sems.at[i]))
        copies[-1].start()
    flags = most[...]
    for ref in b_refs:
        flag = ref[pl.ds(CAPACITY * ROWS, FLAG), :].astype(F32)
        flags = jnp.maximum(flags, jnp.max(flag, axis=0, keepdims=True))
    rounds[0] = (jnp.max(flags).astype(I32) + CAPACITY - 1) // CAPACITY
    for copy in copies:
        copy.wait()


def multiply(base, items, starts, most, a_ready, sums, b_parts, shape):
    first = base is None
    peers = len(b_parts) + 1
    smem_spec = pl.BlockSpec(memory_space=SMEM)
    vmem_spec = pl.BlockSpec(memory_space=VMEM)
    given = [] if first else [base]
    return pl.pallas_call(
        functools.partial(multiply_kernel, first, peers),
        out_shape=[
            jax.ShapeDtypeStruct(shape, F32),
            jax.ShapeDtypeStruct((1,), I32),
            jax.ShapeDtypeStruct(sums.shape, F32),
        ],
        in_specs=[smem_spec] * (len(given) + 2) + [vmem_spec] * (2 + peers),
        out_specs=[pl.BlockSpec(memory_space=pl.ANY), smem_spec, vmem_spec],
        input_output_aliases={len(given) + 4: 2},
        scratch_shapes=[VMEM(shape, F32), pltpu.SemaphoreType.DMA((shape[0],))],
        compiler_params=pltpu.CompilerParams(vmem_limit_bytes=32 << 20),
        cost_estimate=pl.CostEstimate(flops=1 << 26, bytes_accessed=4 << 20, transcendentals=0),
        name="multiply",
    )(*given, items, starts, most, a_ready, sums, *b_parts[::-1])


def shards(a_blocks, a_index, b_blocks, b_cols, c_cols):
    rows = lax.axis_size("row")
    cols = lax.axis_size("col")
    a_slots = a_blocks.shape[1] * cols // rows
    row_count = b_blocks.shape[0]

    def send_rows(parts):
        far_first = range(len(parts), 0, -1)
        return [exchanged(parts[d - 1], "row", d) for d in far_first][::-1]

    def finish(base, most, sums, arrived):
        return multiply(base, items, starts, most, a_ready, sums, arrived, shape)

    shape = (row_count, c_cols.shape[1], BS * BS)
    index_parts = [a_index] + [exchanged(a_index, "col", h) for h in range(1, cols)]
    told = describe(index_parts, b_cols.T, c_cols.T)
    told = [told] + send_rows([told] * (rows - 1))
    flat = flatten(b_blocks)
    packed, most = pack(None, told, flat, cols, row_count, a_slots)
    arrived = send_rows(packed)
    items, starts = work_list(told, cols, row_count, a_slots)
    a_late, _ = lax.optimization_barrier((a_blocks, most))
    a_parts = [a_blocks, exchanged(a_late, "col", 1)]
    for h in range(2, cols, 2):
        far = exchanged(a_late, "col", h)
        a_parts += [far, exchanged(lax.optimization_barrier((far, items))[0], "col", 1)]
    a_ready, sums = stage(a_parts, b_blocks, items, starts)
    out, rounds, sums = finish(None, most, sums, arrived)

    def more(state):
        return state[0] < rounds[0]

    def one_round(state):
        at, sums, _ = state
        base = jnp.reshape(at * CAPACITY, (1,))
        packed, most = pack(base, told, flat, cols, row_count, a_slots)
        out, _, sums = finish(base, most, sums, send_rows(packed))
        return at + 1, sums, out

    return lax.while_loop(more, one_round, (jnp.int32(1), sums, out))[2]


def solution(mesh):
    return jax.shard_map(
        shards,
        mesh=mesh,
        in_specs=(
            P(("sys", "row"), "col", None),
            P(None, ("sys", "row"), "col"),
            P(("sys", "row"), "col", None),
            P(("sys", "row"), "col"),
            P(("sys", "row"), "col"),
        ),
        out_specs=P(("sys", "row"), "col", None),
        check_vma=False,
    )
```

```python
import functools

import jax
import jax.numpy as jnp
from jax import lax
from jax.experimental import pallas as pl
from jax.experimental.layout import Layout, with_layout_constraint
from jax.experimental.pallas import tpu as pltpu
from jax.sharding import PartitionSpec as P

BS = 64
LANES = 128
ROWS = BS * BS // LANES
CAPACITY = 16
UNROLL = 4
SLOTS = 4
FLAG = 16
IDLE = 63
VMEM = pltpu.VMEM
SMEM = pltpu.SMEM
BF16 = jnp.bfloat16
F32 = jnp.float32
I32 = jnp.int32


def exchanged(block, axis, distance):
    size = lax.axis_size(axis)
    return lax.ppermute(block, axis, [(i, i ^ distance) for i in range(size)])


def seen_by_rows(blocks):
    count = blocks.shape[0]
    parted = blocks.reshape(count, SLOTS, ROWS, LANES)
    parted = with_layout_constraint(parted, Layout(major_to_minor=(0, 2, 1, 3)))
    return parted.transpose(0, 2, 1, 3).reshape(count, ROWS * SLOTS, LANES)


def seen_by_blocks(rows):
    count = rows.shape[0]
    parted = rows.reshape(count, ROWS, SLOTS, LANES).transpose(0, 2, 1, 3)
    parted = with_layout_constraint(parted, Layout(major_to_minor=(0, 2, 1, 3)))
    return parted.reshape(count, SLOTS, BS * BS)


def describe(a_parts, b_cols, c_cols):
    cols = len(a_parts)
    total = -(-(2 * cols + 2 * SLOTS) // 8) * 8

    def placed(part, at):
        after = (total - at - part.shape[0], LANES - part.shape[1])
        return jnp.pad(part, ((at, after[0]), (0, after[1])), constant_values=-1)

    own = jnp.maximum(placed(c_cols, 2 * cols), placed(b_cols, 2 * cols + SLOTS))
    told = lax.optimization_barrier(jnp.maximum(own, placed(a_parts[0][:, 0, :], 0)))
    for h in range(1, cols):
        told = jnp.maximum(told, placed(a_parts[h][:, 0, :], 2 * h))
    return told


def offers(told, cols, row_count):
    start = 2 * cols + SLOTS
    rows = told[pl.ds(start, SLOTS), :]
    lane = iota((1, LANES), 1)
    result = rows[0:1]
    for n in range(1, SLOTS):
        moved = pltpu.roll(rows, n * row_count, 1)[n : n + 1]
        result = jnp.where(lane // row_count == n, moved, result)
    return result


def flatten_kernel(b_ref, flat, own, sums, wide):
    row_count = b_ref.shape[0]
    wide[...] = b_ref[...].astype(F32)
    for t in range(ROWS):
        for n in range(SLOTS):
            piece = wide[:, t * SLOTS + n, :].astype(BF16)
            flat[pl.ds(n * row_count, row_count), pl.ds(t * LANES, LANES)] = piece
    for n in range(SLOTS):
        for k in range(row_count):
            block = wide[k, pl.ds(n, ROWS, stride=SLOTS), :].astype(BF16)
            own[pl.ds((n * row_count + k) * ROWS, ROWS), :] = block
    sums[...] = jnp.zeros_like(sums)


def flatten(b_rows):
    vmem_spec = pl.BlockSpec(memory_space=VMEM)
    row_count = b_rows.shape[0]
    return pl.pallas_call(
        flatten_kernel,
        out_shape=(
            jax.ShapeDtypeStruct((row_count * SLOTS, BS * BS), BF16),
            jax.ShapeDtypeStruct((row_count * SLOTS * ROWS, LANES), BF16),
            jax.ShapeDtypeStruct(b_rows.shape, F32),
        ),
        in_specs=[vmem_spec],
        out_specs=(vmem_spec,) * 3,
        scratch_shapes=[VMEM(b_rows.shape, F32)],
        compiler_params=pltpu.CompilerParams(vmem_limit_bytes=24 << 20),
        cost_estimate=pl.CostEstimate(flops=1 << 20, bytes_accessed=8 << 20, transcendentals=0),
        name="flatten",
    )(b_rows)


def iota(shape, axis):
    return lax.broadcasted_iota(I32, shape, axis)


def turn_to_columns(rows, first, count):
    pick = (iota((count, LANES), 0) + first == iota((count, LANES), 1)).astype(BF16)
    return lax.dot_general(
        pick,
        rows.astype(F32).astype(BF16),
        (((1,), (1,)), ((), ())),
        preferred_element_type=F32,
    )


def matches(receiver, offered, holder, cols, row_count, first_slot, a_slots):
    turned = 2 * (holder ^ lax.axis_index("col"))
    rows = [receiver[pl.ds(turned, 1), :], receiver[pl.ds(turned + 1, 1), :]]
    rows += [receiver[pl.ds(2 * cols, SLOTS), :]]
    rows = jnp.concatenate(rows + [jnp.zeros((8 - 2 - SLOTS, LANES), I32)], axis=0)
    kept_columns = turn_to_columns(rows, 0, row_count)
    if isinstance(first_slot, int) and first_slot == 0 and a_slots == row_count:
        slot_columns = kept_columns
    else:
        slot_columns = turn_to_columns(rows, first_slot, a_slots)
    wanted = offered.astype(F32)
    kept = jnp.zeros((row_count, LANES), F32)
    which = jnp.zeros((row_count, LANES), F32)
    for m in range(SLOTS):
        column = kept_columns[:, 2 + m : 3 + m]
        equal = (column == wanted) & (wanted >= 0)
        kept = jnp.where(equal, 1.0, kept)
        which = jnp.where(equal, float(m), which)
    a_rows = slot_columns[:, 0:1]
    a_columns = slot_columns[:, 1:2]
    shape = (a_slots, row_count)
    by_row = (a_rows == iota(shape, 1).astype(F32)).astype(BF16)
    by_column = a_columns == (iota((a_slots, LANES), 1) % row_count).astype(F32)
    both = jnp.concatenate([kept, which], axis=1).astype(BF16)
    both = jnp.dot(by_row, both, preferred_element_type=F32)
    pairs = jnp.where(by_column & (both[:, :LANES] > 0.5), 1.0, 0.0)
    return pairs, both[:, LANES:], a_rows


def places(needed):
    before = (iota((LANES, LANES), 0) < iota((LANES, LANES), 1)).astype(BF16)
    many = jnp.broadcast_to(needed, (8, LANES)).astype(BF16)
    return jnp.dot(many, before, preferred_element_type=F32)[0:1]


def each(count, body, start):
    if count > 8:
        return lax.fori_loop(0, count, body, start)
    for at in range(count):
        start = body(at, start)
    return start


def pack_kernel(first, peers, cols, a_slots, row_count, *refs):
    refs = list(refs)
    base = 0 if first else refs.pop(0)[0]
    told = refs[:peers]
    flat = refs[peers]
    outs = refs[peers + 1 : 2 * peers]
    most, picks, packed = refs[2 * peers :]
    grid_row = lax.axis_index("row")
    per_col = peers // cols
    offered = offers(told[0], cols, row_count)
    top = jnp.zeros((1, 1), F32)
    first_slot = grid_row % per_col * a_slots if per_col > 1 else 0
    for d in range(1, peers):
        pairs, _, _ = matches(
            told[d], offered, grid_row // per_col, cols, row_count, first_slot, a_slots
        )
        needed = jnp.max(pairs, axis=0, keepdims=True)
        place = jnp.where(needed > 0.5, places(needed), -1.0).astype(I32)
        pick = (place == iota((CAPACITY, LANES), 0) + base).astype(BF16)
        picks[pl.ds((d - 1) * CAPACITY, CAPACITY), :] = pick
        top = jnp.maximum(top, jnp.sum(needed, axis=1, keepdims=True))
    most[...] = jnp.broadcast_to(top, most.shape)
    pick = picks[...][:, : flat.shape[0]]
    for t in range(0, ROWS, 2):
        both = flat[:, pl.ds(t * LANES, 2 * LANES)]
        both = jnp.dot(pick, both, preferred_element_type=F32)
        packed[:, t, :] = both[:, :LANES]
        packed[:, t + 1, :] = both[:, LANES:]
    for d in range(1, peers):
        out = outs[d - 1]
        for x in range(CAPACITY):
            out[pl.ds(x * ROWS, ROWS), :] = packed[(d - 1) * CAPACITY + x].astype(BF16)
        out[pl.ds(CAPACITY * ROWS, FLAG), :] = jnp.broadcast_to(top, (FLAG, LANES)).astype(BF16)


def pack(base, told, flat, cols, row_count, a_slots):
    first = base is None
    peers = len(told)
    smem_spec = pl.BlockSpec(memory_space=SMEM)
    vmem_spec = pl.BlockSpec(memory_space=VMEM)
    given = [] if first else [base]
    results = pl.pallas_call(
        functools.partial(pack_kernel, first, peers, cols, a_slots, row_count),
        out_shape=[jax.ShapeDtypeStruct((CAPACITY * ROWS + FLAG, LANES), BF16)] * (peers - 1)
        + [jax.ShapeDtypeStruct((8, LANES), F32)],
        in_specs=[smem_spec] * len(given) + [vmem_spec] * (peers + 1),
        out_specs=[vmem_spec] * peers,
        scratch_shapes=[
            VMEM(((peers - 1) * CAPACITY, LANES), BF16),
            VMEM(((peers - 1) * CAPACITY, ROWS, LANES), F32),
        ],
        compiler_params=pltpu.CompilerParams(vmem_limit_bytes=32 << 20),
        cost_estimate=pl.CostEstimate(flops=1 << 20, bytes_accessed=4 << 20, transcendentals=0),
        name="pack",
    )(*given, *told, flat)
    return results[:-1], results[-1]


def list_kernel(cols, a_slots, row_count, peers, *refs):
    told = refs[:peers]
    items, starts, words, words_s, sem = refs[peers:]
    grid_row = lax.axis_index("row")
    per_col = peers // cols
    lane = iota((a_slots, LANES), 1)
    slot = iota((a_slots, LANES), 0)
    words[...] = jnp.full(words.shape, IDLE, I32)
    for d in range(peers):
        group = grid_row ^ d
        holder = group // per_col
        first_slot = group % per_col * a_slots if per_col > 1 else 0
        offered = offers(told[d], cols, row_count)
        pairs, which, a_rows = matches(
            told[0], offered, holder, cols, row_count, first_slot, a_slots
        )
        if d == 0:
            place = iota((1, LANES), 1).astype(F32)
        else:
            place = places(jnp.max(pairs, axis=0, keepdims=True))
        stacked = jnp.concatenate([pairs, pairs * place, pairs * which], axis=0).astype(BF16)
        to_slot = iota((LANES, LANES), 1) == iota((LANES, LANES), 0) // row_count + d * SLOTS
        by_slot = jnp.dot(stacked, to_slot.astype(BF16), preferred_element_type=F32)
        hit = by_slot[:a_slots] > 0.5
        at = by_slot[a_slots : 2 * a_slots].astype(I32)
        out = (a_rows * SLOTS + by_slot[2 * a_slots :]).astype(I32)
        a_slot = holder * per_col * a_slots + first_slot + slot
        word = ((a_slot * 64 + out) * 64 + at) * 64 + d
        words[...] = jnp.where(hit & (lane // SLOTS == d), word, words[...])
    fetch([(words, words_s)], sem)

    def one_peer(d, length):
        starts[d] = length
        for n in range(SLOTS):
            for s in range(a_slots):
                word = words_s[s, d * SLOTS + n]
                items[length] = word
                length = length + (word & IDLE != IDLE).astype(I32)
        return length

    length = lax.fori_loop(0, peers, one_peer, jnp.int32(0))
    starts[peers] = length
    items[length] = IDLE


def work_list(told, cols, row_count, a_slots):
    peers = len(told)
    most_items = peers * a_slots * SLOTS + 1
    return pl.pallas_call(
        functools.partial(list_kernel, cols, a_slots, row_count, peers),
        out_shape=[
            jax.ShapeDtypeStruct((most_items,), I32),
            jax.ShapeDtypeStruct((peers + 1,), I32),
        ],
        in_specs=[pl.BlockSpec(memory_space=VMEM)] * peers,
        out_specs=[pl.BlockSpec(memory_space=SMEM)] * 2,
        scratch_shapes=[
            VMEM((a_slots, LANES), I32),
            SMEM((a_slots, LANES), I32),
            pltpu.SemaphoreType.DMA((1,)),
        ],
        cost_estimate=pl.CostEstimate(flops=1 << 10, bytes_accessed=1 << 10, transcendentals=0),
        name="work_list",
    )(*told)


def fetch(copies, sems):
    started = [
        pltpu.make_async_copy(source, target, sems.at[at])
        for at, (source, target) in enumerate(copies)
    ]
    for copy in started:
        copy.start()
    for copy in started:
        copy.wait()


def add_products(items, starts, a_ref, peer_refs, sums, window=None):
    low = iota((ROWS, LANES), 1) < BS
    nothing = jnp.zeros((ROWS, LANES), BF16)

    def add_one(word, used, b_ref):
        place = (word >> 6) & 63
        target = (word >> 12) & 63
        used = used & ((word & IDLE) != IDLE)
        if window is not None:
            place = place - window
            used = used & (place >= 0) & (place < CAPACITY)
        place = jnp.where(used, place, 0)
        a_at = pl.multiple_of((word >> 18) * ROWS, ROWS)
        b_at = pl.multiple_of(place * ROWS, ROWS)
        block = jnp.where(used, b_ref[pl.ds(b_at, ROWS), :], nothing)
        turned = jnp.concatenate([block[:, BS:], block[:, :BS]], axis=1)
        right = jnp.concatenate(
            [
                jnp.where(low, block, nothing),
                jnp.where(low, turned, nothing),
                jnp.where(low, nothing, turned),
                jnp.where(low, nothing, block),
            ],
            axis=0,
        )
        term = jnp.dot(a_ref[pl.ds(a_at, ROWS), :], right, preferred_element_type=F32)
        sums[target // SLOTS, pl.ds(target % SLOTS, ROWS, stride=SLOTS), :] += term

    for at in range(0, len(peer_refs), 3):
        chosen = peer_refs[at : at + 3]
        bounds = [(starts[d], starts[d + 1]) for d, _ in chosen]
        longest = functools.reduce(jnp.maximum, [stop - start for start, stop in bounds])
        width = UNROLL if len(chosen) < 3 else UNROLL - 1

        def some_items(step, carry, chosen=chosen, bounds=bounds, width=width):
            for u in range(width):
                for (_, b_ref), (start, stop) in zip(chosen, bounds):
                    y = start + step * width + u
                    used = y < stop
                    add_one(items[jnp.where(used, y, start)], used, b_ref)
            return carry

        lax.fori_loop(0, (longest + width - 1) // width, some_items, 0)


def stage_kernel(cols, *refs):
    a_refs, own, items, starts = refs[:cols], refs[cols], refs[cols + 1], refs[cols + 2]
    a_out, sums, a_wide = refs[cols + 4 :]
    source = iota((LANES, LANES), 0)
    target = iota((LANES, LANES), 1)
    wanted = (target // BS) * BS + 2 * (target % ROWS) + (target // ROWS) % 2
    order = (source == wanted).astype(BF16)
    slots = a_refs[0].shape[1]
    grid_col = lax.axis_index("col")
    for t in range(ROWS):
        pieces = [ref[0, :, pl.ds(t * LANES, LANES)] for ref in a_refs]
        done = jnp.dot(jnp.concatenate(pieces, axis=0), order, preferred_element_type=F32)
        a_wide[:, t, :] = done
    for h in range(cols):
        first = (grid_col ^ h) * slots
        for s in range(slots):
            at = pl.multiple_of((first + s) * ROWS, ROWS)
            a_out[pl.ds(at, ROWS), :] = a_wide[h * slots + s].astype(BF16)
    add_products(items, starts, a_out, [(0, own)], sums)


def stage(a_parts, own, sums, items, starts):
    cols, slots = len(a_parts), a_parts[0].shape[1]
    vmem_spec = pl.BlockSpec(memory_space=VMEM)
    smem_spec = pl.BlockSpec(memory_space=SMEM)
    return pl.pallas_call(
        functools.partial(stage_kernel, cols),
        out_shape=(
            jax.ShapeDtypeStruct((cols * slots * ROWS, LANES), BF16),
            jax.ShapeDtypeStruct(sums.shape, F32),
        ),
        in_specs=[vmem_spec] * (cols + 1) + [smem_spec] * 2 + [vmem_spec],
        out_specs=(vmem_spec,) * 2,
        input_output_aliases={cols + 3: 1},
        scratch_shapes=[VMEM((cols * slots, ROWS, LANES), F32)],
        compiler_params=pltpu.CompilerParams(vmem_limit_bytes=40 << 20),
        cost_estimate=pl.CostEstimate(flops=1 << 10, bytes_accessed=1 << 10, transcendentals=0),
        name="stage",
    )(*a_parts, own, items, starts, sums)


def multiply_kernel(first, peers, *refs):
    refs = list(refs)
    base = 0 if first else refs.pop(0)[0]
    items, starts, most, a_ref = refs[:4]
    b_refs = refs[5 : 4 + peers][::-1]
    out, rounds, sums, sem = refs[4 + peers :]
    add_products(items, starts, a_ref, list(enumerate(b_refs, 1)), sums, window=base)
    copy = pltpu.make_async_copy(sums, out, sem.at[0])
    copy.start()
    flags = most[...]
    for ref in b_refs:
        flag = ref[pl.ds(CAPACITY * ROWS, FLAG), :].astype(F32)
        flags = jnp.maximum(flags, jnp.max(flag, axis=0, keepdims=True))
    rounds[0] = (jnp.max(flags).astype(I32) + CAPACITY - 1) // CAPACITY
    copy.wait()


def multiply(base, items, starts, most, a_ready, sums, b_parts):
    first = base is None
    peers = len(b_parts) + 1
    smem_spec = pl.BlockSpec(memory_space=SMEM)
    vmem_spec = pl.BlockSpec(memory_space=VMEM)
    given = [] if first else [base]
    return pl.pallas_call(
        functools.partial(multiply_kernel, first, peers),
        out_shape=[
            jax.ShapeDtypeStruct(sums.shape, F32),
            jax.ShapeDtypeStruct((1,), I32),
            jax.ShapeDtypeStruct(sums.shape, F32),
        ],
        in_specs=[smem_spec] * (len(given) + 2) + [vmem_spec] * (2 + peers),
        out_specs=[pl.BlockSpec(memory_space=pl.ANY), smem_spec, vmem_spec],
        input_output_aliases={len(given) + 4: 2},
        scratch_shapes=[pltpu.SemaphoreType.DMA((1,))],
        compiler_params=pltpu.CompilerParams(vmem_limit_bytes=32 << 20),
        cost_estimate=pl.CostEstimate(flops=1 << 26, bytes_accessed=4 << 20, transcendentals=0),
        name="multiply",
    )(*given, items, starts, most, a_ready, sums, *b_parts[::-1])


def shards(a_blocks, a_index, b_blocks, b_cols, c_cols):
    rows = lax.axis_size("row")
    cols = lax.axis_size("col")
    a_slots = a_blocks.shape[1] * cols // rows
    row_count = b_blocks.shape[0]

    def send_rows(parts):
        far_first = range(len(parts), 0, -1)
        return [exchanged(parts[d - 1], "row", d) for d in far_first][::-1]

    told = describe([a_index] + [exchanged(a_index, "col", h) for h in range(1, cols)],
                    b_cols.T, c_cols.T)
    told = [told] + send_rows([told] * (rows - 1))
    flat, own, sums = flatten(seen_by_rows(b_blocks))
    packed, most = pack(None, told, flat, cols, row_count, a_slots)
    arrived = send_rows(packed)
    items, starts = work_list(told, cols, row_count, a_slots)
    a_late, _ = lax.optimization_barrier((a_blocks, most))
    a_far = [exchanged(a_late, "col", h) for h in range(2, cols, 2)]
    a_parts = [a_blocks, exchanged(a_late, "col", 1)]
    for far in a_far:
        a_parts += [far, exchanged(lax.optimization_barrier((far, items))[0], "col", 1)]
    a_ready, sums = stage(a_parts, own, sums, items, starts)
    out, rounds, sums = multiply(None, items, starts, most, a_ready, sums, arrived)

    def more(state):
        return state[0] < rounds[0]

    def one_round(state):
        at, sums, _ = state
        base = jnp.reshape(at * CAPACITY, (1,))
        packed, most = pack(base, told, flat, cols, row_count, a_slots)
        arrived = send_rows(packed)
        out, _, sums = multiply(base, items, starts, most, a_ready, sums, arrived)
        return at + 1, sums, out

    return seen_by_blocks(lax.while_loop(more, one_round, (jnp.int32(1), sums, out))[2])


def solution(mesh):
    return jax.shard_map(
        shards,
        mesh=mesh,
        in_specs=(
            P(("sys", "row"), "col", None),
            P(None, ("sys", "row"), "col"),
            P(("sys", "row"), "col", None),
            P(("sys", "row"), "col"),
            P(("sys", "row"), "col"),
        ),
        out_specs=P(("sys", "row"), "col", None),
        check_vma=False,
    )
```

```python
import functools

import jax
import jax.numpy as jnp
from jax import lax
from jax.experimental import pallas as pl
from jax.experimental.layout import Layout, with_layout_constraint
from jax.experimental.pallas import tpu as pltpu
from jax.sharding import PartitionSpec as P

BS = 64
LANES = 128
ROWS = BS * BS // LANES
CAPACITY = 16
UNROLL = 4
SLOTS = 4
VMEM = pltpu.VMEM
SMEM = pltpu.SMEM
BF16 = jnp.bfloat16
F32 = jnp.float32
I32 = jnp.int32


def exchanged(block, axis, distance):
    size = lax.axis_size(axis)
    return lax.ppermute(block, axis, [(i, i ^ distance) for i in range(size)])


def seen_by_rows(blocks):
    count = blocks.shape[0]
    parted = blocks.reshape(count, SLOTS, ROWS, LANES)
    parted = with_layout_constraint(parted, Layout(major_to_minor=(0, 2, 1, 3)))
    return parted.transpose(0, 2, 1, 3).reshape(count, ROWS * SLOTS, LANES)


def seen_by_blocks(rows):
    count = rows.shape[0]
    parted = rows.reshape(count, ROWS, SLOTS, LANES).transpose(0, 2, 1, 3)
    parted = with_layout_constraint(parted, Layout(major_to_minor=(0, 2, 1, 3)))
    return parted.reshape(count, SLOTS, BS * BS)


def describe(a_parts, b_cols, c_cols):
    cols = len(a_parts)
    total = -(-(2 * cols + 2 * SLOTS) // 8) * 8

    def placed(part, at):
        after = (total - at - part.shape[0], LANES - part.shape[1])
        return jnp.pad(part, ((at, after[0]), (0, after[1])), constant_values=-1)

    own = jnp.maximum(placed(c_cols, 2 * cols), placed(b_cols, 2 * cols + SLOTS))
    told = lax.optimization_barrier(jnp.maximum(own, placed(a_parts[0][:, 0, :], 0)))
    for h in range(1, cols):
        told = jnp.maximum(told, placed(a_parts[h][:, 0, :], 2 * h))
    return told


def offers(told, cols, row_count):
    start = 2 * cols + SLOTS
    rows = told[pl.ds(start, SLOTS), :]
    lane = iota((1, LANES), 1)
    result = rows[0:1]
    for n in range(1, SLOTS):
        moved = pltpu.roll(rows, n * row_count, 1)[n : n + 1]
        result = jnp.where(lane // row_count == n, moved, result)
    return result


def flatten_kernel(b_ref, flat, own, sums, wide):
    row_count = b_ref.shape[0]
    wide[...] = b_ref[...].astype(F32)
    for t in range(ROWS):
        for n in range(SLOTS):
            piece = wide[:, t * SLOTS + n, :].astype(BF16)
            flat[pl.ds(n * row_count, row_count), pl.ds(t * LANES, LANES)] = piece
    for n in range(SLOTS):
        for k in range(row_count):
            block = wide[k, pl.ds(n, ROWS, stride=SLOTS), :].astype(BF16)
            own[pl.ds((n * row_count + k) * ROWS, ROWS), :] = block
    sums[...] = jnp.zeros_like(sums)


def flatten(b_rows):
    vmem_spec = pl.BlockSpec(memory_space=VMEM)
    row_count = b_rows.shape[0]
    return pl.pallas_call(
        flatten_kernel,
        out_shape=(
            jax.ShapeDtypeStruct((row_count * SLOTS, BS * BS), BF16),
            jax.ShapeDtypeStruct((row_count * SLOTS * ROWS, LANES), BF16),
            jax.ShapeDtypeStruct(b_rows.shape, F32),
        ),
        in_specs=[vmem_spec],
        out_specs=(vmem_spec,) * 3,
        scratch_shapes=[VMEM(b_rows.shape, F32)],
        compiler_params=pltpu.CompilerParams(vmem_limit_bytes=24 << 20),
        cost_estimate=pl.CostEstimate(flops=1 << 20, bytes_accessed=8 << 20, transcendentals=0),
        name="flatten",
    )(b_rows)


def iota(shape, axis):
    return lax.broadcasted_iota(I32, shape, axis)


def along_lanes(left, right):
    return lax.dot_general(
        left.astype(BF16), right.astype(BF16), (((1,), (1,)), ((), ())), preferred_element_type=F32
    )


def turn_to_columns(rows, first, count):
    pick = (iota((count, LANES), 0) + first == iota((count, LANES), 1)).astype(BF16)
    return lax.dot_general(
        pick,
        rows.astype(F32).astype(BF16),
        (((1,), (1,)), ((), ())),
        preferred_element_type=F32,
    )


def matches(receiver, offered, holder, cols, row_count, first_slot, a_slots):
    turned = 2 * (holder ^ lax.axis_index("col"))
    rows = [receiver[pl.ds(turned, 1), :], receiver[pl.ds(turned + 1, 1), :]]
    rows += [receiver[pl.ds(2 * cols, SLOTS), :]]
    rows = jnp.concatenate(rows + [jnp.zeros((8 - 2 - SLOTS, LANES), I32)], axis=0)
    kept_columns = turn_to_columns(rows, 0, row_count)
    if isinstance(first_slot, int) and first_slot == 0 and a_slots == row_count:
        slot_columns = kept_columns
    else:
        slot_columns = turn_to_columns(rows, first_slot, a_slots)
    wanted = offered.astype(F32)
    kept = jnp.zeros((row_count, LANES), F32)
    which = jnp.zeros((row_count, LANES), F32)
    for m in range(SLOTS):
        column = kept_columns[:, 2 + m : 3 + m]
        equal = (column == wanted) & (wanted >= 0)
        kept = jnp.where(equal, 1.0, kept)
        which = jnp.where(equal, float(m), which)
    a_rows = slot_columns[:, 0:1]
    a_columns = slot_columns[:, 1:2]
    shape = (a_slots, row_count)
    by_row = (a_rows == iota(shape, 1).astype(F32)).astype(BF16)
    by_column = a_columns == (iota((a_slots, LANES), 1) % row_count).astype(F32)
    both = jnp.concatenate([kept, which], axis=1).astype(BF16)
    both = jnp.dot(by_row, both, preferred_element_type=F32)
    pairs = jnp.where(by_column & (both[:, :LANES] > 0.5), 1.0, 0.0)
    return pairs, both[:, LANES:], a_rows


def places(needed):
    before = (iota((LANES, LANES), 0) < iota((LANES, LANES), 1)).astype(BF16)
    many = jnp.broadcast_to(needed, (8, LANES)).astype(BF16)
    return jnp.dot(many, before, preferred_element_type=F32)[0:1]


def pack_kernel(first, peers, cols, a_slots, row_count, *refs):
    refs = list(refs)
    base = 0 if first else refs.pop(0)[0]
    told = refs[:peers]
    flat = refs[peers]
    outs = refs[peers + 1 : 2 * peers]
    picks, packed = refs[2 * peers :]
    grid_row = lax.axis_index("row")
    per_col = peers // cols
    offered = offers(told[0], cols, row_count)
    first_slot = grid_row % per_col * a_slots if per_col > 1 else 0
    for d in range(1, peers):
        pairs, _, _ = matches(
            told[d], offered, grid_row // per_col, cols, row_count, first_slot, a_slots
        )
        needed = jnp.max(pairs, axis=0, keepdims=True)
        place = jnp.where(needed > 0.5, places(needed), -1.0).astype(I32)
        pick = (place == iota((CAPACITY, LANES), 0) + base).astype(BF16)
        picks[pl.ds((d - 1) * CAPACITY, CAPACITY), :] = pick
    pick = picks[...][:, : flat.shape[0]]
    for t in range(0, ROWS, 2):
        both = flat[:, pl.ds(t * LANES, 2 * LANES)]
        both = jnp.dot(pick, both, preferred_element_type=F32)
        packed[:, t, :] = both[:, :LANES]
        packed[:, t + 1, :] = both[:, LANES:]
    for d in range(1, peers):
        out = outs[d - 1]
        for x in range(CAPACITY):
            out[pl.ds(x * ROWS, ROWS), :] = packed[(d - 1) * CAPACITY + x].astype(BF16)


def pack(base, told, flat, cols, row_count, a_slots):
    first = base is None
    peers = len(told)
    smem_spec = pl.BlockSpec(memory_space=SMEM)
    vmem_spec = pl.BlockSpec(memory_space=VMEM)
    given = [] if first else [base]
    return pl.pallas_call(
        functools.partial(pack_kernel, first, peers, cols, a_slots, row_count),
        out_shape=[jax.ShapeDtypeStruct((CAPACITY * ROWS, LANES), BF16)] * (peers - 1),
        in_specs=[smem_spec] * len(given) + [vmem_spec] * (peers + 1),
        out_specs=[vmem_spec] * (peers - 1),
        scratch_shapes=[
            VMEM(((peers - 1) * CAPACITY, LANES), BF16),
            VMEM(((peers - 1) * CAPACITY, ROWS, LANES), F32),
        ],
        compiler_params=pltpu.CompilerParams(vmem_limit_bytes=32 << 20),
        cost_estimate=pl.CostEstimate(flops=1 << 20, bytes_accessed=4 << 20, transcendentals=0),
        name="pack",
    )(*given, *told, flat)


def list_kernel(cols, a_slots, row_count, peers, *refs):
    told, items = refs[:peers], refs[peers]
    grid_row = lax.axis_index("row")
    grid_col = lax.axis_index("col")
    per_col = peers // cols
    blocks = row_count * SLOTS
    lane = iota((1, LANES), 1)
    spot = iota((blocks, LANES), 0)
    before = (iota((LANES, LANES), 0) < iota((LANES, LANES), 1)).astype(BF16)
    below = (iota((blocks, blocks), 1) < iota((blocks, blocks), 0)).astype(BF16)
    same_slot = spot // row_count == iota((blocks, LANES), 1) // a_slots
    for d in range(peers):
        group = grid_row ^ d
        holder = group // per_col
        first_slot = group % per_col * a_slots if per_col > 1 else 0
        at = 2 * (holder ^ grid_col)
        slots = []
        for row in (told[0][pl.ds(at, 1), :], told[0][pl.ds(at + 1, 1), :]):
            if per_col > 1:
                row = pltpu.roll(row, (LANES - first_slot) % LANES, 1)
            spread = row
            for n in range(1, SLOTS):
                spread = jnp.where(lane // a_slots == n, pltpu.roll(row, n * a_slots, 1), spread)
            slots.append(jnp.where(lane < SLOTS * a_slots, spread, -1))
        a_rows, a_columns = slots
        offered = turn_to_columns(
            jnp.broadcast_to(offers(told[d], cols, row_count), (8, LANES)), 0, blocks
        )[:, 0:1]
        kept = jnp.zeros((blocks, LANES), F32)
        which = jnp.zeros((blocks, LANES), F32)
        for m in range(SLOTS):
            column = told[0][pl.ds(2 * cols + m, 1), :].astype(F32)
            equal = (column == offered) & (offered >= 0)
            kept = jnp.where(equal, 1.0, kept)
            which = jnp.where(equal, float(m), which)
        by_row = (a_rows == iota((row_count, LANES), 0)).astype(BF16)
        both = jnp.concatenate([kept, which], axis=0)[:, :row_count].astype(BF16)
        both = jnp.dot(both, by_row, preferred_element_type=F32)
        meets = (both[:blocks] > 0.5) & (a_columns == spot % row_count) & same_slot
        pairs = jnp.where(meets, 1.0, 0.0)
        if d == 0:
            place = spot.astype(F32)
        else:
            needed = jnp.max(pairs, axis=1, keepdims=True)
            many = jnp.broadcast_to(needed, (blocks, LANES)).astype(BF16)
            place = jnp.dot(below, many, preferred_element_type=F32)
        hit = jnp.sum(pairs, axis=0, keepdims=True)
        place = jnp.sum(pairs * place, axis=0, keepdims=True)
        out = jnp.sum(pairs * both[blocks:], axis=0, keepdims=True)
        out = out + a_rows.astype(F32) * SLOTS * hit
        rank = jnp.dot(
            jnp.broadcast_to(hit, (8, LANES)).astype(BF16), before, preferred_element_type=F32
        )[0:1]
        rank = jnp.where(hit > 0.5, rank, -1.0).astype(I32)
        chosen = rank == iota((LANES, LANES), 0)
        zero = jnp.zeros((1, LANES), F32)
        values = [(lane % a_slots).astype(F32) * hit, out, place] + [zero] * 5
        listed = along_lanes(jnp.concatenate(values, axis=0), chosen.astype(F32)).astype(I32)
        a_slot = holder * per_col * a_slots + first_slot + listed[0:1]
        word = (a_slot * 64 + listed[1:2]) * 64 + listed[2:3]
        total = jnp.sum(hit, axis=1, keepdims=True).astype(I32)
        items[pl.ds(d, 1), :] = jnp.where(lane == LANES - 1, total, word)


def work_list(told, cols, row_count, a_slots):
    peers = len(told)
    return pl.pallas_call(
        functools.partial(list_kernel, cols, a_slots, row_count, peers),
        out_shape=jax.ShapeDtypeStruct((-(-peers // 8) * 8, LANES), I32),
        in_specs=[pl.BlockSpec(memory_space=VMEM)] * peers,
        out_specs=pl.BlockSpec(memory_space=VMEM),
        cost_estimate=pl.CostEstimate(flops=1 << 10, bytes_accessed=1 << 10, transcendentals=0),
        name="work_list",
    )(*told)


def rounds_kernel(cols, a_slots, row_count, peers, *refs):
    told_refs, rounds, told = refs[:peers], refs[peers], refs[peers + 1]
    for d, ref in enumerate(told_refs):
        told[d, :, :] = ref[...]
    grid_row = lax.axis_index("row")
    per_col = peers // cols

    def one_pair(receiver, d, most):
        group = grid_row ^ receiver ^ d
        sender = receiver ^ d
        first_slot = group % per_col * a_slots if per_col > 1 else 0
        pairs, _, _ = matches(
            told.at[receiver],
            offers(told.at[sender], cols, row_count),
            group // per_col,
            cols,
            row_count,
            first_slot,
            a_slots,
        )
        needed = jnp.max(pairs, axis=0, keepdims=True)
        return jnp.maximum(most, jnp.sum(needed, axis=1, keepdims=True))

    most = jnp.zeros((1, 1), F32)
    if peers <= 4:
        for receiver in range(peers):
            for d in range(1, peers):
                most = one_pair(receiver, d, most)
    else:

        def step(at, most):
            return one_pair(at // (peers - 1), at % (peers - 1) + 1, most)

        most = lax.fori_loop(0, peers * (peers - 1), step, most)
    rounds[0] = (jnp.max(most).astype(I32) + CAPACITY - 1) // CAPACITY


def count_rounds(told, cols, row_count, a_slots):
    peers = len(told)
    return pl.pallas_call(
        functools.partial(rounds_kernel, cols, a_slots, row_count, peers),
        out_shape=jax.ShapeDtypeStruct((1,), I32),
        in_specs=[pl.BlockSpec(memory_space=VMEM)] * peers,
        out_specs=pl.BlockSpec(memory_space=SMEM),
        scratch_shapes=[VMEM((peers,) + told[0].shape, I32)],
        cost_estimate=pl.CostEstimate(flops=1 << 10, bytes_accessed=1 << 10, transcendentals=0),
        name="count_rounds",
    )(*told)


def add_products(items, a_ref, peer_refs, sums, window=None):
    low = iota((ROWS, LANES), 1) < BS
    nothing = jnp.zeros((ROWS, LANES), BF16)

    def add_one(word, used, b_ref):
        word = jnp.where(used, word, 0)
        place = word & 63
        target = (word >> 6) & 63
        if window is not None:
            place = place - window
            used = used & (place >= 0) & (place < CAPACITY)
            place = jnp.where(used, place, 0)
        a_at = pl.multiple_of((word >> 12) * ROWS, ROWS)
        b_at = pl.multiple_of(place * ROWS, ROWS)
        block = jnp.where(used, b_ref[pl.ds(b_at, ROWS), :], nothing)
        turned = jnp.concatenate([block[:, BS:], block[:, :BS]], axis=1)
        right = jnp.concatenate(
            [
                jnp.where(low, block, nothing),
                jnp.where(low, turned, nothing),
                jnp.where(low, nothing, turned),
                jnp.where(low, nothing, block),
            ],
            axis=0,
        )
        term = jnp.dot(a_ref[pl.ds(a_at, ROWS), :], right, preferred_element_type=F32)
        sums[target // SLOTS, pl.ds(target % SLOTS, ROWS, stride=SLOTS), :] += term

    for at in range(0, len(peer_refs), 3):
        chosen = peer_refs[at : at + 3]
        totals = [items[d, LANES - 1] for d, _ in chosen]
        longest = functools.reduce(jnp.maximum, totals)
        width = UNROLL if len(chosen) < 3 else UNROLL - 1

        def some_items(step, carry, chosen=chosen, totals=totals, width=width):
            for u in range(width):
                for (d, b_ref), total in zip(chosen, totals):
                    y = step * width + u
                    add_one(items[d, y], y < total, b_ref)
            return carry

        lax.fori_loop(0, (longest + width - 1) // width, some_items, 0)


def stage_kernel(cols, *refs):
    a_refs, own, items = refs[:cols], refs[cols], refs[cols + 1]
    a_out, sums, a_wide = refs[cols + 3 :]
    source = iota((LANES, LANES), 0)
    target = iota((LANES, LANES), 1)
    wanted = (target // BS) * BS + 2 * (target % ROWS) + (target // ROWS) % 2
    order = (source == wanted).astype(BF16)
    slots = a_refs[0].shape[1]
    grid_col = lax.axis_index("col")
    for t in range(ROWS):
        pieces = [ref[0, :, pl.ds(t * LANES, LANES)] for ref in a_refs]
        done = jnp.dot(jnp.concatenate(pieces, axis=0), order, preferred_element_type=F32)
        a_wide[:, t, :] = done
    for h in range(cols):
        first = (grid_col ^ h) * slots
        for s in range(slots):
            at = pl.multiple_of((first + s) * ROWS, ROWS)
            a_out[pl.ds(at, ROWS), :] = a_wide[h * slots + s].astype(BF16)
    add_products(items, a_out, [(0, own)], sums)


def stage(a_parts, own, sums, items):
    cols, slots = len(a_parts), a_parts[0].shape[1]
    vmem_spec = pl.BlockSpec(memory_space=VMEM)
    smem_spec = pl.BlockSpec(memory_space=SMEM)
    return pl.pallas_call(
        functools.partial(stage_kernel, cols),
        out_shape=(
            jax.ShapeDtypeStruct((cols * slots * ROWS, LANES), BF16),
            jax.ShapeDtypeStruct(sums.shape, F32),
        ),
        in_specs=[vmem_spec] * (cols + 1) + [smem_spec] + [vmem_spec],
        out_specs=(vmem_spec,) * 2,
        input_output_aliases={cols + 2: 1},
        scratch_shapes=[VMEM((cols * slots, ROWS, LANES), F32)],
        compiler_params=pltpu.CompilerParams(vmem_limit_bytes=40 << 20),
        cost_estimate=pl.CostEstimate(flops=1 << 10, bytes_accessed=1 << 10, transcendentals=0),
        name="stage",
    )(*a_parts, own, items, sums)


def multiply_kernel(first, peers, *refs):
    refs = list(refs)
    base = 0 if first else refs.pop(0)[0]
    items, a_ref = refs[:2]
    b_refs = refs[3 : 2 + peers][::-1]
    sums, out, sem = refs[2 + peers :]
    add_products(items, a_ref, list(enumerate(b_refs, 1)), sums, window=base)
    copy = pltpu.make_async_copy(sums, out, sem.at[0])
    copy.start()
    copy.wait()


def multiply(base, items, a_ready, sums, b_parts):
    first = base is None
    peers = len(b_parts) + 1
    smem_spec = pl.BlockSpec(memory_space=SMEM)
    vmem_spec = pl.BlockSpec(memory_space=VMEM)
    given = [] if first else [base]
    return pl.pallas_call(
        functools.partial(multiply_kernel, first, peers),
        out_shape=[jax.ShapeDtypeStruct(sums.shape, F32)] * 2,
        in_specs=[smem_spec] * (len(given) + 1) + [vmem_spec] * (1 + peers),
        out_specs=[vmem_spec, pl.BlockSpec(memory_space=pl.ANY)],
        input_output_aliases={len(given) + 2: 0},
        scratch_shapes=[pltpu.SemaphoreType.DMA((1,))],
        compiler_params=pltpu.CompilerParams(vmem_limit_bytes=32 << 20),
        cost_estimate=pl.CostEstimate(flops=1 << 26, bytes_accessed=4 << 20, transcendentals=0),
        name="multiply",
    )(*given, items, a_ready, sums, *b_parts[::-1])


def shards(a_blocks, a_index, b_blocks, b_cols, c_cols):
    rows = lax.axis_size("row")
    cols = lax.axis_size("col")
    a_slots = a_blocks.shape[1] * cols // rows
    row_count = b_blocks.shape[0]

    def send_rows(parts):
        far_first = range(len(parts), 0, -1)
        return [exchanged(parts[d - 1], "row", d) for d in far_first][::-1]

    index_parts = [a_index] + [exchanged(a_index, "col", h) for h in range(1, cols)]
    told = describe(index_parts, b_cols.T, c_cols.T)
    a_parts = [exchanged(a_blocks, "col", h) for h in range(1, cols)]
    told, a_parts[0] = lax.optimization_barrier((told, a_parts[0]))
    told = [told] + send_rows([told] * (rows - 1))
    flat, own, sums = flatten(seen_by_rows(b_blocks))
    flat, *a_parts = lax.optimization_barrier((flat, *a_parts))
    packed = pack(None, told, flat, cols, row_count, a_slots)
    arrived = send_rows(packed)
    told_late = lax.optimization_barrier((told, packed[0]))[0]
    items = work_list(told_late, cols, row_count, a_slots)
    rounds = count_rounds(told_late, cols, row_count, a_slots)
    a_ready, sums = stage([a_blocks] + a_parts, own, sums, items)
    sums, out = multiply(None, items, a_ready, sums, arrived)

    def more(state):
        return state[0] < rounds[0]

    def one_round(state):
        at, sums, _ = state
        base = jnp.reshape(at * CAPACITY, (1,))
        arrived = send_rows(pack(base, told, flat, cols, row_count, a_slots))
        return at + 1, *multiply(base, items, a_ready, sums, arrived)

    return seen_by_blocks(lax.while_loop(more, one_round, (jnp.int32(1), sums, out))[2])


def solution(mesh):
    return jax.shard_map(
        shards,
        mesh=mesh,
        in_specs=(
            P(("sys", "row"), "col", None),
            P(None, ("sys", "row"), "col"),
            P(("sys", "row"), "col", None),
            P(("sys", "row"), "col"),
            P(("sys", "row"), "col"),
        ),
        out_specs=P(("sys", "row"), "col", None),
        check_vma=False,
    )
```

```python
import functools

import jax
import jax.numpy as jnp
from jax import lax
from jax.experimental import pallas as pl
from jax.experimental.layout import Layout, with_layout_constraint
from jax.experimental.pallas import tpu as pltpu
from jax.sharding import PartitionSpec as P

BS = 64
LANES = 128
ROWS = BS * BS // LANES
CAPACITY = 16
UNROLL = 4
SLOTS = 4
VMEM = pltpu.VMEM
SMEM = pltpu.SMEM
BF16 = jnp.bfloat16
F32 = jnp.float32
I32 = jnp.int32


def exchanged(block, axis, distance):
    size = lax.axis_size(axis)
    return lax.ppermute(block, axis, [(i, i ^ distance) for i in range(size)])


def seen_by_rows(blocks):
    count = blocks.shape[0]
    parted = blocks.reshape(count, SLOTS, ROWS, LANES)
    parted = with_layout_constraint(parted, Layout(major_to_minor=(0, 2, 1, 3)))
    return parted.transpose(0, 2, 1, 3).reshape(count, ROWS * SLOTS, LANES)


def seen_by_blocks(rows):
    count = rows.shape[0]
    parted = rows.reshape(count, ROWS, SLOTS, LANES).transpose(0, 2, 1, 3)
    parted = with_layout_constraint(parted, Layout(major_to_minor=(0, 2, 1, 3)))
    return parted.reshape(count, SLOTS, BS * BS)


def describe(a_parts, b_cols, c_cols):
    cols = len(a_parts)
    total = -(-(2 * cols + 2 * SLOTS) // 8) * 8

    def placed(part, at):
        after = (total - at - part.shape[0], LANES - part.shape[1])
        return jnp.pad(part, ((at, after[0]), (0, after[1])), constant_values=-1)

    own = jnp.maximum(placed(c_cols, 2 * cols), placed(b_cols, 2 * cols + SLOTS))
    told = lax.optimization_barrier(jnp.maximum(own, placed(a_parts[0][:, 0, :], 0)))
    for h in range(1, cols):
        told = jnp.maximum(told, placed(a_parts[h][:, 0, :], 2 * h))
    return told


def offers(told, cols, row_count):
    start = 2 * cols + SLOTS
    rows = told[pl.ds(start, SLOTS), :]
    lane = iota((1, LANES), 1)
    result = rows[0:1]
    for n in range(1, SLOTS):
        moved = pltpu.roll(rows, n * row_count, 1)[n : n + 1]
        result = jnp.where(lane // row_count == n, moved, result)
    return result


def flatten_kernel(b_ref, flat, own, sums, wide):
    row_count = b_ref.shape[0]
    wide[...] = b_ref[...].astype(F32)
    for t in range(ROWS):
        for n in range(SLOTS):
            piece = wide[:, t * SLOTS + n, :].astype(BF16)
            flat[pl.ds(n * row_count, row_count), pl.ds(t * LANES, LANES)] = piece
    for n in range(SLOTS):
        for k in range(row_count):
            block = wide[k, pl.ds(n, ROWS, stride=SLOTS), :].astype(BF16)
            own[pl.ds((n * row_count + k) * ROWS, ROWS), :] = block
    sums[...] = jnp.zeros_like(sums)


def flatten(b_rows):
    vmem_spec = pl.BlockSpec(memory_space=VMEM)
    row_count = b_rows.shape[0]
    return pl.pallas_call(
        flatten_kernel,
        out_shape=(
            jax.ShapeDtypeStruct((row_count * SLOTS, BS * BS), BF16),
            jax.ShapeDtypeStruct((row_count * SLOTS * ROWS, LANES), BF16),
            jax.ShapeDtypeStruct(b_rows.shape, F32),
        ),
        in_specs=[vmem_spec],
        out_specs=(vmem_spec,) * 3,
        scratch_shapes=[VMEM(b_rows.shape, F32)],
        compiler_params=pltpu.CompilerParams(vmem_limit_bytes=24 << 20),
        cost_estimate=pl.CostEstimate(flops=1 << 20, bytes_accessed=8 << 20, transcendentals=0),
        name="flatten",
    )(b_rows)


def iota(shape, axis):
    return lax.broadcasted_iota(I32, shape, axis)


def along_lanes(left, right):
    return lax.dot_general(
        left.astype(BF16), right.astype(BF16), (((1,), (1,)), ((), ())), preferred_element_type=F32
    )


def turn_to_columns(rows, first, count):
    pick = (iota((count, LANES), 0) + first == iota((count, LANES), 1)).astype(BF16)
    return lax.dot_general(
        pick,
        rows.astype(F32).astype(BF16),
        (((1,), (1,)), ((), ())),
        preferred_element_type=F32,
    )


def matches(receiver, offered, holder, cols, row_count, first_slot, a_slots):
    turned = 2 * (holder ^ lax.axis_index("col"))
    rows = [receiver[pl.ds(turned, 1), :], receiver[pl.ds(turned + 1, 1), :]]
    rows += [receiver[pl.ds(2 * cols, SLOTS), :]]
    rows = jnp.concatenate(rows + [jnp.zeros((8 - 2 - SLOTS, LANES), I32)], axis=0)
    kept_columns = turn_to_columns(rows, 0, row_count)
    if isinstance(first_slot, int) and first_slot == 0 and a_slots == row_count:
        slot_columns = kept_columns
    else:
        slot_columns = turn_to_columns(rows, first_slot, a_slots)
    wanted = offered.astype(F32)
    kept = jnp.zeros((row_count, LANES), F32)
    which = jnp.zeros((row_count, LANES), F32)
    for m in range(SLOTS):
        column = kept_columns[:, 2 + m : 3 + m]
        equal = (column == wanted) & (wanted >= 0)
        kept = jnp.where(equal, 1.0, kept)
        which = jnp.where(equal, float(m), which)
    a_rows = slot_columns[:, 0:1]
    a_columns = slot_columns[:, 1:2]
    shape = (a_slots, row_count)
    by_row = (a_rows == iota(shape, 1).astype(F32)).astype(BF16)
    by_column = a_columns == (iota((a_slots, LANES), 1) % row_count).astype(F32)
    both = jnp.concatenate([kept, which], axis=1).astype(BF16)
    both = jnp.dot(by_row, both, preferred_element_type=F32)
    pairs = jnp.where(by_column & (both[:, :LANES] > 0.5), 1.0, 0.0)
    return pairs, both[:, LANES:], a_rows


def places(needed):
    before = (iota((LANES, LANES), 0) < iota((LANES, LANES), 1)).astype(BF16)
    many = jnp.broadcast_to(needed, (8, LANES)).astype(BF16)
    return jnp.dot(many, before, preferred_element_type=F32)[0:1]


def pack_kernel(first, peers, cols, a_slots, row_count, *refs):
    refs = list(refs)
    base = 0 if first else refs.pop(0)[0]
    grid_row = lax.axis_index("row")
    told = [refs[0].at[grid_row ^ d] for d in range(peers)]
    flat = refs[1]
    outs = refs[2 : 1 + peers]
    picks, packed = refs[1 + peers :]
    per_col = peers // cols
    offered = offers(told[0], cols, row_count)
    first_slot = grid_row % per_col * a_slots if per_col > 1 else 0
    for d in range(1, peers):
        pairs, _, _ = matches(
            told[d], offered, grid_row // per_col, cols, row_count, first_slot, a_slots
        )
        needed = jnp.max(pairs, axis=0, keepdims=True)
        place = jnp.where(needed > 0.5, places(needed), -1.0).astype(I32)
        pick = (place == iota((CAPACITY, LANES), 0) + base).astype(BF16)
        picks[pl.ds((d - 1) * CAPACITY, CAPACITY), :] = pick
    pick = picks[...][:, : flat.shape[0]]
    for t in range(0, ROWS, 2):
        both = flat[:, pl.ds(t * LANES, 2 * LANES)]
        both = jnp.dot(pick, both, preferred_element_type=F32)
        packed[:, t, :] = both[:, :LANES]
        packed[:, t + 1, :] = both[:, LANES:]
    for d in range(1, peers):
        out = outs[d - 1]
        for x in range(CAPACITY):
            out[pl.ds(x * ROWS, ROWS), :] = packed[(d - 1) * CAPACITY + x].astype(BF16)


def pack(base, told, flat, cols, row_count, a_slots):
    first = base is None
    peers = told.shape[0]
    smem_spec = pl.BlockSpec(memory_space=SMEM)
    vmem_spec = pl.BlockSpec(memory_space=VMEM)
    given = [] if first else [base]
    return pl.pallas_call(
        functools.partial(pack_kernel, first, peers, cols, a_slots, row_count),
        out_shape=[jax.ShapeDtypeStruct((CAPACITY * ROWS, LANES), BF16)] * (peers - 1),
        in_specs=[smem_spec] * len(given) + [vmem_spec] * 2,
        out_specs=[vmem_spec] * (peers - 1),
        scratch_shapes=[
            VMEM(((peers - 1) * CAPACITY, LANES), BF16),
            VMEM(((peers - 1) * CAPACITY, ROWS, LANES), F32),
        ],
        compiler_params=pltpu.CompilerParams(vmem_limit_bytes=32 << 20),
        cost_estimate=pl.CostEstimate(flops=1 << 20, bytes_accessed=4 << 20, transcendentals=0),
        name="pack",
    )(*given, told, flat)


def list_kernel(cols, a_slots, row_count, peers, *refs):
    grid_row = lax.axis_index("row")
    told, items = [refs[0].at[grid_row ^ d] for d in range(peers)], refs[1]
    grid_col = lax.axis_index("col")
    per_col = peers // cols
    blocks = row_count * SLOTS
    lane = iota((1, LANES), 1)
    spot = iota((blocks, LANES), 0)
    before = (iota((LANES, LANES), 0) < iota((LANES, LANES), 1)).astype(BF16)
    below = (iota((blocks, blocks), 1) < iota((blocks, blocks), 0)).astype(BF16)
    same_slot = spot // row_count == iota((blocks, LANES), 1) // a_slots
    for d in range(peers):
        group = grid_row ^ d
        holder = group // per_col
        first_slot = group % per_col * a_slots if per_col > 1 else 0
        at = 2 * (holder ^ grid_col)
        slots = []
        for row in (told[0][pl.ds(at, 1), :], told[0][pl.ds(at + 1, 1), :]):
            if per_col > 1:
                row = pltpu.roll(row, (LANES - first_slot) % LANES, 1)
            spread = row
            for n in range(1, SLOTS):
                spread = jnp.where(lane // a_slots == n, pltpu.roll(row, n * a_slots, 1), spread)
            slots.append(jnp.where(lane < SLOTS * a_slots, spread, -1))
        a_rows, a_columns = slots
        offered = turn_to_columns(
            jnp.broadcast_to(offers(told[d], cols, row_count), (8, LANES)), 0, blocks
        )[:, 0:1]
        kept = jnp.zeros((blocks, LANES), F32)
        which = jnp.zeros((blocks, LANES), F32)
        for m in range(SLOTS):
            column = told[0][pl.ds(2 * cols + m, 1), :].astype(F32)
            equal = (column == offered) & (offered >= 0)
            kept = jnp.where(equal, 1.0, kept)
            which = jnp.where(equal, float(m), which)
        by_row = (a_rows == iota((row_count, LANES), 0)).astype(BF16)
        both = jnp.concatenate([kept, which], axis=0)[:, :row_count].astype(BF16)
        both = jnp.dot(both, by_row, preferred_element_type=F32)
        meets = (both[:blocks] > 0.5) & (a_columns == spot % row_count) & same_slot
        pairs = jnp.where(meets, 1.0, 0.0)
        if d == 0:
            place = spot.astype(F32)
        else:
            needed = jnp.max(pairs, axis=1, keepdims=True)
            many = jnp.broadcast_to(needed, (blocks, LANES)).astype(BF16)
            place = jnp.dot(below, many, preferred_element_type=F32)
        hit = jnp.sum(pairs, axis=0, keepdims=True)
        place = jnp.sum(pairs * place, axis=0, keepdims=True)
        out = jnp.sum(pairs * both[blocks:], axis=0, keepdims=True)
        out = out + a_rows.astype(F32) * SLOTS * hit
        rank = jnp.dot(
            jnp.broadcast_to(hit, (8, LANES)).astype(BF16), before, preferred_element_type=F32
        )[0:1]
        rank = jnp.where(hit > 0.5, rank, -1.0).astype(I32)
        chosen = rank == iota((LANES, LANES), 0)
        zero = jnp.zeros((1, LANES), F32)
        values = [(lane % a_slots).astype(F32) * hit, out, place] + [zero] * 5
        listed = along_lanes(jnp.concatenate(values, axis=0), chosen.astype(F32)).astype(I32)
        a_slot = holder * per_col * a_slots + first_slot + listed[0:1]
        word = (a_slot * 64 + listed[1:2]) * 64 + listed[2:3]
        total = jnp.sum(hit, axis=1, keepdims=True).astype(I32)
        items[pl.ds(d, 1), :] = jnp.where(lane == LANES - 1, total, word)


def work_list(told, cols, row_count, a_slots):
    peers = told.shape[0]
    return pl.pallas_call(
        functools.partial(list_kernel, cols, a_slots, row_count, peers),
        out_shape=jax.ShapeDtypeStruct((-(-peers // 8) * 8, LANES), I32),
        in_specs=[pl.BlockSpec(memory_space=VMEM)],
        out_specs=pl.BlockSpec(memory_space=VMEM),
        cost_estimate=pl.CostEstimate(flops=1 << 10, bytes_accessed=1 << 10, transcendentals=0),
        name="work_list",
    )(told)


def rounds_kernel(cols, a_slots, row_count, peers, told, rounds):
    per_col = peers // cols

    def one_pair(receiver, d, most):
        group = sender = receiver ^ d
        first_slot = group % per_col * a_slots if per_col > 1 else 0
        pairs, _, _ = matches(
            told.at[receiver],
            offers(told.at[sender], cols, row_count),
            group // per_col,
            cols,
            row_count,
            first_slot,
            a_slots,
        )
        needed = jnp.max(pairs, axis=0, keepdims=True)
        return jnp.maximum(most, jnp.sum(needed, axis=1, keepdims=True))

    most = jnp.zeros((1, 1), F32)
    if peers <= 4:
        for receiver in range(peers):
            for d in range(1, peers):
                most = one_pair(receiver, d, most)
    else:

        def step(at, most):
            return one_pair(at // (peers - 1), at % (peers - 1) + 1, most)

        most = lax.fori_loop(0, peers * (peers - 1), step, most)
    rounds[0] = (jnp.max(most).astype(I32) + CAPACITY - 1) // CAPACITY


def count_rounds(told, cols, row_count, a_slots):
    peers = told.shape[0]
    return pl.pallas_call(
        functools.partial(rounds_kernel, cols, a_slots, row_count, peers),
        out_shape=jax.ShapeDtypeStruct((1,), I32),
        in_specs=[pl.BlockSpec(memory_space=VMEM)],
        out_specs=pl.BlockSpec(memory_space=SMEM),
        cost_estimate=pl.CostEstimate(flops=1 << 10, bytes_accessed=1 << 10, transcendentals=0),
        name="count_rounds",
    )(told)


def add_products(items, a_ref, peer_refs, sums, window=None):
    low = iota((ROWS, LANES), 1) < BS
    nothing = jnp.zeros((ROWS, LANES), BF16)

    def add_one(word, used, b_ref):
        word = jnp.where(used, word, 0)
        place = word & 63
        target = (word >> 6) & 63
        if window is not None:
            place = place - window
            used = used & (place >= 0) & (place < CAPACITY)
            place = jnp.where(used, place, 0)
        a_at = pl.multiple_of((word >> 12) * ROWS, ROWS)
        b_at = pl.multiple_of(place * ROWS, ROWS)
        block = jnp.where(used, b_ref[pl.ds(b_at, ROWS), :], nothing)
        turned = jnp.concatenate([block[:, BS:], block[:, :BS]], axis=1)
        right = jnp.concatenate(
            [
                jnp.where(low, block, nothing),
                jnp.where(low, turned, nothing),
                jnp.where(low, nothing, turned),
                jnp.where(low, nothing, block),
            ],
            axis=0,
        )
        term = jnp.dot(a_ref[pl.ds(a_at, ROWS), :], right, preferred_element_type=F32)
        sums[target // SLOTS, pl.ds(target % SLOTS, ROWS, stride=SLOTS), :] += term

    for at in range(0, len(peer_refs), 3):
        chosen = peer_refs[at : at + 3]
        totals = [items[d, LANES - 1] for d, _ in chosen]
        longest = functools.reduce(jnp.maximum, totals)
        width = UNROLL if len(chosen) < 3 else UNROLL - 1

        def some_items(step, carry, chosen=chosen, totals=totals, width=width):
            for u in range(width):
                for (d, b_ref), total in zip(chosen, totals):
                    y = step * width + u
                    add_one(items[d, y], y < total, b_ref)
            return carry

        lax.fori_loop(0, (longest + width - 1) // width, some_items, 0)


def stage_kernel(cols, *refs):
    a_refs, own, items = refs[:cols], refs[cols], refs[cols + 1]
    a_out, sums, a_wide = refs[cols + 3 :]
    source = iota((LANES, LANES), 0)
    target = iota((LANES, LANES), 1)
    wanted = (target // BS) * BS + 2 * (target % ROWS) + (target // ROWS) % 2
    order = (source == wanted).astype(BF16)
    slots = a_refs[0].shape[1]
    grid_col = lax.axis_index("col")
    for t in range(ROWS):
        pieces = [ref[0, :, pl.ds(t * LANES, LANES)] for ref in a_refs]
        done = jnp.dot(jnp.concatenate(pieces, axis=0), order, preferred_element_type=F32)
        a_wide[:, t, :] = done
    for h in range(cols):
        first = (grid_col ^ h) * slots
        for s in range(slots):
            at = pl.multiple_of((first + s) * ROWS, ROWS)
            a_out[pl.ds(at, ROWS), :] = a_wide[h * slots + s].astype(BF16)
    add_products(items, a_out, [(0, own)], sums)


def stage(a_parts, own, sums, items):
    cols, slots = len(a_parts), a_parts[0].shape[1]
    vmem_spec = pl.BlockSpec(memory_space=VMEM)
    smem_spec = pl.BlockSpec(memory_space=SMEM)
    return pl.pallas_call(
        functools.partial(stage_kernel, cols),
        out_shape=(
            jax.ShapeDtypeStruct((cols * slots * ROWS, LANES), BF16),
            jax.ShapeDtypeStruct(sums.shape, F32),
        ),
        in_specs=[vmem_spec] * (cols + 1) + [smem_spec] + [vmem_spec],
        out_specs=(vmem_spec,) * 2,
        input_output_aliases={cols + 2: 1},
        scratch_shapes=[VMEM((cols * slots, ROWS, LANES), F32)],
        compiler_params=pltpu.CompilerParams(vmem_limit_bytes=40 << 20),
        cost_estimate=pl.CostEstimate(flops=1 << 10, bytes_accessed=1 << 10, transcendentals=0),
        name="stage",
    )(*a_parts, own, items, sums)


def multiply_kernel(first, peers, *refs):
    refs = list(refs)
    base = 0 if first else refs.pop(0)[0]
    items, a_ref = refs[:2]
    b_refs = refs[3 : 2 + peers][::-1]
    sums, out, sem = refs[2 + peers :]
    add_products(items, a_ref, list(enumerate(b_refs, 1)), sums, window=base)
    copy = pltpu.make_async_copy(sums, out, sem.at[0])
    copy.start()
    copy.wait()


def multiply(base, items, a_ready, sums, b_parts):
    first = base is None
    peers = len(b_parts) + 1
    smem_spec = pl.BlockSpec(memory_space=SMEM)
    vmem_spec = pl.BlockSpec(memory_space=VMEM)
    given = [] if first else [base]
    return pl.pallas_call(
        functools.partial(multiply_kernel, first, peers),
        out_shape=[jax.ShapeDtypeStruct(sums.shape, F32)] * 2,
        in_specs=[smem_spec] * (len(given) + 1) + [vmem_spec] * (1 + peers),
        out_specs=[vmem_spec, pl.BlockSpec(memory_space=pl.ANY)],
        input_output_aliases={len(given) + 2: 0},
        scratch_shapes=[pltpu.SemaphoreType.DMA((1,))],
        compiler_params=pltpu.CompilerParams(vmem_limit_bytes=32 << 20),
        cost_estimate=pl.CostEstimate(flops=1 << 26, bytes_accessed=4 << 20, transcendentals=0),
        name="multiply",
    )(*given, items, a_ready, sums, *b_parts[::-1])


def shards(a_blocks, a_index, b_blocks, b_cols, c_cols):
    rows = lax.axis_size("row")
    cols = lax.axis_size("col")
    a_slots = a_blocks.shape[1] * cols // rows
    row_count = b_blocks.shape[0]

    def send_rows(parts):
        far_first = range(len(parts), 0, -1)
        return [exchanged(parts[d - 1], "row", d) for d in far_first][::-1]

    index_parts = [a_index] + [exchanged(a_index, "col", h) for h in range(1, cols)]
    told = describe(index_parts, b_cols.T, c_cols.T)
    a_parts = [exchanged(a_blocks, "col", h) for h in range(1, cols)]
    told, a_parts[0] = lax.optimization_barrier((told, a_parts[0]))
    told = jnp.broadcast_to(told[None], (rows,) + told.shape)
    told = lax.all_to_all(told, "row", 0, 0)
    flat, own, sums = flatten(seen_by_rows(b_blocks))
    flat, *a_parts = lax.optimization_barrier((flat, *a_parts))
    packed = pack(None, told, flat, cols, row_count, a_slots)
    arrived = send_rows(packed)
    told_late = lax.optimization_barrier((told, packed[0]))[0]
    items = work_list(told_late, cols, row_count, a_slots)
    rounds = count_rounds(told_late, cols, row_count, a_slots)
    a_ready, sums = stage([a_blocks] + a_parts, own, sums, items)
    sums, out = multiply(None, items, a_ready, sums, arrived)

    def more(state):
        return state[0] < rounds[0]

    def one_round(state):
        at, sums, _ = state
        base = jnp.reshape(at * CAPACITY, (1,))
        arrived = send_rows(pack(base, told, flat, cols, row_count, a_slots))
        return at + 1, *multiply(base, items, a_ready, sums, arrived)

    return seen_by_blocks(lax.while_loop(more, one_round, (jnp.int32(1), sums, out))[2])


def solution(mesh):
    return jax.shard_map(
        shards,
        mesh=mesh,
        in_specs=(
            P(("sys", "row"), "col", None),
            P(None, ("sys", "row"), "col"),
            P(("sys", "row"), "col", None),
            P(("sys", "row"), "col"),
            P(("sys", "row"), "col"),
        ),
        out_specs=P(("sys", "row"), "col", None),
        check_vma=False,
    )
```

```python
import functools

import jax
import jax.numpy as jnp
from jax import lax
from jax.experimental import pallas as pl
from jax.experimental.layout import Layout, with_layout_constraint
from jax.experimental.pallas import tpu as pltpu
from jax.sharding import PartitionSpec as P

BS = 64
LANES = 128
ROWS = BS * BS // LANES
CAPACITY = 16
UNROLL = 4
SLOTS = 4
VMEM = pltpu.VMEM
SMEM = pltpu.SMEM
BF16 = jnp.bfloat16
F32 = jnp.float32
I32 = jnp.int32


def exchanged(block, axis, distance):
    size = lax.axis_size(axis)
    return lax.ppermute(block, axis, [(i, i ^ distance) for i in range(size)])


def seen_by_rows(blocks):
    count = blocks.shape[0]
    parted = blocks.reshape(count, SLOTS, ROWS, LANES)
    parted = with_layout_constraint(parted, Layout(major_to_minor=(0, 2, 1, 3)))
    return parted.transpose(0, 2, 1, 3).reshape(count, ROWS * SLOTS, LANES)


def seen_by_blocks(rows):
    count = rows.shape[0]
    parted = rows.reshape(count, ROWS, SLOTS, LANES).transpose(0, 2, 1, 3)
    parted = with_layout_constraint(parted, Layout(major_to_minor=(0, 2, 1, 3)))
    return parted.reshape(count, SLOTS, BS * BS)


def describe(a_parts, b_cols, c_cols):
    cols = len(a_parts)
    total = -(-(2 * cols + 2 * SLOTS) // 8) * 8

    def placed(part, at):
        after = (total - at - part.shape[0], LANES - part.shape[1])
        return jnp.pad(part, ((at, after[0]), (0, after[1])), constant_values=-1)

    own = jnp.maximum(placed(c_cols, 2 * cols), placed(b_cols, 2 * cols + SLOTS))
    told = lax.optimization_barrier(jnp.maximum(own, placed(a_parts[0][:, 0, :], 0)))
    for h in range(1, cols):
        told = jnp.maximum(told, placed(a_parts[h][:, 0, :], 2 * h))
    return told


def offers(told, cols, row_count):
    start = 2 * cols + SLOTS
    rows = told[pl.ds(start, SLOTS), :]
    lane = iota((1, LANES), 1)
    result = rows[0:1]
    for n in range(1, SLOTS):
        moved = pltpu.roll(rows, n * row_count, 1)[n : n + 1]
        result = jnp.where(lane // row_count == n, moved, result)
    return result


def flatten_kernel(b_ref, flat, own, sums, wide):
    row_count = b_ref.shape[0]
    wide[...] = b_ref[...].astype(F32)
    for t in range(ROWS):
        for n in range(SLOTS):
            piece = wide[:, t * SLOTS + n, :].astype(BF16)
            flat[pl.ds(n * row_count, row_count), pl.ds(t * LANES, LANES)] = piece
    for n in range(SLOTS):
        for k in range(row_count):
            block = wide[k, pl.ds(n, ROWS, stride=SLOTS), :].astype(BF16)
            own[pl.ds((n * row_count + k) * ROWS, ROWS), :] = block
    sums[...] = jnp.zeros_like(sums)


def flatten(b_rows):
    vmem_spec = pl.BlockSpec(memory_space=VMEM)
    row_count = b_rows.shape[0]
    return pl.pallas_call(
        flatten_kernel,
        out_shape=(
            jax.ShapeDtypeStruct((row_count * SLOTS, BS * BS), BF16),
            jax.ShapeDtypeStruct((row_count * SLOTS * ROWS, LANES), BF16),
            jax.ShapeDtypeStruct(b_rows.shape, F32),
        ),
        in_specs=[vmem_spec],
        out_specs=(vmem_spec,) * 3,
        scratch_shapes=[VMEM(b_rows.shape, F32)],
        compiler_params=pltpu.CompilerParams(vmem_limit_bytes=24 << 20),
        cost_estimate=pl.CostEstimate(flops=1 << 20, bytes_accessed=8 << 20, transcendentals=0),
        name="flatten",
    )(b_rows)


def iota(shape, axis):
    return lax.broadcasted_iota(I32, shape, axis)


def along_lanes(left, right):
    return lax.dot_general(
        left.astype(BF16), right.astype(BF16), (((1,), (1,)), ((), ())), preferred_element_type=F32
    )


def turn_to_columns(rows, first, count):
    pick = (iota((count, LANES), 0) + first == iota((count, LANES), 1)).astype(BF16)
    return lax.dot_general(
        pick,
        rows.astype(F32).astype(BF16),
        (((1,), (1,)), ((), ())),
        preferred_element_type=F32,
    )


def matches(receiver, offered, holder, cols, row_count, first_slot, a_slots):
    turned = 2 * (holder ^ lax.axis_index("col"))
    rows = [receiver[pl.ds(turned, 1), :], receiver[pl.ds(turned + 1, 1), :]]
    rows += [receiver[pl.ds(2 * cols, SLOTS), :]]
    rows = jnp.concatenate(rows + [jnp.zeros((8 - 2 - SLOTS, LANES), I32)], axis=0)
    kept_columns = turn_to_columns(rows, 0, row_count)
    if isinstance(first_slot, int) and first_slot == 0 and a_slots == row_count:
        slot_columns = kept_columns
    else:
        slot_columns = turn_to_columns(rows, first_slot, a_slots)
    wanted = offered.astype(F32)
    kept = jnp.zeros((row_count, LANES), F32)
    which = jnp.zeros((row_count, LANES), F32)
    for m in range(SLOTS):
        column = kept_columns[:, 2 + m : 3 + m]
        equal = (column == wanted) & (wanted >= 0)
        kept = jnp.where(equal, 1.0, kept)
        which = jnp.where(equal, float(m), which)
    a_rows = slot_columns[:, 0:1]
    a_columns = slot_columns[:, 1:2]
    shape = (a_slots, row_count)
    by_row = (a_rows == iota(shape, 1).astype(F32)).astype(BF16)
    by_column = a_columns == (iota((a_slots, LANES), 1) % row_count).astype(F32)
    both = jnp.concatenate([kept, which], axis=1).astype(BF16)
    both = jnp.dot(by_row, both, preferred_element_type=F32)
    pairs = jnp.where(by_column & (both[:, :LANES] > 0.5), 1.0, 0.0)
    return pairs, both[:, LANES:], a_rows


def places(needed):
    before = (iota((LANES, LANES), 0) < iota((LANES, LANES), 1)).astype(BF16)
    many = jnp.broadcast_to(needed, (8, LANES)).astype(BF16)
    return jnp.dot(many, before, preferred_element_type=F32)[0:1]


def pack_kernel(first, peers, cols, a_slots, row_count, *refs):
    refs = list(refs)
    base = 0 if first else refs.pop(0)[0]
    told = refs[:peers]
    flat = refs[peers]
    outs = refs[peers + 1 : 2 * peers]
    picks, packed = refs[2 * peers :]
    grid_row = lax.axis_index("row")
    per_col = peers // cols
    offered = offers(told[0], cols, row_count)
    first_slot = grid_row % per_col * a_slots if per_col > 1 else 0
    for d in range(1, peers):
        pairs, _, _ = matches(
            told[d], offered, grid_row // per_col, cols, row_count, first_slot, a_slots
        )
        needed = jnp.max(pairs, axis=0, keepdims=True)
        place = jnp.where(needed > 0.5, places(needed), -1.0).astype(I32)
        pick = (place == iota((CAPACITY, LANES), 0) + base).astype(BF16)
        picks[pl.ds((d - 1) * CAPACITY, CAPACITY), :] = pick
    pick = picks[...][:, : flat.shape[0]]
    for t in range(0, ROWS, 2):
        both = flat[:, pl.ds(t * LANES, 2 * LANES)]
        both = jnp.dot(pick, both, preferred_element_type=F32)
        packed[:, t, :] = both[:, :LANES]
        packed[:, t + 1, :] = both[:, LANES:]
    for d in range(1, peers):
        out = outs[d - 1]
        for x in range(CAPACITY):
            out[pl.ds(x * ROWS, ROWS), :] = packed[(d - 1) * CAPACITY + x].astype(BF16)


def pack(base, told, flat, cols, row_count, a_slots):
    first = base is None
    peers = len(told)
    smem_spec = pl.BlockSpec(memory_space=SMEM)
    vmem_spec = pl.BlockSpec(memory_space=VMEM)
    given = [] if first else [base]
    return pl.pallas_call(
        functools.partial(pack_kernel, first, peers, cols, a_slots, row_count),
        out_shape=[jax.ShapeDtypeStruct((CAPACITY * ROWS, LANES), BF16)] * (peers - 1),
        in_specs=[smem_spec] * len(given) + [vmem_spec] * (peers + 1),
        out_specs=[vmem_spec] * (peers - 1),
        scratch_shapes=[
            VMEM(((peers - 1) * CAPACITY, LANES), BF16),
            VMEM(((peers - 1) * CAPACITY, ROWS, LANES), F32),
        ],
        compiler_params=pltpu.CompilerParams(vmem_limit_bytes=32 << 20),
        cost_estimate=pl.CostEstimate(flops=1 << 20, bytes_accessed=4 << 20, transcendentals=0),
        name="pack",
    )(*given, *told, flat)


def list_kernel(cols, a_slots, row_count, peers, *refs):
    told, items = refs[:peers], refs[peers]
    grid_row = lax.axis_index("row")
    grid_col = lax.axis_index("col")
    per_col = peers // cols
    blocks = row_count * SLOTS
    lane = iota((1, LANES), 1)
    spot = iota((blocks, LANES), 0)
    before = (iota((LANES, LANES), 0) < iota((LANES, LANES), 1)).astype(BF16)
    below = (iota((blocks, blocks), 1) < iota((blocks, blocks), 0)).astype(BF16)
    same_slot = spot // row_count == iota((blocks, LANES), 1) // a_slots
    for d in range(peers):
        group = grid_row ^ d
        holder = group // per_col
        first_slot = group % per_col * a_slots if per_col > 1 else 0
        at = 2 * (holder ^ grid_col)
        slots = []
        for row in (told[0][pl.ds(at, 1), :], told[0][pl.ds(at + 1, 1), :]):
            if per_col > 1:
                row = pltpu.roll(row, (LANES - first_slot) % LANES, 1)
            spread = row
            for n in range(1, SLOTS):
                spread = jnp.where(lane // a_slots == n, pltpu.roll(row, n * a_slots, 1), spread)
            slots.append(jnp.where(lane < SLOTS * a_slots, spread, -1))
        a_rows, a_columns = slots
        offered = turn_to_columns(
            jnp.broadcast_to(offers(told[d], cols, row_count), (8, LANES)), 0, blocks
        )[:, 0:1]
        kept = jnp.zeros((blocks, LANES), F32)
        which = jnp.zeros((blocks, LANES), F32)
        for m in range(SLOTS):
            column = told[0][pl.ds(2 * cols + m, 1), :].astype(F32)
            equal = (column == offered) & (offered >= 0)
            kept = jnp.where(equal, 1.0, kept)
            which = jnp.where(equal, float(m), which)
        by_row = (a_rows == iota((row_count, LANES), 0)).astype(BF16)
        both = jnp.concatenate([kept, which], axis=0)[:, :row_count].astype(BF16)
        both = jnp.dot(both, by_row, preferred_element_type=F32)
        meets = (both[:blocks] > 0.5) & (a_columns == spot % row_count) & same_slot
        pairs = jnp.where(meets, 1.0, 0.0)
        if d == 0:
            place = spot.astype(F32)
        else:
            needed = jnp.max(pairs, axis=1, keepdims=True)
            many = jnp.broadcast_to(needed, (blocks, LANES)).astype(BF16)
            place = jnp.dot(below, many, preferred_element_type=F32)
        hit = jnp.sum(pairs, axis=0, keepdims=True)
        place = jnp.sum(pairs * place, axis=0, keepdims=True)
        out = jnp.sum(pairs * both[blocks:], axis=0, keepdims=True)
        out = out + a_rows.astype(F32) * SLOTS * hit
        rank = jnp.dot(
            jnp.broadcast_to(hit, (8, LANES)).astype(BF16), before, preferred_element_type=F32
        )[0:1]
        rank = jnp.where(hit > 0.5, rank, -1.0).astype(I32)
        chosen = rank == iota((LANES, LANES), 0)
        zero = jnp.zeros((1, LANES), F32)
        values = [(lane % a_slots).astype(F32) * hit, out, place] + [zero] * 5
        listed = along_lanes(jnp.concatenate(values, axis=0), chosen.astype(F32)).astype(I32)
        a_slot = holder * per_col * a_slots + first_slot + listed[0:1]
        word = (a_slot * 64 + listed[1:2]) * 64 + listed[2:3]
        total = jnp.sum(hit, axis=1, keepdims=True).astype(I32)
        items[pl.ds(d, 1), :] = jnp.where(lane == LANES - 1, total, word)


def work_list(told, cols, row_count, a_slots):
    peers = len(told)
    return pl.pallas_call(
        functools.partial(list_kernel, cols, a_slots, row_count, peers),
        out_shape=jax.ShapeDtypeStruct((-(-peers // 8) * 8, LANES), I32),
        in_specs=[pl.BlockSpec(memory_space=VMEM)] * peers,
        out_specs=pl.BlockSpec(memory_space=VMEM),
        cost_estimate=pl.CostEstimate(flops=1 << 10, bytes_accessed=1 << 10, transcendentals=0),
        name="work_list",
    )(*told)


def rounds_kernel(cols, a_slots, row_count, peers, *refs):
    told_refs, rounds, told = refs[:peers], refs[peers], refs[peers + 1]
    for d, ref in enumerate(told_refs):
        told[d, :, :] = ref[...]
    grid_row = lax.axis_index("row")
    per_col = peers // cols

    def one_pair(receiver, d, most):
        group = grid_row ^ receiver ^ d
        sender = receiver ^ d
        first_slot = group % per_col * a_slots if per_col > 1 else 0
        pairs, _, _ = matches(
            told.at[receiver],
            offers(told.at[sender], cols, row_count),
            group // per_col,
            cols,
            row_count,
            first_slot,
            a_slots,
        )
        needed = jnp.max(pairs, axis=0, keepdims=True)
        return jnp.maximum(most, jnp.sum(needed, axis=1, keepdims=True))

    most = jnp.zeros((1, 1), F32)
    if peers <= 4:
        for receiver in range(peers):
            for d in range(1, peers):
                most = one_pair(receiver, d, most)
    else:

        def step(at, most):
            return one_pair(at // (peers - 1), at % (peers - 1) + 1, most)

        most = lax.fori_loop(0, peers * (peers - 1), step, most)
    rounds[0] = (jnp.max(most).astype(I32) + CAPACITY - 1) // CAPACITY


def count_rounds(told, cols, row_count, a_slots):
    peers = len(told)
    return pl.pallas_call(
        functools.partial(rounds_kernel, cols, a_slots, row_count, peers),
        out_shape=jax.ShapeDtypeStruct((1,), I32),
        in_specs=[pl.BlockSpec(memory_space=VMEM)] * peers,
        out_specs=pl.BlockSpec(memory_space=SMEM),
        scratch_shapes=[VMEM((peers,) + told[0].shape, I32)],
        cost_estimate=pl.CostEstimate(flops=1 << 10, bytes_accessed=1 << 10, transcendentals=0),
        name="count_rounds",
    )(*told)


def add_products(items, a_ref, peer_refs, sums, window=None):
    low = iota((ROWS, LANES), 1) < BS
    nothing = jnp.zeros((ROWS, LANES), BF16)

    def add_one(word, used, b_ref):
        word = jnp.where(used, word, 0)
        place = word & 63
        target = (word >> 6) & 63
        if window is not None:
            place = place - window
            used = used & (place >= 0) & (place < CAPACITY)
            place = jnp.where(used, place, 0)
        a_at = pl.multiple_of((word >> 12) * ROWS, ROWS)
        b_at = pl.multiple_of(place * ROWS, ROWS)
        block = jnp.where(used, b_ref[pl.ds(b_at, ROWS), :], nothing)
        turned = jnp.concatenate([block[:, BS:], block[:, :BS]], axis=1)
        right = jnp.concatenate(
            [
                jnp.where(low, block, nothing),
                jnp.where(low, turned, nothing),
                jnp.where(low, nothing, turned),
                jnp.where(low, nothing, block),
            ],
            axis=0,
        )
        term = jnp.dot(a_ref[pl.ds(a_at, ROWS), :], right, preferred_element_type=F32)
        sums[target // SLOTS, pl.ds(target % SLOTS, ROWS, stride=SLOTS), :] += term

    for at in range(0, len(peer_refs), 3):
        chosen = peer_refs[at : at + 3]
        totals = [items[d, LANES - 1] for d, _ in chosen]
        longest = functools.reduce(jnp.maximum, totals)
        width = UNROLL if len(chosen) < 3 else UNROLL - 1

        def some_items(step, carry, chosen=chosen, totals=totals, width=width):
            for u in range(width):
                for (d, b_ref), total in zip(chosen, totals):
                    y = step * width + u
                    add_one(items[d, y], y < total, b_ref)
            return carry

        lax.fori_loop(0, (longest + width - 1) // width, some_items, 0)


def stage_kernel(cols, *refs):
    a_refs, own, items = refs[:cols], refs[cols], refs[cols + 1]
    a_out, sums, a_wide = refs[cols + 3 :]
    source = iota((LANES, LANES), 0)
    target = iota((LANES, LANES), 1)
    wanted = (target // BS) * BS + 2 * (target % ROWS) + (target // ROWS) % 2
    order = (source == wanted).astype(BF16)
    slots = a_refs[0].shape[1]
    grid_col = lax.axis_index("col")
    for t in range(ROWS):
        pieces = [ref[0, :, pl.ds(t * LANES, LANES)] for ref in a_refs]
        done = jnp.dot(jnp.concatenate(pieces, axis=0), order, preferred_element_type=F32)
        a_wide[:, t, :] = done
    for h in range(cols):
        first = (grid_col ^ h) * slots
        for s in range(slots):
            at = pl.multiple_of((first + s) * ROWS, ROWS)
            a_out[pl.ds(at, ROWS), :] = a_wide[h * slots + s].astype(BF16)
    add_products(items, a_out, [(0, own)], sums)


def stage(a_parts, own, sums, items):
    cols, slots = len(a_parts), a_parts[0].shape[1]
    vmem_spec = pl.BlockSpec(memory_space=VMEM)
    smem_spec = pl.BlockSpec(memory_space=SMEM)
    return pl.pallas_call(
        functools.partial(stage_kernel, cols),
        out_shape=(
            jax.ShapeDtypeStruct((cols * slots * ROWS, LANES), BF16),
            jax.ShapeDtypeStruct(sums.shape, F32),
        ),
        in_specs=[vmem_spec] * (cols + 1) + [smem_spec] + [vmem_spec],
        out_specs=(vmem_spec,) * 2,
        input_output_aliases={cols + 2: 1},
        scratch_shapes=[VMEM((cols * slots, ROWS, LANES), F32)],
        compiler_params=pltpu.CompilerParams(vmem_limit_bytes=40 << 20),
        cost_estimate=pl.CostEstimate(flops=1 << 10, bytes_accessed=1 << 10, transcendentals=0),
        name="stage",
    )(*a_parts, own, items, sums)


def multiply_kernel(first, peers, *refs):
    refs = list(refs)
    base = 0 if first else refs.pop(0)[0]
    items, a_ref = refs[:2]
    b_refs = refs[3 : 2 + peers][::-1]
    sums, out, sem = refs[2 + peers :]
    add_products(items, a_ref, list(enumerate(b_refs, 1)), sums, window=base)
    copy = pltpu.make_async_copy(sums, out, sem.at[0])
    copy.start()
    copy.wait()


def multiply(base, items, a_ready, sums, b_parts):
    first = base is None
    peers = len(b_parts) + 1
    smem_spec = pl.BlockSpec(memory_space=SMEM)
    vmem_spec = pl.BlockSpec(memory_space=VMEM)
    given = [] if first else [base]
    return pl.pallas_call(
        functools.partial(multiply_kernel, first, peers),
        out_shape=[jax.ShapeDtypeStruct(sums.shape, F32)] * 2,
        in_specs=[smem_spec] * (len(given) + 1) + [vmem_spec] * (1 + peers),
        out_specs=[vmem_spec, pl.BlockSpec(memory_space=pl.ANY)],
        input_output_aliases={len(given) + 2: 0},
        scratch_shapes=[pltpu.SemaphoreType.DMA((1,))],
        compiler_params=pltpu.CompilerParams(vmem_limit_bytes=32 << 20),
        cost_estimate=pl.CostEstimate(flops=1 << 26, bytes_accessed=4 << 20, transcendentals=0),
        name="multiply",
    )(*given, items, a_ready, sums, *b_parts[::-1])


def shards(a_blocks, a_index, b_blocks, b_cols, c_cols):
    rows = lax.axis_size("row")
    cols = lax.axis_size("col")
    a_slots = a_blocks.shape[1] * cols // rows
    row_count = b_blocks.shape[0]

    def send_rows(parts):
        far_first = range(len(parts), 0, -1)
        return [exchanged(parts[d - 1], "row", d) for d in far_first][::-1]

    index_parts = [a_index] + [exchanged(a_index, "col", h) for h in range(1, cols)]
    told = describe(index_parts, b_cols.T, c_cols.T)
    a_far = [exchanged(a_blocks, "col", h) for h in range(2, cols, 2)]
    told = [told] + send_rows([told] * (rows - 1))
    flat, own, sums = flatten(seen_by_rows(b_blocks))
    flat, *a_far = lax.optimization_barrier((flat, *a_far))
    packed = pack(None, told, flat, cols, row_count, a_slots)
    arrived = send_rows(packed)
    told_late, a_late, *a_far = lax.optimization_barrier((told, a_blocks, *a_far, packed[0]))[:-1]
    items = work_list(told_late, cols, row_count, a_slots)
    rounds = jnp.minimum(count_rounds(told_late, cols, row_count, a_slots)[0], LANES)
    a_parts = [a_blocks, exchanged(a_late, "col", 1)]
    for far in a_far:
        a_parts += [far, exchanged(far, "col", 1)]
    a_ready, sums = stage(a_parts, own, sums, items)
    sums, rounds = lax.optimization_barrier((sums, rounds))
    sums, out = multiply(None, items, a_ready, sums, arrived)

    def more(state):
        return state[0] < rounds

    def one_round(state):
        at, sums, _ = state
        base = jnp.reshape(at * CAPACITY, (1,))
        arrived = send_rows(pack(base, told, flat, cols, row_count, a_slots))
        return at + 1, *multiply(base, items, a_ready, sums, arrived)

    return seen_by_blocks(lax.while_loop(more, one_round, (jnp.int32(1), sums, out))[2])


def solution(mesh):
    return jax.shard_map(
        shards,
        mesh=mesh,
        in_specs=(
            P(("sys", "row"), "col", None),
            P(None, ("sys", "row"), "col"),
            P(("sys", "row"), "col", None),
            P(("sys", "row"), "col"),
            P(("sys", "row"), "col"),
        ),
        out_specs=P(("sys", "row"), "col", None),
        check_vma=False,
    )
```

```python
import functools

import jax
import jax.numpy as jnp
from jax import lax
from jax.experimental import pallas as pl
from jax.experimental.layout import Layout, with_layout_constraint
from jax.experimental.pallas import tpu as pltpu
from jax.sharding import PartitionSpec as P

BS = 64
LANES = 128
ROWS = BS * BS // LANES
CAPACITY = 16
UNROLL = 4
SLOTS = 4
VMEM = pltpu.VMEM
SMEM = pltpu.SMEM
BF16 = jnp.bfloat16
F32 = jnp.float32
I32 = jnp.int32


def exchanged(block, axis, distance):
    size = lax.axis_size(axis)
    return lax.ppermute(block, axis, [(i, i ^ distance) for i in range(size)])


def seen_by_rows(blocks):
    count = blocks.shape[0]
    parted = blocks.reshape(count, SLOTS, ROWS, LANES)
    parted = with_layout_constraint(parted, Layout(major_to_minor=(0, 2, 1, 3)))
    return parted.transpose(0, 2, 1, 3).reshape(count, ROWS * SLOTS, LANES)


def seen_by_blocks(rows):
    count = rows.shape[0]
    parted = rows.reshape(count, ROWS, SLOTS, LANES).transpose(0, 2, 1, 3)
    parted = with_layout_constraint(parted, Layout(major_to_minor=(0, 2, 1, 3)))
    return parted.reshape(count, SLOTS, BS * BS)


def describe(a_parts, b_cols, c_cols):
    cols = len(a_parts)
    total = -(-(2 * cols + 2 * SLOTS) // 8) * 8

    def placed(part, at):
        after = (total - at - part.shape[0], LANES - part.shape[1])
        return jnp.pad(part, ((at, after[0]), (0, after[1])), constant_values=-1)

    own = jnp.maximum(placed(c_cols, 2 * cols), placed(b_cols, 2 * cols + SLOTS))
    told = lax.optimization_barrier(jnp.maximum(own, placed(a_parts[0][:, 0, :], 0)))
    for h in range(1, cols):
        told = jnp.maximum(told, placed(a_parts[h][:, 0, :], 2 * h))
    return told


def offers(told, cols, row_count):
    start = 2 * cols + SLOTS
    rows = told[pl.ds(start, SLOTS), :]
    lane = iota((1, LANES), 1)
    result = rows[0:1]
    for n in range(1, SLOTS):
        moved = pltpu.roll(rows, n * row_count, 1)[n : n + 1]
        result = jnp.where(lane // row_count == n, moved, result)
    return result


def flatten_kernel(b_ref, flat, own, sums, wide):
    row_count = b_ref.shape[0]
    wide[...] = b_ref[...].astype(F32)
    for t in range(ROWS):
        for n in range(SLOTS):
            piece = wide[:, t * SLOTS + n, :].astype(BF16)
            flat[pl.ds(n * row_count, row_count), pl.ds(t * LANES, LANES)] = piece
    for n in range(SLOTS):
        for k in range(row_count):
            block = wide[k, pl.ds(n, ROWS, stride=SLOTS), :].astype(BF16)
            own[pl.ds((n * row_count + k) * ROWS, ROWS), :] = block
    sums[...] = jnp.zeros_like(sums)


def flatten(b_rows):
    vmem_spec = pl.BlockSpec(memory_space=VMEM)
    row_count = b_rows.shape[0]
    return pl.pallas_call(
        flatten_kernel,
        out_shape=(
            jax.ShapeDtypeStruct((row_count * SLOTS, BS * BS), BF16),
            jax.ShapeDtypeStruct((row_count * SLOTS * ROWS, LANES), BF16),
            jax.ShapeDtypeStruct(b_rows.shape, F32),
        ),
        in_specs=[vmem_spec],
        out_specs=(vmem_spec,) * 3,
        scratch_shapes=[VMEM(b_rows.shape, F32)],
        compiler_params=pltpu.CompilerParams(vmem_limit_bytes=24 << 20),
        cost_estimate=pl.CostEstimate(flops=1 << 20, bytes_accessed=8 << 20, transcendentals=0),
        name="flatten",
    )(b_rows)


def iota(shape, axis):
    return lax.broadcasted_iota(I32, shape, axis)


def along_lanes(left, right):
    return lax.dot_general(
        left.astype(BF16), right.astype(BF16), (((1,), (1,)), ((), ())), preferred_element_type=F32
    )


def turn_to_columns(rows, first, count):
    pick = (iota((count, LANES), 0) + first == iota((count, LANES), 1)).astype(BF16)
    return lax.dot_general(
        pick,
        rows.astype(F32).astype(BF16),
        (((1,), (1,)), ((), ())),
        preferred_element_type=F32,
    )


def matches(receiver, offered, holder, cols, row_count, first_slot, a_slots):
    turned = 2 * (holder ^ lax.axis_index("col"))
    rows = [receiver[pl.ds(turned, 1), :], receiver[pl.ds(turned + 1, 1), :]]
    rows += [receiver[pl.ds(2 * cols, SLOTS), :]]
    rows = jnp.concatenate(rows + [jnp.zeros((8 - 2 - SLOTS, LANES), I32)], axis=0)
    kept_columns = turn_to_columns(rows, 0, row_count)
    if isinstance(first_slot, int) and first_slot == 0 and a_slots == row_count:
        slot_columns = kept_columns
    else:
        slot_columns = turn_to_columns(rows, first_slot, a_slots)
    wanted = offered.astype(F32)
    kept = jnp.zeros((row_count, LANES), F32)
    which = jnp.zeros((row_count, LANES), F32)
    for m in range(SLOTS):
        column = kept_columns[:, 2 + m : 3 + m]
        equal = (column == wanted) & (wanted >= 0)
        kept = jnp.where(equal, 1.0, kept)
        which = jnp.where(equal, float(m), which)
    a_rows = slot_columns[:, 0:1]
    a_columns = slot_columns[:, 1:2]
    shape = (a_slots, row_count)
    by_row = (a_rows == iota(shape, 1).astype(F32)).astype(BF16)
    by_column = a_columns == (iota((a_slots, LANES), 1) % row_count).astype(F32)
    both = jnp.concatenate([kept, which], axis=1).astype(BF16)
    both = jnp.dot(by_row, both, preferred_element_type=F32)
    pairs = jnp.where(by_column & (both[:, :LANES] > 0.5), 1.0, 0.0)
    return pairs, both[:, LANES:], a_rows


def places(needed):
    before = (iota((LANES, LANES), 0) < iota((LANES, LANES), 1)).astype(BF16)
    many = jnp.broadcast_to(needed, (8, LANES)).astype(BF16)
    return jnp.dot(many, before, preferred_element_type=F32)[0:1]


def pack_kernel(first, peers, cols, a_slots, row_count, *refs):
    refs = list(refs)
    base = 0 if first else refs.pop(0)[0]
    told = refs[:peers]
    flat = refs[peers]
    outs = refs[peers + 1 : 2 * peers]
    picks, packed = refs[2 * peers :]
    grid_row = lax.axis_index("row")
    per_col = peers // cols
    offered = offers(told[0], cols, row_count)
    first_slot = grid_row % per_col * a_slots if per_col > 1 else 0
    for d in range(1, peers):
        pairs, _, _ = matches(
            told[d], offered, grid_row // per_col, cols, row_count, first_slot, a_slots
        )
        needed = jnp.max(pairs, axis=0, keepdims=True)
        place = jnp.where(needed > 0.5, places(needed), -1.0).astype(I32)
        pick = (place == iota((CAPACITY, LANES), 0) + base).astype(BF16)
        picks[pl.ds((d - 1) * CAPACITY, CAPACITY), :] = pick
    pick = picks[...][:, : flat.shape[0]]
    for t in range(0, ROWS, 2):
        both = flat[:, pl.ds(t * LANES, 2 * LANES)]
        both = jnp.dot(pick, both, preferred_element_type=F32)
        packed[:, t, :] = both[:, :LANES]
        packed[:, t + 1, :] = both[:, LANES:]
    for d in range(1, peers):
        out = outs[d - 1]
        for x in range(CAPACITY):
            out[pl.ds(x * ROWS, ROWS), :] = packed[(d - 1) * CAPACITY + x].astype(BF16)


def pack(base, told, flat, cols, row_count, a_slots):
    first = base is None
    peers = len(told)
    smem_spec = pl.BlockSpec(memory_space=SMEM)
    vmem_spec = pl.BlockSpec(memory_space=VMEM)
    given = [] if first else [base]
    return pl.pallas_call(
        functools.partial(pack_kernel, first, peers, cols, a_slots, row_count),
        out_shape=[jax.ShapeDtypeStruct((CAPACITY * ROWS, LANES), BF16)] * (peers - 1),
        in_specs=[smem_spec] * len(given) + [vmem_spec] * (peers + 1),
        out_specs=[vmem_spec] * (peers - 1),
        scratch_shapes=[
            VMEM(((peers - 1) * CAPACITY, LANES), BF16),
            VMEM(((peers - 1) * CAPACITY, ROWS, LANES), F32),
        ],
        compiler_params=pltpu.CompilerParams(vmem_limit_bytes=32 << 20),
        cost_estimate=pl.CostEstimate(flops=1 << 20, bytes_accessed=4 << 20, transcendentals=0),
        name="pack",
    )(*given, *told, flat)


def list_kernel(cols, a_slots, row_count, peers, *refs):
    told, items = refs[:peers], refs[peers]
    grid_row = lax.axis_index("row")
    grid_col = lax.axis_index("col")
    per_col = peers // cols
    blocks = row_count * SLOTS
    lane = iota((1, LANES), 1)
    spot = iota((blocks, LANES), 0)
    before = (iota((LANES, LANES), 0) < iota((LANES, LANES), 1)).astype(BF16)
    below = (iota((blocks, blocks), 1) < iota((blocks, blocks), 0)).astype(BF16)
    same_slot = spot // row_count == iota((blocks, LANES), 1) // a_slots
    for d in range(peers):
        group = grid_row ^ d
        holder = group // per_col
        first_slot = group % per_col * a_slots if per_col > 1 else 0
        at = 2 * (holder ^ grid_col)
        slots = []
        for row in (told[0][pl.ds(at, 1), :], told[0][pl.ds(at + 1, 1), :]):
            if per_col > 1:
                row = pltpu.roll(row, (LANES - first_slot) % LANES, 1)
            spread = row
            for n in range(1, SLOTS):
                spread = jnp.where(lane // a_slots == n, pltpu.roll(row, n * a_slots, 1), spread)
            slots.append(jnp.where(lane < SLOTS * a_slots, spread, -1))
        a_rows, a_columns = slots
        offered = turn_to_columns(
            jnp.broadcast_to(offers(told[d], cols, row_count), (8, LANES)), 0, blocks
        )[:, 0:1]
        kept = jnp.zeros((blocks, LANES), F32)
        which = jnp.zeros((blocks, LANES), F32)
        for m in range(SLOTS):
            column = told[0][pl.ds(2 * cols + m, 1), :].astype(F32)
            equal = (column == offered) & (offered >= 0)
            kept = jnp.where(equal, 1.0, kept)
            which = jnp.where(equal, float(m), which)
        by_row = (a_rows == iota((row_count, LANES), 0)).astype(BF16)
        both = jnp.concatenate([kept, which], axis=0)[:, :row_count].astype(BF16)
        both = jnp.dot(both, by_row, preferred_element_type=F32)
        meets = (both[:blocks] > 0.5) & (a_columns == spot % row_count) & same_slot
        pairs = jnp.where(meets, 1.0, 0.0)
        if d == 0:
            place = spot.astype(F32)
        else:
            needed = jnp.max(pairs, axis=1, keepdims=True)
            many = jnp.broadcast_to(needed, (blocks, LANES)).astype(BF16)
            place = jnp.dot(below, many, preferred_element_type=F32)
        hit = jnp.sum(pairs, axis=0, keepdims=True)
        place = jnp.sum(pairs * place, axis=0, keepdims=True)
        out = jnp.sum(pairs * both[blocks:], axis=0, keepdims=True)
        out = out + a_rows.astype(F32) * SLOTS * hit
        rank = jnp.dot(
            jnp.broadcast_to(hit, (8, LANES)).astype(BF16), before, preferred_element_type=F32
        )[0:1]
        rank = jnp.where(hit > 0.5, rank, -1.0).astype(I32)
        chosen = rank == iota((LANES, LANES), 0)
        zero = jnp.zeros((1, LANES), F32)
        values = [(lane % a_slots).astype(F32) * hit, out, place] + [zero] * 5
        listed = along_lanes(jnp.concatenate(values, axis=0), chosen.astype(F32)).astype(I32)
        a_slot = holder * per_col * a_slots + first_slot + listed[0:1]
        word = (a_slot * 64 + listed[1:2]) * 64 + listed[2:3]
        total = jnp.sum(hit, axis=1, keepdims=True).astype(I32)
        items[pl.ds(d, 1), :] = jnp.where(lane == LANES - 1, total, word)


def work_list(told, cols, row_count, a_slots):
    peers = len(told)
    return pl.pallas_call(
        functools.partial(list_kernel, cols, a_slots, row_count, peers),
        out_shape=jax.ShapeDtypeStruct((-(-peers // 8) * 8, LANES), I32),
        in_specs=[pl.BlockSpec(memory_space=VMEM)] * peers,
        out_specs=pl.BlockSpec(memory_space=VMEM),
        cost_estimate=pl.CostEstimate(flops=1 << 10, bytes_accessed=1 << 10, transcendentals=0),
        name="work_list",
    )(*told)


def rounds_kernel(cols, a_slots, row_count, peers, *refs):
    told_refs, rounds, told = refs[:peers], refs[peers], refs[peers + 1]
    for d, ref in enumerate(told_refs):
        told[d, :, :] = ref[...]
    grid_row = lax.axis_index("row")
    per_col = peers // cols

    def one_pair(receiver, d, most):
        group = grid_row ^ receiver ^ d
        sender = receiver ^ d
        first_slot = group % per_col * a_slots if per_col > 1 else 0
        pairs, _, _ = matches(
            told.at[receiver],
            offers(told.at[sender], cols, row_count),
            group // per_col,
            cols,
            row_count,
            first_slot,
            a_slots,
        )
        needed = jnp.max(pairs, axis=0, keepdims=True)
        return jnp.maximum(most, jnp.sum(needed, axis=1, keepdims=True))

    most = jnp.zeros((1, 1), F32)
    if peers <= 4:
        for receiver in range(peers):
            for d in range(1, peers):
                most = one_pair(receiver, d, most)
    else:

        def step(at, most):
            return one_pair(at // (peers - 1), at % (peers - 1) + 1, most)

        most = lax.fori_loop(0, peers * (peers - 1), step, most)
    rounds[0] = (jnp.max(most).astype(I32) + CAPACITY - 1) // CAPACITY


def count_rounds(told, cols, row_count, a_slots):
    peers = len(told)
    return pl.pallas_call(
        functools.partial(rounds_kernel, cols, a_slots, row_count, peers),
        out_shape=jax.ShapeDtypeStruct((1,), I32),
        in_specs=[pl.BlockSpec(memory_space=VMEM)] * peers,
        out_specs=pl.BlockSpec(memory_space=SMEM),
        scratch_shapes=[VMEM((peers,) + told[0].shape, I32)],
        cost_estimate=pl.CostEstimate(flops=1 << 10, bytes_accessed=1 << 10, transcendentals=0),
        name="count_rounds",
    )(*told)


def add_products(items, a_ref, peer_refs, sums, window=None):
    low = iota((ROWS, LANES), 1) < BS
    nothing = jnp.zeros((ROWS, LANES), BF16)

    def add_one(word, used, b_ref):
        word = jnp.where(used, word, 0)
        place = word & 63
        target = (word >> 6) & 63
        if window is not None:
            place = place - window
            used = used & (place >= 0) & (place < CAPACITY)
            place = jnp.where(used, place, 0)
        a_at = pl.multiple_of((word >> 12) * ROWS, ROWS)
        b_at = pl.multiple_of(place * ROWS, ROWS)
        block = jnp.where(used, b_ref[pl.ds(b_at, ROWS), :], nothing)
        turned = jnp.concatenate([block[:, BS:], block[:, :BS]], axis=1)
        right = jnp.concatenate(
            [
                jnp.where(low, block, nothing),
                jnp.where(low, turned, nothing),
                jnp.where(low, nothing, turned),
                jnp.where(low, nothing, block),
            ],
            axis=0,
        )
        term = jnp.dot(a_ref[pl.ds(a_at, ROWS), :], right, preferred_element_type=F32)
        sums[target // SLOTS, pl.ds(target % SLOTS, ROWS, stride=SLOTS), :] += term

    for at in range(0, len(peer_refs), 3):
        chosen = peer_refs[at : at + 3]
        totals = [items[d, LANES - 1] for d, _ in chosen]
        longest = functools.reduce(jnp.maximum, totals)
        width = UNROLL if len(chosen) < 3 else UNROLL - 1

        def some_items(step, carry, chosen=chosen, totals=totals, width=width):
            for u in range(width):
                for (d, b_ref), total in zip(chosen, totals):
                    y = step * width + u
                    add_one(items[d, y], y < total, b_ref)
            return carry

        lax.fori_loop(0, (longest + width - 1) // width, some_items, 0)


def stage_kernel(cols, *refs):
    a_refs, own, items = refs[:cols], refs[cols], refs[cols + 1]
    a_out, sums, a_wide = refs[cols + 3 :]
    source = iota((LANES, LANES), 0)
    target = iota((LANES, LANES), 1)
    wanted = (target // BS) * BS + 2 * (target % ROWS) + (target // ROWS) % 2
    order = (source == wanted).astype(BF16)
    slots = a_refs[0].shape[1]
    grid_col = lax.axis_index("col")
    for t in range(ROWS):
        pieces = [ref[0, :, pl.ds(t * LANES, LANES)] for ref in a_refs]
        done = jnp.dot(jnp.concatenate(pieces, axis=0), order, preferred_element_type=F32)
        a_wide[:, t, :] = done
    for h in range(cols):
        first = (grid_col ^ h) * slots
        for s in range(slots):
            at = pl.multiple_of((first + s) * ROWS, ROWS)
            a_out[pl.ds(at, ROWS), :] = a_wide[h * slots + s].astype(BF16)
    add_products(items, a_out, [(0, own)], sums)


def stage(a_parts, own, sums, items):
    cols, slots = len(a_parts), a_parts[0].shape[1]
    vmem_spec = pl.BlockSpec(memory_space=VMEM)
    smem_spec = pl.BlockSpec(memory_space=SMEM)
    return pl.pallas_call(
        functools.partial(stage_kernel, cols),
        out_shape=(
            jax.ShapeDtypeStruct((cols * slots * ROWS, LANES), BF16),
            jax.ShapeDtypeStruct(sums.shape, F32),
        ),
        in_specs=[vmem_spec] * (cols + 1) + [smem_spec] + [vmem_spec],
        out_specs=(vmem_spec,) * 2,
        input_output_aliases={cols + 2: 1},
        scratch_shapes=[VMEM((cols * slots, ROWS, LANES), F32)],
        compiler_params=pltpu.CompilerParams(vmem_limit_bytes=40 << 20),
        cost_estimate=pl.CostEstimate(flops=1 << 10, bytes_accessed=1 << 10, transcendentals=0),
        name="stage",
    )(*a_parts, own, items, sums)


def near_kernel(first, chosen, *refs):
    refs = list(refs)
    base = 0 if first else refs.pop(0)[0]
    items, a_ref = refs[:2]
    b_refs, sums = refs[3:-1], refs[-1]
    add_products(items, a_ref, list(zip(chosen, b_refs)), sums, window=base)


def near_products(base, chosen, items, a_ready, sums, b_parts):
    first = base is None
    smem_spec = pl.BlockSpec(memory_space=SMEM)
    vmem_spec = pl.BlockSpec(memory_space=VMEM)
    given = [] if first else [base]
    return pl.pallas_call(
        functools.partial(near_kernel, first, chosen),
        out_shape=jax.ShapeDtypeStruct(sums.shape, F32),
        in_specs=[smem_spec] * (len(given) + 1) + [vmem_spec] * (2 + len(chosen)),
        out_specs=vmem_spec,
        input_output_aliases={len(given) + 2: 0},
        compiler_params=pltpu.CompilerParams(vmem_limit_bytes=32 << 20),
        cost_estimate=pl.CostEstimate(flops=1 << 10, bytes_accessed=1 << 10, transcendentals=0),
        name="near_products",
    )(*given, items, a_ready, sums, *b_parts)


def multiply_kernel(first, chosen, *refs):
    refs = list(refs)
    base = 0 if first else refs.pop(0)[0]
    items, a_ref = refs[:2]
    b_refs = refs[3 : 3 + len(chosen)]
    sums, out, sem = refs[3 + len(chosen) :]
    add_products(items, a_ref, list(zip(chosen, b_refs)), sums, window=base)
    copy = pltpu.make_async_copy(sums, out, sem.at[0])
    copy.start()
    copy.wait()


def multiply(base, chosen, items, a_ready, sums, b_parts):
    first = base is None
    smem_spec = pl.BlockSpec(memory_space=SMEM)
    vmem_spec = pl.BlockSpec(memory_space=VMEM)
    given = [] if first else [base]
    return pl.pallas_call(
        functools.partial(multiply_kernel, first, chosen),
        out_shape=[jax.ShapeDtypeStruct(sums.shape, F32)] * 2,
        in_specs=[smem_spec] * (len(given) + 1) + [vmem_spec] * (2 + len(chosen)),
        out_specs=[vmem_spec, pl.BlockSpec(memory_space=pl.ANY)],
        input_output_aliases={len(given) + 2: 0},
        scratch_shapes=[pltpu.SemaphoreType.DMA((1,))],
        compiler_params=pltpu.CompilerParams(vmem_limit_bytes=32 << 20),
        cost_estimate=pl.CostEstimate(flops=1 << 26, bytes_accessed=4 << 20, transcendentals=0),
        name="multiply",
    )(*given, items, a_ready, sums, *b_parts)


def shards(a_blocks, a_index, b_blocks, b_cols, c_cols):
    rows = lax.axis_size("row")
    cols = lax.axis_size("col")
    a_slots = a_blocks.shape[1] * cols // rows
    row_count = b_blocks.shape[0]

    def send_rows(parts):
        far_first = range(len(parts), 0, -1)
        return [exchanged(parts[d - 1], "row", d) for d in far_first][::-1]

    def finish(base, sums, arrived):
        split = max(rows - 1, 1) - 1
        near, last = list(range(split + 1, rows)), list(range(split, 0, -1))
        sums = near_products(base, near, items, a_ready, sums, [arrived[d - 1] for d in near])
        return multiply(base, last, items, a_ready, sums, [arrived[d - 1] for d in last])

    index_parts = [a_index] + [exchanged(a_index, "col", h) for h in range(1, cols)]
    told = describe(index_parts, b_cols.T, c_cols.T)
    a_parts = [exchanged(a_blocks, "col", 1)]
    told, a_parts[0] = lax.optimization_barrier((told, a_parts[0]))
    for h in range(2, cols, 2):
        far = exchanged(a_blocks, "col", h)
        a_parts += [far, exchanged(a_blocks, "col", h + 1)]
    told = [told] + send_rows([told] * (rows - 1))
    flat, own, sums = flatten(seen_by_rows(b_blocks))
    flat, *a_parts = lax.optimization_barrier((flat, *a_parts))
    packed = pack(None, told, flat, cols, row_count, a_slots)
    arrived = send_rows(packed)
    told_late = lax.optimization_barrier((told, packed[0]))[0]
    items = work_list(told_late, cols, row_count, a_slots)
    rounds = jnp.minimum(count_rounds(told_late, cols, row_count, a_slots)[0], LANES)
    a_ready, sums = stage([a_blocks] + a_parts, own, sums, items)
    sums, rounds = lax.optimization_barrier((sums, rounds))
    sums, out = finish(None, sums, arrived)

    def more(state):
        return state[0] < rounds

    def one_round(state):
        at, sums, _ = state
        base = jnp.reshape(at * CAPACITY, (1,))
        arrived = send_rows(pack(base, told, flat, cols, row_count, a_slots))
        return at + 1, *finish(base, sums, arrived)

    return seen_by_blocks(lax.while_loop(more, one_round, (jnp.int32(1), sums, out))[2])


def solution(mesh):
    return jax.shard_map(
        shards,
        mesh=mesh,
        in_specs=(
            P(("sys", "row"), "col", None),
            P(None, ("sys", "row"), "col"),
            P(("sys", "row"), "col", None),
            P(("sys", "row"), "col"),
            P(("sys", "row"), "col"),
        ),
        out_specs=P(("sys", "row"), "col", None),
        check_vma=False,
    )
```

```python
import functools

import jax
import jax.numpy as jnp
from jax import lax
from jax.experimental import pallas as pl
from jax.experimental.layout import Layout, with_layout_constraint
from jax.experimental.pallas import tpu as pltpu
from jax.sharding import PartitionSpec as P

BS = 64
LANES = 128
ROWS = BS * BS // LANES
CAPACITY = 16
UNROLL = 4
SLOTS = 4
VMEM = pltpu.VMEM
SMEM = pltpu.SMEM
BF16 = jnp.bfloat16
F32 = jnp.float32
I32 = jnp.int32


def exchanged(block, axis, distance):
    size = lax.axis_size(axis)
    return lax.ppermute(block, axis, [(i, i ^ distance) for i in range(size)])


def seen_by_rows(blocks):
    count = blocks.shape[0]
    parted = blocks.reshape(count, SLOTS, ROWS, LANES)
    parted = with_layout_constraint(parted, Layout(major_to_minor=(0, 2, 1, 3)))
    return parted.transpose(0, 2, 1, 3).reshape(count, ROWS * SLOTS, LANES)


def seen_by_blocks(rows):
    count = rows.shape[0]
    parted = rows.reshape(count, ROWS, SLOTS, LANES).transpose(0, 2, 1, 3)
    parted = with_layout_constraint(parted, Layout(major_to_minor=(0, 2, 1, 3)))
    return parted.reshape(count, SLOTS, BS * BS)


def describe(a_parts, b_cols, c_cols):
    cols = len(a_parts)
    total = -(-(2 * cols + 2 * SLOTS) // 8) * 8

    def placed(part, at):
        after = (total - at - part.shape[0], LANES - part.shape[1])
        return jnp.pad(part, ((at, after[0]), (0, after[1])), constant_values=-1)

    own = jnp.maximum(placed(c_cols, 2 * cols), placed(b_cols, 2 * cols + SLOTS))
    told = lax.optimization_barrier(jnp.maximum(own, placed(a_parts[0][:, 0, :], 0)))
    for h in range(1, cols):
        told = jnp.maximum(told, placed(a_parts[h][:, 0, :], 2 * h))
    return told


def offers(told, cols, row_count):
    start = 2 * cols + SLOTS
    rows = told[pl.ds(start, SLOTS), :]
    lane = iota((1, LANES), 1)
    result = rows[0:1]
    for n in range(1, SLOTS):
        moved = pltpu.roll(rows, n * row_count, 1)[n : n + 1]
        result = jnp.where(lane // row_count == n, moved, result)
    return result


def flatten_kernel(b_ref, flat, wide):
    row_count = b_ref.shape[0]
    wide[...] = b_ref[...].astype(F32)
    for t in range(ROWS):
        for n in range(SLOTS):
            piece = wide[:, t * SLOTS + n, :].astype(BF16)
            flat[pl.ds(n * row_count, row_count), pl.ds(t * LANES, LANES)] = piece


def flatten(b_rows):
    vmem_spec = pl.BlockSpec(memory_space=VMEM)
    return pl.pallas_call(
        flatten_kernel,
        out_shape=(
            jax.ShapeDtypeStruct((b_rows.shape[0] * SLOTS, BS * BS), BF16),
            jax.ShapeDtypeStruct(b_rows.shape, F32),
        ),
        in_specs=[vmem_spec],
        out_specs=(vmem_spec,) * 2,
        compiler_params=pltpu.CompilerParams(vmem_limit_bytes=24 << 20),
        cost_estimate=pl.CostEstimate(flops=1 << 20, bytes_accessed=8 << 20, transcendentals=0),
        name="flatten",
    )(b_rows)


def iota(shape, axis):
    return lax.broadcasted_iota(I32, shape, axis)


def along_lanes(left, right):
    return lax.dot_general(
        left.astype(BF16), right.astype(BF16), (((1,), (1,)), ((), ())), preferred_element_type=F32
    )


def turn_to_columns(rows, first, count):
    pick = (iota((count, LANES), 0) + first == iota((count, LANES), 1)).astype(BF16)
    return lax.dot_general(
        pick,
        rows.astype(F32).astype(BF16),
        (((1,), (1,)), ((), ())),
        preferred_element_type=F32,
    )


def matches(receiver, offered, holder, cols, row_count, first_slot, a_slots):
    turned = 2 * (holder ^ lax.axis_index("col"))
    rows = [receiver[pl.ds(turned, 1), :], receiver[pl.ds(turned + 1, 1), :]]
    rows += [receiver[pl.ds(2 * cols, SLOTS), :]]
    rows = jnp.concatenate(rows + [jnp.zeros((8 - 2 - SLOTS, LANES), I32)], axis=0)
    kept_columns = turn_to_columns(rows, 0, row_count)
    if isinstance(first_slot, int) and first_slot == 0 and a_slots == row_count:
        slot_columns = kept_columns
    else:
        slot_columns = turn_to_columns(rows, first_slot, a_slots)
    wanted = offered.astype(F32)
    kept = jnp.zeros((row_count, LANES), F32)
    which = jnp.zeros((row_count, LANES), F32)
    for m in range(SLOTS):
        column = kept_columns[:, 2 + m : 3 + m]
        equal = (column == wanted) & (wanted >= 0)
        kept = jnp.where(equal, 1.0, kept)
        which = jnp.where(equal, float(m), which)
    a_rows = slot_columns[:, 0:1]
    a_columns = slot_columns[:, 1:2]
    shape = (a_slots, row_count)
    by_row = (a_rows == iota(shape, 1).astype(F32)).astype(BF16)
    by_column = a_columns == (iota((a_slots, LANES), 1) % row_count).astype(F32)
    both = jnp.concatenate([kept, which], axis=1).astype(BF16)
    both = jnp.dot(by_row, both, preferred_element_type=F32)
    pairs = jnp.where(by_column & (both[:, :LANES] > 0.5), 1.0, 0.0)
    return pairs, both[:, LANES:], a_rows


def places(needed):
    before = (iota((LANES, LANES), 0) < iota((LANES, LANES), 1)).astype(BF16)
    many = jnp.broadcast_to(needed, (8, LANES)).astype(BF16)
    return jnp.dot(many, before, preferred_element_type=F32)[0:1]


def pack_kernel(first, peers, cols, a_slots, row_count, *refs):
    refs = list(refs)
    base = 0 if first else refs.pop(0)[0]
    told = refs[:peers]
    flat = refs[peers]
    outs = refs[peers + 1 : 2 * peers]
    picks, packed = refs[2 * peers :]
    grid_row = lax.axis_index("row")
    per_col = peers // cols
    offered = offers(told[0], cols, row_count)
    first_slot = grid_row % per_col * a_slots if per_col > 1 else 0
    for d in range(1, peers):
        pairs, _, _ = matches(
            told[d], offered, grid_row // per_col, cols, row_count, first_slot, a_slots
        )
        needed = jnp.max(pairs, axis=0, keepdims=True)
        place = jnp.where(needed > 0.5, places(needed), -1.0).astype(I32)
        pick = (place == iota((CAPACITY, LANES), 0) + base).astype(BF16)
        picks[pl.ds((d - 1) * CAPACITY, CAPACITY), :] = pick
    pick = picks[...][:, : flat.shape[0]]
    for t in range(0, ROWS, 2):
        both = flat[:, pl.ds(t * LANES, 2 * LANES)]
        both = jnp.dot(pick, both, preferred_element_type=F32)
        packed[:, t, :] = both[:, :LANES]
        packed[:, t + 1, :] = both[:, LANES:]
    for d in range(1, peers):
        out = outs[d - 1]
        for x in range(CAPACITY):
            out[pl.ds(x * ROWS, ROWS), :] = packed[(d - 1) * CAPACITY + x].astype(BF16)


def pack(base, told, flat, cols, row_count, a_slots):
    first = base is None
    peers = len(told)
    smem_spec = pl.BlockSpec(memory_space=SMEM)
    vmem_spec = pl.BlockSpec(memory_space=VMEM)
    given = [] if first else [base]
    return pl.pallas_call(
        functools.partial(pack_kernel, first, peers, cols, a_slots, row_count),
        out_shape=[jax.ShapeDtypeStruct((CAPACITY * ROWS, LANES), BF16)] * (peers - 1),
        in_specs=[smem_spec] * len(given) + [vmem_spec] * (peers + 1),
        out_specs=[vmem_spec] * (peers - 1),
        scratch_shapes=[
            VMEM(((peers - 1) * CAPACITY, LANES), BF16),
            VMEM(((peers - 1) * CAPACITY, ROWS, LANES), F32),
        ],
        compiler_params=pltpu.CompilerParams(vmem_limit_bytes=32 << 20),
        cost_estimate=pl.CostEstimate(flops=1 << 20, bytes_accessed=4 << 20, transcendentals=0),
        name="pack",
    )(*given, *told, flat)


def list_kernel(cols, a_slots, row_count, peers, *refs):
    told, items = refs[:peers], refs[peers]
    grid_row = lax.axis_index("row")
    grid_col = lax.axis_index("col")
    per_col = peers // cols
    blocks = row_count * SLOTS
    lane = iota((1, LANES), 1)
    spot = iota((blocks, LANES), 0)
    before = (iota((LANES, LANES), 0) < iota((LANES, LANES), 1)).astype(BF16)
    below = (iota((blocks, blocks), 1) < iota((blocks, blocks), 0)).astype(BF16)
    same_slot = spot // row_count == iota((blocks, LANES), 1) // a_slots
    for d in range(peers):
        group = grid_row ^ d
        holder = group // per_col
        first_slot = group % per_col * a_slots if per_col > 1 else 0
        at = 2 * (holder ^ grid_col)
        slots = []
        for row in (told[0][pl.ds(at, 1), :], told[0][pl.ds(at + 1, 1), :]):
            if per_col > 1:
                row = pltpu.roll(row, (LANES - first_slot) % LANES, 1)
            spread = row
            for n in range(1, SLOTS):
                spread = jnp.where(lane // a_slots == n, pltpu.roll(row, n * a_slots, 1), spread)
            slots.append(jnp.where(lane < SLOTS * a_slots, spread, -1))
        a_rows, a_columns = slots
        offered = turn_to_columns(
            jnp.broadcast_to(offers(told[d], cols, row_count), (8, LANES)), 0, blocks
        )[:, 0:1]
        kept = jnp.zeros((blocks, LANES), F32)
        which = jnp.zeros((blocks, LANES), F32)
        for m in range(SLOTS):
            column = told[0][pl.ds(2 * cols + m, 1), :].astype(F32)
            equal = (column == offered) & (offered >= 0)
            kept = jnp.where(equal, 1.0, kept)
            which = jnp.where(equal, float(m), which)
        by_row = (a_rows == iota((row_count, LANES), 0)).astype(BF16)
        both = jnp.concatenate([kept, which], axis=0)[:, :row_count].astype(BF16)
        both = jnp.dot(both, by_row, preferred_element_type=F32)
        meets = (both[:blocks] > 0.5) & (a_columns == spot % row_count) & same_slot
        pairs = jnp.where(meets, 1.0, 0.0)
        if d == 0:
            place = spot.astype(F32)
        else:
            needed = jnp.max(pairs, axis=1, keepdims=True)
            many = jnp.broadcast_to(needed, (blocks, LANES)).astype(BF16)
            place = jnp.dot(below, many, preferred_element_type=F32)
        hit = jnp.sum(pairs, axis=0, keepdims=True)
        place = jnp.sum(pairs * place, axis=0, keepdims=True)
        out = jnp.sum(pairs * both[blocks:], axis=0, keepdims=True)
        out = out + a_rows.astype(F32) * SLOTS * hit
        rank = jnp.dot(
            jnp.broadcast_to(hit, (8, LANES)).astype(BF16), before, preferred_element_type=F32
        )[0:1]
        rank = jnp.where(hit > 0.5, rank, -1.0).astype(I32)
        chosen = rank == iota((LANES, LANES), 0)
        zero = jnp.zeros((1, LANES), F32)
        values = [(lane % a_slots).astype(F32) * hit, out, place] + [zero] * 5
        listed = along_lanes(jnp.concatenate(values, axis=0), chosen.astype(F32)).astype(I32)
        a_slot = holder * per_col * a_slots + first_slot + listed[0:1]
        word = (a_slot * 64 + listed[1:2]) * 64 + listed[2:3]
        total = jnp.sum(hit, axis=1, keepdims=True).astype(I32)
        items[pl.ds(d, 1), :] = jnp.where(lane == LANES - 1, total, word)


def work_list(told, cols, row_count, a_slots):
    peers = len(told)
    return pl.pallas_call(
        functools.partial(list_kernel, cols, a_slots, row_count, peers),
        out_shape=jax.ShapeDtypeStruct((-(-peers // 8) * 8, LANES), I32),
        in_specs=[pl.BlockSpec(memory_space=VMEM)] * peers,
        out_specs=pl.BlockSpec(memory_space=VMEM),
        cost_estimate=pl.CostEstimate(flops=1 << 10, bytes_accessed=1 << 10, transcendentals=0),
        name="work_list",
    )(*told)


def rounds_kernel(cols, a_slots, row_count, peers, *refs):
    told_refs, rounds, told = refs[:peers], refs[peers], refs[peers + 1]
    for d, ref in enumerate(told_refs):
        told[d, :, :] = ref[...]
    grid_row = lax.axis_index("row")
    per_col = peers // cols

    def one_pair(receiver, d, most):
        group = grid_row ^ receiver ^ d
        sender = receiver ^ d
        first_slot = group % per_col * a_slots if per_col > 1 else 0
        pairs, _, _ = matches(
            told.at[receiver],
            offers(told.at[sender], cols, row_count),
            group // per_col,
            cols,
            row_count,
            first_slot,
            a_slots,
        )
        needed = jnp.max(pairs, axis=0, keepdims=True)
        return jnp.maximum(most, jnp.sum(needed, axis=1, keepdims=True))

    most = jnp.zeros((1, 1), F32)
    if peers <= 4:
        for receiver in range(peers):
            for d in range(1, peers):
                most = one_pair(receiver, d, most)
    else:

        def step(at, most):
            return one_pair(at // (peers - 1), at % (peers - 1) + 1, most)

        most = lax.fori_loop(0, peers * (peers - 1), step, most)
    rounds[0] = (jnp.max(most).astype(I32) + CAPACITY - 1) // CAPACITY


def count_rounds(told, cols, row_count, a_slots):
    peers = len(told)
    return pl.pallas_call(
        functools.partial(rounds_kernel, cols, a_slots, row_count, peers),
        out_shape=jax.ShapeDtypeStruct((1,), I32),
        in_specs=[pl.BlockSpec(memory_space=VMEM)] * peers,
        out_specs=pl.BlockSpec(memory_space=SMEM),
        scratch_shapes=[VMEM((peers,) + told[0].shape, I32)],
        cost_estimate=pl.CostEstimate(flops=1 << 10, bytes_accessed=1 << 10, transcendentals=0),
        name="count_rounds",
    )(*told)


def add_products(items, a_ref, peer_refs, sums, window=None):
    low = iota((ROWS, LANES), 1) < BS
    nothing = jnp.zeros((ROWS, LANES), BF16)

    def add_one(word, used, b_ref):
        word = jnp.where(used, word, 0)
        place = word & 63
        target = (word >> 6) & 63
        if window is not None:
            place = place - window
            used = used & (place >= 0) & (place < CAPACITY)
            place = jnp.where(used, place, 0)
        a_at = pl.multiple_of((word >> 12) * ROWS, ROWS)
        b_at = pl.multiple_of(place * ROWS, ROWS)
        block = jnp.where(used, b_ref[pl.ds(b_at, ROWS), :], nothing)
        turned = jnp.concatenate([block[:, BS:], block[:, :BS]], axis=1)
        right = jnp.concatenate(
            [
                jnp.where(low, block, nothing),
                jnp.where(low, turned, nothing),
                jnp.where(low, nothing, turned),
                jnp.where(low, nothing, block),
            ],
            axis=0,
        )
        term = jnp.dot(a_ref[pl.ds(a_at, ROWS), :], right, preferred_element_type=F32)
        sums[target // SLOTS, pl.ds(target % SLOTS, ROWS, stride=SLOTS), :] += term

    for at in range(0, len(peer_refs), 3):
        chosen = peer_refs[at : at + 3]
        totals = [items[d, LANES - 1] for d, _ in chosen]
        longest = functools.reduce(jnp.maximum, totals)
        width = UNROLL if len(chosen) < 3 else UNROLL - 1

        def some_items(step, carry, chosen=chosen, totals=totals, width=width):
            for u in range(width):
                for (d, b_ref), total in zip(chosen, totals):
                    y = step * width + u
                    add_one(items[d, y], y < total, b_ref)
            return carry

        lax.fori_loop(0, (longest + width - 1) // width, some_items, 0)


def stage_kernel(cols, *refs):
    a_refs, wide, items = refs[:cols], refs[cols], refs[cols + 1]
    a_out, sums, a_wide, own = refs[cols + 2 :]
    sums[...] = jnp.zeros_like(sums)
    row_count = wide.shape[0]
    for n in range(SLOTS):
        for k in range(row_count):
            block = wide[k, pl.ds(n, ROWS, stride=SLOTS), :].astype(BF16)
            own[pl.ds((n * row_count + k) * ROWS, ROWS), :] = block
    source = iota((LANES, LANES), 0)
    target = iota((LANES, LANES), 1)
    wanted = (target // BS) * BS + 2 * (target % ROWS) + (target // ROWS) % 2
    order = (source == wanted).astype(BF16)
    slots = a_refs[0].shape[1]
    grid_col = lax.axis_index("col")
    for t in range(ROWS):
        pieces = [ref[0, :, pl.ds(t * LANES, LANES)] for ref in a_refs]
        done = jnp.dot(jnp.concatenate(pieces, axis=0), order, preferred_element_type=F32)
        a_wide[:, t, :] = done
    for h in range(cols):
        first = (grid_col ^ h) * slots
        for s in range(slots):
            at = pl.multiple_of((first + s) * ROWS, ROWS)
            a_out[pl.ds(at, ROWS), :] = a_wide[h * slots + s].astype(BF16)
    add_products(items, a_out, [(0, own)], sums)


def stage(a_parts, wide, items):
    cols, slots = len(a_parts), a_parts[0].shape[1]
    vmem_spec = pl.BlockSpec(memory_space=VMEM)
    smem_spec = pl.BlockSpec(memory_space=SMEM)
    return pl.pallas_call(
        functools.partial(stage_kernel, cols),
        out_shape=(
            jax.ShapeDtypeStruct((cols * slots * ROWS, LANES), BF16),
            jax.ShapeDtypeStruct(wide.shape, F32),
        ),
        in_specs=[vmem_spec] * (cols + 1) + [smem_spec],
        out_specs=(vmem_spec,) * 2,
        scratch_shapes=[
            VMEM((cols * slots, ROWS, LANES), F32),
            VMEM((wide.shape[0] * SLOTS * ROWS, LANES), BF16),
        ],
        compiler_params=pltpu.CompilerParams(vmem_limit_bytes=40 << 20),
        cost_estimate=pl.CostEstimate(flops=1 << 10, bytes_accessed=1 << 10, transcendentals=0),
        name="stage",
    )(*a_parts, wide, items)


def near_kernel(first, chosen, *refs):
    refs = list(refs)
    base = 0 if first else refs.pop(0)[0]
    items, a_ref = refs[:2]
    b_refs, sums = refs[3:-1], refs[-1]
    add_products(items, a_ref, list(zip(chosen, b_refs)), sums, window=base)


def near_products(base, chosen, items, a_ready, sums, b_parts):
    first = base is None
    smem_spec = pl.BlockSpec(memory_space=SMEM)
    vmem_spec = pl.BlockSpec(memory_space=VMEM)
    given = [] if first else [base]
    return pl.pallas_call(
        functools.partial(near_kernel, first, chosen),
        out_shape=jax.ShapeDtypeStruct(sums.shape, F32),
        in_specs=[smem_spec] * (len(given) + 1) + [vmem_spec] * (2 + len(chosen)),
        out_specs=vmem_spec,
        input_output_aliases={len(given) + 2: 0},
        compiler_params=pltpu.CompilerParams(vmem_limit_bytes=32 << 20),
        cost_estimate=pl.CostEstimate(flops=1 << 10, bytes_accessed=1 << 10, transcendentals=0),
        name="near_products",
    )(*given, items, a_ready, sums, *b_parts)


def multiply_kernel(first, chosen, *refs):
    refs = list(refs)
    base = 0 if first else refs.pop(0)[0]
    items, a_ref = refs[:2]
    b_refs = refs[3 : 3 + len(chosen)]
    sums, out, sem = refs[3 + len(chosen) :]
    add_products(items, a_ref, list(zip(chosen, b_refs)), sums, window=base)
    copy = pltpu.make_async_copy(sums, out, sem.at[0])
    copy.start()
    copy.wait()


def multiply(base, chosen, items, a_ready, sums, b_parts):
    first = base is None
    smem_spec = pl.BlockSpec(memory_space=SMEM)
    vmem_spec = pl.BlockSpec(memory_space=VMEM)
    given = [] if first else [base]
    return pl.pallas_call(
        functools.partial(multiply_kernel, first, chosen),
        out_shape=[jax.ShapeDtypeStruct(sums.shape, F32)] * 2,
        in_specs=[smem_spec] * (len(given) + 1) + [vmem_spec] * (2 + len(chosen)),
        out_specs=[vmem_spec, pl.BlockSpec(memory_space=pl.ANY)],
        input_output_aliases={len(given) + 2: 0},
        scratch_shapes=[pltpu.SemaphoreType.DMA((1,))],
        compiler_params=pltpu.CompilerParams(vmem_limit_bytes=32 << 20),
        cost_estimate=pl.CostEstimate(flops=1 << 26, bytes_accessed=4 << 20, transcendentals=0),
        name="multiply",
    )(*given, items, a_ready, sums, *b_parts)


def shards(a_blocks, a_index, b_blocks, b_cols, c_cols):
    rows = lax.axis_size("row")
    cols = lax.axis_size("col")
    a_slots = a_blocks.shape[1] * cols // rows
    row_count = b_blocks.shape[0]

    def send_rows(parts):
        far_first = range(len(parts), 0, -1)
        return [exchanged(parts[d - 1], "row", d) for d in far_first][::-1]

    def finish(base, sums, arrived):
        split = max(rows - 1, 1) - 1
        near, last = list(range(split + 1, rows)), list(range(split, 0, -1))
        sums = near_products(base, near, items, a_ready, sums, [arrived[d - 1] for d in near])
        return multiply(base, last, items, a_ready, sums, [arrived[d - 1] for d in last])

    index_parts = [a_index] + [exchanged(a_index, "col", h) for h in range(1, cols)]
    told = describe(index_parts, b_cols.T, c_cols.T)
    a_parts = [exchanged(a_blocks, "col", 1)]
    told, a_parts[0] = lax.optimization_barrier((told, a_parts[0]))
    for h in range(2, cols, 2):
        far = exchanged(a_blocks, "col", h)
        a_parts += [far, exchanged(a_blocks, "col", h + 1)]
    told = [told] + send_rows([told] * (rows - 1))
    flat, wide = flatten(seen_by_rows(b_blocks))
    flat, *a_parts = lax.optimization_barrier((flat, *a_parts))
    packed = pack(None, told, flat, cols, row_count, a_slots)
    arrived = send_rows(packed)
    told_late = lax.optimization_barrier((told, packed[0]))[0]
    items = work_list(told_late, cols, row_count, a_slots)
    rounds = jnp.minimum(count_rounds(told_late, cols, row_count, a_slots)[0], LANES)
    a_ready, sums = stage([a_blocks] + a_parts, wide, items)
    sums, rounds = lax.optimization_barrier((sums, rounds))
    sums, out = finish(None, sums, arrived)

    def more(state):
        return state[0] < rounds

    def one_round(state):
        at, sums, _ = state
        base = jnp.reshape(at * CAPACITY, (1,))
        arrived = send_rows(pack(base, told, flat, cols, row_count, a_slots))
        return at + 1, *finish(base, sums, arrived)

    return seen_by_blocks(lax.while_loop(more, one_round, (jnp.int32(1), sums, out))[2])


def solution(mesh):
    return jax.shard_map(
        shards,
        mesh=mesh,
        in_specs=(
            P(("sys", "row"), "col", None),
            P(None, ("sys", "row"), "col"),
            P(("sys", "row"), "col", None),
            P(("sys", "row"), "col"),
            P(("sys", "row"), "col"),
        ),
        out_specs=P(("sys", "row"), "col", None),
        check_vma=False,
    )
```

```python
import functools

import jax
import jax.numpy as jnp
from jax import lax
from jax.experimental import pallas as pl
from jax.experimental.layout import Layout, with_layout_constraint
from jax.experimental.pallas import tpu as pltpu
from jax.sharding import PartitionSpec as P

BS = 64
LANES = 128
ROWS = BS * BS // LANES
PADDING = 8
CAPACITY = 16
UNROLL = 4
SLOTS = 4
VMEM = pltpu.VMEM
SMEM = pltpu.SMEM
BF16 = jnp.bfloat16
F32 = jnp.float32
I32 = jnp.int32


def exchanged(block, axis, distance):
    size = lax.axis_size(axis)
    return lax.ppermute(block, axis, [(i, i ^ distance) for i in range(size)])


def seen_by_rows(blocks):
    count = blocks.shape[0]
    parted = blocks.reshape(count, SLOTS, ROWS, LANES)
    parted = with_layout_constraint(parted, Layout(major_to_minor=(0, 2, 1, 3)))
    return parted.transpose(0, 2, 1, 3).reshape(count, ROWS * SLOTS, LANES)


def seen_by_blocks(rows):
    count = rows.shape[0]
    parted = rows.reshape(count, ROWS, SLOTS, LANES).transpose(0, 2, 1, 3)
    parted = with_layout_constraint(parted, Layout(major_to_minor=(0, 2, 1, 3)))
    return parted.reshape(count, SLOTS, BS * BS)


def describe(a_parts, b_cols, c_cols):
    cols = len(a_parts)
    total = -(-(2 * cols + 2 * SLOTS) // 8) * 8

    def placed(part, at):
        after = (total - at - part.shape[0], LANES - part.shape[1])
        return jnp.pad(part, ((at, after[0]), (0, after[1])), constant_values=-1)

    own = jnp.maximum(placed(c_cols, 2 * cols), placed(b_cols, 2 * cols + SLOTS))
    told = lax.optimization_barrier(jnp.maximum(own, placed(a_parts[0][:, 0, :], 0)))
    for h in range(1, cols):
        told = jnp.maximum(told, placed(a_parts[h][:, 0, :], 2 * h))
    return told


def offers(told, cols, row_count):
    start = 2 * cols + SLOTS
    rows = told[pl.ds(start, SLOTS), :]
    lane = iota((1, LANES), 1)
    result = rows[0:1]
    for n in range(1, SLOTS):
        moved = pltpu.roll(rows, n * row_count, 1)[n : n + 1]
        result = jnp.where(lane // row_count == n, moved, result)
    return result


def flatten_kernel(b_ref, flat, wide):
    row_count = b_ref.shape[0]
    wide[:, 0 : SLOTS * ROWS, :] = b_ref[...].astype(F32)
    for t in range(ROWS):
        for n in range(SLOTS):
            piece = wide[:, t * SLOTS + n, :].astype(BF16)
            flat[pl.ds(n * row_count, row_count), pl.ds(t * LANES, LANES)] = piece


def flatten(b_rows):
    vmem_spec = pl.BlockSpec(memory_space=VMEM)
    return pl.pallas_call(
        flatten_kernel,
        out_shape=(
            jax.ShapeDtypeStruct((b_rows.shape[0] * SLOTS, BS * BS), BF16),
            jax.ShapeDtypeStruct((b_rows.shape[0], SLOTS * ROWS + PADDING, LANES), F32),
        ),
        in_specs=[vmem_spec],
        out_specs=(vmem_spec,) * 2,
        compiler_params=pltpu.CompilerParams(vmem_limit_bytes=24 << 20),
        cost_estimate=pl.CostEstimate(flops=1 << 20, bytes_accessed=8 << 20, transcendentals=0),
        name="flatten",
    )(b_rows)


def iota(shape, axis):
    return lax.broadcasted_iota(I32, shape, axis)


def along_lanes(left, right):
    return lax.dot_general(
        left.astype(BF16), right.astype(BF16), (((1,), (1,)), ((), ())), preferred_element_type=F32
    )


def turn_to_columns(rows, first, count):
    pick = (iota((count, LANES), 0) + first == iota((count, LANES), 1)).astype(BF16)
    return lax.dot_general(
        pick,
        rows.astype(F32).astype(BF16),
        (((1,), (1,)), ((), ())),
        preferred_element_type=F32,
    )


def matches(receiver, offered, holder, cols, row_count, first_slot, a_slots):
    turned = 2 * (holder ^ lax.axis_index("col"))
    rows = [receiver[pl.ds(turned, 1), :], receiver[pl.ds(turned + 1, 1), :]]
    rows += [receiver[pl.ds(2 * cols, SLOTS), :]]
    rows = jnp.concatenate(rows + [jnp.zeros((8 - 2 - SLOTS, LANES), I32)], axis=0)
    kept_columns = turn_to_columns(rows, 0, row_count)
    if isinstance(first_slot, int) and first_slot == 0 and a_slots == row_count:
        slot_columns = kept_columns
    else:
        slot_columns = turn_to_columns(rows, first_slot, a_slots)
    wanted = offered.astype(F32)
    kept = jnp.zeros((row_count, LANES), F32)
    which = jnp.zeros((row_count, LANES), F32)
    for m in range(SLOTS):
        column = kept_columns[:, 2 + m : 3 + m]
        equal = (column == wanted) & (wanted >= 0)
        kept = jnp.where(equal, 1.0, kept)
        which = jnp.where(equal, float(m), which)
    a_rows = slot_columns[:, 0:1]
    a_columns = slot_columns[:, 1:2]
    shape = (a_slots, row_count)
    by_row = (a_rows == iota(shape, 1).astype(F32)).astype(BF16)
    by_column = a_columns == (iota((a_slots, LANES), 1) % row_count).astype(F32)
    both = jnp.concatenate([kept, which], axis=1).astype(BF16)
    both = jnp.dot(by_row, both, preferred_element_type=F32)
    pairs = jnp.where(by_column & (both[:, :LANES] > 0.5), 1.0, 0.0)
    return pairs, both[:, LANES:], a_rows


def places(needed):
    before = (iota((LANES, LANES), 0) < iota((LANES, LANES), 1)).astype(BF16)
    many = jnp.broadcast_to(needed, (8, LANES)).astype(BF16)
    return jnp.dot(many, before, preferred_element_type=F32)[0:1]


def pack_kernel(first, peers, cols, a_slots, row_count, *refs):
    refs = list(refs)
    base = 0 if first else refs.pop(0)[0]
    told = refs[:peers]
    flat = refs[peers]
    outs = refs[peers + 1 : 2 * peers]
    picks, packed = refs[2 * peers :]
    grid_row = lax.axis_index("row")
    per_col = peers // cols
    offered = offers(told[0], cols, row_count)
    first_slot = grid_row % per_col * a_slots if per_col > 1 else 0
    for d in range(1, peers):
        pairs, _, _ = matches(
            told[d], offered, grid_row // per_col, cols, row_count, first_slot, a_slots
        )
        needed = jnp.max(pairs, axis=0, keepdims=True)
        place = jnp.where(needed > 0.5, places(needed), -1.0).astype(I32)
        pick = (place == iota((CAPACITY, LANES), 0) + base).astype(BF16)
        picks[pl.ds((d - 1) * CAPACITY, CAPACITY), :] = pick
    pick = picks[...][:, : flat.shape[0]]
    for t in range(0, ROWS, 2):
        both = flat[:, pl.ds(t * LANES, 2 * LANES)]
        both = jnp.dot(pick, both, preferred_element_type=F32)
        packed[:, t, :] = both[:, :LANES]
        packed[:, t + 1, :] = both[:, LANES:]
    for d in range(1, peers):
        out = outs[d - 1]
        for x in range(CAPACITY):
            out[pl.ds(x * ROWS, ROWS), :] = packed[(d - 1) * CAPACITY + x, 0:ROWS, :].astype(BF16)


def pack(base, told, flat, cols, row_count, a_slots):
    first = base is None
    peers = len(told)
    smem_spec = pl.BlockSpec(memory_space=SMEM)
    vmem_spec = pl.BlockSpec(memory_space=VMEM)
    given = [] if first else [base]
    return pl.pallas_call(
        functools.partial(pack_kernel, first, peers, cols, a_slots, row_count),
        out_shape=[jax.ShapeDtypeStruct((CAPACITY * ROWS, LANES), BF16)] * (peers - 1),
        in_specs=[smem_spec] * len(given) + [vmem_spec] * (peers + 1),
        out_specs=[vmem_spec] * (peers - 1),
        scratch_shapes=[
            VMEM(((peers - 1) * CAPACITY, LANES), BF16),
            VMEM(((peers - 1) * CAPACITY, ROWS + PADDING, LANES), F32),
        ],
        compiler_params=pltpu.CompilerParams(vmem_limit_bytes=32 << 20),
        cost_estimate=pl.CostEstimate(flops=1 << 20, bytes_accessed=4 << 20, transcendentals=0),
        name="pack",
    )(*given, *told, flat)


def list_kernel(cols, a_slots, row_count, peers, *refs):
    told, items = refs[:peers], refs[peers]
    grid_row = lax.axis_index("row")
    grid_col = lax.axis_index("col")
    per_col = peers // cols
    blocks = row_count * SLOTS
    lane = iota((1, LANES), 1)
    spot = iota((blocks, LANES), 0)
    before = (iota((LANES, LANES), 0) < iota((LANES, LANES), 1)).astype(BF16)
    below = (iota((blocks, blocks), 1) < iota((blocks, blocks), 0)).astype(BF16)
    same_slot = spot // row_count == iota((blocks, LANES), 1) // a_slots
    for d in range(peers):
        group = grid_row ^ d
        holder = group // per_col
        first_slot = group % per_col * a_slots if per_col > 1 else 0
        at = 2 * (holder ^ grid_col)
        slots = []
        for row in (told[0][pl.ds(at, 1), :], told[0][pl.ds(at + 1, 1), :]):
            if per_col > 1:
                row = pltpu.roll(row, (LANES - first_slot) % LANES, 1)
            spread = row
            for n in range(1, SLOTS):
                spread = jnp.where(lane // a_slots == n, pltpu.roll(row, n * a_slots, 1), spread)
            slots.append(jnp.where(lane < SLOTS * a_slots, spread, -1))
        a_rows, a_columns = slots
        offered = turn_to_columns(
            jnp.broadcast_to(offers(told[d], cols, row_count), (8, LANES)), 0, blocks
        )[:, 0:1]
        kept = jnp.zeros((blocks, LANES), F32)
        which = jnp.zeros((blocks, LANES), F32)
        for m in range(SLOTS):
            column = told[0][pl.ds(2 * cols + m, 1), :].astype(F32)
            equal = (column == offered) & (offered >= 0)
            kept = jnp.where(equal, 1.0, kept)
            which = jnp.where(equal, float(m), which)
        by_row = (a_rows == iota((row_count, LANES), 0)).astype(BF16)
        both = jnp.concatenate([kept, which], axis=0)[:, :row_count].astype(BF16)
        both = jnp.dot(both, by_row, preferred_element_type=F32)
        meets = (both[:blocks] > 0.5) & (a_columns == spot % row_count) & same_slot
        pairs = jnp.where(meets, 1.0, 0.0)
        if d == 0:
            place = spot.astype(F32)
        else:
            needed = jnp.max(pairs, axis=1, keepdims=True)
            many = jnp.broadcast_to(needed, (blocks, LANES)).astype(BF16)
            place = jnp.dot(below, many, preferred_element_type=F32)
        hit = jnp.sum(pairs, axis=0, keepdims=True)
        place = jnp.sum(pairs * place, axis=0, keepdims=True)
        out = jnp.sum(pairs * both[blocks:], axis=0, keepdims=True)
        out = out + a_rows.astype(F32) * SLOTS * hit
        rank = jnp.dot(
            jnp.broadcast_to(hit, (8, LANES)).astype(BF16), before, preferred_element_type=F32
        )[0:1]
        rank = jnp.where(hit > 0.5, rank, -1.0).astype(I32)
        chosen = rank == iota((LANES, LANES), 0)
        zero = jnp.zeros((1, LANES), F32)
        values = [(lane % a_slots).astype(F32) * hit, out, place] + [zero] * 5
        listed = along_lanes(jnp.concatenate(values, axis=0), chosen.astype(F32)).astype(I32)
        a_slot = holder * per_col * a_slots + first_slot + listed[0:1]
        word = (a_slot * 64 + listed[1:2]) * 64 + listed[2:3]
        total = jnp.sum(hit, axis=1, keepdims=True).astype(I32)
        items[pl.ds(d, 1), :] = jnp.where(lane == LANES - 1, total, word)


def work_list(told, cols, row_count, a_slots):
    peers = len(told)
    return pl.pallas_call(
        functools.partial(list_kernel, cols, a_slots, row_count, peers),
        out_shape=jax.ShapeDtypeStruct((-(-peers // 8) * 8, LANES), I32),
        in_specs=[pl.BlockSpec(memory_space=VMEM)] * peers,
        out_specs=pl.BlockSpec(memory_space=VMEM),
        cost_estimate=pl.CostEstimate(flops=1 << 10, bytes_accessed=1 << 10, transcendentals=0),
        name="work_list",
    )(*told)


def rounds_kernel(cols, a_slots, row_count, peers, *refs):
    told_refs, rounds, told = refs[:peers], refs[peers], refs[peers + 1]
    for d, ref in enumerate(told_refs):
        told[d, :, :] = ref[...]
    grid_row = lax.axis_index("row")
    per_col = peers // cols

    def one_pair(receiver, d, most):
        group = grid_row ^ receiver ^ d
        sender = receiver ^ d
        first_slot = group % per_col * a_slots if per_col > 1 else 0
        pairs, _, _ = matches(
            told.at[receiver],
            offers(told.at[sender], cols, row_count),
            group // per_col,
            cols,
            row_count,
            first_slot,
            a_slots,
        )
        needed = jnp.max(pairs, axis=0, keepdims=True)
        return jnp.maximum(most, jnp.sum(needed, axis=1, keepdims=True))

    most = jnp.zeros((1, 1), F32)
    if peers <= 4:
        for receiver in range(peers):
            for d in range(1, peers):
                most = one_pair(receiver, d, most)
    else:

        def step(at, most):
            return one_pair(at // (peers - 1), at % (peers - 1) + 1, most)

        most = lax.fori_loop(0, peers * (peers - 1), step, most)
    rounds[0] = (jnp.max(most).astype(I32) + CAPACITY - 1) // CAPACITY


def count_rounds(told, cols, row_count, a_slots):
    peers = len(told)
    return pl.pallas_call(
        functools.partial(rounds_kernel, cols, a_slots, row_count, peers),
        out_shape=jax.ShapeDtypeStruct((1,), I32),
        in_specs=[pl.BlockSpec(memory_space=VMEM)] * peers,
        out_specs=pl.BlockSpec(memory_space=SMEM),
        scratch_shapes=[VMEM((peers,) + told[0].shape, I32)],
        cost_estimate=pl.CostEstimate(flops=1 << 10, bytes_accessed=1 << 10, transcendentals=0),
        name="count_rounds",
    )(*told)


def add_products(items, a_ref, peer_refs, sums, window=None):
    low = iota((ROWS, LANES), 1) < BS
    nothing = jnp.zeros((ROWS, LANES), BF16)

    def add_one(word, used, b_ref):
        word = jnp.where(used, word, 0)
        place = word & 63
        target = (word >> 6) & 63
        if window is not None:
            place = place - window
            used = used & (place >= 0) & (place < CAPACITY)
            place = jnp.where(used, place, 0)
        a_at = pl.multiple_of((word >> 12) * ROWS, ROWS)
        b_at = pl.multiple_of(place * ROWS, ROWS)
        block = jnp.where(used, b_ref[pl.ds(b_at, ROWS), :], nothing)
        turned = jnp.concatenate([block[:, BS:], block[:, :BS]], axis=1)
        right = jnp.concatenate(
            [
                jnp.where(low, block, nothing),
                jnp.where(low, turned, nothing),
                jnp.where(low, nothing, turned),
                jnp.where(low, nothing, block),
            ],
            axis=0,
        )
        term = jnp.dot(a_ref[pl.ds(a_at, ROWS), :], right, preferred_element_type=F32)
        sums[target // SLOTS, pl.ds(target % SLOTS, ROWS, stride=SLOTS), :] += term

    for at in range(0, len(peer_refs), 3):
        chosen = peer_refs[at : at + 3]
        totals = [items[d, LANES - 1] for d, _ in chosen]
        longest = functools.reduce(jnp.maximum, totals)
        width = UNROLL if len(chosen) < 3 else UNROLL - 1

        def some_items(step, carry, chosen=chosen, totals=totals, width=width):
            for u in range(width):
                for (d, b_ref), total in zip(chosen, totals):
                    y = step * width + u
                    add_one(items[d, y], y < total, b_ref)
            return carry

        lax.fori_loop(0, (longest + width - 1) // width, some_items, 0)


def stage_kernel(cols, *refs):
    a_refs, wide, items = refs[:cols], refs[cols], refs[cols + 1]
    a_out, sums, a_wide, own = refs[cols + 2 :]
    sums[...] = jnp.zeros_like(sums)
    row_count = wide.shape[0]
    for n in range(SLOTS):
        for k in range(row_count):
            block = wide[k, pl.ds(n, ROWS, stride=SLOTS), :].astype(BF16)
            own[pl.ds((n * row_count + k) * ROWS, ROWS), :] = block
    source = iota((LANES, LANES), 0)
    target = iota((LANES, LANES), 1)
    wanted = (target // BS) * BS + 2 * (target % ROWS) + (target // ROWS) % 2
    order = (source == wanted).astype(BF16)
    slots = a_refs[0].shape[1]
    grid_col = lax.axis_index("col")
    for t in range(ROWS):
        pieces = [ref[0, :, pl.ds(t * LANES, LANES)] for ref in a_refs]
        done = jnp.dot(jnp.concatenate(pieces, axis=0), order, preferred_element_type=F32)
        a_wide[:, t, :] = done
    for h in range(cols):
        first = (grid_col ^ h) * slots
        for s in range(slots):
            at = pl.multiple_of((first + s) * ROWS, ROWS)
            a_out[pl.ds(at, ROWS), :] = a_wide[h * slots + s, 0:ROWS, :].astype(BF16)
    add_products(items, a_out, [(0, own)], sums)


def stage(a_parts, wide, items):
    cols, slots = len(a_parts), a_parts[0].shape[1]
    vmem_spec = pl.BlockSpec(memory_space=VMEM)
    smem_spec = pl.BlockSpec(memory_space=SMEM)
    return pl.pallas_call(
        functools.partial(stage_kernel, cols),
        out_shape=(
            jax.ShapeDtypeStruct((cols * slots * ROWS, LANES), BF16),
            jax.ShapeDtypeStruct((wide.shape[0], SLOTS * ROWS, LANES), F32),
        ),
        in_specs=[vmem_spec] * (cols + 1) + [smem_spec],
        out_specs=(vmem_spec,) * 2,
        scratch_shapes=[
            VMEM((cols * slots, ROWS + PADDING, LANES), F32),
            VMEM((wide.shape[0] * SLOTS * ROWS, LANES), BF16),
        ],
        compiler_params=pltpu.CompilerParams(vmem_limit_bytes=40 << 20),
        cost_estimate=pl.CostEstimate(flops=1 << 10, bytes_accessed=1 << 10, transcendentals=0),
        name="stage",
    )(*a_parts, wide, items)


def near_kernel(first, chosen, *refs):
    refs = list(refs)
    base = 0 if first else refs.pop(0)[0]
    items, a_ref = refs[:2]
    b_refs, sums = refs[3:-1], refs[-1]
    add_products(items, a_ref, list(zip(chosen, b_refs)), sums, window=base)


def near_products(base, chosen, items, a_ready, sums, b_parts):
    first = base is None
    smem_spec = pl.BlockSpec(memory_space=SMEM)
    vmem_spec = pl.BlockSpec(memory_space=VMEM)
    given = [] if first else [base]
    return pl.pallas_call(
        functools.partial(near_kernel, first, chosen),
        out_shape=jax.ShapeDtypeStruct(sums.shape, F32),
        in_specs=[smem_spec] * (len(given) + 1) + [vmem_spec] * (2 + len(chosen)),
        out_specs=vmem_spec,
        input_output_aliases={len(given) + 2: 0},
        compiler_params=pltpu.CompilerParams(vmem_limit_bytes=32 << 20),
        cost_estimate=pl.CostEstimate(flops=1 << 10, bytes_accessed=1 << 10, transcendentals=0),
        name="near_products",
    )(*given, items, a_ready, sums, *b_parts)


def multiply_kernel(first, chosen, *refs):
    refs = list(refs)
    base = 0 if first else refs.pop(0)[0]
    items, a_ref = refs[:2]
    b_refs = refs[3 : 3 + len(chosen)]
    sums, out, sem = refs[3 + len(chosen) :]
    add_products(items, a_ref, list(zip(chosen, b_refs)), sums, window=base)
    copy = pltpu.make_async_copy(sums, out, sem.at[0])
    copy.start()
    copy.wait()


def multiply(base, chosen, items, a_ready, sums, b_parts):
    first = base is None
    smem_spec = pl.BlockSpec(memory_space=SMEM)
    vmem_spec = pl.BlockSpec(memory_space=VMEM)
    given = [] if first else [base]
    return pl.pallas_call(
        functools.partial(multiply_kernel, first, chosen),
        out_shape=[jax.ShapeDtypeStruct(sums.shape, F32)] * 2,
        in_specs=[smem_spec] * (len(given) + 1) + [vmem_spec] * (2 + len(chosen)),
        out_specs=[vmem_spec, pl.BlockSpec(memory_space=pl.ANY)],
        input_output_aliases={len(given) + 2: 0},
        scratch_shapes=[pltpu.SemaphoreType.DMA((1,))],
        compiler_params=pltpu.CompilerParams(vmem_limit_bytes=32 << 20),
        cost_estimate=pl.CostEstimate(flops=1 << 26, bytes_accessed=4 << 20, transcendentals=0),
        name="multiply",
    )(*given, items, a_ready, sums, *b_parts)


def shards(a_blocks, a_index, b_blocks, b_cols, c_cols):
    rows = lax.axis_size("row")
    cols = lax.axis_size("col")
    a_slots = a_blocks.shape[1] * cols // rows
    row_count = b_blocks.shape[0]

    def send_rows(parts):
        far_first = range(len(parts), 0, -1)
        return [exchanged(parts[d - 1], "row", d) for d in far_first][::-1]

    def finish(base, sums, arrived):
        split = max(rows - 1, 1) - 1
        near, last = list(range(split + 1, rows)), list(range(split, 0, -1))
        sums = near_products(base, near, items, a_ready, sums, [arrived[d - 1] for d in near])
        return multiply(base, last, items, a_ready, sums, [arrived[d - 1] for d in last])

    index_parts = [a_index] + [exchanged(a_index, "col", h) for h in range(1, cols)]
    told = describe(index_parts, b_cols.T, c_cols.T)
    a_parts = [exchanged(a_blocks, "col", 1)]
    told, a_parts[0] = lax.optimization_barrier((told, a_parts[0]))
    for h in range(2, cols, 2):
        far = exchanged(a_blocks, "col", h)
        a_parts += [far, exchanged(a_blocks, "col", h + 1)]
    told = [told] + send_rows([told] * (rows - 1))
    flat, wide = flatten(seen_by_rows(b_blocks))
    flat, *a_parts = lax.optimization_barrier((flat, *a_parts))
    packed = pack(None, told, flat, cols, row_count, a_slots)
    arrived = send_rows(packed)
    told_late = lax.optimization_barrier((told, packed[0]))[0]
    items = work_list(told_late, cols, row_count, a_slots)
    rounds = jnp.minimum(count_rounds(told_late, cols, row_count, a_slots)[0], LANES)
    a_ready, sums = stage([a_blocks] + a_parts, wide, items)
    sums, rounds = lax.optimization_barrier((sums, rounds))
    sums, out = finish(None, sums, arrived)

    def more(state):
        return state[0] < rounds

    def one_round(state):
        at, sums, _ = state
        base = jnp.reshape(at * CAPACITY, (1,))
        arrived = send_rows(pack(base, told, flat, cols, row_count, a_slots))
        return at + 1, *finish(base, sums, arrived)

    return seen_by_blocks(lax.while_loop(more, one_round, (jnp.int32(1), sums, out))[2])


def solution(mesh):
    return jax.shard_map(
        shards,
        mesh=mesh,
        in_specs=(
            P(("sys", "row"), "col", None),
            P(None, ("sys", "row"), "col"),
            P(("sys", "row"), "col", None),
            P(("sys", "row"), "col"),
            P(("sys", "row"), "col"),
        ),
        out_specs=P(("sys", "row"), "col", None),
        check_vma=False,
    )
```

```python
import functools

import jax
import jax.numpy as jnp
from jax import lax
from jax.experimental import pallas as pl
from jax.experimental.layout import Layout, with_layout_constraint
from jax.experimental.pallas import tpu as pltpu
from jax.sharding import PartitionSpec as P

BS = 64
LANES = 128
ROWS = BS * BS // LANES
GROUP = 16
PIECES = 4
PADDING = 8
CAPACITY = 16
UNROLL = 4
SLOTS = 4
VMEM = pltpu.VMEM
SMEM = pltpu.SMEM
BF16 = jnp.bfloat16
F32 = jnp.float32
I32 = jnp.int32


def exchanged(block, axis, distance):
    size = lax.axis_size(axis)
    return lax.ppermute(block, axis, [(i, i ^ distance) for i in range(size)])


def seen_by_rows(blocks):
    count = blocks.shape[0]
    parted = blocks.reshape(count, SLOTS, ROWS, LANES)
    parted = with_layout_constraint(parted, Layout(major_to_minor=(0, 2, 1, 3)))
    return parted.transpose(0, 2, 1, 3).reshape(count, ROWS * SLOTS, LANES)


def seen_by_blocks(rows):
    count = rows.shape[0]
    parted = rows.reshape(count, ROWS, SLOTS, LANES).transpose(0, 2, 1, 3)
    parted = with_layout_constraint(parted, Layout(major_to_minor=(0, 2, 1, 3)))
    return parted.reshape(count, SLOTS, BS * BS)


def describe(a_parts, b_cols, c_cols):
    cols = len(a_parts)
    total = -(-(2 * cols + 2 * SLOTS) // 8) * 8

    def placed(part, at):
        after = (total - at - part.shape[0], LANES - part.shape[1])
        return jnp.pad(part, ((at, after[0]), (0, after[1])), constant_values=-1)

    own = jnp.maximum(placed(c_cols, 2 * cols), placed(b_cols, 2 * cols + SLOTS))
    told = lax.optimization_barrier(jnp.maximum(own, placed(a_parts[0][:, 0, :], 0)))
    for h in range(1, cols):
        told = jnp.maximum(told, placed(a_parts[h][:, 0, :], 2 * h))
    return told


def offers(told, cols, row_count):
    start = 2 * cols + SLOTS
    rows = told[pl.ds(start, SLOTS), :]
    lane = iota((1, LANES), 1)
    result = rows[0:1]
    for n in range(1, SLOTS):
        moved = pltpu.roll(rows, n * row_count, 1)[n : n + 1]
        result = jnp.where(lane // row_count == n, moved, result)
    return result


def iota(shape, axis):
    return lax.broadcasted_iota(I32, shape, axis)


def along_lanes(left, right):
    return lax.dot_general(
        left.astype(BF16), right.astype(BF16), (((1,), (1,)), ((), ())), preferred_element_type=F32
    )


def turn_to_columns(rows, first, count):
    pick = (iota((count, LANES), 0) + first == iota((count, LANES), 1)).astype(BF16)
    return lax.dot_general(
        pick,
        rows.astype(F32).astype(BF16),
        (((1,), (1,)), ((), ())),
        preferred_element_type=F32,
    )


def matches(receiver, offered, holder, cols, row_count, first_slot, a_slots):
    turned = 2 * (holder ^ lax.axis_index("col"))
    rows = [receiver[pl.ds(turned, 1), :], receiver[pl.ds(turned + 1, 1), :]]
    rows += [receiver[pl.ds(2 * cols, SLOTS), :]]
    rows = jnp.concatenate(rows + [jnp.zeros((8 - 2 - SLOTS, LANES), I32)], axis=0)
    kept_columns = turn_to_columns(rows, 0, row_count)
    if isinstance(first_slot, int) and first_slot == 0 and a_slots == row_count:
        slot_columns = kept_columns
    else:
        slot_columns = turn_to_columns(rows, first_slot, a_slots)
    wanted = offered.astype(F32)
    kept = jnp.zeros((row_count, LANES), F32)
    which = jnp.zeros((row_count, LANES), F32)
    for m in range(SLOTS):
        column = kept_columns[:, 2 + m : 3 + m]
        equal = (column == wanted) & (wanted >= 0)
        kept = jnp.where(equal, 1.0, kept)
        which = jnp.where(equal, float(m), which)
    a_rows = slot_columns[:, 0:1]
    a_columns = slot_columns[:, 1:2]
    shape = (a_slots, row_count)
    by_row = (a_rows == iota(shape, 1).astype(F32)).astype(BF16)
    by_column = a_columns == (iota((a_slots, LANES), 1) % row_count).astype(F32)
    both = jnp.concatenate([kept, which], axis=1).astype(BF16)
    both = jnp.dot(by_row, both, preferred_element_type=F32)
    pairs = jnp.where(by_column & (both[:, :LANES] > 0.5), 1.0, 0.0)
    return pairs, both[:, LANES:], a_rows


def places(needed):
    before = (iota((LANES, LANES), 0) < iota((LANES, LANES), 1)).astype(BF16)
    many = jnp.broadcast_to(needed, (8, LANES)).astype(BF16)
    return jnp.dot(many, before, preferred_element_type=F32)[0:1]


def pack_kernel(first, peers, cols, a_slots, row_count, *refs):
    refs = list(refs)
    base = 0 if first else refs.pop(0)[0]
    told = refs[:peers]
    b_any = refs[peers]
    outs = refs[peers + 1 : 2 * peers]
    b_ref, picks, packed, sem = refs[2 * peers :]
    loading = pltpu.make_async_copy(b_any, b_ref, sem.at[0])
    loading.start()
    grid_row = lax.axis_index("row")
    per_col = peers // cols
    offered = offers(told[0], cols, row_count)
    first_slot = grid_row % per_col * a_slots if per_col > 1 else 0
    for d in range(1, peers):
        pairs, _, _ = matches(
            told[d], offered, grid_row // per_col, cols, row_count, first_slot, a_slots
        )
        needed = jnp.max(pairs, axis=0, keepdims=True)
        place = jnp.where(needed > 0.5, places(needed), -1.0).astype(I32)
        pick = (place == iota((CAPACITY, LANES), 0) + base).astype(BF16)
        picks[pl.ds((d - 1) * CAPACITY, CAPACITY), :] = pick
    steps = GROUP // SLOTS
    count = row_count * GROUP
    lane = iota((LANES, count), 1)
    spread = iota((LANES, count), 0) == lane % SLOTS * row_count + lane // GROUP
    spread = jnp.dot(picks[...], spread.astype(BF16), preferred_element_type=F32)
    lane = iota(spread.shape, 1)
    wanted = [jnp.where(lane // SLOTS % steps == t, spread, 0.0) for t in range(steps)]
    wanted = jnp.concatenate(wanted, axis=0).astype(BF16)
    total = spread.shape[0]
    loading.wait()
    for at in range(0, ROWS, steps):
        rows = b_ref[:, at * SLOTS : (at + steps) * SLOTS, :].reshape(count, LANES)
        found = jnp.dot(wanted, rows, preferred_element_type=F32)
        for t in range(steps):
            packed[:, at + t, :] = found[t * total : (t + 1) * total]
    for d in range(1, peers):
        out = outs[d - 1]
        for x in range(CAPACITY):
            out[pl.ds(x * ROWS, ROWS), :] = packed[(d - 1) * CAPACITY + x, 0:ROWS, :].astype(BF16)


def pack(base, told, b_rows, cols, row_count, a_slots):
    first = base is None
    peers = len(told)
    smem_spec = pl.BlockSpec(memory_space=SMEM)
    vmem_spec = pl.BlockSpec(memory_space=VMEM)
    given = [] if first else [base]
    return pl.pallas_call(
        functools.partial(pack_kernel, first, peers, cols, a_slots, row_count),
        out_shape=[jax.ShapeDtypeStruct((CAPACITY * ROWS, LANES), BF16)] * (peers - 1),
        in_specs=[smem_spec] * len(given)
        + [vmem_spec] * peers
        + [pl.BlockSpec(memory_space=pl.ANY)],
        out_specs=[vmem_spec] * (peers - 1),
        scratch_shapes=[
            VMEM(b_rows.shape, BF16),
            VMEM(((peers - 1) * CAPACITY, LANES), BF16),
            VMEM(((peers - 1) * CAPACITY, ROWS + PADDING, LANES), F32),
            pltpu.SemaphoreType.DMA((1,)),
        ],
        compiler_params=pltpu.CompilerParams(vmem_limit_bytes=32 << 20),
        cost_estimate=pl.CostEstimate(flops=1 << 20, bytes_accessed=4 << 20, transcendentals=0),
        name="pack",
    )(*given, *told, b_rows)


def list_kernel(cols, a_slots, row_count, peers, *refs):
    told, items = refs[:peers], refs[peers]
    grid_row = lax.axis_index("row")
    grid_col = lax.axis_index("col")
    per_col = peers // cols
    blocks = row_count * SLOTS
    lane = iota((1, LANES), 1)
    spot = iota((blocks, LANES), 0)
    before = (iota((LANES, LANES), 0) < iota((LANES, LANES), 1)).astype(BF16)
    below = (iota((blocks, blocks), 1) < iota((blocks, blocks), 0)).astype(BF16)
    same_slot = spot // row_count == iota((blocks, LANES), 1) // a_slots
    for d in range(peers):
        group = grid_row ^ d
        holder = group // per_col
        first_slot = group % per_col * a_slots if per_col > 1 else 0
        at = 2 * (holder ^ grid_col)
        slots = []
        for row in (told[0][pl.ds(at, 1), :], told[0][pl.ds(at + 1, 1), :]):
            if per_col > 1:
                row = pltpu.roll(row, (LANES - first_slot) % LANES, 1)
            spread = row
            for n in range(1, SLOTS):
                spread = jnp.where(lane // a_slots == n, pltpu.roll(row, n * a_slots, 1), spread)
            slots.append(jnp.where(lane < SLOTS * a_slots, spread, -1))
        a_rows, a_columns = slots
        offered = turn_to_columns(
            jnp.broadcast_to(offers(told[d], cols, row_count), (8, LANES)), 0, blocks
        )[:, 0:1]
        kept = jnp.zeros((blocks, LANES), F32)
        which = jnp.zeros((blocks, LANES), F32)
        for m in range(SLOTS):
            column = told[0][pl.ds(2 * cols + m, 1), :].astype(F32)
            equal = (column == offered) & (offered >= 0)
            kept = jnp.where(equal, 1.0, kept)
            which = jnp.where(equal, float(m), which)
        by_row = (a_rows == iota((row_count, LANES), 0)).astype(BF16)
        both = jnp.concatenate([kept, which], axis=0)[:, :row_count].astype(BF16)
        both = jnp.dot(both, by_row, preferred_element_type=F32)
        meets = (both[:blocks] > 0.5) & (a_columns == spot % row_count) & same_slot
        pairs = jnp.where(meets, 1.0, 0.0)
        if d == 0:
            place = spot.astype(F32)
        else:
            needed = jnp.max(pairs, axis=1, keepdims=True)
            many = jnp.broadcast_to(needed, (blocks, LANES)).astype(BF16)
            place = jnp.dot(below, many, preferred_element_type=F32)
        hit = jnp.sum(pairs, axis=0, keepdims=True)
        place = jnp.sum(pairs * place, axis=0, keepdims=True)
        out = jnp.sum(pairs * both[blocks:], axis=0, keepdims=True)
        out = out + a_rows.astype(F32) * SLOTS * hit
        rank = jnp.dot(
            jnp.broadcast_to(hit, (8, LANES)).astype(BF16), before, preferred_element_type=F32
        )[0:1]
        rank = jnp.where(hit > 0.5, rank, -1.0).astype(I32)
        chosen = rank == iota((LANES, LANES), 0)
        zero = jnp.zeros((1, LANES), F32)
        values = [(lane % a_slots).astype(F32) * hit, out, place] + [zero] * 5
        listed = along_lanes(jnp.concatenate(values, axis=0), chosen.astype(F32)).astype(I32)
        a_slot = holder * per_col * a_slots + first_slot + listed[0:1]
        word = (a_slot * 64 + listed[1:2]) * 64 + listed[2:3]
        total = jnp.sum(hit, axis=1, keepdims=True).astype(I32)
        items[pl.ds(d, 1), :] = jnp.where(lane == LANES - 1, total, word)


def work_list(told, cols, row_count, a_slots):
    peers = len(told)
    return pl.pallas_call(
        functools.partial(list_kernel, cols, a_slots, row_count, peers),
        out_shape=jax.ShapeDtypeStruct((-(-peers // 8) * 8, LANES), I32),
        in_specs=[pl.BlockSpec(memory_space=VMEM)] * peers,
        out_specs=pl.BlockSpec(memory_space=VMEM),
        cost_estimate=pl.CostEstimate(flops=1 << 10, bytes_accessed=1 << 10, transcendentals=0),
        name="work_list",
    )(*told)


def rounds_kernel(cols, a_slots, row_count, peers, *refs):
    told_refs, rounds, told = refs[:peers], refs[peers], refs[peers + 1]
    for d, ref in enumerate(told_refs):
        told[d, :, :] = ref[...]
    grid_row = lax.axis_index("row")
    per_col = peers // cols

    def one_pair(receiver, d, most):
        group = grid_row ^ receiver ^ d
        sender = receiver ^ d
        first_slot = group % per_col * a_slots if per_col > 1 else 0
        pairs, _, _ = matches(
            told.at[receiver],
            offers(told.at[sender], cols, row_count),
            group // per_col,
            cols,
            row_count,
            first_slot,
            a_slots,
        )
        needed = jnp.max(pairs, axis=0, keepdims=True)
        return jnp.maximum(most, jnp.sum(needed, axis=1, keepdims=True))

    most = jnp.zeros((1, 1), F32)
    if peers <= 4:
        for receiver in range(peers):
            for d in range(1, peers):
                most = one_pair(receiver, d, most)
    else:

        def step(at, most):
            return one_pair(at // (peers - 1), at % (peers - 1) + 1, most)

        most = lax.fori_loop(0, peers * (peers - 1), step, most)
    rounds[0] = (jnp.max(most).astype(I32) + CAPACITY - 1) // CAPACITY


def count_rounds(told, cols, row_count, a_slots):
    peers = len(told)
    return pl.pallas_call(
        functools.partial(rounds_kernel, cols, a_slots, row_count, peers),
        out_shape=jax.ShapeDtypeStruct((1,), I32),
        in_specs=[pl.BlockSpec(memory_space=VMEM)] * peers,
        out_specs=pl.BlockSpec(memory_space=SMEM),
        scratch_shapes=[VMEM((peers,) + told[0].shape, I32)],
        cost_estimate=pl.CostEstimate(flops=1 << 10, bytes_accessed=1 << 10, transcendentals=0),
        name="count_rounds",
    )(*told)


def add_products(items, a_ref, peer_refs, sums, window=None):
    low = iota((ROWS, LANES), 1) < BS
    nothing = jnp.zeros((ROWS, LANES), BF16)

    def add_one(word, used, b_ref):
        word = jnp.where(used, word, 0)
        place = word & 63
        target = (word >> 6) & 63
        if window is not None:
            place = place - window
            used = used & (place >= 0) & (place < CAPACITY)
            place = jnp.where(used, place, 0)
        a_at = pl.multiple_of((word >> 12) * ROWS, ROWS)
        b_at = pl.multiple_of(place * ROWS, ROWS)
        block = jnp.where(used, b_ref[pl.ds(b_at, ROWS), :], nothing)
        turned = jnp.concatenate([block[:, BS:], block[:, :BS]], axis=1)
        right = jnp.concatenate(
            [
                jnp.where(low, block, nothing),
                jnp.where(low, turned, nothing),
                jnp.where(low, nothing, turned),
                jnp.where(low, nothing, block),
            ],
            axis=0,
        )
        term = jnp.dot(a_ref[pl.ds(a_at, ROWS), :], right, preferred_element_type=F32)
        sums[target // SLOTS, pl.ds(target % SLOTS, ROWS, stride=SLOTS), :] += term

    for at in range(0, len(peer_refs), 3):
        chosen = peer_refs[at : at + 3]
        totals = [items[d, LANES - 1] for d, _ in chosen]
        longest = functools.reduce(jnp.maximum, totals)
        width = UNROLL if len(chosen) < 3 else UNROLL - 1

        def some_items(step, carry, chosen=chosen, totals=totals, width=width):
            for u in range(width):
                for (d, b_ref), total in zip(chosen, totals):
                    y = step * width + u
                    add_one(items[d, y], y < total, b_ref)
            return carry

        lax.fori_loop(0, (longest + width - 1) // width, some_items, 0)


def stage_kernel(cols, *refs):
    a_refs, b_ref, items = refs[:cols], refs[cols], refs[cols + 1]
    a_out, sums, a_wide, wide, own = refs[cols + 2 :]
    wide[...] = b_ref[...].astype(F32)
    sums[...] = jnp.zeros_like(sums)
    row_count = wide.shape[0]
    for n in range(SLOTS):
        for k in range(row_count):
            block = wide[k, pl.ds(n, ROWS, stride=SLOTS), :].astype(BF16)
            own[pl.ds((n * row_count + k) * ROWS, ROWS), :] = block
    source = iota((LANES, LANES), 0)
    target = iota((LANES, LANES), 1)
    wanted = (target // BS) * BS + 2 * (target % ROWS) + (target // ROWS) % 2
    order = (source == wanted).astype(BF16)
    slots = a_refs[0].shape[1]
    grid_col = lax.axis_index("col")
    for t in range(ROWS):
        pieces = [ref[0, :, pl.ds(t * LANES, LANES)] for ref in a_refs]
        done = jnp.dot(jnp.concatenate(pieces, axis=0), order, preferred_element_type=F32)
        a_wide[:, t, :] = done
    for h in range(cols):
        first = (grid_col ^ h) * slots
        for s in range(slots):
            at = pl.multiple_of((first + s) * ROWS, ROWS)
            a_out[pl.ds(at, ROWS), :] = a_wide[h * slots + s, 0:ROWS, :].astype(BF16)
    add_products(items, a_out, [(0, own)], sums)


def stage(a_parts, b_rows, items):
    cols, slots = len(a_parts), a_parts[0].shape[1]
    vmem_spec = pl.BlockSpec(memory_space=VMEM)
    smem_spec = pl.BlockSpec(memory_space=SMEM)
    return pl.pallas_call(
        functools.partial(stage_kernel, cols),
        out_shape=(
            jax.ShapeDtypeStruct((cols * slots * ROWS, LANES), BF16),
            jax.ShapeDtypeStruct(b_rows.shape, F32),
        ),
        in_specs=[vmem_spec] * (cols + 1) + [smem_spec],
        out_specs=(vmem_spec,) * 2,
        scratch_shapes=[
            VMEM((cols * slots, ROWS + PADDING, LANES), F32),
            VMEM(b_rows.shape, F32),
            VMEM((b_rows.shape[0] * SLOTS * ROWS, LANES), BF16),
        ],
        compiler_params=pltpu.CompilerParams(vmem_limit_bytes=40 << 20),
        cost_estimate=pl.CostEstimate(flops=1 << 10, bytes_accessed=1 << 10, transcendentals=0),
        name="stage",
    )(*a_parts, b_rows, items)


def near_kernel(first, chosen, *refs):
    refs = list(refs)
    base = 0 if first else refs.pop(0)[0]
    items, a_ref = refs[:2]
    b_refs, sums = refs[3:-1], refs[-1]
    add_products(items, a_ref, list(zip(chosen, b_refs)), sums, window=base)


def near_products(base, chosen, items, a_ready, sums, b_parts):
    first = base is None
    smem_spec = pl.BlockSpec(memory_space=SMEM)
    vmem_spec = pl.BlockSpec(memory_space=VMEM)
    given = [] if first else [base]
    return pl.pallas_call(
        functools.partial(near_kernel, first, chosen),
        out_shape=jax.ShapeDtypeStruct(sums.shape, F32),
        in_specs=[smem_spec] * (len(given) + 1) + [vmem_spec] * (2 + len(chosen)),
        out_specs=vmem_spec,
        input_output_aliases={len(given) + 2: 0},
        compiler_params=pltpu.CompilerParams(vmem_limit_bytes=32 << 20),
        cost_estimate=pl.CostEstimate(flops=1 << 10, bytes_accessed=1 << 10, transcendentals=0),
        name="near_products",
    )(*given, items, a_ready, sums, *b_parts)


def multiply_kernel(first, chosen, *refs):
    refs = list(refs)
    base = 0 if first else refs.pop(0)[0]
    items, a_ref = refs[:2]
    b_refs = refs[3 : 3 + len(chosen)]
    sums, out, sem = refs[3 + len(chosen) :]
    add_products(items, a_ref, list(zip(chosen, b_refs)), sums, window=base)
    part = out.shape[0] // PIECES
    copies = [
        pltpu.make_async_copy(sums.at[pl.ds(p * part, part)], out.at[pl.ds(p * part, part)], sem.at[p])
        for p in range(PIECES)
    ]
    for copy in copies:
        copy.start()
    for copy in copies:
        copy.wait()


def multiply(base, chosen, items, a_ready, sums, b_parts):
    first = base is None
    smem_spec = pl.BlockSpec(memory_space=SMEM)
    vmem_spec = pl.BlockSpec(memory_space=VMEM)
    given = [] if first else [base]
    return pl.pallas_call(
        functools.partial(multiply_kernel, first, chosen),
        out_shape=[jax.ShapeDtypeStruct(sums.shape, F32)] * 2,
        in_specs=[smem_spec] * (len(given) + 1) + [vmem_spec] * (2 + len(chosen)),
        out_specs=[vmem_spec, pl.BlockSpec(memory_space=pl.ANY)],
        input_output_aliases={len(given) + 2: 0},
        scratch_shapes=[pltpu.SemaphoreType.DMA((PIECES,))],
        compiler_params=pltpu.CompilerParams(vmem_limit_bytes=32 << 20),
        cost_estimate=pl.CostEstimate(flops=1 << 26, bytes_accessed=4 << 20, transcendentals=0),
        name="multiply",
    )(*given, items, a_ready, sums, *b_parts)


def shards(a_blocks, a_index, b_blocks, b_cols, c_cols):
    rows = lax.axis_size("row")
    cols = lax.axis_size("col")
    a_slots = a_blocks.shape[1] * cols // rows
    row_count = b_blocks.shape[0]

    def send_rows(parts):
        far_first = range(len(parts), 0, -1)
        return [exchanged(parts[d - 1], "row", d) for d in far_first][::-1]

    def finish(base, sums, arrived):
        split = max(rows - 1, 1) - 1
        near, last = list(range(split + 1, rows)), list(range(split, 0, -1))
        sums = near_products(base, near, items, a_ready, sums, [arrived[d - 1] for d in near])
        return multiply(base, last, items, a_ready, sums, [arrived[d - 1] for d in last])

    index_parts = [a_index] + [exchanged(a_index, "col", h) for h in range(1, cols)]
    told = describe(index_parts, b_cols.T, c_cols.T)
    a_parts = [exchanged(a_blocks, "col", 1)]
    told, a_parts[0] = lax.optimization_barrier((told, a_parts[0]))
    for h in range(2, cols, 2):
        far = exchanged(a_blocks, "col", h)
        a_parts += [far, exchanged(a_blocks, "col", h + 1)]
    told = [told] + send_rows([told] * (rows - 1))
    b_rows = seen_by_rows(b_blocks)
    *a_parts, b_rows = lax.optimization_barrier((*a_parts, b_rows))
    packed = pack(None, told, b_rows, cols, row_count, a_slots)
    arrived = send_rows(packed)
    told_late = lax.optimization_barrier((told, packed[0]))[0]
    items = work_list(told_late, cols, row_count, a_slots)
    rounds = jnp.minimum(count_rounds(told_late, cols, row_count, a_slots)[0], LANES)
    a_ready, sums = stage([a_blocks] + a_parts, b_rows, items)
    sums, rounds = lax.optimization_barrier((sums, rounds))
    sums, out = finish(None, sums, arrived)

    def more(state):
        return state[0] < rounds

    def one_round(state):
        at, sums, _ = state
        base = jnp.reshape(at * CAPACITY, (1,))
        arrived = send_rows(pack(base, told, b_rows, cols, row_count, a_slots))
        return at + 1, *finish(base, sums, arrived)

    return seen_by_blocks(lax.while_loop(more, one_round, (jnp.int32(1), sums, out))[2])


def solution(mesh):
    return jax.shard_map(
        shards,
        mesh=mesh,
        in_specs=(
            P(("sys", "row"), "col", None),
            P(None, ("sys", "row"), "col"),
            P(("sys", "row"), "col", None),
            P(("sys", "row"), "col"),
            P(("sys", "row"), "col"),
        ),
        out_specs=P(("sys", "row"), "col", None),
        check_vma=False,
    )
```

```python
import functools

import jax
import jax.numpy as jnp
from jax import lax
from jax.experimental import pallas as pl
from jax.experimental.layout import Layout, with_layout_constraint
from jax.experimental.pallas import tpu as pltpu
from jax.sharding import PartitionSpec as P

BS = 64
LANES = 128
ROWS = BS * BS // LANES
GROUP = 16
PIECES = 4
PADDING = 8
CAPACITY = 16
UNROLL = 4
SLOTS = 4
VMEM = pltpu.VMEM
SMEM = pltpu.SMEM
BF16 = jnp.bfloat16
F32 = jnp.float32
I32 = jnp.int32


def exchanged(block, axis, distance):
    size = lax.axis_size(axis)
    return lax.ppermute(block, axis, [(i, i ^ distance) for i in range(size)])


def seen_by_rows(blocks):
    count = blocks.shape[0]
    parted = blocks.reshape(count, SLOTS, ROWS, LANES)
    parted = with_layout_constraint(parted, Layout(major_to_minor=(0, 2, 1, 3)))
    return parted.transpose(0, 2, 1, 3).reshape(count, ROWS * SLOTS, LANES)


def seen_by_blocks(rows):
    count = rows.shape[0]
    parted = rows.reshape(count, ROWS, SLOTS, LANES).transpose(0, 2, 1, 3)
    parted = with_layout_constraint(parted, Layout(major_to_minor=(0, 2, 1, 3)))
    return parted.reshape(count, SLOTS, BS * BS)


def describe(a_parts, b_cols, c_cols):
    cols = len(a_parts)
    total = -(-(2 * cols + 2 * SLOTS) // 8) * 8

    def placed(part, at):
        after = (total - at - part.shape[0], LANES - part.shape[1])
        return jnp.pad(part, ((at, after[0]), (0, after[1])), constant_values=-1)

    own = jnp.maximum(placed(c_cols, 2 * cols), placed(b_cols, 2 * cols + SLOTS))
    told = lax.optimization_barrier(jnp.maximum(own, placed(a_parts[0][:, 0, :], 0)))
    for h in range(1, cols):
        told = jnp.maximum(told, placed(a_parts[h][:, 0, :], 2 * h))
    return told


def offers(told, cols, row_count):
    start = 2 * cols + SLOTS
    rows = told[pl.ds(start, SLOTS), :]
    lane = iota((1, LANES), 1)
    result = rows[0:1]
    for n in range(1, SLOTS):
        moved = pltpu.roll(rows, n * row_count, 1)[n : n + 1]
        result = jnp.where(lane // row_count == n, moved, result)
    return result


def iota(shape, axis):
    return lax.broadcasted_iota(I32, shape, axis)


def along_lanes(left, right):
    return lax.dot_general(
        left.astype(BF16), right.astype(BF16), (((1,), (1,)), ((), ())), preferred_element_type=F32
    )


def turn_to_columns(rows, first, count):
    pick = (iota((count, LANES), 0) + first == iota((count, LANES), 1)).astype(BF16)
    return lax.dot_general(
        pick,
        rows.astype(F32).astype(BF16),
        (((1,), (1,)), ((), ())),
        preferred_element_type=F32,
    )


def matches(receiver, offered, holder, cols, row_count, first_slot, a_slots):
    turned = 2 * (holder ^ lax.axis_index("col"))
    rows = [receiver[pl.ds(turned, 1), :], receiver[pl.ds(turned + 1, 1), :]]
    rows += [receiver[pl.ds(2 * cols, SLOTS), :]]
    rows = jnp.concatenate(rows + [jnp.zeros((8 - 2 - SLOTS, LANES), I32)], axis=0)
    kept_columns = turn_to_columns(rows, 0, row_count)
    if isinstance(first_slot, int) and first_slot == 0 and a_slots == row_count:
        slot_columns = kept_columns
    else:
        slot_columns = turn_to_columns(rows, first_slot, a_slots)
    wanted = offered.astype(F32)
    kept = jnp.zeros((row_count, LANES), F32)
    which = jnp.zeros((row_count, LANES), F32)
    for m in range(SLOTS):
        column = kept_columns[:, 2 + m : 3 + m]
        equal = (column == wanted) & (wanted >= 0)
        kept = jnp.where(equal, 1.0, kept)
        which = jnp.where(equal, float(m), which)
    a_rows = slot_columns[:, 0:1]
    a_columns = slot_columns[:, 1:2]
    shape = (a_slots, row_count)
    by_row = (a_rows == iota(shape, 1).astype(F32)).astype(BF16)
    by_column = a_columns == (iota((a_slots, LANES), 1) % row_count).astype(F32)
    both = jnp.concatenate([kept, which], axis=1).astype(BF16)
    both = jnp.dot(by_row, both, preferred_element_type=F32)
    pairs = jnp.where(by_column & (both[:, :LANES] > 0.5), 1.0, 0.0)
    return pairs, both[:, LANES:], a_rows


def places(needed):
    before = (iota((LANES, LANES), 0) < iota((LANES, LANES), 1)).astype(BF16)
    many = jnp.broadcast_to(needed, (8, LANES)).astype(BF16)
    return jnp.dot(many, before, preferred_element_type=F32)[0:1]


def pack_kernel(first, load, chosen, peers, cols, a_slots, row_count, *refs):
    refs = list(refs)
    base = 0 if first else refs.pop(0)[0]
    count = len(chosen)
    told, refs = refs[: count + 1], refs[count + 1 :]
    b_ref, outs, refs = refs[0], refs[1 : count + 1], refs[count + 1 :]
    if load:
        b_any, b_ref, sem = b_ref, refs.pop(), refs.pop()
        loading = pltpu.make_async_copy(b_any, b_ref, sem.at[0])
        loading.start()
    picks, packed = refs
    grid_row = lax.axis_index("row")
    per_col = peers // cols
    offered = offers(told[0], cols, row_count)
    first_slot = grid_row % per_col * a_slots if per_col > 1 else 0
    for at in range(count):
        pairs, _, _ = matches(
            told[at + 1], offered, grid_row // per_col, cols, row_count, first_slot, a_slots
        )
        needed = jnp.max(pairs, axis=0, keepdims=True)
        place = jnp.where(needed > 0.5, places(needed), -1.0).astype(I32)
        pick = (place == iota((CAPACITY, LANES), 0) + base).astype(BF16)
        picks[pl.ds(at * CAPACITY, CAPACITY), :] = pick
    steps = GROUP // SLOTS
    depth = row_count * GROUP
    lane = iota((LANES, depth), 1)
    spread = iota((LANES, depth), 0) == lane % SLOTS * row_count + lane // GROUP
    spread = jnp.dot(picks[...], spread.astype(BF16), preferred_element_type=F32)
    lane = iota(spread.shape, 1)
    wanted = [jnp.where(lane // SLOTS % steps == t, spread, 0.0) for t in range(steps)]
    wanted = jnp.concatenate(wanted, axis=0).astype(BF16)
    total = spread.shape[0]
    if load:
        loading.wait()
    for at in range(0, ROWS, steps):
        rows = b_ref[:, at * SLOTS : (at + steps) * SLOTS, :].reshape(depth, LANES)
        found = jnp.dot(wanted, rows, preferred_element_type=F32)
        for t in range(steps):
            packed[:, at + t, :] = found[t * total : (t + 1) * total]
    for at in range(count):
        for x in range(CAPACITY):
            block = packed[at * CAPACITY + x, 0:ROWS, :].astype(BF16)
            outs[at][pl.ds(x * ROWS, ROWS), :] = block


def pack(base, load, chosen, told, b_rows, cols, row_count, a_slots):
    first = base is None
    peers = len(told)
    smem_spec = pl.BlockSpec(memory_space=SMEM)
    vmem_spec = pl.BlockSpec(memory_space=VMEM)
    given = [] if first else [base]
    message = jax.ShapeDtypeStruct((CAPACITY * ROWS, LANES), BF16)
    loaded = [pltpu.SemaphoreType.DMA((1,)), VMEM(b_rows.shape, BF16)] if load else []
    held = len(chosen) * CAPACITY
    return pl.pallas_call(
        functools.partial(pack_kernel, first, load, chosen, peers, cols, a_slots, row_count),
        out_shape=[message] * len(chosen),
        in_specs=[smem_spec] * len(given)
        + [vmem_spec] * (len(chosen) + 1)
        + [pl.BlockSpec(memory_space=pl.ANY) if load else vmem_spec],
        out_specs=[vmem_spec] * len(chosen),
        scratch_shapes=[VMEM((held, LANES), BF16), VMEM((held, ROWS + PADDING, LANES), F32)]
        + loaded,
        compiler_params=pltpu.CompilerParams(vmem_limit_bytes=32 << 20),
        cost_estimate=pl.CostEstimate(flops=1 << 20, bytes_accessed=4 << 20, transcendentals=0),
        name="pack",
    )(*given, told[0], *[told[d] for d in chosen], b_rows)


def list_kernel(cols, a_slots, row_count, peers, *refs):
    told, items = refs[:peers], refs[peers]
    grid_row = lax.axis_index("row")
    grid_col = lax.axis_index("col")
    per_col = peers // cols
    blocks = row_count * SLOTS
    lane = iota((1, LANES), 1)
    spot = iota((blocks, LANES), 0)
    before = (iota((LANES, LANES), 0) < iota((LANES, LANES), 1)).astype(BF16)
    below = (iota((blocks, blocks), 1) < iota((blocks, blocks), 0)).astype(BF16)
    same_slot = spot // row_count == iota((blocks, LANES), 1) // a_slots
    for d in range(peers):
        group = grid_row ^ d
        holder = group // per_col
        first_slot = group % per_col * a_slots if per_col > 1 else 0
        at = 2 * (holder ^ grid_col)
        slots = []
        for row in (told[0][pl.ds(at, 1), :], told[0][pl.ds(at + 1, 1), :]):
            if per_col > 1:
                row = pltpu.roll(row, (LANES - first_slot) % LANES, 1)
            spread = row
            for n in range(1, SLOTS):
                spread = jnp.where(lane // a_slots == n, pltpu.roll(row, n * a_slots, 1), spread)
            slots.append(jnp.where(lane < SLOTS * a_slots, spread, -1))
        a_rows, a_columns = slots
        offered = turn_to_columns(
            jnp.broadcast_to(offers(told[d], cols, row_count), (8, LANES)), 0, blocks
        )[:, 0:1]
        kept = jnp.zeros((blocks, LANES), F32)
        which = jnp.zeros((blocks, LANES), F32)
        for m in range(SLOTS):
            column = told[0][pl.ds(2 * cols + m, 1), :].astype(F32)
            equal = (column == offered) & (offered >= 0)
            kept = jnp.where(equal, 1.0, kept)
            which = jnp.where(equal, float(m), which)
        by_row = (a_rows == iota((row_count, LANES), 0)).astype(BF16)
        both = jnp.concatenate([kept, which], axis=0)[:, :row_count].astype(BF16)
        both = jnp.dot(both, by_row, preferred_element_type=F32)
        meets = (both[:blocks] > 0.5) & (a_columns == spot % row_count) & same_slot
        pairs = jnp.where(meets, 1.0, 0.0)
        if d == 0:
            place = spot.astype(F32)
        else:
            needed = jnp.max(pairs, axis=1, keepdims=True)
            many = jnp.broadcast_to(needed, (blocks, LANES)).astype(BF16)
            place = jnp.dot(below, many, preferred_element_type=F32)
        hit = jnp.sum(pairs, axis=0, keepdims=True)
        place = jnp.sum(pairs * place, axis=0, keepdims=True)
        out = jnp.sum(pairs * both[blocks:], axis=0, keepdims=True)
        out = out + a_rows.astype(F32) * SLOTS * hit
        rank = jnp.dot(
            jnp.broadcast_to(hit, (8, LANES)).astype(BF16), before, preferred_element_type=F32
        )[0:1]
        rank = jnp.where(hit > 0.5, rank, -1.0).astype(I32)
        chosen = rank == iota((LANES, LANES), 0)
        zero = jnp.zeros((1, LANES), F32)
        values = [(lane % a_slots).astype(F32) * hit, out, place] + [zero] * 5
        listed = along_lanes(jnp.concatenate(values, axis=0), chosen.astype(F32)).astype(I32)
        a_slot = holder * per_col * a_slots + first_slot + listed[0:1]
        word = (a_slot * 64 + listed[1:2]) * 64 + listed[2:3]
        total = jnp.sum(hit, axis=1, keepdims=True).astype(I32)
        items[pl.ds(d, 1), :] = jnp.where(lane == LANES - 1, total, word)


def work_list(told, cols, row_count, a_slots):
    peers = len(told)
    return pl.pallas_call(
        functools.partial(list_kernel, cols, a_slots, row_count, peers),
        out_shape=jax.ShapeDtypeStruct((-(-peers // 8) * 8, LANES), I32),
        in_specs=[pl.BlockSpec(memory_space=VMEM)] * peers,
        out_specs=pl.BlockSpec(memory_space=VMEM),
        cost_estimate=pl.CostEstimate(flops=1 << 10, bytes_accessed=1 << 10, transcendentals=0),
        name="work_list",
    )(*told)


def rounds_kernel(cols, a_slots, row_count, peers, *refs):
    told_refs, rounds, told = refs[:peers], refs[peers], refs[peers + 1]
    for d, ref in enumerate(told_refs):
        told[d, :, :] = ref[...]
    grid_row = lax.axis_index("row")
    per_col = peers // cols

    def one_pair(receiver, d, most):
        group = grid_row ^ receiver ^ d
        sender = receiver ^ d
        first_slot = group % per_col * a_slots if per_col > 1 else 0
        pairs, _, _ = matches(
            told.at[receiver],
            offers(told.at[sender], cols, row_count),
            group // per_col,
            cols,
            row_count,
            first_slot,
            a_slots,
        )
        needed = jnp.max(pairs, axis=0, keepdims=True)
        return jnp.maximum(most, jnp.sum(needed, axis=1, keepdims=True))

    most = jnp.zeros((1, 1), F32)
    if peers <= 4:
        for receiver in range(peers):
            for d in range(1, peers):
                most = one_pair(receiver, d, most)
    else:

        def step(at, most):
            return one_pair(at // (peers - 1), at % (peers - 1) + 1, most)

        most = lax.fori_loop(0, peers * (peers - 1), step, most)
    rounds[0] = (jnp.max(most).astype(I32) + CAPACITY - 1) // CAPACITY


def count_rounds(told, cols, row_count, a_slots):
    peers = len(told)
    return pl.pallas_call(
        functools.partial(rounds_kernel, cols, a_slots, row_count, peers),
        out_shape=jax.ShapeDtypeStruct((1,), I32),
        in_specs=[pl.BlockSpec(memory_space=VMEM)] * peers,
        out_specs=pl.BlockSpec(memory_space=SMEM),
        scratch_shapes=[VMEM((peers,) + told[0].shape, I32)],
        cost_estimate=pl.CostEstimate(flops=1 << 10, bytes_accessed=1 << 10, transcendentals=0),
        name="count_rounds",
    )(*told)


def add_products(items, a_ref, peer_refs, sums, window=None):
    low = iota((ROWS, LANES), 1) < BS
    nothing = jnp.zeros((ROWS, LANES), BF16)

    def add_one(word, used, b_ref):
        word = jnp.where(used, word, 0)
        place = word & 63
        target = (word >> 6) & 63
        if window is not None:
            place = place - window
            used = used & (place >= 0) & (place < CAPACITY)
            place = jnp.where(used, place, 0)
        a_at = pl.multiple_of((word >> 12) * ROWS, ROWS)
        b_at = pl.multiple_of(place * ROWS, ROWS)
        block = jnp.where(used, b_ref[pl.ds(b_at, ROWS), :], nothing)
        turned = jnp.concatenate([block[:, BS:], block[:, :BS]], axis=1)
        right = jnp.concatenate(
            [
                jnp.where(low, block, nothing),
                jnp.where(low, turned, nothing),
                jnp.where(low, nothing, turned),
                jnp.where(low, nothing, block),
            ],
            axis=0,
        )
        term = jnp.dot(a_ref[pl.ds(a_at, ROWS), :], right, preferred_element_type=F32)
        sums[target // SLOTS, pl.ds(target % SLOTS, ROWS, stride=SLOTS), :] += term

    for at in range(0, len(peer_refs), 3):
        chosen = peer_refs[at : at + 3]
        totals = [items[d, LANES - 1] for d, _ in chosen]
        longest = functools.reduce(jnp.maximum, totals)
        width = UNROLL if len(chosen) < 3 else UNROLL - 1

        def some_items(step, carry, chosen=chosen, totals=totals, width=width):
            for u in range(width):
                for (d, b_ref), total in zip(chosen, totals):
                    y = step * width + u
                    add_one(items[d, y], y < total, b_ref)
            return carry

        lax.fori_loop(0, (longest + width - 1) // width, some_items, 0)


def stage_kernel(cols, *refs):
    a_refs, b_ref, items = refs[:cols], refs[cols], refs[cols + 1]
    a_out, sums, a_wide, wide, own = refs[cols + 2 :]
    wide[...] = b_ref[...].astype(F32)
    sums[...] = jnp.zeros_like(sums)
    row_count = wide.shape[0]
    for n in range(SLOTS):
        for k in range(row_count):
            block = wide[k, pl.ds(n, ROWS, stride=SLOTS), :].astype(BF16)
            own[pl.ds((n * row_count + k) * ROWS, ROWS), :] = block
    source = iota((LANES, LANES), 0)
    target = iota((LANES, LANES), 1)
    wanted = (target // BS) * BS + 2 * (target % ROWS) + (target // ROWS) % 2
    order = (source == wanted).astype(BF16)
    slots = a_refs[0].shape[1]
    grid_col = lax.axis_index("col")
    for t in range(ROWS):
        pieces = [ref[0, :, pl.ds(t * LANES, LANES)] for ref in a_refs]
        done = jnp.dot(jnp.concatenate(pieces, axis=0), order, preferred_element_type=F32)
        a_wide[:, t, :] = done
    for h in range(cols):
        first = (grid_col ^ h) * slots
        for s in range(slots):
            at = pl.multiple_of((first + s) * ROWS, ROWS)
            a_out[pl.ds(at, ROWS), :] = a_wide[h * slots + s, 0:ROWS, :].astype(BF16)
    add_products(items, a_out, [(0, own)], sums)


def stage(a_parts, b_rows, items):
    cols, slots = len(a_parts), a_parts[0].shape[1]
    vmem_spec = pl.BlockSpec(memory_space=VMEM)
    smem_spec = pl.BlockSpec(memory_space=SMEM)
    return pl.pallas_call(
        functools.partial(stage_kernel, cols),
        out_shape=(
            jax.ShapeDtypeStruct((cols * slots * ROWS, LANES), BF16),
            jax.ShapeDtypeStruct(b_rows.shape, F32),
        ),
        in_specs=[vmem_spec] * (cols + 1) + [smem_spec],
        out_specs=(vmem_spec,) * 2,
        scratch_shapes=[
            VMEM((cols * slots, ROWS + PADDING, LANES), F32),
            VMEM(b_rows.shape, F32),
            VMEM((b_rows.shape[0] * SLOTS * ROWS, LANES), BF16),
        ],
        compiler_params=pltpu.CompilerParams(vmem_limit_bytes=40 << 20),
        cost_estimate=pl.CostEstimate(flops=1 << 10, bytes_accessed=1 << 10, transcendentals=0),
        name="stage",
    )(*a_parts, b_rows, items)


def near_kernel(first, chosen, *refs):
    refs = list(refs)
    base = 0 if first else refs.pop(0)[0]
    items, a_ref = refs[:2]
    b_refs, sums = refs[3:-1], refs[-1]
    add_products(items, a_ref, list(zip(chosen, b_refs)), sums, window=base)


def near_products(base, chosen, items, a_ready, sums, b_parts):
    first = base is None
    smem_spec = pl.BlockSpec(memory_space=SMEM)
    vmem_spec = pl.BlockSpec(memory_space=VMEM)
    given = [] if first else [base]
    return pl.pallas_call(
        functools.partial(near_kernel, first, chosen),
        out_shape=jax.ShapeDtypeStruct(sums.shape, F32),
        in_specs=[smem_spec] * (len(given) + 1) + [vmem_spec] * (2 + len(chosen)),
        out_specs=vmem_spec,
        input_output_aliases={len(given) + 2: 0},
        compiler_params=pltpu.CompilerParams(vmem_limit_bytes=32 << 20),
        cost_estimate=pl.CostEstimate(flops=1 << 10, bytes_accessed=1 << 10, transcendentals=0),
        name="near_products",
    )(*given, items, a_ready, sums, *b_parts)


def multiply_kernel(first, chosen, *refs):
    refs = list(refs)
    base = 0 if first else refs.pop(0)[0]
    items, a_ref = refs[:2]
    b_refs = refs[3 : 3 + len(chosen)]
    sums, out, sem = refs[3 + len(chosen) :]
    add_products(items, a_ref, list(zip(chosen, b_refs)), sums, window=base)
    part = out.shape[0] // PIECES
    copies = [
        pltpu.make_async_copy(sums.at[pl.ds(p * part, part)], out.at[pl.ds(p * part, part)], sem.at[p])
        for p in range(PIECES)
    ]
    for copy in copies:
        copy.start()
    for copy in copies:
        copy.wait()


def multiply(base, chosen, items, a_ready, sums, b_parts):
    first = base is None
    smem_spec = pl.BlockSpec(memory_space=SMEM)
    vmem_spec = pl.BlockSpec(memory_space=VMEM)
    given = [] if first else [base]
    return pl.pallas_call(
        functools.partial(multiply_kernel, first, chosen),
        out_shape=[jax.ShapeDtypeStruct(sums.shape, F32)] * 2,
        in_specs=[smem_spec] * (len(given) + 1) + [vmem_spec] * (2 + len(chosen)),
        out_specs=[vmem_spec, pl.BlockSpec(memory_space=pl.ANY)],
        input_output_aliases={len(given) + 2: 0},
        scratch_shapes=[pltpu.SemaphoreType.DMA((PIECES,))],
        compiler_params=pltpu.CompilerParams(vmem_limit_bytes=32 << 20),
        cost_estimate=pl.CostEstimate(flops=1 << 26, bytes_accessed=4 << 20, transcendentals=0),
        name="multiply",
    )(*given, items, a_ready, sums, *b_parts)


def shards(a_blocks, a_index, b_blocks, b_cols, c_cols):
    rows = lax.axis_size("row")
    cols = lax.axis_size("col")
    a_slots = a_blocks.shape[1] * cols // rows
    row_count = b_blocks.shape[0]

    def send_rows(parts):
        far_first = range(len(parts), 0, -1)
        return [exchanged(parts[d - 1], "row", d) for d in far_first][::-1]

    def finish(base, sums, arrived):
        split = max(rows - 1, 1) - 1
        near, last = list(range(split + 1, rows)), list(range(split, 0, -1))
        sums = near_products(base, near, items, a_ready, sums, [arrived[d - 1] for d in near])
        return multiply(base, last, items, a_ready, sums, [arrived[d - 1] for d in last])

    index_parts = [a_index] + [exchanged(a_index, "col", h) for h in range(1, cols)]
    told = describe(index_parts, b_cols.T, c_cols.T)
    a_parts = [exchanged(a_blocks, "col", 1)]
    told, a_parts[0] = lax.optimization_barrier((told, a_parts[0]))
    for h in range(2, cols, 2):
        far = exchanged(a_blocks, "col", h)
        a_parts += [far, exchanged(a_blocks, "col", h + 1)]
    told = [told] + send_rows([told] * (rows - 1))
    far = rows - 1
    others = list(range(1, far))
    b_rows = seen_by_rows(b_blocks)
    message = pack(None, True, [far], told, b_rows, cols, row_count, a_slots)[0]
    arrived_far = exchanged(message, "row", far)
    *a_parts, b_rows = lax.optimization_barrier((*a_parts, b_rows))
    packed = pack(None, False, others, told, b_rows, cols, row_count, a_slots)
    arrived = [exchanged(packed[d - 1], "row", d) for d in others[::-1]][::-1] + [arrived_far]
    told_late = lax.optimization_barrier((told, packed[0]))[0]
    items = work_list(told_late, cols, row_count, a_slots)
    rounds = jnp.minimum(count_rounds(told_late, cols, row_count, a_slots)[0], LANES)
    a_ready, sums = stage([a_blocks] + a_parts, b_rows, items)
    sums, rounds = lax.optimization_barrier((sums, rounds))
    sums, out = finish(None, sums, arrived)

    def more(state):
        return state[0] < rounds

    def one_round(state):
        at, sums, _ = state
        base = jnp.reshape(at * CAPACITY, (1,))
        arrived = send_rows(
            pack(base, False, list(range(1, rows)), told, b_rows, cols, row_count, a_slots)
        )
        return at + 1, *finish(base, sums, arrived)

    return seen_by_blocks(lax.while_loop(more, one_round, (jnp.int32(1), sums, out))[2])


def solution(mesh):
    return jax.shard_map(
        shards,
        mesh=mesh,
        in_specs=(
            P(("sys", "row"), "col", None),
            P(None, ("sys", "row"), "col"),
            P(("sys", "row"), "col", None),
            P(("sys", "row"), "col"),
            P(("sys", "row"), "col"),
        ),
        out_specs=P(("sys", "row"), "col", None),
        check_vma=False,
    )
```

```python
import functools

import jax
import jax.numpy as jnp
from jax import lax
from jax.experimental import pallas as pl
from jax.experimental.layout import Layout, with_layout_constraint
from jax.experimental.pallas import tpu as pltpu
from jax.sharding import PartitionSpec as P

BS = 64
LANES = 128
ROWS = BS * BS // LANES
GROUP = 16
PIECES = 4
PADDING = 8
CAPACITY = 16
UNROLL = 4
SLOTS = 4
VMEM = pltpu.VMEM
SMEM = pltpu.SMEM
BF16 = jnp.bfloat16
F32 = jnp.float32
I32 = jnp.int32


def exchanged(block, axis, distance):
    size = lax.axis_size(axis)
    return lax.ppermute(block, axis, [(i, i ^ distance) for i in range(size)])


def seen_by_rows(blocks):
    count = blocks.shape[0]
    parted = blocks.reshape(count, SLOTS, ROWS, LANES)
    parted = with_layout_constraint(parted, Layout(major_to_minor=(0, 2, 1, 3)))
    return parted.transpose(0, 2, 1, 3).reshape(count, ROWS * SLOTS, LANES)


def seen_by_blocks(rows):
    count = rows.shape[0]
    parted = rows.reshape(count, ROWS, SLOTS, LANES).transpose(0, 2, 1, 3)
    parted = with_layout_constraint(parted, Layout(major_to_minor=(0, 2, 1, 3)))
    return parted.reshape(count, SLOTS, BS * BS)


def describe(a_parts, b_cols, c_cols):
    cols = len(a_parts)
    total = -(-(2 * cols + 2 * SLOTS) // 8) * 8

    def placed(part, at):
        after = (total - at - part.shape[0], LANES - part.shape[1])
        return jnp.pad(part, ((at, after[0]), (0, after[1])), constant_values=-1)

    own = jnp.maximum(placed(c_cols, 2 * cols), placed(b_cols, 2 * cols + SLOTS))
    told = lax.optimization_barrier(jnp.maximum(own, placed(a_parts[0][:, 0, :], 0)))
    for h in range(1, cols):
        told = jnp.maximum(told, placed(a_parts[h][:, 0, :], 2 * h))
    return told


def offers(told, cols, row_count):
    start = 2 * cols + SLOTS
    rows = told[pl.ds(start, SLOTS), :]
    lane = iota((1, LANES), 1)
    result = rows[0:1]
    for n in range(1, SLOTS):
        moved = pltpu.roll(rows, n * row_count, 1)[n : n + 1]
        result = jnp.where(lane // row_count == n, moved, result)
    return result


def iota(shape, axis):
    return lax.broadcasted_iota(I32, shape, axis)


def along_lanes(left, right):
    return lax.dot_general(
        left.astype(BF16), right.astype(BF16), (((1,), (1,)), ((), ())), preferred_element_type=F32
    )


def turn_to_columns(rows, first, count):
    pick = (iota((count, LANES), 0) + first == iota((count, LANES), 1)).astype(BF16)
    return lax.dot_general(
        pick,
        rows.astype(F32).astype(BF16),
        (((1,), (1,)), ((), ())),
        preferred_element_type=F32,
    )


def matches(receiver, offered, holder, cols, row_count, first_slot, a_slots):
    turned = 2 * (holder ^ lax.axis_index("col"))
    rows = [receiver[pl.ds(turned, 1), :], receiver[pl.ds(turned + 1, 1), :]]
    rows += [receiver[pl.ds(2 * cols, SLOTS), :]]
    rows = jnp.concatenate(rows + [jnp.zeros((8 - 2 - SLOTS, LANES), I32)], axis=0)
    kept_columns = turn_to_columns(rows, 0, row_count)
    if isinstance(first_slot, int) and first_slot == 0 and a_slots == row_count:
        slot_columns = kept_columns
    else:
        slot_columns = turn_to_columns(rows, first_slot, a_slots)
    wanted = offered.astype(F32)
    kept = jnp.zeros((row_count, LANES), F32)
    which = jnp.zeros((row_count, LANES), F32)
    for m in range(SLOTS):
        column = kept_columns[:, 2 + m : 3 + m]
        equal = (column == wanted) & (wanted >= 0)
        kept = jnp.where(equal, 1.0, kept)
        which = jnp.where(equal, float(m), which)
    a_rows = slot_columns[:, 0:1]
    a_columns = slot_columns[:, 1:2]
    shape = (a_slots, row_count)
    by_row = (a_rows == iota(shape, 1).astype(F32)).astype(BF16)
    by_column = a_columns == (iota((a_slots, LANES), 1) % row_count).astype(F32)
    both = jnp.concatenate([kept, which], axis=1).astype(BF16)
    both = jnp.dot(by_row, both, preferred_element_type=F32)
    pairs = jnp.where(by_column & (both[:, :LANES] > 0.5), 1.0, 0.0)
    return pairs, both[:, LANES:], a_rows


def places(needed):
    before = (iota((LANES, LANES), 0) < iota((LANES, LANES), 1)).astype(BF16)
    many = jnp.broadcast_to(needed, (8, LANES)).astype(BF16)
    return jnp.dot(many, before, preferred_element_type=F32)[0:1]


def pack_kernel(first, load, chosen, peers, cols, a_slots, row_count, *refs):
    refs = list(refs)
    base = 0 if first else refs.pop(0)[0]
    count = len(chosen)
    told, refs = refs[: count + 1], refs[count + 1 :]
    b_ref, outs, refs = refs[0], refs[1 : count + 1], refs[count + 1 :]
    if load:
        b_any, b_ref, sem = b_ref, refs.pop(), refs.pop()
        loading = pltpu.make_async_copy(b_any, b_ref, sem.at[0])
        loading.start()
    picks, packed = refs
    grid_row = lax.axis_index("row")
    per_col = peers // cols
    offered = offers(told[0], cols, row_count)
    first_slot = grid_row % per_col * a_slots if per_col > 1 else 0
    for at in range(count):
        pairs, _, _ = matches(
            told[at + 1], offered, grid_row // per_col, cols, row_count, first_slot, a_slots
        )
        needed = jnp.max(pairs, axis=0, keepdims=True)
        place = jnp.where(needed > 0.5, places(needed), -1.0).astype(I32)
        pick = (place == iota((CAPACITY, LANES), 0) + base).astype(BF16)
        picks[pl.ds(at * CAPACITY, CAPACITY), :] = pick
    steps = GROUP // SLOTS
    depth = row_count * GROUP
    lane = iota((LANES, depth), 1)
    spread = iota((LANES, depth), 0) == lane % SLOTS * row_count + lane // GROUP
    spread = jnp.dot(picks[...], spread.astype(BF16), preferred_element_type=F32)
    lane = iota(spread.shape, 1)
    wanted = [jnp.where(lane // SLOTS % steps == t, spread, 0.0) for t in range(steps)]
    wanted = jnp.concatenate(wanted, axis=0).astype(BF16)
    total = spread.shape[0]
    if load:
        loading.wait()
    for at in range(0, ROWS, steps):
        rows = b_ref[:, at * SLOTS : (at + steps) * SLOTS, :].reshape(depth, LANES)
        found = jnp.dot(wanted, rows, preferred_element_type=F32)
        for t in range(steps):
            packed[:, at + t, :] = found[t * total : (t + 1) * total]
    for at in range(count):
        for x in range(CAPACITY):
            block = packed[at * CAPACITY + x, 0:ROWS, :].astype(BF16)
            outs[at][pl.ds(x * ROWS, ROWS), :] = block


def pack(base, load, chosen, told, b_rows, cols, row_count, a_slots):
    first = base is None
    peers = len(told)
    smem_spec = pl.BlockSpec(memory_space=SMEM)
    vmem_spec = pl.BlockSpec(memory_space=VMEM)
    given = [] if first else [base]
    message = jax.ShapeDtypeStruct((CAPACITY * ROWS, LANES), BF16)
    loaded = [pltpu.SemaphoreType.DMA((1,)), VMEM(b_rows.shape, BF16)] if load else []
    held = len(chosen) * CAPACITY
    return pl.pallas_call(
        functools.partial(pack_kernel, first, load, chosen, peers, cols, a_slots, row_count),
        out_shape=[message] * len(chosen),
        in_specs=[smem_spec] * len(given)
        + [vmem_spec] * (len(chosen) + 1)
        + [pl.BlockSpec(memory_space=pl.ANY) if load else vmem_spec],
        out_specs=[vmem_spec] * len(chosen),
        scratch_shapes=[VMEM((held, LANES), BF16), VMEM((held, ROWS + PADDING, LANES), F32)]
        + loaded,
        compiler_params=pltpu.CompilerParams(vmem_limit_bytes=32 << 20),
        cost_estimate=pl.CostEstimate(flops=1 << 20, bytes_accessed=4 << 20, transcendentals=0),
        name="pack",
    )(*given, told[0], *[told[d] for d in chosen], b_rows)


def list_kernel(cols, a_slots, row_count, peers, *refs):
    told, items = refs[:peers], refs[peers]
    grid_row = lax.axis_index("row")
    grid_col = lax.axis_index("col")
    per_col = peers // cols
    blocks = row_count * SLOTS
    lane = iota((1, LANES), 1)
    spot = iota((blocks, LANES), 0)
    before = (iota((LANES, LANES), 0) < iota((LANES, LANES), 1)).astype(BF16)
    below = (iota((blocks, blocks), 1) < iota((blocks, blocks), 0)).astype(BF16)
    same_slot = spot // row_count == iota((blocks, LANES), 1) // a_slots
    for d in range(peers):
        group = grid_row ^ d
        holder = group // per_col
        first_slot = group % per_col * a_slots if per_col > 1 else 0
        at = 2 * (holder ^ grid_col)
        slots = []
        for row in (told[0][pl.ds(at, 1), :], told[0][pl.ds(at + 1, 1), :]):
            if per_col > 1:
                row = pltpu.roll(row, (LANES - first_slot) % LANES, 1)
            spread = row
            for n in range(1, SLOTS):
                spread = jnp.where(lane // a_slots == n, pltpu.roll(row, n * a_slots, 1), spread)
            slots.append(jnp.where(lane < SLOTS * a_slots, spread, -1))
        a_rows, a_columns = slots
        offered = turn_to_columns(
            jnp.broadcast_to(offers(told[d], cols, row_count), (8, LANES)), 0, blocks
        )[:, 0:1]
        kept = jnp.zeros((blocks, LANES), F32)
        which = jnp.zeros((blocks, LANES), F32)
        for m in range(SLOTS):
            column = told[0][pl.ds(2 * cols + m, 1), :].astype(F32)
            equal = (column == offered) & (offered >= 0)
            kept = jnp.where(equal, 1.0, kept)
            which = jnp.where(equal, float(m), which)
        by_row = (a_rows == iota((row_count, LANES), 0)).astype(BF16)
        both = jnp.concatenate([kept, which], axis=0)[:, :row_count].astype(BF16)
        both = jnp.dot(both, by_row, preferred_element_type=F32)
        meets = (both[:blocks] > 0.5) & (a_columns == spot % row_count) & same_slot
        pairs = jnp.where(meets, 1.0, 0.0)
        if d == 0:
            place = spot.astype(F32)
        else:
            needed = jnp.max(pairs, axis=1, keepdims=True)
            many = jnp.broadcast_to(needed, (blocks, LANES)).astype(BF16)
            place = jnp.dot(below, many, preferred_element_type=F32)
        hit = jnp.sum(pairs, axis=0, keepdims=True)
        place = jnp.sum(pairs * place, axis=0, keepdims=True)
        out = jnp.sum(pairs * both[blocks:], axis=0, keepdims=True)
        out = out + a_rows.astype(F32) * SLOTS * hit
        rank = jnp.dot(
            jnp.broadcast_to(hit, (8, LANES)).astype(BF16), before, preferred_element_type=F32
        )[0:1]
        rank = jnp.where(hit > 0.5, rank, -1.0).astype(I32)
        chosen = rank == iota((LANES, LANES), 0)
        zero = jnp.zeros((1, LANES), F32)
        values = [(lane % a_slots).astype(F32) * hit, out, place] + [zero] * 5
        listed = along_lanes(jnp.concatenate(values, axis=0), chosen.astype(F32)).astype(I32)
        a_slot = holder * per_col * a_slots + first_slot + listed[0:1]
        word = (a_slot * 64 + listed[1:2]) * 64 + listed[2:3]
        total = jnp.sum(hit, axis=1, keepdims=True).astype(I32)
        items[pl.ds(d, 1), :] = jnp.where(lane == LANES - 1, total, word)


def rounds_kernel(cols, a_slots, row_count, peers, *refs):
    told_refs, rounds, told = refs[:peers], refs[peers], refs[peers + 1]
    for d, ref in enumerate(told_refs):
        told[d, :, :] = ref[...]
    grid_row = lax.axis_index("row")
    per_col = peers // cols

    def one_pair(receiver, d, most):
        group = grid_row ^ receiver ^ d
        sender = receiver ^ d
        first_slot = group % per_col * a_slots if per_col > 1 else 0
        pairs, _, _ = matches(
            told.at[receiver],
            offers(told.at[sender], cols, row_count),
            group // per_col,
            cols,
            row_count,
            first_slot,
            a_slots,
        )
        needed = jnp.max(pairs, axis=0, keepdims=True)
        return jnp.maximum(most, jnp.sum(needed, axis=1, keepdims=True))

    most = jnp.zeros((1, 1), F32)
    if peers <= 4:
        for receiver in range(peers):
            for d in range(1, peers):
                most = one_pair(receiver, d, most)
    else:

        def step(at, most):
            return one_pair(at // (peers - 1), at % (peers - 1) + 1, most)

        most = lax.fori_loop(0, peers * (peers - 1), step, most)
    rounds[0] = (jnp.max(most).astype(I32) + CAPACITY - 1) // CAPACITY


def plan_kernel(cols, a_slots, row_count, peers, *refs):
    told, (items, rounds, scratch) = refs[:peers], refs[peers:]
    list_kernel(cols, a_slots, row_count, peers, *told, items)
    rounds_kernel(cols, a_slots, row_count, peers, *told, rounds, scratch)


def plan(told, cols, row_count, a_slots):
    peers = len(told)
    return pl.pallas_call(
        functools.partial(plan_kernel, cols, a_slots, row_count, peers),
        out_shape=(
            jax.ShapeDtypeStruct((-(-peers // 8) * 8, LANES), I32),
            jax.ShapeDtypeStruct((1,), I32),
        ),
        in_specs=[pl.BlockSpec(memory_space=VMEM)] * peers,
        out_specs=(pl.BlockSpec(memory_space=VMEM), pl.BlockSpec(memory_space=SMEM)),
        scratch_shapes=[VMEM((peers,) + told[0].shape, I32)],
        cost_estimate=pl.CostEstimate(flops=1 << 10, bytes_accessed=1 << 10, transcendentals=0),
        name="plan",
    )(*told)


def add_products(items, a_ref, peer_refs, sums, window=None):
    low = iota((ROWS, LANES), 1) < BS
    nothing = jnp.zeros((ROWS, LANES), BF16)

    def add_one(word, used, b_ref):
        word = jnp.where(used, word, 0)
        place = word & 63
        target = (word >> 6) & 63
        if window is not None:
            place = place - window
            used = used & (place >= 0) & (place < CAPACITY)
            place = jnp.where(used, place, 0)
        a_at = pl.multiple_of((word >> 12) * ROWS, ROWS)
        b_at = pl.multiple_of(place * ROWS, ROWS)
        block = jnp.where(used, b_ref[pl.ds(b_at, ROWS), :], nothing)
        turned = jnp.concatenate([block[:, BS:], block[:, :BS]], axis=1)
        right = jnp.concatenate(
            [
                jnp.where(low, block, nothing),
                jnp.where(low, turned, nothing),
                jnp.where(low, nothing, turned),
                jnp.where(low, nothing, block),
            ],
            axis=0,
        )
        term = jnp.dot(a_ref[pl.ds(a_at, ROWS), :], right, preferred_element_type=F32)
        sums[target // SLOTS, pl.ds(target % SLOTS, ROWS, stride=SLOTS), :] += term

    for at in range(0, len(peer_refs), 3):
        chosen = peer_refs[at : at + 3]
        totals = [items[d, LANES - 1] for d, _ in chosen]
        longest = functools.reduce(jnp.maximum, totals)
        width = UNROLL if len(chosen) < 3 else UNROLL - 1

        def some_items(step, carry, chosen=chosen, totals=totals, width=width):
            for u in range(width):
                for (d, b_ref), total in zip(chosen, totals):
                    y = step * width + u
                    add_one(items[d, y], y < total, b_ref)
            return carry

        lax.fori_loop(0, (longest + width - 1) // width, some_items, 0)


def stage_kernel(cols, *refs):
    a_refs, b_ref, items = refs[:cols], refs[cols], refs[cols + 1]
    a_out, sums, a_wide, wide, own = refs[cols + 2 :]
    wide[...] = b_ref[...].astype(F32)
    sums[...] = jnp.zeros_like(sums)
    row_count = wide.shape[0]
    for n in range(SLOTS):
        for k in range(row_count):
            block = wide[k, pl.ds(n, ROWS, stride=SLOTS), :].astype(BF16)
            own[pl.ds((n * row_count + k) * ROWS, ROWS), :] = block
    source = iota((LANES, LANES), 0)
    target = iota((LANES, LANES), 1)
    wanted = (target // BS) * BS + 2 * (target % ROWS) + (target // ROWS) % 2
    order = (source == wanted).astype(BF16)
    slots = a_refs[0].shape[1]
    grid_col = lax.axis_index("col")
    for t in range(ROWS):
        pieces = [ref[0, :, pl.ds(t * LANES, LANES)] for ref in a_refs]
        done = jnp.dot(jnp.concatenate(pieces, axis=0), order, preferred_element_type=F32)
        a_wide[:, t, :] = done
    for h in range(cols):
        first = (grid_col ^ h) * slots
        for s in range(slots):
            at = pl.multiple_of((first + s) * ROWS, ROWS)
            a_out[pl.ds(at, ROWS), :] = a_wide[h * slots + s, 0:ROWS, :].astype(BF16)
    add_products(items, a_out, [(0, own)], sums)


def stage(a_parts, b_rows, items):
    cols, slots = len(a_parts), a_parts[0].shape[1]
    vmem_spec = pl.BlockSpec(memory_space=VMEM)
    smem_spec = pl.BlockSpec(memory_space=SMEM)
    return pl.pallas_call(
        functools.partial(stage_kernel, cols),
        out_shape=(
            jax.ShapeDtypeStruct((cols * slots * ROWS, LANES), BF16),
            jax.ShapeDtypeStruct(b_rows.shape, F32),
        ),
        in_specs=[vmem_spec] * (cols + 1) + [smem_spec],
        out_specs=(vmem_spec,) * 2,
        scratch_shapes=[
            VMEM((cols * slots, ROWS + PADDING, LANES), F32),
            VMEM(b_rows.shape, F32),
            VMEM((b_rows.shape[0] * SLOTS * ROWS, LANES), BF16),
        ],
        compiler_params=pltpu.CompilerParams(vmem_limit_bytes=40 << 20),
        cost_estimate=pl.CostEstimate(flops=1 << 10, bytes_accessed=1 << 10, transcendentals=0),
        name="stage",
    )(*a_parts, b_rows, items)


def near_kernel(first, chosen, *refs):
    refs = list(refs)
    base = 0 if first else refs.pop(0)[0]
    items, a_ref = refs[:2]
    b_refs, sums = refs[3:-1], refs[-1]
    add_products(items, a_ref, list(zip(chosen, b_refs)), sums, window=base)


def near_products(base, chosen, items, a_ready, sums, b_parts):
    first = base is None
    smem_spec = pl.BlockSpec(memory_space=SMEM)
    vmem_spec = pl.BlockSpec(memory_space=VMEM)
    given = [] if first else [base]
    return pl.pallas_call(
        functools.partial(near_kernel, first, chosen),
        out_shape=jax.ShapeDtypeStruct(sums.shape, F32),
        in_specs=[smem_spec] * (len(given) + 1) + [vmem_spec] * (2 + len(chosen)),
        out_specs=vmem_spec,
        input_output_aliases={len(given) + 2: 0},
        compiler_params=pltpu.CompilerParams(vmem_limit_bytes=32 << 20),
        cost_estimate=pl.CostEstimate(flops=1 << 10, bytes_accessed=1 << 10, transcendentals=0),
        name="near_products",
    )(*given, items, a_ready, sums, *b_parts)


def multiply_kernel(first, chosen, *refs):
    refs = list(refs)
    base = 0 if first else refs.pop(0)[0]
    items, a_ref = refs[:2]
    b_refs = refs[3 : 3 + len(chosen)]
    sums, out, sem = refs[3 + len(chosen) :]
    add_products(items, a_ref, list(zip(chosen, b_refs)), sums, window=base)
    part = out.shape[0] // PIECES
    copies = [
        pltpu.make_async_copy(sums.at[pl.ds(p * part, part)], out.at[pl.ds(p * part, part)], sem.at[p])
        for p in range(PIECES)
    ]
    for copy in copies:
        copy.start()
    for copy in copies:
        copy.wait()


def multiply(base, chosen, items, a_ready, sums, b_parts):
    first = base is None
    smem_spec = pl.BlockSpec(memory_space=SMEM)
    vmem_spec = pl.BlockSpec(memory_space=VMEM)
    given = [] if first else [base]
    return pl.pallas_call(
        functools.partial(multiply_kernel, first, chosen),
        out_shape=[jax.ShapeDtypeStruct(sums.shape, F32)] * 2,
        in_specs=[smem_spec] * (len(given) + 1) + [vmem_spec] * (2 + len(chosen)),
        out_specs=[vmem_spec, pl.BlockSpec(memory_space=pl.ANY)],
        input_output_aliases={len(given) + 2: 0},
        scratch_shapes=[pltpu.SemaphoreType.DMA((PIECES,))],
        compiler_params=pltpu.CompilerParams(vmem_limit_bytes=32 << 20),
        cost_estimate=pl.CostEstimate(flops=1 << 26, bytes_accessed=4 << 20, transcendentals=0),
        name="multiply",
    )(*given, items, a_ready, sums, *b_parts)


def shards(a_blocks, a_index, b_blocks, b_cols, c_cols):
    rows = lax.axis_size("row")
    cols = lax.axis_size("col")
    a_slots = a_blocks.shape[1] * cols // rows
    row_count = b_blocks.shape[0]

    def send_rows(parts):
        far_first = range(len(parts), 0, -1)
        return [exchanged(parts[d - 1], "row", d) for d in far_first][::-1]

    def finish(base, sums, arrived):
        split = max(rows - 1, 1) - 1
        near, last = list(range(split + 1, rows)), list(range(split, 0, -1))
        sums = near_products(base, near, items, a_ready, sums, [arrived[d - 1] for d in near])
        return multiply(base, last, items, a_ready, sums, [arrived[d - 1] for d in last])

    index_parts = [a_index] + [exchanged(a_index, "col", h) for h in range(1, cols)]
    told = describe(index_parts, b_cols.T, c_cols.T)
    a_parts = [exchanged(a_blocks, "col", 1)]
    told, a_parts[0] = lax.optimization_barrier((told, a_parts[0]))
    for h in range(2, cols, 2):
        far = exchanged(a_blocks, "col", h)
        a_parts += [far, exchanged(a_blocks, "col", h + 1)]
    told = [told] + send_rows([told] * (rows - 1))
    b_rows = seen_by_rows(b_blocks)
    arrived = []
    for d in range(rows - 1, 0, -1):
        message = pack(None, d == rows - 1, [d], told, b_rows, cols, row_count, a_slots)[0]
        arrived.insert(0, exchanged(message, "row", d))
        if d == rows - 1:
            *a_parts, b_rows = lax.optimization_barrier((*a_parts, b_rows))
    told_late = lax.optimization_barrier((told, message))[0]
    items, rounds = plan(told_late, cols, row_count, a_slots)
    rounds = jnp.minimum(rounds[0], LANES)
    a_ready, sums = stage([a_blocks] + a_parts, b_rows, items)
    sums, rounds = lax.optimization_barrier((sums, rounds))
    sums, out = finish(None, sums, arrived)

    def more(state):
        return state[0] < rounds

    def one_round(state):
        at, sums, _ = state
        base = jnp.reshape(at * CAPACITY, (1,))
        arrived = send_rows(
            pack(base, False, list(range(1, rows)), told, b_rows, cols, row_count, a_slots)
        )
        return at + 1, *finish(base, sums, arrived)

    return seen_by_blocks(lax.while_loop(more, one_round, (jnp.int32(1), sums, out))[2])


def solution(mesh):
    return jax.shard_map(
        shards,
        mesh=mesh,
        in_specs=(
            P(("sys", "row"), "col", None),
            P(None, ("sys", "row"), "col"),
            P(("sys", "row"), "col", None),
            P(("sys", "row"), "col"),
            P(("sys", "row"), "col"),
        ),
        out_specs=P(("sys", "row"), "col", None),
        check_vma=False,
    )
```

```python
import functools

import jax
import jax.numpy as jnp
from jax import lax
from jax.experimental import pallas as pl
from jax.experimental.layout import Layout, with_layout_constraint
from jax.experimental.pallas import tpu as pltpu
from jax.sharding import PartitionSpec as P

BS = 64
LANES = 128
ROWS = BS * BS // LANES
GROUP = 16
PIECES = 4
PADDING = 8
CAPACITY = 16
UNROLL = 4
SLOTS = 4
VMEM = pltpu.VMEM
SMEM = pltpu.SMEM
BF16 = jnp.bfloat16
F32 = jnp.float32
I32 = jnp.int32


def exchanged(block, axis, distance):
    size = lax.axis_size(axis)
    return lax.ppermute(block, axis, [(i, i ^ distance) for i in range(size)])


def seen_by_rows(blocks):
    count = blocks.shape[0]
    parted = blocks.reshape(count, SLOTS, ROWS, LANES)
    parted = with_layout_constraint(parted, Layout(major_to_minor=(0, 2, 1, 3)))
    return parted.transpose(0, 2, 1, 3).reshape(count, ROWS * SLOTS, LANES)


def seen_by_blocks(rows):
    count = rows.shape[0]
    parted = rows.reshape(count, ROWS, SLOTS, LANES).transpose(0, 2, 1, 3)
    parted = with_layout_constraint(parted, Layout(major_to_minor=(0, 2, 1, 3)))
    return parted.reshape(count, SLOTS, BS * BS)


def describe(a_parts, b_cols, c_cols):
    cols = len(a_parts)
    total = -(-(2 * cols + 2 * SLOTS) // 8) * 8

    def placed(part, at):
        after = (total - at - part.shape[0], LANES - part.shape[1])
        return jnp.pad(part, ((at, after[0]), (0, after[1])), constant_values=-1)

    own = jnp.maximum(placed(c_cols, 2 * cols), placed(b_cols, 2 * cols + SLOTS))
    told = lax.optimization_barrier(jnp.maximum(own, placed(a_parts[0][:, 0, :], 0)))
    for h in range(1, cols):
        told = jnp.maximum(told, placed(a_parts[h][:, 0, :], 2 * h))
    return told


def offers(told, cols, row_count):
    start = 2 * cols + SLOTS
    rows = told[pl.ds(start, SLOTS), :]
    lane = iota((1, LANES), 1)
    result = rows[0:1]
    for n in range(1, SLOTS):
        moved = pltpu.roll(rows, n * row_count, 1)[n : n + 1]
        result = jnp.where(lane // row_count == n, moved, result)
    return result


def iota(shape, axis):
    return lax.broadcasted_iota(I32, shape, axis)


def along_lanes(left, right):
    return lax.dot_general(
        left.astype(BF16), right.astype(BF16), (((1,), (1,)), ((), ())), preferred_element_type=F32
    )


def turn_to_columns(rows, first, count):
    pick = (iota((count, LANES), 0) + first == iota((count, LANES), 1)).astype(BF16)
    return lax.dot_general(
        pick,
        rows.astype(F32).astype(BF16),
        (((1,), (1,)), ((), ())),
        preferred_element_type=F32,
    )


def matches(receiver, offered, holder, cols, row_count, first_slot, a_slots):
    turned = 2 * (holder ^ lax.axis_index("col"))
    rows = [receiver[pl.ds(turned, 1), :], receiver[pl.ds(turned + 1, 1), :]]
    rows += [receiver[pl.ds(2 * cols, SLOTS), :]]
    rows = jnp.concatenate(rows + [jnp.zeros((8 - 2 - SLOTS, LANES), I32)], axis=0)
    kept_columns = turn_to_columns(rows, 0, row_count)
    if isinstance(first_slot, int) and first_slot == 0 and a_slots == row_count:
        slot_columns = kept_columns
    else:
        slot_columns = turn_to_columns(rows, first_slot, a_slots)
    wanted = offered.astype(F32)
    kept = jnp.zeros((row_count, LANES), F32)
    which = jnp.zeros((row_count, LANES), F32)
    for m in range(SLOTS):
        column = kept_columns[:, 2 + m : 3 + m]
        equal = (column == wanted) & (wanted >= 0)
        kept = jnp.where(equal, 1.0, kept)
        which = jnp.where(equal, float(m), which)
    a_rows = slot_columns[:, 0:1]
    a_columns = slot_columns[:, 1:2]
    shape = (a_slots, row_count)
    by_row = (a_rows == iota(shape, 1).astype(F32)).astype(BF16)
    by_column = a_columns == (iota((a_slots, LANES), 1) % row_count).astype(F32)
    both = jnp.concatenate([kept, which], axis=1).astype(BF16)
    both = jnp.dot(by_row, both, preferred_element_type=F32)
    pairs = jnp.where(by_column & (both[:, :LANES] > 0.5), 1.0, 0.0)
    return pairs, both[:, LANES:], a_rows


def places(needed):
    before = (iota((LANES, LANES), 0) < iota((LANES, LANES), 1)).astype(BF16)
    many = jnp.broadcast_to(needed, (8, LANES)).astype(BF16)
    return jnp.dot(many, before, preferred_element_type=F32)[0:1]


def pack_kernel(first, load, chosen, peers, cols, a_slots, row_count, *refs):
    refs = list(refs)
    base = 0 if first else refs.pop(0)[0]
    count = len(chosen)
    told, refs = refs[: count + 1], refs[count + 1 :]
    b_ref, outs, refs = refs[0], refs[1 : count + 1], refs[count + 1 :]
    if load:
        b_any, b_ref, sem = b_ref, refs.pop(), refs.pop()
        loading = pltpu.make_async_copy(b_any, b_ref, sem.at[0])
        loading.start()
    picks, packed = refs
    grid_row = lax.axis_index("row")
    per_col = peers // cols
    offered = offers(told[0], cols, row_count)
    first_slot = grid_row % per_col * a_slots if per_col > 1 else 0
    for at in range(count):
        pairs, _, _ = matches(
            told[at + 1], offered, grid_row // per_col, cols, row_count, first_slot, a_slots
        )
        needed = jnp.max(pairs, axis=0, keepdims=True)
        place = jnp.where(needed > 0.5, places(needed), -1.0).astype(I32)
        pick = (place == iota((CAPACITY, LANES), 0) + base).astype(BF16)
        picks[pl.ds(at * CAPACITY, CAPACITY), :] = pick
    steps = GROUP // SLOTS
    depth = row_count * GROUP
    lane = iota((LANES, depth), 1)
    spread = iota((LANES, depth), 0) == lane % SLOTS * row_count + lane // GROUP
    spread = jnp.dot(picks[...], spread.astype(BF16), preferred_element_type=F32)
    lane = iota(spread.shape, 1)
    wanted = [jnp.where(lane // SLOTS % steps == t, spread, 0.0) for t in range(steps)]
    wanted = jnp.concatenate(wanted, axis=0).astype(BF16)
    total = spread.shape[0]
    if load:
        loading.wait()
    for at in range(0, ROWS, steps):
        rows = b_ref[:, at * SLOTS : (at + steps) * SLOTS, :].reshape(depth, LANES)
        found = jnp.dot(wanted, rows, preferred_element_type=F32)
        for t in range(steps):
            packed[:, at + t, :] = found[t * total : (t + 1) * total]
    for at in range(count):
        for x in range(CAPACITY):
            block = packed[at * CAPACITY + x, 0:ROWS, :].astype(BF16)
            outs[at][pl.ds(x * ROWS, ROWS), :] = block


def pack(base, load, chosen, told, b_rows, cols, row_count, a_slots):
    first = base is None
    peers = len(told)
    smem_spec = pl.BlockSpec(memory_space=SMEM)
    vmem_spec = pl.BlockSpec(memory_space=VMEM)
    given = [] if first else [base]
    message = jax.ShapeDtypeStruct((CAPACITY * ROWS, LANES), BF16)
    loaded = [pltpu.SemaphoreType.DMA((1,)), VMEM(b_rows.shape, BF16)] if load else []
    held = len(chosen) * CAPACITY
    return pl.pallas_call(
        functools.partial(pack_kernel, first, load, chosen, peers, cols, a_slots, row_count),
        out_shape=[message] * len(chosen),
        in_specs=[smem_spec] * len(given)
        + [vmem_spec] * (len(chosen) + 1)
        + [pl.BlockSpec(memory_space=pl.ANY) if load else vmem_spec],
        out_specs=[vmem_spec] * len(chosen),
        scratch_shapes=[VMEM((held, LANES), BF16), VMEM((held, ROWS + PADDING, LANES), F32)]
        + loaded,
        compiler_params=pltpu.CompilerParams(vmem_limit_bytes=32 << 20),
        cost_estimate=pl.CostEstimate(flops=1 << 20, bytes_accessed=4 << 20, transcendentals=0),
        name="pack",
    )(*given, told[0], *[told[d] for d in chosen], b_rows)


def list_kernel(cols, a_slots, row_count, peers, *refs):
    told, items = refs[:peers], refs[peers]
    grid_row = lax.axis_index("row")
    grid_col = lax.axis_index("col")
    per_col = peers // cols
    blocks = row_count * SLOTS
    lane = iota((1, LANES), 1)
    spot = iota((blocks, LANES), 0)
    before = (iota((LANES, LANES), 0) < iota((LANES, LANES), 1)).astype(BF16)
    below = (iota((blocks, blocks), 1) < iota((blocks, blocks), 0)).astype(BF16)
    same_slot = spot // row_count == iota((blocks, LANES), 1) // a_slots
    most = jnp.zeros((1, 1), F32)
    for d in range(peers):
        group = grid_row ^ d
        holder = group // per_col
        first_slot = group % per_col * a_slots if per_col > 1 else 0
        at = 2 * (holder ^ grid_col)
        slots = []
        for row in (told[0][pl.ds(at, 1), :], told[0][pl.ds(at + 1, 1), :]):
            if per_col > 1:
                row = pltpu.roll(row, (LANES - first_slot) % LANES, 1)
            spread = row
            for n in range(1, SLOTS):
                spread = jnp.where(lane // a_slots == n, pltpu.roll(row, n * a_slots, 1), spread)
            slots.append(jnp.where(lane < SLOTS * a_slots, spread, -1))
        a_rows, a_columns = slots
        offered = turn_to_columns(
            jnp.broadcast_to(offers(told[d], cols, row_count), (8, LANES)), 0, blocks
        )[:, 0:1]
        kept = jnp.zeros((blocks, LANES), F32)
        which = jnp.zeros((blocks, LANES), F32)
        for m in range(SLOTS):
            column = told[0][pl.ds(2 * cols + m, 1), :].astype(F32)
            equal = (column == offered) & (offered >= 0)
            kept = jnp.where(equal, 1.0, kept)
            which = jnp.where(equal, float(m), which)
        by_row = (a_rows == iota((row_count, LANES), 0)).astype(BF16)
        both = jnp.concatenate([kept, which], axis=0)[:, :row_count].astype(BF16)
        both = jnp.dot(both, by_row, preferred_element_type=F32)
        meets = (both[:blocks] > 0.5) & (a_columns == spot % row_count) & same_slot
        pairs = jnp.where(meets, 1.0, 0.0)
        if d == 0:
            place = spot.astype(F32)
        else:
            needed = jnp.max(pairs, axis=1, keepdims=True)
            many = jnp.broadcast_to(needed, (blocks, LANES)).astype(BF16)
            place = jnp.dot(below, many, preferred_element_type=F32)
            most = jnp.maximum(most, jnp.sum(needed, axis=0, keepdims=True))
        hit = jnp.sum(pairs, axis=0, keepdims=True)
        place = jnp.sum(pairs * place, axis=0, keepdims=True)
        out = jnp.sum(pairs * both[blocks:], axis=0, keepdims=True)
        out = out + a_rows.astype(F32) * SLOTS * hit
        rank = jnp.dot(
            jnp.broadcast_to(hit, (8, LANES)).astype(BF16), before, preferred_element_type=F32
        )[0:1]
        rank = jnp.where(hit > 0.5, rank, -1.0).astype(I32)
        chosen = rank == iota((LANES, LANES), 0)
        zero = jnp.zeros((1, LANES), F32)
        values = [(lane % a_slots).astype(F32) * hit, out, place] + [zero] * 5
        listed = along_lanes(jnp.concatenate(values, axis=0), chosen.astype(F32)).astype(I32)
        a_slot = holder * per_col * a_slots + first_slot + listed[0:1]
        word = (a_slot * 64 + listed[1:2]) * 64 + listed[2:3]
        total = jnp.sum(hit, axis=1, keepdims=True).astype(I32)
        items[pl.ds(d, 1), :] = jnp.where(lane == LANES - 1, total, word)
    return most


def rounds_kernel(cols, a_slots, row_count, peers, most, *refs):
    told_refs, rounds, told = refs[:peers], refs[peers], refs[peers + 1]
    for d, ref in enumerate(told_refs):
        told[d, :, :] = ref[...]
    grid_row = lax.axis_index("row")
    per_col = peers // cols

    def one_pair(receiver, d, most):
        group = grid_row ^ receiver ^ d
        sender = receiver ^ d
        first_slot = group % per_col * a_slots if per_col > 1 else 0
        pairs, _, _ = matches(
            told.at[receiver],
            offers(told.at[sender], cols, row_count),
            group // per_col,
            cols,
            row_count,
            first_slot,
            a_slots,
        )
        needed = jnp.max(pairs, axis=0, keepdims=True)
        return jnp.maximum(most, jnp.sum(needed, axis=1, keepdims=True))

    if peers <= 4:
        for receiver in range(1, peers):
            for d in range(1, peers):
                most = one_pair(receiver, d, most)
    else:

        def step(at, most):
            return one_pair(at // (peers - 1) + 1, at % (peers - 1) + 1, most)

        most = lax.fori_loop(0, (peers - 1) * (peers - 1), step, most)
    rounds[0] = (jnp.max(most).astype(I32) + CAPACITY - 1) // CAPACITY


def plan_kernel(cols, a_slots, row_count, peers, *refs):
    told, (items, rounds, scratch) = refs[:peers], refs[peers:]
    most = list_kernel(cols, a_slots, row_count, peers, *told, items)
    rounds_kernel(cols, a_slots, row_count, peers, most, *told, rounds, scratch)


def plan(told, cols, row_count, a_slots):
    peers = len(told)
    return pl.pallas_call(
        functools.partial(plan_kernel, cols, a_slots, row_count, peers),
        out_shape=(
            jax.ShapeDtypeStruct((-(-peers // 8) * 8, LANES), I32),
            jax.ShapeDtypeStruct((1,), I32),
        ),
        in_specs=[pl.BlockSpec(memory_space=VMEM)] * peers,
        out_specs=(pl.BlockSpec(memory_space=VMEM), pl.BlockSpec(memory_space=SMEM)),
        scratch_shapes=[VMEM((peers,) + told[0].shape, I32)],
        cost_estimate=pl.CostEstimate(flops=1 << 10, bytes_accessed=1 << 10, transcendentals=0),
        name="plan",
    )(*told)


def packed_loader(b_ref):
    return lambda place: b_ref[pl.ds(pl.multiple_of(place * ROWS, ROWS), ROWS), :]


def add_products(items, a_ref, peer_refs, sums, window=None):
    low = iota((ROWS, LANES), 1) < BS
    nothing = jnp.zeros((ROWS, LANES), BF16)

    def add_one(word, used, load):
        word = jnp.where(used, word, 0)
        place = word & 63
        target = (word >> 6) & 63
        if window is not None:
            place = place - window
            used = used & (place >= 0) & (place < CAPACITY)
            place = jnp.where(used, place, 0)
        a_at = pl.multiple_of((word >> 12) * ROWS, ROWS)
        block = jnp.where(used, load(place), nothing)
        turned = jnp.concatenate([block[:, BS:], block[:, :BS]], axis=1)
        right = jnp.concatenate(
            [
                jnp.where(low, block, nothing),
                jnp.where(low, turned, nothing),
                jnp.where(low, nothing, turned),
                jnp.where(low, nothing, block),
            ],
            axis=0,
        )
        term = jnp.dot(a_ref[pl.ds(a_at, ROWS), :], right, preferred_element_type=F32)
        sums[target // SLOTS, pl.ds(target % SLOTS, ROWS, stride=SLOTS), :] += term

    for at in range(0, len(peer_refs), 3):
        chosen = peer_refs[at : at + 3]
        totals = [items[d, LANES - 1] for d, _ in chosen]
        longest = functools.reduce(jnp.maximum, totals)
        width = UNROLL if len(chosen) < 3 else UNROLL - 1

        def some_items(step, carry, chosen=chosen, totals=totals, width=width):
            for u in range(width):
                for (d, load), total in zip(chosen, totals):
                    y = step * width + u
                    add_one(items[d, y], y < total, load)
            return carry

        lax.fori_loop(0, (longest + width - 1) // width, some_items, 0)


def stage_kernel(cols, *refs):
    a_refs, b_ref, items = refs[:cols], refs[cols], refs[cols + 1]
    a_out, sums, a_wide, wide = refs[cols + 2 :]
    wide[...] = b_ref[...].astype(F32)
    sums[...] = jnp.zeros_like(sums)
    row_count = wide.shape[0]

    def load_own(place):
        at = pl.ds(place // row_count, ROWS, stride=SLOTS)
        return wide[place % row_count, at, :].astype(BF16)

    source = iota((LANES, LANES), 0)
    target = iota((LANES, LANES), 1)
    wanted = (target // BS) * BS + 2 * (target % ROWS) + (target // ROWS) % 2
    order = (source == wanted).astype(BF16)
    slots = a_refs[0].shape[1]
    grid_col = lax.axis_index("col")
    for t in range(ROWS):
        pieces = [ref[0, :, pl.ds(t * LANES, LANES)] for ref in a_refs]
        done = jnp.dot(jnp.concatenate(pieces, axis=0), order, preferred_element_type=F32)
        a_wide[:, t, :] = done
    for h in range(cols):
        first = (grid_col ^ h) * slots
        for s in range(slots):
            at = pl.multiple_of((first + s) * ROWS, ROWS)
            a_out[pl.ds(at, ROWS), :] = a_wide[h * slots + s, 0:ROWS, :].astype(BF16)
    add_products(items, a_out, [(0, load_own)], sums)


def stage(a_parts, b_rows, items):
    cols, slots = len(a_parts), a_parts[0].shape[1]
    vmem_spec = pl.BlockSpec(memory_space=VMEM)
    smem_spec = pl.BlockSpec(memory_space=SMEM)
    return pl.pallas_call(
        functools.partial(stage_kernel, cols),
        out_shape=(
            jax.ShapeDtypeStruct((cols * slots * ROWS, LANES), BF16),
            jax.ShapeDtypeStruct(b_rows.shape, F32),
        ),
        in_specs=[vmem_spec] * (cols + 1) + [smem_spec],
        out_specs=(vmem_spec,) * 2,
        scratch_shapes=[
            VMEM((cols * slots, ROWS + PADDING, LANES), F32),
            VMEM(b_rows.shape, F32),
        ],
        compiler_params=pltpu.CompilerParams(vmem_limit_bytes=40 << 20),
        cost_estimate=pl.CostEstimate(flops=1 << 10, bytes_accessed=1 << 10, transcendentals=0),
        name="stage",
    )(*a_parts, b_rows, items)


def near_kernel(first, chosen, *refs):
    refs = list(refs)
    base = 0 if first else refs.pop(0)[0]
    items, a_ref = refs[:2]
    b_refs, sums = refs[3:-1], refs[-1]
    add_products(items, a_ref, list(zip(chosen, map(packed_loader, b_refs))), sums, window=base)


def near_products(base, chosen, items, a_ready, sums, b_parts):
    first = base is None
    smem_spec = pl.BlockSpec(memory_space=SMEM)
    vmem_spec = pl.BlockSpec(memory_space=VMEM)
    given = [] if first else [base]
    return pl.pallas_call(
        functools.partial(near_kernel, first, chosen),
        out_shape=jax.ShapeDtypeStruct(sums.shape, F32),
        in_specs=[smem_spec] * (len(given) + 1) + [vmem_spec] * (2 + len(chosen)),
        out_specs=vmem_spec,
        input_output_aliases={len(given) + 2: 0},
        compiler_params=pltpu.CompilerParams(vmem_limit_bytes=32 << 20),
        cost_estimate=pl.CostEstimate(flops=1 << 10, bytes_accessed=1 << 10, transcendentals=0),
        name="near_products",
    )(*given, items, a_ready, sums, *b_parts)


def multiply_kernel(first, chosen, *refs):
    refs = list(refs)
    base = 0 if first else refs.pop(0)[0]
    items, a_ref = refs[:2]
    b_refs = refs[3 : 3 + len(chosen)]
    sums, out, sem = refs[3 + len(chosen) :]
    add_products(items, a_ref, list(zip(chosen, map(packed_loader, b_refs))), sums, window=base)
    part = out.shape[0] // PIECES
    copies = [
        pltpu.make_async_copy(sums.at[pl.ds(p * part, part)], out.at[pl.ds(p * part, part)], sem.at[p])
        for p in range(PIECES)
    ]
    for copy in copies:
        copy.start()
    for copy in copies:
        copy.wait()


def multiply(base, chosen, items, a_ready, sums, b_parts):
    first = base is None
    smem_spec = pl.BlockSpec(memory_space=SMEM)
    vmem_spec = pl.BlockSpec(memory_space=VMEM)
    given = [] if first else [base]
    return pl.pallas_call(
        functools.partial(multiply_kernel, first, chosen),
        out_shape=[jax.ShapeDtypeStruct(sums.shape, F32)] * 2,
        in_specs=[smem_spec] * (len(given) + 1) + [vmem_spec] * (2 + len(chosen)),
        out_specs=[vmem_spec, pl.BlockSpec(memory_space=pl.ANY)],
        input_output_aliases={len(given) + 2: 0},
        scratch_shapes=[pltpu.SemaphoreType.DMA((PIECES,))],
        compiler_params=pltpu.CompilerParams(vmem_limit_bytes=32 << 20),
        cost_estimate=pl.CostEstimate(flops=1 << 26, bytes_accessed=4 << 20, transcendentals=0),
        name="multiply",
    )(*given, items, a_ready, sums, *b_parts)


def shards(a_blocks, a_index, b_blocks, b_cols, c_cols):
    rows = lax.axis_size("row")
    cols = lax.axis_size("col")
    a_slots = a_blocks.shape[1] * cols // rows
    row_count = b_blocks.shape[0]

    def send_rows(parts):
        far_first = range(len(parts), 0, -1)
        return [exchanged(parts[d - 1], "row", d) for d in far_first][::-1]

    def finish(base, sums, arrived):
        split = max(rows - 1, 1) - 1
        near, last = list(range(split + 1, rows)), list(range(split, 0, -1))
        sums = near_products(base, near, items, a_ready, sums, [arrived[d - 1] for d in near])
        return multiply(base, last, items, a_ready, sums, [arrived[d - 1] for d in last])

    index_parts = [a_index] + [exchanged(a_index, "col", h) for h in range(1, cols)]
    told = describe(index_parts, b_cols.T, c_cols.T)
    a_parts = [exchanged(a_blocks, "col", 1)]
    told, a_parts[0] = lax.optimization_barrier((told, a_parts[0]))
    for h in range(2, cols, 2):
        far = exchanged(a_blocks, "col", h)
        a_parts += [far, exchanged(a_blocks, "col", h + 1)]
    told = [told] + send_rows([told] * (rows - 1))
    b_rows = seen_by_rows(b_blocks)
    arrived = []
    for d in range(rows - 1, 0, -1):
        message = pack(None, d == rows - 1, [d], told, b_rows, cols, row_count, a_slots)[0]
        arrived.insert(0, exchanged(message, "row", d))
        if d == rows - 1:
            *a_parts, b_rows = lax.optimization_barrier((*a_parts, b_rows))
    told_late = lax.optimization_barrier((told, message))[0]
    items, rounds = plan(told_late, cols, row_count, a_slots)
    rounds = jnp.minimum(rounds[0], LANES)
    a_ready, sums = stage([a_blocks] + a_parts, b_rows, items)
    sums, rounds = lax.optimization_barrier((sums, rounds))
    sums, out = finish(None, sums, arrived)

    def more(state):
        return state[0] < rounds

    def one_round(state):
        at, sums, _ = state
        base = jnp.reshape(at * CAPACITY, (1,))
        arrived = send_rows(
            pack(base, False, list(range(1, rows)), told, b_rows, cols, row_count, a_slots)
        )
        return at + 1, *finish(base, sums, arrived)

    return seen_by_blocks(lax.while_loop(more, one_round, (jnp.int32(1), sums, out))[2])


def solution(mesh):
    return jax.shard_map(
        shards,
        mesh=mesh,
        in_specs=(
            P(("sys", "row"), "col", None),
            P(None, ("sys", "row"), "col"),
            P(("sys", "row"), "col", None),
            P(("sys", "row"), "col"),
            P(("sys", "row"), "col"),
        ),
        out_specs=P(("sys", "row"), "col", None),
        check_vma=False,
    )
```

```python
import functools

import jax
import jax.numpy as jnp
from jax import lax
from jax.experimental import pallas as pl
from jax.experimental.layout import Layout, with_layout_constraint
from jax.experimental.pallas import tpu as pltpu
from jax.sharding import PartitionSpec as P

BS = 64
LANES = 128
ROWS = BS * BS // LANES
GROUP = 16
PIECES = 4
PADDING = 8
CAPACITY = 16
UNROLL = 4
SLOTS = 4
VMEM = pltpu.VMEM
SMEM = pltpu.SMEM
BF16 = jnp.bfloat16
F32 = jnp.float32
I32 = jnp.int32


def exchanged(block, axis, distance):
    size = lax.axis_size(axis)
    return lax.ppermute(block, axis, [(i, i ^ distance) for i in range(size)])


def seen_by_rows(blocks):
    count = blocks.shape[0]
    parted = blocks.reshape(count, SLOTS, ROWS, LANES)
    parted = with_layout_constraint(parted, Layout(major_to_minor=(0, 2, 1, 3)))
    return parted.transpose(0, 2, 1, 3).reshape(count, ROWS * SLOTS, LANES)


def seen_by_blocks(rows):
    count = rows.shape[0]
    parted = rows.reshape(count, ROWS, SLOTS, LANES).transpose(0, 2, 1, 3)
    parted = with_layout_constraint(parted, Layout(major_to_minor=(0, 2, 1, 3)))
    return parted.reshape(count, SLOTS, BS * BS)


def describe(a_parts, b_cols, c_cols):
    cols = len(a_parts)
    total = -(-(2 * cols + 2 * SLOTS) // 8) * 8

    def placed(part, at):
        after = (total - at - part.shape[0], LANES - part.shape[1])
        return jnp.pad(part, ((at, after[0]), (0, after[1])), constant_values=-1)

    own = jnp.maximum(placed(c_cols, 2 * cols), placed(b_cols, 2 * cols + SLOTS))
    told = lax.optimization_barrier(jnp.maximum(own, placed(a_parts[0][:, 0, :], 0)))
    for h in range(1, cols):
        told = jnp.maximum(told, placed(a_parts[h][:, 0, :], 2 * h))
    return told


def offers(told, cols, row_count):
    start = 2 * cols + SLOTS
    rows = told[pl.ds(start, SLOTS), :]
    lane = iota((1, LANES), 1)
    result = rows[0:1]
    for n in range(1, SLOTS):
        moved = pltpu.roll(rows, n * row_count, 1)[n : n + 1]
        result = jnp.where(lane // row_count == n, moved, result)
    return result


def iota(shape, axis):
    return lax.broadcasted_iota(I32, shape, axis)


def along_lanes(left, right):
    return lax.dot_general(
        left.astype(BF16), right.astype(BF16), (((1,), (1,)), ((), ())), preferred_element_type=F32
    )


def turn_to_columns(rows, first, count):
    pick = (iota((count, LANES), 0) + first == iota((count, LANES), 1)).astype(BF16)
    return lax.dot_general(
        pick,
        rows.astype(F32).astype(BF16),
        (((1,), (1,)), ((), ())),
        preferred_element_type=F32,
    )


def matches(receiver, offered, holder, cols, row_count, first_slot, a_slots):
    turned = 2 * (holder ^ lax.axis_index("col"))
    rows = [receiver[pl.ds(turned, 1), :], receiver[pl.ds(turned + 1, 1), :]]
    rows += [receiver[pl.ds(2 * cols, SLOTS), :]]
    rows = jnp.concatenate(rows + [jnp.zeros((8 - 2 - SLOTS, LANES), I32)], axis=0)
    kept_columns = turn_to_columns(rows, 0, row_count)
    if isinstance(first_slot, int) and first_slot == 0 and a_slots == row_count:
        slot_columns = kept_columns
    else:
        slot_columns = turn_to_columns(rows, first_slot, a_slots)
    wanted = offered.astype(F32)
    kept = jnp.zeros((row_count, LANES), F32)
    which = jnp.zeros((row_count, LANES), F32)
    for m in range(SLOTS):
        column = kept_columns[:, 2 + m : 3 + m]
        equal = (column == wanted) & (wanted >= 0)
        kept = jnp.where(equal, 1.0, kept)
        which = jnp.where(equal, float(m), which)
    a_rows = slot_columns[:, 0:1]
    a_columns = slot_columns[:, 1:2]
    shape = (a_slots, row_count)
    by_row = (a_rows == iota(shape, 1).astype(F32)).astype(BF16)
    by_column = a_columns == (iota((a_slots, LANES), 1) % row_count).astype(F32)
    both = jnp.concatenate([kept, which], axis=1).astype(BF16)
    both = jnp.dot(by_row, both, preferred_element_type=F32)
    pairs = jnp.where(by_column & (both[:, :LANES] > 0.5), 1.0, 0.0)
    return pairs, both[:, LANES:], a_rows


def places(needed):
    before = (iota((LANES, LANES), 0) < iota((LANES, LANES), 1)).astype(BF16)
    many = jnp.broadcast_to(needed, (8, LANES)).astype(BF16)
    return jnp.dot(many, before, preferred_element_type=F32)[0:1]


def pack_kernel(first, load, chosen, peers, cols, a_slots, row_count, *refs):
    refs = list(refs)
    base = 0 if first else refs.pop(0)[0]
    count = len(chosen)
    told, refs = refs[: count + 1], refs[count + 1 :]
    b_ref, outs, refs = refs[0], refs[1 : count + 1], refs[count + 1 :]
    if load:
        b_any, b_ref, sem = b_ref, refs.pop(), refs.pop()
        loading = [
            pltpu.make_async_copy(
                b_any.at[:, pl.ds(at, GROUP), :], b_ref.at[:, pl.ds(at, GROUP), :], sem.at[at // GROUP]
            )
            for at in range(0, SLOTS * ROWS, GROUP)
        ]
        for copy in loading:
            copy.start()
    picks, packed = refs
    grid_row = lax.axis_index("row")
    per_col = peers // cols
    offered = offers(told[0], cols, row_count)
    first_slot = grid_row % per_col * a_slots if per_col > 1 else 0
    for at in range(count):
        pairs, _, _ = matches(
            told[at + 1], offered, grid_row // per_col, cols, row_count, first_slot, a_slots
        )
        needed = jnp.max(pairs, axis=0, keepdims=True)
        place = jnp.where(needed > 0.5, places(needed), -1.0).astype(I32)
        pick = (place == iota((CAPACITY, LANES), 0) + base).astype(BF16)
        picks[pl.ds(at * CAPACITY, CAPACITY), :] = pick
    steps = GROUP // SLOTS
    depth = row_count * GROUP
    lane = iota((LANES, depth), 1)
    spread = iota((LANES, depth), 0) == lane % SLOTS * row_count + lane // GROUP
    spread = jnp.dot(picks[...], spread.astype(BF16), preferred_element_type=F32)
    lane = iota(spread.shape, 1)
    wanted = [jnp.where(lane // SLOTS % steps == t, spread, 0.0) for t in range(steps)]
    wanted = jnp.concatenate(wanted, axis=0).astype(BF16)
    total = spread.shape[0]
    for at in range(0, ROWS, steps):
        if load:
            loading[at // steps].wait()
        rows = b_ref[:, at * SLOTS : (at + steps) * SLOTS, :].reshape(depth, LANES)
        found = jnp.dot(wanted, rows, preferred_element_type=F32)
        for t in range(steps):
            packed[:, at + t, :] = found[t * total : (t + 1) * total]
    for at in range(count):
        for x in range(CAPACITY):
            block = packed[at * CAPACITY + x, 0:ROWS, :].astype(BF16)
            outs[at][pl.ds(x * ROWS, ROWS), :] = block


def pack(base, load, chosen, told, b_rows, cols, row_count, a_slots):
    first = base is None
    peers = len(told)
    smem_spec = pl.BlockSpec(memory_space=SMEM)
    vmem_spec = pl.BlockSpec(memory_space=VMEM)
    given = [] if first else [base]
    message = jax.ShapeDtypeStruct((CAPACITY * ROWS, LANES), BF16)
    loaded = [pltpu.SemaphoreType.DMA((SLOTS * ROWS // GROUP,)), VMEM(b_rows.shape, BF16)] if load else []
    held = len(chosen) * CAPACITY
    return pl.pallas_call(
        functools.partial(pack_kernel, first, load, chosen, peers, cols, a_slots, row_count),
        out_shape=[message] * len(chosen),
        in_specs=[smem_spec] * len(given)
        + [vmem_spec] * (len(chosen) + 1)
        + [pl.BlockSpec(memory_space=pl.ANY) if load else vmem_spec],
        out_specs=[vmem_spec] * len(chosen),
        scratch_shapes=[VMEM((held, LANES), BF16), VMEM((held, ROWS + PADDING, LANES), F32)]
        + loaded,
        compiler_params=pltpu.CompilerParams(vmem_limit_bytes=32 << 20),
        cost_estimate=pl.CostEstimate(flops=1 << 20, bytes_accessed=4 << 20, transcendentals=0),
        name="pack",
    )(*given, told[0], *[told[d] for d in chosen], b_rows)


def list_kernel(cols, a_slots, row_count, peers, *refs):
    told, items = refs[:peers], refs[peers]
    grid_row = lax.axis_index("row")
    grid_col = lax.axis_index("col")
    per_col = peers // cols
    blocks = row_count * SLOTS
    lane = iota((1, LANES), 1)
    spot = iota((blocks, LANES), 0)
    before = (iota((LANES, LANES), 0) < iota((LANES, LANES), 1)).astype(BF16)
    below = (iota((blocks, blocks), 1) < iota((blocks, blocks), 0)).astype(BF16)
    same_slot = spot // row_count == iota((blocks, LANES), 1) // a_slots
    most = jnp.zeros((1, 1), F32)
    for d in range(peers):
        group = grid_row ^ d
        holder = group // per_col
        first_slot = group % per_col * a_slots if per_col > 1 else 0
        at = 2 * (holder ^ grid_col)
        slots = []
        for row in (told[0][pl.ds(at, 1), :], told[0][pl.ds(at + 1, 1), :]):
            if per_col > 1:
                row = pltpu.roll(row, (LANES - first_slot) % LANES, 1)
            spread = row
            for n in range(1, SLOTS):
                spread = jnp.where(lane // a_slots == n, pltpu.roll(row, n * a_slots, 1), spread)
            slots.append(jnp.where(lane < SLOTS * a_slots, spread, -1))
        a_rows, a_columns = slots
        offered = turn_to_columns(
            jnp.broadcast_to(offers(told[d], cols, row_count), (8, LANES)), 0, blocks
        )[:, 0:1]
        kept = jnp.zeros((blocks, LANES), F32)
        which = jnp.zeros((blocks, LANES), F32)
        for m in range(SLOTS):
            column = told[0][pl.ds(2 * cols + m, 1), :].astype(F32)
            equal = (column == offered) & (offered >= 0)
            kept = jnp.where(equal, 1.0, kept)
            which = jnp.where(equal, float(m), which)
        by_row = (a_rows == iota((row_count, LANES), 0)).astype(BF16)
        both = jnp.concatenate([kept, which], axis=0)[:, :row_count].astype(BF16)
        both = jnp.dot(both, by_row, preferred_element_type=F32)
        meets = (both[:blocks] > 0.5) & (a_columns == spot % row_count) & same_slot
        pairs = jnp.where(meets, 1.0, 0.0)
        if d == 0:
            place = spot.astype(F32)
        else:
            needed = jnp.max(pairs, axis=1, keepdims=True)
            many = jnp.broadcast_to(needed, (blocks, LANES)).astype(BF16)
            place = jnp.dot(below, many, preferred_element_type=F32)
            most = jnp.maximum(most, jnp.sum(needed, axis=0, keepdims=True))
        hit = jnp.sum(pairs, axis=0, keepdims=True)
        place = jnp.sum(pairs * place, axis=0, keepdims=True)
        out = jnp.sum(pairs * both[blocks:], axis=0, keepdims=True)
        out = out + a_rows.astype(F32) * SLOTS * hit
        rank = jnp.dot(
            jnp.broadcast_to(hit, (8, LANES)).astype(BF16), before, preferred_element_type=F32
        )[0:1]
        rank = jnp.where(hit > 0.5, rank, -1.0).astype(I32)
        chosen = rank == iota((LANES, LANES), 0)
        zero = jnp.zeros((1, LANES), F32)
        values = [(lane % a_slots).astype(F32) * hit, out, place] + [zero] * 5
        listed = along_lanes(jnp.concatenate(values, axis=0), chosen.astype(F32)).astype(I32)
        a_slot = holder * per_col * a_slots + first_slot + listed[0:1]
        word = (a_slot * 64 + listed[1:2]) * 64 + listed[2:3]
        total = jnp.sum(hit, axis=1, keepdims=True).astype(I32)
        items[pl.ds(d, 1), :] = jnp.where(lane == LANES - 1, total, word)
    return most


def rounds_kernel(cols, a_slots, row_count, peers, most, *refs):
    told_refs, rounds, told = refs[:peers], refs[peers], refs[peers + 1]
    for d, ref in enumerate(told_refs):
        told[d, :, :] = ref[...]
    grid_row = lax.axis_index("row")
    per_col = peers // cols

    def one_pair(receiver, d, most):
        group = grid_row ^ receiver ^ d
        sender = receiver ^ d
        first_slot = group % per_col * a_slots if per_col > 1 else 0
        pairs, _, _ = matches(
            told.at[receiver],
            offers(told.at[sender], cols, row_count),
            group // per_col,
            cols,
            row_count,
            first_slot,
            a_slots,
        )
        needed = jnp.max(pairs, axis=0, keepdims=True)
        return jnp.maximum(most, jnp.sum(needed, axis=1, keepdims=True))

    if peers <= 4:
        for receiver in range(1, peers):
            for d in range(1, peers):
                most = one_pair(receiver, d, most)
    else:

        def step(at, most):
            return one_pair(at // (peers - 1) + 1, at % (peers - 1) + 1, most)

        most = lax.fori_loop(0, (peers - 1) * (peers - 1), step, most)
    rounds[0] = (jnp.max(most).astype(I32) + CAPACITY - 1) // CAPACITY


def plan_kernel(cols, a_slots, row_count, peers, *refs):
    told, (items, rounds, scratch) = refs[:peers], refs[peers:]
    most = list_kernel(cols, a_slots, row_count, peers, *told, items)
    rounds_kernel(cols, a_slots, row_count, peers, most, *told, rounds, scratch)


def plan(told, cols, row_count, a_slots):
    peers = len(told)
    return pl.pallas_call(
        functools.partial(plan_kernel, cols, a_slots, row_count, peers),
        out_shape=(
            jax.ShapeDtypeStruct((-(-peers // 8) * 8, LANES), I32),
            jax.ShapeDtypeStruct((1,), I32),
        ),
        in_specs=[pl.BlockSpec(memory_space=VMEM)] * peers,
        out_specs=(pl.BlockSpec(memory_space=VMEM), pl.BlockSpec(memory_space=SMEM)),
        scratch_shapes=[VMEM((peers,) + told[0].shape, I32)],
        cost_estimate=pl.CostEstimate(flops=1 << 10, bytes_accessed=1 << 10, transcendentals=0),
        name="plan",
    )(*told)


def packed_loader(b_ref):
    return lambda place: b_ref[pl.ds(pl.multiple_of(place * ROWS, ROWS), ROWS), :]


def add_products(items, a_ref, peer_refs, sums, window=None):
    low = iota((ROWS, LANES), 1) < BS
    nothing = jnp.zeros((ROWS, LANES), BF16)

    def add_one(word, used, load):
        word = jnp.where(used, word, 0)
        place = word & 63
        target = (word >> 6) & 63
        if window is not None:
            place = place - window
            used = used & (place >= 0) & (place < CAPACITY)
            place = jnp.where(used, place, 0)
        a_at = pl.multiple_of((word >> 12) * ROWS, ROWS)
        block = jnp.where(used, load(place), nothing)
        turned = jnp.concatenate([block[:, BS:], block[:, :BS]], axis=1)
        right = jnp.concatenate(
            [
                jnp.where(low, block, nothing),
                jnp.where(low, turned, nothing),
                jnp.where(low, nothing, turned),
                jnp.where(low, nothing, block),
            ],
            axis=0,
        )
        term = jnp.dot(a_ref[pl.ds(a_at, ROWS), :], right, preferred_element_type=F32)
        sums[target // SLOTS, pl.ds(target % SLOTS, ROWS, stride=SLOTS), :] += term

    for at in range(0, len(peer_refs), 3):
        chosen = peer_refs[at : at + 3]
        totals = [items[d, LANES - 1] for d, _ in chosen]
        longest = functools.reduce(jnp.maximum, totals)
        width = UNROLL if len(chosen) < 3 else UNROLL - 1

        def some_items(step, carry, chosen=chosen, totals=totals, width=width):
            for u in range(width):
                for (d, load), total in zip(chosen, totals):
                    y = step * width + u
                    add_one(items[d, y], y < total, load)
            return carry

        lax.fori_loop(0, (longest + width - 1) // width, some_items, 0)


def stage_kernel(cols, *refs):
    a_refs, b_ref, items = refs[:cols], refs[cols], refs[cols + 1]
    a_out, sums, a_wide, wide = refs[cols + 2 :]
    wide[...] = b_ref[...].astype(F32)
    sums[...] = jnp.zeros_like(sums)
    row_count = wide.shape[0]

    def load_own(place):
        at = pl.ds(place // row_count, ROWS, stride=SLOTS)
        return wide[place % row_count, at, :].astype(BF16)

    source = iota((LANES, LANES), 0)
    target = iota((LANES, LANES), 1)
    wanted = (target // BS) * BS + 2 * (target % ROWS) + (target // ROWS) % 2
    order = (source == wanted).astype(BF16)
    slots = a_refs[0].shape[1]
    grid_col = lax.axis_index("col")
    for t in range(ROWS):
        pieces = [ref[0, :, pl.ds(t * LANES, LANES)] for ref in a_refs]
        done = jnp.dot(jnp.concatenate(pieces, axis=0), order, preferred_element_type=F32)
        a_wide[:, t, :] = done
    for h in range(cols):
        first = (grid_col ^ h) * slots
        for s in range(slots):
            at = pl.multiple_of((first + s) * ROWS, ROWS)
            a_out[pl.ds(at, ROWS), :] = a_wide[h * slots + s, 0:ROWS, :].astype(BF16)
    add_products(items, a_out, [(0, load_own)], sums)


def stage(a_parts, b_rows, items):
    cols, slots = len(a_parts), a_parts[0].shape[1]
    vmem_spec = pl.BlockSpec(memory_space=VMEM)
    smem_spec = pl.BlockSpec(memory_space=SMEM)
    return pl.pallas_call(
        functools.partial(stage_kernel, cols),
        out_shape=(
            jax.ShapeDtypeStruct((cols * slots * ROWS, LANES), BF16),
            jax.ShapeDtypeStruct(b_rows.shape, F32),
        ),
        in_specs=[vmem_spec] * (cols + 1) + [smem_spec],
        out_specs=(vmem_spec,) * 2,
        scratch_shapes=[
            VMEM((cols * slots, ROWS + PADDING, LANES), F32),
            VMEM(b_rows.shape, F32),
        ],
        compiler_params=pltpu.CompilerParams(vmem_limit_bytes=40 << 20),
        cost_estimate=pl.CostEstimate(flops=1 << 10, bytes_accessed=1 << 10, transcendentals=0),
        name="stage",
    )(*a_parts, b_rows, items)


def near_kernel(first, chosen, *refs):
    refs = list(refs)
    base = 0 if first else refs.pop(0)[0]
    items, a_ref = refs[:2]
    b_refs, sums = refs[3:-1], refs[-1]
    add_products(items, a_ref, list(zip(chosen, map(packed_loader, b_refs))), sums, window=base)


def near_products(base, chosen, items, a_ready, sums, b_parts):
    first = base is None
    smem_spec = pl.BlockSpec(memory_space=SMEM)
    vmem_spec = pl.BlockSpec(memory_space=VMEM)
    given = [] if first else [base]
    return pl.pallas_call(
        functools.partial(near_kernel, first, chosen),
        out_shape=jax.ShapeDtypeStruct(sums.shape, F32),
        in_specs=[smem_spec] * (len(given) + 1) + [vmem_spec] * (2 + len(chosen)),
        out_specs=vmem_spec,
        input_output_aliases={len(given) + 2: 0},
        compiler_params=pltpu.CompilerParams(vmem_limit_bytes=32 << 20),
        cost_estimate=pl.CostEstimate(flops=1 << 10, bytes_accessed=1 << 10, transcendentals=0),
        name="near_products",
    )(*given, items, a_ready, sums, *b_parts)


def multiply_kernel(first, chosen, *refs):
    refs = list(refs)
    base = 0 if first else refs.pop(0)[0]
    items, a_ref = refs[:2]
    b_refs = refs[3 : 3 + len(chosen)]
    sums, out, sem = refs[3 + len(chosen) :]
    add_products(items, a_ref, list(zip(chosen, map(packed_loader, b_refs))), sums, window=base)
    part = out.shape[0] // PIECES
    copies = [
        pltpu.make_async_copy(sums.at[pl.ds(p * part, part)], out.at[pl.ds(p * part, part)], sem.at[p])
        for p in range(PIECES)
    ]
    for copy in copies:
        copy.start()
    for copy in copies:
        copy.wait()


def multiply(base, chosen, items, a_ready, sums, b_parts):
    first = base is None
    smem_spec = pl.BlockSpec(memory_space=SMEM)
    vmem_spec = pl.BlockSpec(memory_space=VMEM)
    given = [] if first else [base]
    return pl.pallas_call(
        functools.partial(multiply_kernel, first, chosen),
        out_shape=[jax.ShapeDtypeStruct(sums.shape, F32)] * 2,
        in_specs=[smem_spec] * (len(given) + 1) + [vmem_spec] * (2 + len(chosen)),
        out_specs=[vmem_spec, pl.BlockSpec(memory_space=pl.ANY)],
        input_output_aliases={len(given) + 2: 0},
        scratch_shapes=[pltpu.SemaphoreType.DMA((PIECES,))],
        compiler_params=pltpu.CompilerParams(vmem_limit_bytes=32 << 20),
        cost_estimate=pl.CostEstimate(flops=1 << 26, bytes_accessed=4 << 20, transcendentals=0),
        name="multiply",
    )(*given, items, a_ready, sums, *b_parts)


def shards(a_blocks, a_index, b_blocks, b_cols, c_cols):
    rows = lax.axis_size("row")
    cols = lax.axis_size("col")
    a_slots = a_blocks.shape[1] * cols // rows
    row_count = b_blocks.shape[0]

    def send_rows(parts):
        far_first = range(len(parts), 0, -1)
        return [exchanged(parts[d - 1], "row", d) for d in far_first][::-1]

    def finish(base, sums, arrived):
        split = max(rows - 1, 1) - 1
        near, last = list(range(split + 1, rows)), list(range(split, 0, -1))
        sums = near_products(base, near, items, a_ready, sums, [arrived[d - 1] for d in near])
        return multiply(base, last, items, a_ready, sums, [arrived[d - 1] for d in last])

    index_parts = [a_index] + [exchanged(a_index, "col", h) for h in range(1, cols)]
    told = describe(index_parts, b_cols.T, c_cols.T)
    a_parts = [exchanged(a_blocks, "col", 1)]
    told, a_parts[0] = lax.optimization_barrier((told, a_parts[0]))
    for h in range(2, cols, 2):
        far = exchanged(a_blocks, "col", h)
        a_parts += [far, exchanged(a_blocks, "col", h + 1)]
    told = [told] + send_rows([told] * (rows - 1))
    b_rows = seen_by_rows(b_blocks)
    arrived = []
    for d in range(rows - 1, 0, -1):
        message = pack(None, d == rows - 1, [d], told, b_rows, cols, row_count, a_slots)[0]
        arrived.insert(0, exchanged(message, "row", d))
        if d == rows - 1:
            *a_parts, b_rows = lax.optimization_barrier((*a_parts, b_rows))
    told_late = lax.optimization_barrier((told, message))[0]
    items, rounds = plan(told_late, cols, row_count, a_slots)
    rounds = jnp.minimum(rounds[0], LANES)
    a_ready, sums = stage([a_blocks] + a_parts, b_rows, items)
    sums, rounds = lax.optimization_barrier((sums, rounds))
    sums, out = finish(None, sums, arrived)

    def more(state):
        return state[0] < rounds

    def one_round(state):
        at, sums, _ = state
        base = jnp.reshape(at * CAPACITY, (1,))
        arrived = send_rows(
            pack(base, False, list(range(1, rows)), told, b_rows, cols, row_count, a_slots)
        )
        return at + 1, *finish(base, sums, arrived)

    return seen_by_blocks(lax.while_loop(more, one_round, (jnp.int32(1), sums, out))[2])


def solution(mesh):
    return jax.shard_map(
        shards,
        mesh=mesh,
        in_specs=(
            P(("sys", "row"), "col", None),
            P(None, ("sys", "row"), "col"),
            P(("sys", "row"), "col", None),
            P(("sys", "row"), "col"),
            P(("sys", "row"), "col"),
        ),
        out_specs=P(("sys", "row"), "col", None),
        check_vma=False,
    )
```
